32 devices in a mesh: seq: 8 (over y, x, core), head: 4 (over z).
Axes of the slice: x: 2, y: 2, z: 4, core: 2. Of those that a mesh axis runs over, the one named last changes fastest.
Arguments:
- queries: bfloat16 [64, 64, 192], P('seq', 'head'), may hold values from -120 to 120
- new_latent: bfloat16 [64, 576], P('seq'), may hold values from -6 to 6
- cache: bfloat16 [16, 1024, 576], P('head', 'seq'), may hold values from -6 to 6
- lengths: int32 [16], replicated, may hold values from 8 to 1024, as said below
- w_uk: bfloat16 [64, 128, 512], P('head'), may hold values from -0.5 to 0.5
- w_uv: bfloat16 [64, 512, 128], P('head'), may hold values from -0.25 to 0.25
Outputs:
- attended: bfloat16 [64, 64, 128], P('seq', 'head')
The draws below stay inside these ranges and needn't reach their ends.
Inputs may be any that keep to these rules, and one draw needn't show every extreme that they name: `lengths`: each sequence keeps at least 8 cached slots; some sequence has exactly 1024.
All inputs are finite; a program needn't handle non-finite values.
Results may differ from the reference program's by a relative error of at most 0.039.
Values may be sent and summed in bfloat16 or wider, within the bound.
No kernel may reach another device: no remote copies, remote signals or barrier semaphores. Data moves between devices by JAX's collectives and lax.ppermute only.
A program may use at most 64 MiB of HBM per device.

```python
import jax
import jax.numpy as jnp
from jax import lax

HEADS = 64
NOPE = 128
ROPE = 64
LATENT = 512
VDIM = 128
SPEC = 4
SEQS = 16
CACHE_LEN = 1024
ROWS = 64


def draw_queries(key, part):
    shape = (ROWS, HEADS, NOPE + ROPE)
    values = jnp.clip(jax.random.normal(jax.random.fold_in(key, 32), shape, jnp.float32), -5.0, 5.0)
    return values.astype(jnp.bfloat16)


def draw_cache(key, part):
    shape = (SEQS, CACHE_LEN, LATENT + ROPE)
    values = jnp.clip(jax.random.normal(jax.random.fold_in(key, 42), shape, jnp.float32), -5.0, 5.0)
    return values.astype(jnp.bfloat16)


def draw_lengths(key, part):
    drawn = jax.random.randint(jax.random.fold_in(key, 21), (SEQS,), 8, CACHE_LEN + 1)
    longest = jax.random.randint(jax.random.fold_in(key, 22), (), 0, SEQS)
    return drawn.at[longest].set(CACHE_LEN).astype(jnp.int32)


def block_levels(own_key, dims, split, least, top_value):
    loudness, own = 1.0, jax.random.fold_in(own_key, 6)
    for position, blocks in split:
        draws = jnp.exp(jax.random.uniform(jax.random.fold_in(own, position), (blocks,), jnp.float32, least / len(split), top_value / len(split)))
        loudness = loudness * jnp.repeat(draws, dims[position] // blocks).reshape([-1 if axis == position else 1 for axis in range(len(dims))])
    return loudness


def gaussian(own_key, extent, width, bound, cuts=(), kind=jnp.bfloat16):
    result = width * jax.random.normal(own_key, extent, jnp.float32)
    if cuts:
        result = result * block_levels(own_key, extent, cuts, -0.22, 0.18)
    return jnp.clip(result, -bound, bound).astype(kind)


def setup_inputs(seed: int = 0) -> dict:
    streams_of = jax.random.split(jax.random.key(seed), 7)
    return {
        "queries": draw_queries(jax.random.fold_in(streams_of[6], 71), 0),
        "new_latent": gaussian(streams_of[1], (ROWS, LATENT + ROPE), 1.0, 6.0, ((0, 8),)),
        "cache": draw_cache(jax.random.fold_in(streams_of[6], 71), 0),
        "lengths": draw_lengths(jax.random.fold_in(streams_of[6], 71), 0),
        "w_uk": gaussian(streams_of[4], (HEADS, NOPE, LATENT), NOPE ** -0.5, 0.5, ((0, 4),)),
        "w_uv": gaussian(streams_of[5], (HEADS, LATENT, VDIM), LATENT ** -0.5, 0.25, ((0, 4),)),
    }


masked_value = -1.0e30


def reference(queries, new_latent, cache, lengths, w_uk, w_uv):
    row_count, head_count, _ = queries.shape
    q_nope = queries[:, :, :NOPE].astype(jnp.float32)
    absorbed = jnp.einsum("rhn,hnc->rhc", q_nope, w_uk.astype(jnp.float32)).astype(jnp.bfloat16)
    q_full = jnp.concatenate([absorbed, queries[:, :, NOPE:]], axis=2)
    q_seq = q_full.reshape(SEQS, SPEC * head_count, LATENT + ROPE)
    new_seq = new_latent.reshape(SEQS, SPEC, LATENT + ROPE)
    score_scale = (NOPE + ROPE) ** -0.5

    def one_sequence(packed):
        query_tile_block, key_tile_block, incoming_keys, length = packed
        scores = jnp.dot(query_tile_block, key_tile_block.T, preferred_element_type=jnp.float32) * score_scale
        visible = jnp.arange(key_tile_block.shape[0], dtype=jnp.int32)[None, :] < length
        fresh_scores = jnp.dot(query_tile_block, incoming_keys.T, preferred_element_type=jnp.float32) * score_scale
        row_spec = jnp.arange(SPEC * head_count, dtype=jnp.int32)[:, None] // head_count
        causal = jnp.arange(SPEC, dtype=jnp.int32)[None, :] <= row_spec
        row_top = jnp.maximum(jnp.max(jnp.where(visible, scores, masked_value), axis=1),
                              jnp.max(jnp.where(causal, fresh_scores, masked_value), axis=1))
        weights = jnp.where(visible, jnp.exp(scores - row_top[:, None]), 0.0)
        fresh_weights = jnp.where(causal, jnp.exp(fresh_scores - row_top[:, None]), 0.0)
        running_totals = jnp.sum(weights, axis=1) + jnp.sum(fresh_weights, axis=1)
        weighted = jnp.dot(weights.astype(jnp.bfloat16), key_tile_block[:, :LATENT], preferred_element_type=jnp.float32)
        weighted = weighted + jnp.dot(fresh_weights.astype(jnp.bfloat16), incoming_keys[:, :LATENT], preferred_element_type=jnp.float32)
        return weighted / running_totals[:, None]

    latent_output = lax.map(one_sequence, (q_seq, cache, new_seq, lengths))
    latent_output = latent_output.reshape(row_count, head_count, LATENT)
    return jnp.einsum("rhc,hcv->rhv", latent_output, w_uv.astype(jnp.float32),
                      precision=lax.Precision.HIGHEST).astype(jnp.bfloat16)
```

```python
import functools

import jax
import jax.numpy as jnp
from jax import lax
from jax.experimental import pallas as pl
from jax.experimental.pallas import tpu as pltpu
from jax.sharding import PartitionSpec as P

NOPE = 128
ROPE = 64
LATENT = 512
SPEC = 4
SCORE_SCALE = (NOPE + ROPE) ** (-0.5)
VMEM_LIMIT = 16 * 1024 * 1024

masked_value = -1e30


def pick_kernel(owners, copies, cache_ref, *rest):
    outs, sem = rest[:-1], rest[-1]
    group = lax.axis_index("seq") // copies
    moves = [
        pltpu.make_async_copy(cache_ref.at[group ^ k], outs[k], sem.at[k])
        for k in range(owners)
    ]
    for move in moves:
        move.start()
    for move in moves:
        move.wait()


def absorb_kernel(per_device, fresh_pad, q_ref, new_ref, w_ref, *outs):
    rows, heads, width = q_ref.shape
    q = q_ref[...].reshape(rows * heads, width)
    nope = q[:, :NOPE]
    own_head = lax.broadcasted_iota(jnp.int32, (rows * heads, NOPE), 0) % heads
    spread = jnp.concatenate(
        [jnp.where(own_head == h, nope, jnp.zeros_like(nope)) for h in range(heads)], axis=1
    )
    absorbed = jnp.dot(
        spread, w_ref[...].reshape(heads * NOPE, LATENT), preferred_element_type=jnp.float32
    ).astype(jnp.bfloat16)
    piece = SPEC * heads
    fresh = new_ref[...].astype(jnp.float32)
    fresh = jnp.concatenate(
        [fresh, jnp.zeros((fresh_pad - rows, fresh.shape[1]), jnp.float32)], axis=0
    ).astype(jnp.bfloat16)
    head_shard = lax.axis_index("head")
    for k in range(per_device):
        which = (head_shard + k) % per_device
        for a in range(per_device):

            @pl.when(which == a)
            def _():
                outs[k][:piece, :LATENT] = absorbed[a * piece : (a + 1) * piece]
                outs[k][:piece, LATENT:] = q[a * piece : (a + 1) * piece, NOPE:]

        if k == 0:
            outs[k][piece:, :] = fresh


def attend_kernel(owners, copies, per_device, heads, len_ref, *refs):
    block_count = owners * copies
    q_refs = refs[:per_device]
    key_refs = refs[per_device : per_device + block_count]
    outs = refs[per_device + block_count :]
    seq_index = lax.axis_index("seq")
    group, core = seq_index // copies, seq_index % copies
    sequence = lax.axis_index("head") * owners + group
    length = len_ref[sequence]
    piece = SPEC * heads
    q = jnp.concatenate([ref[:piece, :] for ref in q_refs], axis=0)
    fresh = q_refs[0][piece:, :]
    slots = key_refs[0].shape[1]
    lane = lax.broadcasted_iota(jnp.int32, (1, slots), 1)
    scores = []
    for k in range(owners):
        for e in range(copies):
            start = ((group ^ k) * copies + (core + copies - e) % copies) * slots
            s = jnp.dot(q, key_refs[k * copies + e][...], preferred_element_type=jnp.float32)
            scores.append(jnp.where(lane + start < length, s * SCORE_SCALE, masked_value))
    s = lax.dot_general(
        q, fresh, (((1,), (1,)), ((), ())), preferred_element_type=jnp.float32
    )
    row = lax.broadcasted_iota(jnp.int32, s.shape, 0)
    key = lax.broadcasted_iota(jnp.int32, s.shape, 1)
    causal = (key // SPEC == sequence % per_device) & (key % SPEC <= (row % piece) // heads)
    scores.append(jnp.where(causal, s * SCORE_SCALE, masked_value))
    top = functools.reduce(jnp.maximum, [jnp.max(s, axis=1, keepdims=True) for s in scores])
    total = jnp.zeros_like(top)
    out = jnp.zeros((q.shape[0], LATENT), jnp.float32)
    for s, ref in zip(scores, list(key_refs) + [None]):
        w = jnp.exp(s - top)
        total += jnp.sum(w, axis=1, keepdims=True)
        w = w.astype(jnp.bfloat16)
        if ref is None:
            out += jnp.dot(w, fresh[:, :LATENT], preferred_element_type=jnp.float32)
        else:
            out += lax.dot_general(
                w, ref[:LATENT, :], (((1,), (1,)), ((), ())), preferred_element_type=jnp.float32
            )
    out = (out / total).astype(jnp.bfloat16)
    for k in range(per_device):
        outs[k][...] = out[k * piece : (k + 1) * piece]


def project_kernel(per_device, w_ref, *refs):
    lat_refs, out_ref = refs[:-1], refs[-1]
    rows, heads, width = out_ref.shape
    piece = SPEC * heads
    head_shard = lax.axis_index("head")
    parts = []
    for a in range(per_device):
        part = lat_refs[0][...]
        for k in range(1, per_device):
            part = jnp.where((head_shard + k) % per_device == a, lat_refs[k][...], part)
        parts.append(part)
    latent = jnp.concatenate(parts, axis=0)
    own_head = lax.broadcasted_iota(jnp.int32, latent.shape, 0) % heads
    out = jnp.zeros((rows * heads, width), jnp.float32)
    for h in range(heads):
        out += jnp.dot(
            jnp.where(own_head == h, latent, jnp.zeros_like(latent)),
            w_ref[h],
            preferred_element_type=jnp.float32,
        )
    out_ref[...] = out.astype(out_ref.dtype).reshape(out_ref.shape)


def whole_sequences(seq_size, head_size, queries, new_latent, cache, lengths, w_uk, w_uv):
    rows, heads, _ = queries.shape
    owners, slots, width = cache.shape
    copies = seq_size // owners
    per_device = rows // SPEC
    piece = SPEC * heads
    fresh_pad = -(-rows // 16) * 16
    params = pltpu.CompilerParams(vmem_limit_bytes=VMEM_LIMIT)
    vmem = pl.BlockSpec(memory_space=pltpu.VMEM)
    anywhere = pl.BlockSpec(memory_space=pl.ANY)
    both = ("seq", "head")

    def flat(seq_index, head_index):
        return seq_index * head_size + head_index

    turned = jnp.swapaxes(cache, 1, 2)
    picked = pl.pallas_call(
        functools.partial(pick_kernel, owners, copies),
        out_shape=[jax.ShapeDtypeStruct((width, slots), cache.dtype)] * owners,
        in_specs=[anywhere],
        out_specs=[anywhere] * owners,
        scratch_shapes=[pltpu.SemaphoreType.DMA((owners,))],
        compiler_params=params,
    )(turned)
    keys = []
    for k in range(owners):
        for e in range(copies):
            if k == 0 and e == 0:
                keys.append(picked[0])
                continue
            perm = [
                (g * copies + t, (g ^ k) * copies + (t + e) % copies)
                for g in range(owners)
                for t in range(copies)
            ]
            keys.append(lax.ppermute(picked[k], "seq", perm))

    pieces = pl.pallas_call(
        functools.partial(absorb_kernel, per_device, fresh_pad),
        out_shape=[
            jax.ShapeDtypeStruct((piece + (fresh_pad if k == 0 else 0), width), cache.dtype)
            for k in range(per_device)
        ],
        in_specs=[vmem] * 3,
        out_specs=[vmem] * per_device,
        compiler_params=params,
    )(queries, new_latent, w_uk)
    there = []
    for k in range(per_device):
        perm = []
        for i in range(seq_size):
            for j in range(head_size):
                sequence = i * per_device + (j + k) % per_device
                target = (sequence % owners) * copies + j // per_device
                perm.append((flat(i, j), flat(target, sequence // owners)))
        there.append(perm)
    arrived = [lax.ppermute(pieces[k], both, there[k]) for k in range(per_device)]

    latent = pl.pallas_call(
        functools.partial(attend_kernel, owners, copies, per_device, heads),
        out_shape=[jax.ShapeDtypeStruct((piece, LATENT), jnp.bfloat16)] * per_device,
        in_specs=[pl.BlockSpec(memory_space=pltpu.SMEM)] + [vmem] * (per_device + len(keys)),
        out_specs=[vmem] * per_device,
        compiler_params=params,
    )(lengths, *arrived, *keys)

    back = [
        lax.ppermute(latent[k], both, [(b, a) for a, b in there[k]]) for k in range(per_device)
    ]
    return pl.pallas_call(
        functools.partial(project_kernel, per_device),
        out_shape=jax.ShapeDtypeStruct((rows, heads, w_uv.shape[2]), jnp.bfloat16),
        in_specs=[vmem] * (1 + per_device),
        out_specs=vmem,
        compiler_params=params,
    )(w_uv, *back)


def local_partial(
    query_tile_block,
    key_tile_block,
    incoming_keys,
    len_block,
    offset,
    own_first,
    score_scale,
    head_count,
):
    scores = (
        jnp.einsum(
            "vfa,vja->vfj", query_tile_block, key_tile_block, preferred_element_type=jnp.float32
        )
        * score_scale
    )
    positions = offset + lax.broadcasted_iota(jnp.int32, (1, 1, key_tile_block.shape[1]), 2)
    visible = positions < len_block[:, None, None]
    fresh_scores = (
        jnp.einsum(
            "vfa,vja->vfj", query_tile_block, incoming_keys, preferred_element_type=jnp.float32
        )
        * score_scale
    )
    spec_count = incoming_keys.shape[1]
    row_spec = (
        lax.broadcasted_iota(jnp.int32, (1, query_tile_block.shape[1], spec_count), 1) // head_count
    )
    key_spec = lax.broadcasted_iota(jnp.int32, (1, query_tile_block.shape[1], spec_count), 2)
    causal = (key_spec <= row_spec) & own_first
    row_top = jnp.maximum(
        jnp.max(jnp.where(visible, scores, masked_value), axis=2),
        jnp.max(jnp.where(causal, fresh_scores, masked_value), axis=2),
    )
    weights = jnp.where(visible, jnp.exp(scores - row_top[..., None]), 0.0)
    fresh_weights = jnp.where(causal, jnp.exp(fresh_scores - row_top[..., None]), 0.0)
    running_totals = jnp.sum(weights, axis=2) + jnp.sum(fresh_weights, axis=2)
    weighted = jnp.einsum(
        "mpu,mui->mpi",
        weights.astype(jnp.bfloat16),
        key_tile_block[:, :, :LATENT],
        preferred_element_type=jnp.float32,
    )
    weighted = weighted + jnp.einsum(
        "mpu,mui->mpi",
        fresh_weights.astype(jnp.bfloat16),
        incoming_keys[:, :, :LATENT],
        preferred_element_type=jnp.float32,
    )
    return (row_top, running_totals, weighted)


def project_values(latent_rows, value_weight):
    return jnp.einsum("rhc,hcv->rhv", latent_rows, value_weight, precision=lax.Precision.HIGHEST)


def split_positions(queries, new_latent, cache, lengths, w_uk, w_uv):
    own_rows, head_count, _ = queries.shape
    score_scale = (NOPE + ROPE) ** (-0.5)
    gathered, new_all = (
        lax.all_gather(queries, "seq", axis=0, tiled=True),
        lax.all_gather(new_latent, "seq", axis=0, tiled=True),
    )
    absorbed = jnp.einsum(
        "rhn,hnc->rhc", gathered[:, :, :NOPE], w_uk, preferred_element_type=jnp.float32
    ).astype(jnp.bfloat16)
    q_all = jnp.concatenate([absorbed, gathered[:, :, NOPE:]], axis=2)
    total_rows = q_all.shape[0]
    seq_count = total_rows // SPEC
    query_slots = SPEC * head_count
    q_seq = q_all.reshape(seq_count, query_slots, q_all.shape[2])
    new_seq = new_all.reshape(seq_count, SPEC, new_all.shape[1])
    seq_index = lax.axis_index("seq")
    offset = seq_index * cache.shape[1]
    own_first = seq_index == 0
    row_top, running_totals, weighted = local_partial(
        q_seq,
        lax.all_gather(cache, "head", axis=0, tiled=True),
        new_seq,
        lengths,
        offset,
        own_first,
        score_scale,
        head_count,
    )
    value_weight = w_uv.astype(jnp.float32)
    global_top = lax.pmax(row_top, "seq")
    factor = jnp.exp(row_top - global_top)
    scaled_totals = (running_totals * factor).reshape(total_rows, head_count)
    scaled_weighted = (weighted * factor[..., None]).reshape(total_rows, head_count, LATENT)
    row_totals, row_weighted = (
        lax.psum_scatter(scaled_totals, "seq", scatter_dimension=0, tiled=True),
        lax.psum_scatter(scaled_weighted, "seq", scatter_dimension=0, tiled=True),
    )
    latent_output = row_weighted / row_totals[..., None]
    result = project_values(latent_output, value_weight)
    return result.astype(jnp.bfloat16)


def shards(seq_size, head_size, queries, new_latent, cache, lengths, w_uk, w_uv):
    rows, owners = queries.shape[0], cache.shape[0]
    per_device = rows // SPEC
    if (
        rows % SPEC == 0
        and owners & (owners - 1) == 0
        and seq_size % owners == 0
        and head_size == per_device * (seq_size // owners)
    ):
        return whole_sequences(
            seq_size, head_size, queries, new_latent, cache, lengths, w_uk, w_uv
        )
    return split_positions(queries, new_latent, cache, lengths, w_uk, w_uv)


def solution(mesh):
    return jax.shard_map(
        functools.partial(shards, mesh.shape["seq"], mesh.shape["head"]),
        mesh=mesh,
        in_specs=(
            P("seq", "head", None),
            P("seq", None),
            P("head", "seq", None),
            P(),
            P("head", None, None),
            P("head", None, None),
        ),
        out_specs=P("seq", "head", None),
        check_vma=False,
    )
```

```python
import functools

import jax
import jax.numpy as jnp
from jax import lax
from jax.experimental import pallas as pl
from jax.experimental.pallas import tpu as pltpu
from jax.sharding import PartitionSpec as P

NOPE = 128
ROPE = 64
LATENT = 512
SPEC = 4
SCORE_SCALE = (NOPE + ROPE) ** (-0.5)
VMEM_LIMIT = 16 * 1024 * 1024

masked_value = -1e30


def absorb_kernel(per_device, fresh_pad, parts, q_hbm, new_hbm, w_hbm, *rest):
    outs, (q_ref, new_ref, w_ref, sem) = rest[:per_device], rest[per_device:]
    rows, heads, width = q_ref.shape
    share = heads // parts
    small = [
        pltpu.make_async_copy(q_hbm, q_ref, sem.at[parts]),
        pltpu.make_async_copy(new_hbm, new_ref, sem.at[parts + 1]),
    ]
    weights = [
        pltpu.make_async_copy(
            w_hbm.at[pl.ds(n * share, share)], w_ref.at[pl.ds(n * share, share)], sem.at[n]
        )
        for n in range(parts)
    ]
    for move in small + weights:
        move.start()
    for move in small:
        move.wait()
    q = q_ref[...].reshape(rows * heads, width)
    nope = q[:, :NOPE]
    own_head = lax.broadcasted_iota(jnp.int32, nope.shape, 0) % heads
    absorbed = jnp.zeros((rows * heads, LATENT), jnp.float32)
    for n in range(parts):
        spread = jnp.concatenate(
            [
                jnp.where(own_head == h, nope, jnp.zeros_like(nope))
                for h in range(n * share, (n + 1) * share)
            ],
            axis=1,
        )
        weights[n].wait()
        absorbed += jnp.dot(
            spread,
            w_ref[n * share : (n + 1) * share].reshape(share * NOPE, LATENT),
            preferred_element_type=jnp.float32,
        )
    absorbed = absorbed.astype(jnp.bfloat16)
    piece = SPEC * heads
    fresh = new_ref[...].astype(jnp.float32)
    fresh = jnp.concatenate(
        [fresh, jnp.zeros((fresh_pad - rows, fresh.shape[1]), jnp.float32)], axis=0
    ).astype(jnp.bfloat16)
    head_shard = lax.axis_index("head")
    for k in range(per_device):
        which = (head_shard + k) % per_device
        for a in range(per_device):

            @pl.when(which == a)
            def _():
                outs[k][:piece, :LATENT] = absorbed[a * piece : (a + 1) * piece]
                outs[k][:piece, LATENT:] = q[a * piece : (a + 1) * piece, NOPE:]

        if k == 0:
            outs[k][piece:, :] = fresh


def attend_kernel(owners, copies, per_device, heads, len_ref, *refs):
    q_refs = refs[:per_device]
    key_refs = refs[per_device : per_device + copies]
    outs = refs[per_device + copies :]
    seq_index = lax.axis_index("seq")
    group, core = seq_index // copies, seq_index % copies
    sequence = lax.axis_index("head") * owners + group
    length = len_ref[sequence]
    piece = SPEC * heads
    q = jnp.concatenate([ref[:piece, :] for ref in q_refs], axis=0)
    fresh = q_refs[0][piece:, :]
    slots = key_refs[0].shape[2]
    lane = lax.broadcasted_iota(jnp.int32, (1, slots), 1)
    scores = []
    for e in range(copies):
        for g in range(owners):
            start = (g * copies + (core + copies - e) % copies) * slots
            s = jnp.dot(q, key_refs[e][g], preferred_element_type=jnp.float32)
            scores.append(jnp.where(lane + start < length, s * SCORE_SCALE, masked_value))
    s = lax.dot_general(
        q, fresh, (((1,), (1,)), ((), ())), preferred_element_type=jnp.float32
    )
    row = lax.broadcasted_iota(jnp.int32, s.shape, 0)
    key = lax.broadcasted_iota(jnp.int32, s.shape, 1)
    causal = (key // SPEC == sequence % per_device) & (key % SPEC <= (row % piece) // heads)
    scores.append(jnp.where(causal, s * SCORE_SCALE, masked_value))
    top = functools.reduce(jnp.maximum, [jnp.max(s, axis=1, keepdims=True) for s in scores])
    total = jnp.zeros_like(top)
    out = jnp.zeros((q.shape[0], LATENT), jnp.float32)
    for n, s in enumerate(scores):
        w = jnp.exp(s - top)
        total += jnp.sum(w, axis=1, keepdims=True)
        w = w.astype(jnp.bfloat16)
        if n == owners * copies:
            out += jnp.dot(w, fresh[:, :LATENT], preferred_element_type=jnp.float32)
        else:
            out += lax.dot_general(
                w,
                key_refs[n // owners][n % owners, :LATENT, :],
                (((1,), (1,)), ((), ())),
                preferred_element_type=jnp.float32,
            )
    out = (out / total).astype(jnp.bfloat16)
    for k in range(per_device):
        outs[k][...] = out[k * piece : (k + 1) * piece]


def project_kernel(per_device, w_ref, *refs):
    lat_refs, out_ref = refs[:-1], refs[-1]
    rows, heads, width = out_ref.shape
    piece = SPEC * heads
    head_shard = lax.axis_index("head")
    parts = []
    for a in range(per_device):
        part = lat_refs[0][...]
        for k in range(1, per_device):
            part = jnp.where((head_shard + k) % per_device == a, lat_refs[k][...], part)
        parts.append(part)
    latent = jnp.concatenate(parts, axis=0)
    own_head = lax.broadcasted_iota(jnp.int32, latent.shape, 0) % heads
    out = jnp.zeros((rows * heads, width), jnp.float32)
    for h in range(heads):
        out += jnp.dot(
            jnp.where(own_head == h, latent, jnp.zeros_like(latent)),
            w_ref[h],
            preferred_element_type=jnp.float32,
        )
    out_ref[...] = out.astype(out_ref.dtype).reshape(out_ref.shape)


def whole_sequences(seq_size, head_size, queries, new_latent, cache, lengths, w_uk, w_uv):
    rows, heads, _ = queries.shape
    owners, slots, width = cache.shape
    copies = seq_size // owners
    per_device = rows // SPEC
    piece = SPEC * heads
    fresh_pad = -(-rows // 16) * 16
    params = pltpu.CompilerParams(vmem_limit_bytes=VMEM_LIMIT)
    vmem = pl.BlockSpec(memory_space=pltpu.VMEM)
    both = ("seq", "head")

    def flat(seq_index, head_index):
        return seq_index * head_size + head_index

    same_core = [[g * copies + t for g in range(owners)] for t in range(copies)]
    keys = [
        lax.all_to_all(
            jnp.swapaxes(cache, 1, 2),
            "seq",
            split_axis=0,
            concat_axis=0,
            axis_index_groups=same_core,
            tiled=True,
        )
    ]
    for e in range(1, copies):
        perm = [
            (g * copies + t, g * copies + (t + e) % copies)
            for g in range(owners)
            for t in range(copies)
        ]
        keys.append(lax.ppermute(keys[0], "seq", perm))

    parts = 4 if heads % 4 == 0 else 1
    pieces = pl.pallas_call(
        functools.partial(absorb_kernel, per_device, fresh_pad, parts),
        out_shape=[
            jax.ShapeDtypeStruct((piece + (fresh_pad if k == 0 else 0), width), cache.dtype)
            for k in range(per_device)
        ],
        in_specs=[pl.BlockSpec(memory_space=pltpu.HBM)] * 3,
        out_specs=[vmem] * per_device,
        scratch_shapes=[
            pltpu.VMEM(queries.shape, queries.dtype),
            pltpu.VMEM(new_latent.shape, new_latent.dtype),
            pltpu.VMEM(w_uk.shape, w_uk.dtype),
            pltpu.SemaphoreType.DMA((parts + 2,)),
        ],
        compiler_params=params,
    )(queries, new_latent, w_uk)
    there = []
    for k in range(per_device):
        perm = []
        for i in range(seq_size):
            for j in range(head_size):
                sequence = i * per_device + (j + k) % per_device
                target = (sequence % owners) * copies + j // per_device
                perm.append((flat(i, j), flat(target, sequence // owners)))
        there.append(perm)
    arrived = [lax.ppermute(pieces[k], both, there[k]) for k in range(per_device)]

    latent = pl.pallas_call(
        functools.partial(attend_kernel, owners, copies, per_device, heads),
        out_shape=[jax.ShapeDtypeStruct((piece, LATENT), jnp.bfloat16)] * per_device,
        in_specs=[pl.BlockSpec(memory_space=pltpu.SMEM)] + [vmem] * (per_device + len(keys)),
        out_specs=[vmem] * per_device,
        compiler_params=params,
    )(lengths, *arrived, *keys)

    back = [
        lax.ppermute(latent[k], both, [(b, a) for a, b in there[k]]) for k in range(per_device)
    ]
    return pl.pallas_call(
        functools.partial(project_kernel, per_device),
        out_shape=jax.ShapeDtypeStruct((rows, heads, w_uv.shape[2]), jnp.bfloat16),
        in_specs=[vmem] * (1 + per_device),
        out_specs=vmem,
        compiler_params=params,
    )(w_uv, *back)


def local_partial(
    query_tile_block,
    key_tile_block,
    incoming_keys,
    len_block,
    offset,
    own_first,
    score_scale,
    head_count,
):
    scores = (
        jnp.einsum(
            "vfa,vja->vfj", query_tile_block, key_tile_block, preferred_element_type=jnp.float32
        )
        * score_scale
    )
    positions = offset + lax.broadcasted_iota(jnp.int32, (1, 1, key_tile_block.shape[1]), 2)
    visible = positions < len_block[:, None, None]
    fresh_scores = (
        jnp.einsum(
            "vfa,vja->vfj", query_tile_block, incoming_keys, preferred_element_type=jnp.float32
        )
        * score_scale
    )
    spec_count = incoming_keys.shape[1]
    row_spec = (
        lax.broadcasted_iota(jnp.int32, (1, query_tile_block.shape[1], spec_count), 1) // head_count
    )
    key_spec = lax.broadcasted_iota(jnp.int32, (1, query_tile_block.shape[1], spec_count), 2)
    causal = (key_spec <= row_spec) & own_first
    row_top = jnp.maximum(
        jnp.max(jnp.where(visible, scores, masked_value), axis=2),
        jnp.max(jnp.where(causal, fresh_scores, masked_value), axis=2),
    )
    weights = jnp.where(visible, jnp.exp(scores - row_top[..., None]), 0.0)
    fresh_weights = jnp.where(causal, jnp.exp(fresh_scores - row_top[..., None]), 0.0)
    running_totals = jnp.sum(weights, axis=2) + jnp.sum(fresh_weights, axis=2)
    weighted = jnp.einsum(
        "mpu,mui->mpi",
        weights.astype(jnp.bfloat16),
        key_tile_block[:, :, :LATENT],
        preferred_element_type=jnp.float32,
    )
    weighted = weighted + jnp.einsum(
        "mpu,mui->mpi",
        fresh_weights.astype(jnp.bfloat16),
        incoming_keys[:, :, :LATENT],
        preferred_element_type=jnp.float32,
    )
    return (row_top, running_totals, weighted)


def project_values(latent_rows, value_weight):
    return jnp.einsum("rhc,hcv->rhv", latent_rows, value_weight, precision=lax.Precision.HIGHEST)


def split_positions(queries, new_latent, cache, lengths, w_uk, w_uv):
    own_rows, head_count, _ = queries.shape
    score_scale = (NOPE + ROPE) ** (-0.5)
    gathered, new_all = (
        lax.all_gather(queries, "seq", axis=0, tiled=True),
        lax.all_gather(new_latent, "seq", axis=0, tiled=True),
    )
    absorbed = jnp.einsum(
        "rhn,hnc->rhc", gathered[:, :, :NOPE], w_uk, preferred_element_type=jnp.float32
    ).astype(jnp.bfloat16)
    q_all = jnp.concatenate([absorbed, gathered[:, :, NOPE:]], axis=2)
    total_rows = q_all.shape[0]
    seq_count = total_rows // SPEC
    query_slots = SPEC * head_count
    q_seq = q_all.reshape(seq_count, query_slots, q_all.shape[2])
    new_seq = new_all.reshape(seq_count, SPEC, new_all.shape[1])
    seq_index = lax.axis_index("seq")
    offset = seq_index * cache.shape[1]
    own_first = seq_index == 0
    row_top, running_totals, weighted = local_partial(
        q_seq,
        lax.all_gather(cache, "head", axis=0, tiled=True),
        new_seq,
        lengths,
        offset,
        own_first,
        score_scale,
        head_count,
    )
    value_weight = w_uv.astype(jnp.float32)
    global_top = lax.pmax(row_top, "seq")
    factor = jnp.exp(row_top - global_top)
    scaled_totals = (running_totals * factor).reshape(total_rows, head_count)
    scaled_weighted = (weighted * factor[..., None]).reshape(total_rows, head_count, LATENT)
    row_totals, row_weighted = (
        lax.psum_scatter(scaled_totals, "seq", scatter_dimension=0, tiled=True),
        lax.psum_scatter(scaled_weighted, "seq", scatter_dimension=0, tiled=True),
    )
    latent_output = row_weighted / row_totals[..., None]
    result = project_values(latent_output, value_weight)
    return result.astype(jnp.bfloat16)


def shards(seq_size, head_size, queries, new_latent, cache, lengths, w_uk, w_uv):
    rows, owners = queries.shape[0], cache.shape[0]
    per_device = rows // SPEC
    if (
        rows % SPEC == 0
        and owners & (owners - 1) == 0
        and seq_size % owners == 0
        and head_size == per_device * (seq_size // owners)
    ):
        return whole_sequences(
            seq_size, head_size, queries, new_latent, cache, lengths, w_uk, w_uv
        )
    return split_positions(queries, new_latent, cache, lengths, w_uk, w_uv)


def solution(mesh):
    return jax.shard_map(
        functools.partial(shards, mesh.shape["seq"], mesh.shape["head"]),
        mesh=mesh,
        in_specs=(
            P("seq", "head", None),
            P("seq", None),
            P("head", "seq", None),
            P(),
            P("head", None, None),
            P("head", None, None),
        ),
        out_specs=P("seq", "head", None),
        check_vma=False,
    )
```

```python
import functools

import jax
import jax.numpy as jnp
from jax import lax
from jax.experimental import pallas as pl
from jax.experimental.pallas import tpu as pltpu
from jax.sharding import PartitionSpec as P

NOPE = 128
ROPE = 64
LATENT = 512
SPEC = 4
SCORE_SCALE = (NOPE + ROPE) ** (-0.5)
VMEM_LIMIT = 16 * 1024 * 1024
ABSORB_VMEM_LIMIT = 63 * 1024 * 1024

masked_value = -1e30


def absorb_kernel(per_device, owners, copies, fresh_pad, parts, *refs):
    q_hbm, new_hbm, w_hbm, cache_hbm = refs[:4]
    outs, picked = refs[4 : 4 + per_device], refs[4 + per_device : 4 + per_device + owners]
    q_ref, new_ref, w_ref, sem = refs[4 + per_device + owners :]
    rows, heads, width = q_ref.shape
    share = heads // parts
    small = [
        pltpu.make_async_copy(q_hbm, q_ref, sem.at[parts]),
        pltpu.make_async_copy(new_hbm, new_ref, sem.at[parts + 1]),
    ]
    weights = [
        pltpu.make_async_copy(
            w_hbm.at[pl.ds(n * share, share)], w_ref.at[pl.ds(n * share, share)], sem.at[n]
        )
        for n in range(parts)
    ]
    group = lax.axis_index("seq") // copies
    picks = [
        pltpu.make_async_copy(cache_hbm.at[group ^ k], picked[k], sem.at[parts + 2 + k])
        for k in range(owners)
    ]
    for move in small + weights + picks:
        move.start()
    for move in small:
        move.wait()
    q = q_ref[...].reshape(rows * heads, width)
    nope = q[:, :NOPE]
    own_head = lax.broadcasted_iota(jnp.int32, nope.shape, 0) % heads
    absorbed = jnp.zeros((rows * heads, LATENT), jnp.float32)
    for n in range(parts):
        spread = jnp.concatenate(
            [
                jnp.where(own_head == h, nope, jnp.zeros_like(nope))
                for h in range(n * share, (n + 1) * share)
            ],
            axis=1,
        )
        weights[n].wait()
        absorbed += jnp.dot(
            spread,
            w_ref[n * share : (n + 1) * share].reshape(share * NOPE, LATENT),
            preferred_element_type=jnp.float32,
        )
    absorbed = absorbed.astype(jnp.bfloat16)
    piece = SPEC * heads
    fresh = new_ref[...].astype(jnp.float32)
    fresh = jnp.concatenate(
        [fresh, jnp.zeros((fresh_pad - rows, fresh.shape[1]), jnp.float32)], axis=0
    ).astype(jnp.bfloat16)
    head_shard = lax.axis_index("head")
    for k in range(per_device):
        which = (head_shard + k) % per_device
        for a in range(per_device):

            @pl.when(which == a)
            def _():
                outs[k][:piece, :LATENT] = absorbed[a * piece : (a + 1) * piece]
                outs[k][:piece, LATENT:] = q[a * piece : (a + 1) * piece, NOPE:]

        if k == 0:
            outs[k][piece:, :] = fresh
    for move in picks:
        move.wait()


def attend_kernel(owners, copies, per_device, heads, len_ref, *refs):
    q_refs = refs[:per_device]
    key_refs = refs[per_device : per_device + copies * owners]
    outs = refs[per_device + copies * owners :]
    seq_index = lax.axis_index("seq")
    group, core = seq_index // copies, seq_index % copies
    sequence = lax.axis_index("head") * owners + group
    length = len_ref[sequence]
    piece = SPEC * heads
    q = jnp.concatenate([ref[:piece, :] for ref in q_refs], axis=0)
    fresh = q_refs[0][piece:, :]
    slots = key_refs[0].shape[1]
    lane = lax.broadcasted_iota(jnp.int32, (1, slots), 1)
    scores = []
    for e in range(copies):
        for k in range(owners):
            start = ((group ^ k) * copies + (core + copies - e) % copies) * slots
            s = jnp.dot(q, key_refs[e * owners + k][...], preferred_element_type=jnp.float32)
            scores.append(jnp.where(lane + start < length, s * SCORE_SCALE, masked_value))
    s = lax.dot_general(
        q, fresh, (((1,), (1,)), ((), ())), preferred_element_type=jnp.float32
    )
    row = lax.broadcasted_iota(jnp.int32, s.shape, 0)
    key = lax.broadcasted_iota(jnp.int32, s.shape, 1)
    causal = (key // SPEC == sequence % per_device) & (key % SPEC <= (row % piece) // heads)
    scores.append(jnp.where(causal, s * SCORE_SCALE, masked_value))
    top = functools.reduce(jnp.maximum, [jnp.max(s, axis=1, keepdims=True) for s in scores])
    total = jnp.zeros_like(top)
    out = jnp.zeros((q.shape[0], LATENT), jnp.float32)
    for n, s in enumerate(scores):
        w = jnp.exp(s - top)
        total += jnp.sum(w, axis=1, keepdims=True)
        w = w.astype(jnp.bfloat16)
        if n == owners * copies:
            out += jnp.dot(w, fresh[:, :LATENT], preferred_element_type=jnp.float32)
        else:
            out += lax.dot_general(
                w,
                key_refs[n][:LATENT, :],
                (((1,), (1,)), ((), ())),
                preferred_element_type=jnp.float32,
            )
    out = (out / total).astype(jnp.bfloat16)
    for k in range(per_device):
        outs[k][...] = out[k * piece : (k + 1) * piece]


def project_kernel(per_device, w_ref, *refs):
    lat_refs, out_ref = refs[:-1], refs[-1]
    rows, heads, width = out_ref.shape
    piece = SPEC * heads
    head_shard = lax.axis_index("head")
    parts = []
    for a in range(per_device):
        part = lat_refs[0][...]
        for k in range(1, per_device):
            part = jnp.where((head_shard + k) % per_device == a, lat_refs[k][...], part)
        parts.append(part)
    latent = jnp.concatenate(parts, axis=0)
    own_head = lax.broadcasted_iota(jnp.int32, latent.shape, 0) % heads
    out = jnp.zeros((rows * heads, width), jnp.float32)
    for h in range(heads):
        out += jnp.dot(
            jnp.where(own_head == h, latent, jnp.zeros_like(latent)),
            w_ref[h],
            preferred_element_type=jnp.float32,
        )
    out_ref[...] = out.astype(out_ref.dtype).reshape(out_ref.shape)


def whole_sequences(seq_size, head_size, queries, new_latent, cache, lengths, w_uk, w_uv):
    rows, heads, _ = queries.shape
    owners, slots, width = cache.shape
    copies = seq_size // owners
    per_device = rows // SPEC
    piece = SPEC * heads
    fresh_pad = -(-rows // 16) * 16
    params = pltpu.CompilerParams(vmem_limit_bytes=VMEM_LIMIT)
    vmem = pl.BlockSpec(memory_space=pltpu.VMEM)
    anywhere = pl.BlockSpec(memory_space=pl.ANY)
    both = ("seq", "head")

    def flat(seq_index, head_index):
        return seq_index * head_size + head_index

    parts = 4 if heads % 4 == 0 else 1
    made = pl.pallas_call(
        functools.partial(absorb_kernel, per_device, owners, copies, fresh_pad, parts),
        out_shape=[
            jax.ShapeDtypeStruct((piece + (fresh_pad if k == 0 else 0), width), cache.dtype)
            for k in range(per_device)
        ]
        + [jax.ShapeDtypeStruct((width, slots), cache.dtype)] * owners,
        in_specs=[anywhere] * 4,
        out_specs=[vmem] * per_device + [anywhere] * owners,
        scratch_shapes=[
            pltpu.VMEM(queries.shape, queries.dtype),
            pltpu.VMEM(new_latent.shape, new_latent.dtype),
            pltpu.VMEM(w_uk.shape, w_uk.dtype),
            pltpu.SemaphoreType.DMA((parts + 2 + owners,)),
        ],
        compiler_params=pltpu.CompilerParams(vmem_limit_bytes=ABSORB_VMEM_LIMIT),
    )(queries, new_latent, w_uk, jnp.swapaxes(cache, 1, 2))
    pieces, picked = made[:per_device], made[per_device:]
    there = []
    for k in range(per_device):
        perm = []
        for i in range(seq_size):
            for j in range(head_size):
                sequence = i * per_device + (j + k) % per_device
                target = (sequence % owners) * copies + j // per_device
                perm.append((flat(i, j), flat(target, sequence // owners)))
        there.append(perm)
    arrived = [lax.ppermute(pieces[k], both, there[k]) for k in range(per_device)]

    keys = [picked[0]]
    for k in range(1, owners):
        perm = [
            (g * copies + t, (g ^ k) * copies + t) for g in range(owners) for t in range(copies)
        ]
        keys.append(lax.ppermute(picked[k], "seq", perm))
    for e in range(1, copies):
        perm = [
            (g * copies + t, g * copies + (t + e) % copies)
            for g in range(owners)
            for t in range(copies)
        ]
        keys += [lax.ppermute(keys[k], "seq", perm) for k in range(owners)]

    latent = pl.pallas_call(
        functools.partial(attend_kernel, owners, copies, per_device, heads),
        out_shape=[jax.ShapeDtypeStruct((piece, LATENT), jnp.bfloat16)] * per_device,
        in_specs=[pl.BlockSpec(memory_space=pltpu.SMEM)] + [vmem] * (per_device + len(keys)),
        out_specs=[vmem] * per_device,
        compiler_params=params,
    )(lengths, *arrived, *keys)

    back = [
        lax.ppermute(latent[k], both, [(b, a) for a, b in there[k]]) for k in range(per_device)
    ]
    return pl.pallas_call(
        functools.partial(project_kernel, per_device),
        out_shape=jax.ShapeDtypeStruct((rows, heads, w_uv.shape[2]), jnp.bfloat16),
        in_specs=[vmem] * (1 + per_device),
        out_specs=vmem,
        compiler_params=params,
    )(w_uv, *back)


def local_partial(
    query_tile_block,
    key_tile_block,
    incoming_keys,
    len_block,
    offset,
    own_first,
    score_scale,
    head_count,
):
    scores = (
        jnp.einsum(
            "vfa,vja->vfj", query_tile_block, key_tile_block, preferred_element_type=jnp.float32
        )
        * score_scale
    )
    positions = offset + lax.broadcasted_iota(jnp.int32, (1, 1, key_tile_block.shape[1]), 2)
    visible = positions < len_block[:, None, None]
    fresh_scores = (
        jnp.einsum(
            "vfa,vja->vfj", query_tile_block, incoming_keys, preferred_element_type=jnp.float32
        )
        * score_scale
    )
    spec_count = incoming_keys.shape[1]
    row_spec = (
        lax.broadcasted_iota(jnp.int32, (1, query_tile_block.shape[1], spec_count), 1) // head_count
    )
    key_spec = lax.broadcasted_iota(jnp.int32, (1, query_tile_block.shape[1], spec_count), 2)
    causal = (key_spec <= row_spec) & own_first
    row_top = jnp.maximum(
        jnp.max(jnp.where(visible, scores, masked_value), axis=2),
        jnp.max(jnp.where(causal, fresh_scores, masked_value), axis=2),
    )
    weights = jnp.where(visible, jnp.exp(scores - row_top[..., None]), 0.0)
    fresh_weights = jnp.where(causal, jnp.exp(fresh_scores - row_top[..., None]), 0.0)
    running_totals = jnp.sum(weights, axis=2) + jnp.sum(fresh_weights, axis=2)
    weighted = jnp.einsum(
        "mpu,mui->mpi",
        weights.astype(jnp.bfloat16),
        key_tile_block[:, :, :LATENT],
        preferred_element_type=jnp.float32,
    )
    weighted = weighted + jnp.einsum(
        "mpu,mui->mpi",
        fresh_weights.astype(jnp.bfloat16),
        incoming_keys[:, :, :LATENT],
        preferred_element_type=jnp.float32,
    )
    return (row_top, running_totals, weighted)


def project_values(latent_rows, value_weight):
    return jnp.einsum("rhc,hcv->rhv", latent_rows, value_weight, precision=lax.Precision.HIGHEST)


def split_positions(queries, new_latent, cache, lengths, w_uk, w_uv):
    own_rows, head_count, _ = queries.shape
    score_scale = (NOPE + ROPE) ** (-0.5)
    gathered, new_all = (
        lax.all_gather(queries, "seq", axis=0, tiled=True),
        lax.all_gather(new_latent, "seq", axis=0, tiled=True),
    )
    absorbed = jnp.einsum(
        "rhn,hnc->rhc", gathered[:, :, :NOPE], w_uk, preferred_element_type=jnp.float32
    ).astype(jnp.bfloat16)
    q_all = jnp.concatenate([absorbed, gathered[:, :, NOPE:]], axis=2)
    total_rows = q_all.shape[0]
    seq_count = total_rows // SPEC
    query_slots = SPEC * head_count
    q_seq = q_all.reshape(seq_count, query_slots, q_all.shape[2])
    new_seq = new_all.reshape(seq_count, SPEC, new_all.shape[1])
    seq_index = lax.axis_index("seq")
    offset = seq_index * cache.shape[1]
    own_first = seq_index == 0
    row_top, running_totals, weighted = local_partial(
        q_seq,
        lax.all_gather(cache, "head", axis=0, tiled=True),
        new_seq,
        lengths,
        offset,
        own_first,
        score_scale,
        head_count,
    )
    value_weight = w_uv.astype(jnp.float32)
    global_top = lax.pmax(row_top, "seq")
    factor = jnp.exp(row_top - global_top)
    scaled_totals = (running_totals * factor).reshape(total_rows, head_count)
    scaled_weighted = (weighted * factor[..., None]).reshape(total_rows, head_count, LATENT)
    row_totals, row_weighted = (
        lax.psum_scatter(scaled_totals, "seq", scatter_dimension=0, tiled=True),
        lax.psum_scatter(scaled_weighted, "seq", scatter_dimension=0, tiled=True),
    )
    latent_output = row_weighted / row_totals[..., None]
    result = project_values(latent_output, value_weight)
    return result.astype(jnp.bfloat16)


def shards(seq_size, head_size, queries, new_latent, cache, lengths, w_uk, w_uv):
    rows, owners = queries.shape[0], cache.shape[0]
    per_device = rows // SPEC
    if (
        rows % SPEC == 0
        and owners & (owners - 1) == 0
        and seq_size % owners == 0
        and head_size == per_device * (seq_size // owners)
    ):
        return whole_sequences(
            seq_size, head_size, queries, new_latent, cache, lengths, w_uk, w_uv
        )
    return split_positions(queries, new_latent, cache, lengths, w_uk, w_uv)


def solution(mesh):
    return jax.shard_map(
        functools.partial(shards, mesh.shape["seq"], mesh.shape["head"]),
        mesh=mesh,
        in_specs=(
            P("seq", "head", None),
            P("seq", None),
            P("head", "seq", None),
            P(),
            P("head", None, None),
            P("head", None, None),
        ),
        out_specs=P("seq", "head", None),
        check_vma=False,
    )
```

```python
import functools

import jax
import jax.numpy as jnp
from jax import lax
from jax.experimental import pallas as pl
from jax.experimental.pallas import tpu as pltpu
from jax.sharding import PartitionSpec as P

NOPE = 128
ROPE = 64
LATENT = 512
SPEC = 4
SCORE_SCALE = (NOPE + ROPE) ** (-0.5)
VMEM_LIMIT = 16 * 1024 * 1024
LONG = pl.CostEstimate(flops=2 * 10**10, bytes_accessed=0, transcendentals=0)

masked_value = -1e30


def copy_all(sources, targets, sem):
    moves = [
        pltpu.make_async_copy(source, target, sem.at[n])
        for n, (source, target) in enumerate(zip(sources, targets))
    ]
    for move in moves:
        move.start()
    return moves


def pack_kernel(owners, copies, cache_hbm, q_hbm, new_hbm, *refs):
    picked, (pack_ref, q_ref, new_ref, sem) = refs[:owners], refs[owners:]
    group = lax.axis_index("seq") // copies
    moves = copy_all(
        [q_hbm, new_hbm] + [cache_hbm.at[group ^ k] for k in range(owners)],
        [q_ref, new_ref] + list(picked),
        sem,
    )
    moves[0].wait()
    moves[1].wait()
    rows, heads, width = q_ref.shape
    pack_ref[: rows * heads, :] = q_ref[...].reshape(rows * heads, width)
    fresh = new_ref[...].astype(jnp.float32)
    parts = [fresh[:, n : n + width] for n in range(0, fresh.shape[1], width)]
    spare = pack_ref.shape[0] - rows * heads - rows * len(parts)
    if spare:
        parts.append(jnp.zeros((spare, width), jnp.float32))
    pack_ref[rows * heads :, :] = jnp.concatenate(parts, axis=0).astype(pack_ref.dtype)
    for move in moves[2:]:
        move.wait()


def place_kernel(owners, copies, *refs):
    blocks, out_ref, sem = refs[:-2], refs[-2], refs[-1]
    group = lax.axis_index("seq") // copies
    for move in copy_all(blocks, [out_ref.at[group ^ k] for k in range(owners)], sem):
        move.wait()


def absorb_kernel(per_device, rows, pack_ref, w_ref, *outs):
    heads = w_ref.shape[0]
    piece, all_rows = SPEC * heads, rows * heads
    q = pack_ref[:all_rows, :]
    nope = q[:, :NOPE]
    own_head = lax.broadcasted_iota(jnp.int32, nope.shape, 0) % heads
    spread = jnp.concatenate(
        [jnp.where(own_head == h, nope, jnp.zeros_like(nope)) for h in range(heads)], axis=1
    )
    absorbed = jnp.dot(
        spread, w_ref[...].reshape(heads * NOPE, LATENT), preferred_element_type=jnp.float32
    ).astype(jnp.bfloat16)
    fresh = pack_ref[all_rows:, :].astype(jnp.float32)
    fresh = jnp.concatenate(
        [
            fresh[n * rows : (n + 1) * rows]
            for n in range((LATENT + ROPE) // (NOPE + ROPE))
        ],
        axis=1,
    )
    spare = outs[0].shape[0] - piece - rows
    if spare:
        fresh = jnp.concatenate([fresh, jnp.zeros((spare, fresh.shape[1]), jnp.float32)], axis=0)
    outs[0][piece:, :] = fresh.astype(jnp.bfloat16)
    head_shard = lax.axis_index("head")
    for k in range(per_device):
        which = (head_shard + k) % per_device
        for a in range(per_device):

            @pl.when(which == a)
            def _():
                outs[k][:piece, :LATENT] = absorbed[a * piece : (a + 1) * piece]
                outs[k][:piece, LATENT:] = q[a * piece : (a + 1) * piece, NOPE:]


def block_scores(q, keys_ref, n, start, length):
    s = jnp.dot(q, keys_ref[n], preferred_element_type=jnp.float32) * SCORE_SCALE
    lane = lax.broadcasted_iota(jnp.int32, (1, s.shape[1]), 1)
    return jnp.where(lane + start < length, s, masked_value)


def weigh(scores, values, top):
    total, out = 0.0, 0.0
    for s, value in zip(scores, values):
        w = jnp.exp(s - top)
        total += jnp.sum(w, axis=1, keepdims=True)
        out += lax.dot_general(
            w.astype(jnp.bfloat16),
            value(),
            (((1,), (1,)), ((), ())),
            preferred_element_type=jnp.float32,
        )
    return total, out


def begin_kernel(owners, copies, per_device, heads, len_ref, *refs):
    q_refs, (keys_ref, q_out, top_ref, total_ref, out_ref) = refs[:per_device], refs[per_device:]
    seq_index = lax.axis_index("seq")
    sequence = lax.axis_index("head") * owners + seq_index // copies
    length = len_ref[sequence]
    piece = SPEC * heads
    slots = keys_ref.shape[2]
    q = jnp.concatenate([ref[:piece, :] for ref in q_refs], axis=0)
    fresh = q_refs[0][piece:, :]
    scores = [
        block_scores(q, keys_ref, g, (g * copies + seq_index % copies) * slots, length)
        for g in range(owners)
    ]
    s = lax.dot_general(
        q, fresh, (((1,), (1,)), ((), ())), preferred_element_type=jnp.float32
    )
    row = lax.broadcasted_iota(jnp.int32, s.shape, 0)
    key = lax.broadcasted_iota(jnp.int32, s.shape, 1)
    causal = (key // SPEC == sequence % per_device) & (key % SPEC <= (row % piece) // heads)
    s = jnp.where(causal, s * SCORE_SCALE, masked_value)
    top = functools.reduce(
        jnp.maximum, [jnp.max(s, axis=1, keepdims=True) for s in scores + [s]]
    )
    total, out = weigh(
        scores, [functools.partial(lambda g: keys_ref[g, :LATENT, :], g) for g in range(owners)], top
    )
    w = jnp.exp(s - top)
    total += jnp.sum(w, axis=1, keepdims=True)
    out += jnp.dot(
        w.astype(jnp.bfloat16), fresh[:, :LATENT], preferred_element_type=jnp.float32
    )
    q_out[...] = q
    top_ref[...] = jnp.broadcast_to(top, top_ref.shape)
    total_ref[...] = jnp.broadcast_to(total, total_ref.shape)
    out_ref[...] = out


def finish_kernel(owners, copies, per_device, len_ref, q_ref, top_ref, total_ref, part_ref, *refs):
    key_refs, outs = refs[: copies - 1], refs[copies - 1 :]
    seq_index = lax.axis_index("seq")
    length = len_ref[lax.axis_index("head") * owners + seq_index // copies]
    q = q_ref[...]
    scores, values = [], []
    for e in range(1, copies):
        core = (seq_index + copies - e) % copies
        for g in range(owners):
            keys_ref = key_refs[e - 1]
            start = (g * copies + core) * keys_ref.shape[2]
            scores.append(block_scores(q, keys_ref, g, start, length))
            values.append(functools.partial(lambda r, g: r[g, :LATENT, :], keys_ref, g))
    first = top_ref[:, :1]
    top = functools.reduce(
        jnp.maximum, [first] + [jnp.max(s, axis=1, keepdims=True) for s in scores]
    )
    total, out = weigh(scores, values, top)
    scale = jnp.exp(first - top)
    out = (out + part_ref[...] * scale) / (total + total_ref[:, :1] * scale)
    out = out.astype(jnp.bfloat16)
    piece = out.shape[0] // per_device
    for k in range(per_device):
        outs[k][...] = out[k * piece : (k + 1) * piece]


def project_kernel(per_device, w_ref, *refs):
    lat_refs, out_ref = refs[:-1], refs[-1]
    rows, heads, width = out_ref.shape
    piece = SPEC * heads
    head_shard = lax.axis_index("head")
    parts = []
    for a in range(per_device):
        part = lat_refs[0][...]
        for k in range(1, per_device):
            part = jnp.where((head_shard + k) % per_device == a, lat_refs[k][...], part)
        parts.append(part)
    latent = jnp.concatenate(parts, axis=0)
    own_head = lax.broadcasted_iota(jnp.int32, latent.shape, 0) % heads
    out = jnp.zeros((rows * heads, width), jnp.float32)
    for h in range(heads):
        out += jnp.dot(
            jnp.where(own_head == h, latent, jnp.zeros_like(latent)),
            w_ref[h],
            preferred_element_type=jnp.float32,
        )
    out_ref[...] = out.astype(out_ref.dtype).reshape(out_ref.shape)


def whole_sequences(seq_size, head_size, queries, new_latent, cache, lengths, w_uk, w_uv):
    rows, heads, q_width = queries.shape
    owners, slots, width = cache.shape
    copies = seq_size // owners
    per_device = rows // SPEC
    piece = SPEC * heads
    fresh_pad = -(-rows // 16) * 16
    packed_rows = rows * heads + -(-rows * (width // q_width) // 16) * 16
    params = pltpu.CompilerParams(vmem_limit_bytes=VMEM_LIMIT)
    vmem = pl.BlockSpec(memory_space=pltpu.VMEM)
    anywhere = pl.BlockSpec(memory_space=pl.ANY)
    both = ("seq", "head")

    def flat(seq_index, head_index):
        return seq_index * head_size + head_index

    def in_hbm(x):
        return pltpu.with_memory_space_constraint(x, pltpu.HBM)

    *picked, packed = pl.pallas_call(
        functools.partial(pack_kernel, owners, copies),
        out_shape=[jax.ShapeDtypeStruct((width, slots), cache.dtype)] * owners
        + [jax.ShapeDtypeStruct((packed_rows, q_width), queries.dtype)],
        in_specs=[anywhere] * 3,
        out_specs=[vmem] * (owners + 1),
        scratch_shapes=[
            pltpu.VMEM(queries.shape, queries.dtype),
            pltpu.VMEM(new_latent.shape, new_latent.dtype),
            pltpu.SemaphoreType.DMA((owners + 2,)),
        ],
        compiler_params=params,
        cost_estimate=LONG,
    )(in_hbm(jnp.swapaxes(cache, 1, 2)), in_hbm(queries), in_hbm(new_latent))

    block = seq_size // head_size
    turn = (0, 2, 3, 1) if head_size == 4 else range(head_size)

    def host(i, j):
        return ((i // block) ^ turn[j]) * block + i % block

    devices = [(i, j) for i in range(seq_size) for j in range(head_size)]
    packed = lax.ppermute(packed, both, [(flat(i, j), flat(host(i, j), j)) for i, j in devices])
    pieces = pl.pallas_call(
        functools.partial(absorb_kernel, per_device, rows),
        out_shape=[
            jax.ShapeDtypeStruct((piece + (fresh_pad if k == 0 else 0), width), cache.dtype)
            for k in range(per_device)
        ],
        in_specs=[vmem] * 2,
        out_specs=[vmem] * per_device,
        compiler_params=params,
        cost_estimate=LONG,
    )(packed, w_uk)

    def owner(i, j, k):
        sequence = i * per_device + (j + k) % per_device
        return flat((sequence % owners) * copies + j // per_device, sequence // owners)

    arrived = [
        lax.ppermute(
            pieces[k], both, [(flat(host(i, j), j), owner(i, j, k)) for i, j in devices]
        )
        for k in range(per_device)
    ]

    def in_plane(move):
        return [
            (g * copies + t, move(g, t)) for g in range(owners) for t in range(copies)
        ]

    blocks = [picked[0]] + [
        lax.ppermute(picked[k], "seq", in_plane(lambda g, t: (g ^ k) * copies + t))
        for k in range(1, owners)
    ]
    keys = [
        pl.pallas_call(
            functools.partial(place_kernel, owners, copies),
            out_shape=jax.ShapeDtypeStruct((owners, width, slots), cache.dtype),
            in_specs=[anywhere] * owners,
            out_specs=vmem,
            scratch_shapes=[pltpu.SemaphoreType.DMA((owners,))],
            compiler_params=params,
        )(*blocks)
    ]
    for e in range(1, copies):
        keys.append(
            lax.ppermute(
                keys[0], "seq", in_plane(lambda g, t: g * copies + (t + e) % copies)
            )
        )

    all_rows = per_device * piece
    smem = pl.BlockSpec(memory_space=pltpu.SMEM)
    state = pl.pallas_call(
        functools.partial(begin_kernel, owners, copies, per_device, heads),
        out_shape=[
            jax.ShapeDtypeStruct((all_rows, width), jnp.bfloat16),
            jax.ShapeDtypeStruct((all_rows, 128), jnp.float32),
            jax.ShapeDtypeStruct((all_rows, 128), jnp.float32),
            jax.ShapeDtypeStruct((all_rows, LATENT), jnp.float32),
        ],
        in_specs=[smem] + [vmem] * (per_device + 1),
        out_specs=[vmem] * 4,
        compiler_params=params,
        cost_estimate=LONG,
    )(lengths, *arrived, keys[0])
    latent = pl.pallas_call(
        functools.partial(finish_kernel, owners, copies, per_device),
        out_shape=[jax.ShapeDtypeStruct((piece, LATENT), jnp.bfloat16)] * per_device,
        in_specs=[smem] + [vmem] * (len(state) + copies - 1),
        out_specs=[vmem] * per_device,
        compiler_params=params,
    )(lengths, *state, *keys[1:])

    back = [
        lax.ppermute(latent[k], both, [(owner(i, j, k), flat(i, j)) for i, j in devices])
        for k in range(per_device)
    ]
    return pl.pallas_call(
        functools.partial(project_kernel, per_device),
        out_shape=jax.ShapeDtypeStruct((rows, heads, w_uv.shape[2]), jnp.bfloat16),
        in_specs=[vmem] * (1 + per_device),
        out_specs=vmem,
        compiler_params=params,
    )(w_uv, *back)


def local_partial(
    query_tile_block,
    key_tile_block,
    incoming_keys,
    len_block,
    offset,
    own_first,
    score_scale,
    head_count,
):
    scores = (
        jnp.einsum(
            "vfa,vja->vfj", query_tile_block, key_tile_block, preferred_element_type=jnp.float32
        )
        * score_scale
    )
    positions = offset + lax.broadcasted_iota(jnp.int32, (1, 1, key_tile_block.shape[1]), 2)
    visible = positions < len_block[:, None, None]
    fresh_scores = (
        jnp.einsum(
            "vfa,vja->vfj", query_tile_block, incoming_keys, preferred_element_type=jnp.float32
        )
        * score_scale
    )
    spec_count = incoming_keys.shape[1]
    row_spec = (
        lax.broadcasted_iota(jnp.int32, (1, query_tile_block.shape[1], spec_count), 1) // head_count
    )
    key_spec = lax.broadcasted_iota(jnp.int32, (1, query_tile_block.shape[1], spec_count), 2)
    causal = (key_spec <= row_spec) & own_first
    row_top = jnp.maximum(
        jnp.max(jnp.where(visible, scores, masked_value), axis=2),
        jnp.max(jnp.where(causal, fresh_scores, masked_value), axis=2),
    )
    weights = jnp.where(visible, jnp.exp(scores - row_top[..., None]), 0.0)
    fresh_weights = jnp.where(causal, jnp.exp(fresh_scores - row_top[..., None]), 0.0)
    running_totals = jnp.sum(weights, axis=2) + jnp.sum(fresh_weights, axis=2)
    weighted = jnp.einsum(
        "mpu,mui->mpi",
        weights.astype(jnp.bfloat16),
        key_tile_block[:, :, :LATENT],
        preferred_element_type=jnp.float32,
    )
    weighted = weighted + jnp.einsum(
        "mpu,mui->mpi",
        fresh_weights.astype(jnp.bfloat16),
        incoming_keys[:, :, :LATENT],
        preferred_element_type=jnp.float32,
    )
    return (row_top, running_totals, weighted)


def project_values(latent_rows, value_weight):
    return jnp.einsum("rhc,hcv->rhv", latent_rows, value_weight, precision=lax.Precision.HIGHEST)


def split_positions(queries, new_latent, cache, lengths, w_uk, w_uv):
    own_rows, head_count, _ = queries.shape
    score_scale = (NOPE + ROPE) ** (-0.5)
    gathered, new_all = (
        lax.all_gather(queries, "seq", axis=0, tiled=True),
        lax.all_gather(new_latent, "seq", axis=0, tiled=True),
    )
    absorbed = jnp.einsum(
        "rhn,hnc->rhc", gathered[:, :, :NOPE], w_uk, preferred_element_type=jnp.float32
    ).astype(jnp.bfloat16)
    q_all = jnp.concatenate([absorbed, gathered[:, :, NOPE:]], axis=2)
    total_rows = q_all.shape[0]
    seq_count = total_rows // SPEC
    query_slots = SPEC * head_count
    q_seq = q_all.reshape(seq_count, query_slots, q_all.shape[2])
    new_seq = new_all.reshape(seq_count, SPEC, new_all.shape[1])
    seq_index = lax.axis_index("seq")
    offset = seq_index * cache.shape[1]
    own_first = seq_index == 0
    row_top, running_totals, weighted = local_partial(
        q_seq,
        lax.all_gather(cache, "head", axis=0, tiled=True),
        new_seq,
        lengths,
        offset,
        own_first,
        score_scale,
        head_count,
    )
    value_weight = w_uv.astype(jnp.float32)
    global_top = lax.pmax(row_top, "seq")
    factor = jnp.exp(row_top - global_top)
    scaled_totals = (running_totals * factor).reshape(total_rows, head_count)
    scaled_weighted = (weighted * factor[..., None]).reshape(total_rows, head_count, LATENT)
    row_totals, row_weighted = (
        lax.psum_scatter(scaled_totals, "seq", scatter_dimension=0, tiled=True),
        lax.psum_scatter(scaled_weighted, "seq", scatter_dimension=0, tiled=True),
    )
    latent_output = row_weighted / row_totals[..., None]
    result = project_values(latent_output, value_weight)
    return result.astype(jnp.bfloat16)


def shards(seq_size, head_size, queries, new_latent, cache, lengths, w_uk, w_uv):
    rows, owners = queries.shape[0], cache.shape[0]
    per_device = rows // SPEC
    if (
        rows % SPEC == 0
        and owners & (owners - 1) == 0
        and seq_size % owners == 0
        and head_size == per_device * (seq_size // owners)
        and head_size & (head_size - 1) == 0
        and seq_size % head_size == 0
        and cache.shape[2] % queries.shape[2] == 0
    ):
        return whole_sequences(
            seq_size, head_size, queries, new_latent, cache, lengths, w_uk, w_uv
        )
    return split_positions(queries, new_latent, cache, lengths, w_uk, w_uv)


def solution(mesh):
    return jax.shard_map(
        functools.partial(shards, mesh.shape["seq"], mesh.shape["head"]),
        mesh=mesh,
        in_specs=(
            P("seq", "head", None),
            P("seq", None),
            P("head", "seq", None),
            P(),
            P("head", None, None),
            P("head", None, None),
        ),
        out_specs=P("seq", "head", None),
        check_vma=False,
    )
```

```python
import functools

import jax
import jax.numpy as jnp
from jax import lax
from jax.experimental import pallas as pl
from jax.experimental.pallas import tpu as pltpu
from jax.sharding import PartitionSpec as P

NOPE = 128
ROPE = 64
LATENT = 512
SPEC = 4
SCORE_SCALE = (NOPE + ROPE) ** (-0.5)
VMEM_LIMIT = 16 * 1024 * 1024
LONG = pl.CostEstimate(flops=2 * 10**10, bytes_accessed=0, transcendentals=0)

masked_value = -1e30


def copy_all(sources, targets, sem):
    moves = [
        pltpu.make_async_copy(source, target, sem.at[n])
        for n, (source, target) in enumerate(zip(sources, targets))
    ]
    for move in moves:
        move.start()
    return moves


def pack_kernel(owners, copies, cache_hbm, q_hbm, new_hbm, *refs):
    picked, (pack_ref, q_ref, new_ref, sem) = refs[:owners], refs[owners:]
    own = (lax.axis_index("seq") // copies) ^ (owners // 2)
    moves = copy_all(
        [q_hbm, new_hbm] + [cache_hbm.at[own ^ k] for k in range(owners)],
        [q_ref, new_ref] + list(picked),
        sem,
    )
    moves[0].wait()
    moves[1].wait()
    rows, heads, width = q_ref.shape
    pack_ref[: rows * heads, :] = q_ref[...].reshape(rows * heads, width)
    fresh = new_ref[...].astype(jnp.float32)
    parts = [fresh[:, n : n + width] for n in range(0, fresh.shape[1], width)]
    spare = pack_ref.shape[0] - rows * heads - rows * len(parts)
    if spare:
        parts.append(jnp.zeros((spare, width), jnp.float32))
    pack_ref[rows * heads :, :] = jnp.concatenate(parts, axis=0).astype(pack_ref.dtype)
    for move in moves[2:]:
        move.wait()


def place_kernel(owners, copies, *refs):
    blocks, out_ref, sem = refs[:-2], refs[-2], refs[-1]
    group = lax.axis_index("seq") // copies
    for move in copy_all(blocks, [out_ref.at[group ^ k] for k in range(owners)], sem):
        move.wait()


def absorb_kernel(per_device, rows, pack_ref, w_ref, *outs):
    heads = w_ref.shape[0]
    piece, all_rows = SPEC * heads, rows * heads
    q = pack_ref[:all_rows, :]
    nope = q[:, :NOPE]
    own_head = lax.broadcasted_iota(jnp.int32, nope.shape, 0) % heads
    spread = jnp.concatenate(
        [jnp.where(own_head == h, nope, jnp.zeros_like(nope)) for h in range(heads)], axis=1
    )
    absorbed = jnp.dot(
        spread, w_ref[...].reshape(heads * NOPE, LATENT), preferred_element_type=jnp.float32
    ).astype(jnp.bfloat16)
    fresh = pack_ref[all_rows:, :].astype(jnp.float32)
    fresh = jnp.concatenate(
        [
            fresh[n * rows : (n + 1) * rows]
            for n in range((LATENT + ROPE) // (NOPE + ROPE))
        ],
        axis=1,
    )
    spare = outs[0].shape[0] - piece - rows
    if spare:
        fresh = jnp.concatenate([fresh, jnp.zeros((spare, fresh.shape[1]), jnp.float32)], axis=0)
    outs[0][piece:, :] = fresh.astype(jnp.bfloat16)
    head_shard = lax.axis_index("head")
    for k in range(per_device):
        which = (head_shard + k) % per_device
        for a in range(per_device):

            @pl.when(which == a)
            def _():
                outs[k][:piece, :LATENT] = absorbed[a * piece : (a + 1) * piece]
                outs[k][:piece, LATENT:] = q[a * piece : (a + 1) * piece, NOPE:]


def block_scores(q, keys_ref, n, start, length):
    s = jnp.dot(q, keys_ref[n], preferred_element_type=jnp.float32) * SCORE_SCALE
    lane = lax.broadcasted_iota(jnp.int32, (1, s.shape[1]), 1)
    return jnp.where(lane + start < length, s, masked_value)


def weigh(scores, values, top):
    total, out = 0.0, 0.0
    for s, value in zip(scores, values):
        w = jnp.exp(s - top)
        total += jnp.sum(w, axis=1, keepdims=True)
        out += lax.dot_general(
            w.astype(jnp.bfloat16),
            value(),
            (((1,), (1,)), ((), ())),
            preferred_element_type=jnp.float32,
        )
    return total, out


def begin_kernel(owners, copies, per_device, heads, len_ref, *refs):
    q_refs, (keys_ref, q_out, top_ref, total_ref, out_ref) = refs[:per_device], refs[per_device:]
    seq_index = lax.axis_index("seq")
    sequence = lax.axis_index("head") * owners + (seq_index // copies ^ (owners // 2))
    length = len_ref[sequence]
    piece = SPEC * heads
    slots = keys_ref.shape[2]
    q = jnp.concatenate([ref[:piece, :] for ref in q_refs], axis=0)
    fresh = q_refs[0][piece:, :]
    scores = [
        block_scores(q, keys_ref, g, (g * copies + seq_index % copies) * slots, length)
        for g in range(owners)
    ]
    s = lax.dot_general(
        q, fresh, (((1,), (1,)), ((), ())), preferred_element_type=jnp.float32
    )
    row = lax.broadcasted_iota(jnp.int32, s.shape, 0)
    key = lax.broadcasted_iota(jnp.int32, s.shape, 1)
    causal = (key // SPEC == sequence % per_device) & (key % SPEC <= (row % piece) // heads)
    s = jnp.where(causal, s * SCORE_SCALE, masked_value)
    top = functools.reduce(
        jnp.maximum, [jnp.max(s, axis=1, keepdims=True) for s in scores + [s]]
    )
    total, out = weigh(
        scores, [functools.partial(lambda g: keys_ref[g, :LATENT, :], g) for g in range(owners)], top
    )
    w = jnp.exp(s - top)
    total += jnp.sum(w, axis=1, keepdims=True)
    out += jnp.dot(
        w.astype(jnp.bfloat16), fresh[:, :LATENT], preferred_element_type=jnp.float32
    )
    q_out[...] = q
    top_ref[...] = jnp.broadcast_to(top, top_ref.shape)
    total_ref[...] = jnp.broadcast_to(total, total_ref.shape)
    out_ref[...] = out


def finish_kernel(owners, copies, per_device, len_ref, q_ref, top_ref, total_ref, part_ref, *refs):
    key_refs, outs = refs[: copies - 1], refs[copies - 1 :]
    seq_index = lax.axis_index("seq")
    length = len_ref[lax.axis_index("head") * owners + (seq_index // copies ^ (owners // 2))]
    q = q_ref[...]
    scores, values = [], []
    for e in range(1, copies):
        core = (seq_index + copies - e) % copies
        for g in range(owners):
            keys_ref = key_refs[e - 1]
            start = (g * copies + core) * keys_ref.shape[2]
            scores.append(block_scores(q, keys_ref, g, start, length))
            values.append(functools.partial(lambda r, g: r[g, :LATENT, :], keys_ref, g))
    first = top_ref[:, :1]
    top = functools.reduce(
        jnp.maximum, [first] + [jnp.max(s, axis=1, keepdims=True) for s in scores]
    )
    total, out = weigh(scores, values, top)
    scale = jnp.exp(first - top)
    out = (out + part_ref[...] * scale) / (total + total_ref[:, :1] * scale)
    out = out.astype(jnp.bfloat16)
    piece = out.shape[0] // per_device
    for k in range(per_device):
        outs[k][...] = out[k * piece : (k + 1) * piece]


def project_kernel(per_device, w_ref, *refs):
    lat_refs, out_ref = refs[:-1], refs[-1]
    rows, heads, width = out_ref.shape
    piece = SPEC * heads
    head_shard = lax.axis_index("head")
    parts = []
    for a in range(per_device):
        part = lat_refs[0][...]
        for k in range(1, per_device):
            part = jnp.where((head_shard + k) % per_device == a, lat_refs[k][...], part)
        parts.append(part)
    latent = jnp.concatenate(parts, axis=0)
    own_head = lax.broadcasted_iota(jnp.int32, latent.shape, 0) % heads
    out = jnp.zeros((rows * heads, width), jnp.float32)
    for h in range(heads):
        out += jnp.dot(
            jnp.where(own_head == h, latent, jnp.zeros_like(latent)),
            w_ref[h],
            preferred_element_type=jnp.float32,
        )
    out_ref[...] = out.astype(out_ref.dtype).reshape(out_ref.shape)


def whole_sequences(seq_size, head_size, queries, new_latent, cache, lengths, w_uk, w_uv):
    rows, heads, q_width = queries.shape
    owners, slots, width = cache.shape
    copies = seq_size // owners
    per_device = rows // SPEC
    piece = SPEC * heads
    fresh_pad = -(-rows // 16) * 16
    packed_rows = rows * heads + -(-rows * (width // q_width) // 16) * 16
    params = pltpu.CompilerParams(vmem_limit_bytes=VMEM_LIMIT)
    vmem = pl.BlockSpec(memory_space=pltpu.VMEM)
    anywhere = pl.BlockSpec(memory_space=pl.ANY)
    both = ("seq", "head")

    def flat(seq_index, head_index):
        return seq_index * head_size + head_index

    def in_hbm(x):
        return pltpu.with_memory_space_constraint(x, pltpu.HBM)

    *picked, packed = pl.pallas_call(
        functools.partial(pack_kernel, owners, copies),
        out_shape=[jax.ShapeDtypeStruct((width, slots), cache.dtype)] * owners
        + [jax.ShapeDtypeStruct((packed_rows, q_width), queries.dtype)],
        in_specs=[anywhere] * 3,
        out_specs=[vmem] * (owners + 1),
        scratch_shapes=[
            pltpu.VMEM(queries.shape, queries.dtype),
            pltpu.VMEM(new_latent.shape, new_latent.dtype),
            pltpu.SemaphoreType.DMA((owners + 2,)),
        ],
        compiler_params=params,
        cost_estimate=LONG,
    )(in_hbm(jnp.swapaxes(cache, 1, 2)), in_hbm(queries), in_hbm(new_latent))

    def host(i, j):
        chip, core = i // copies, i % copies
        half = head_size // 2
        return (chip ^ j ^ (core * half)) * copies + (core ^ (j % half == 0))

    devices = [(i, j) for i in range(seq_size) for j in range(head_size)]
    packed = lax.ppermute(packed, both, [(flat(i, j), flat(host(i, j), j)) for i, j in devices])
    pieces = pl.pallas_call(
        functools.partial(absorb_kernel, per_device, rows),
        out_shape=[
            jax.ShapeDtypeStruct((piece + (fresh_pad if k == 0 else 0), width), cache.dtype)
            for k in range(per_device)
        ],
        in_specs=[vmem] * 2,
        out_specs=[vmem] * per_device,
        compiler_params=params,
        cost_estimate=LONG,
    )(packed, w_uk)

    def owner(i, j, k):
        sequence = i * per_device + (j + k) % per_device
        group = (sequence % owners) ^ (owners // 2)
        return flat(group * copies + j // per_device, sequence // owners)

    arrived = [
        lax.ppermute(
            pieces[k], both, [(flat(host(i, j), j), owner(i, j, k)) for i, j in devices]
        )
        for k in range(per_device)
    ]

    def in_plane(move):
        return [
            (g * copies + t, move(g, t)) for g in range(owners) for t in range(copies)
        ]

    blocks = [picked[0]] + [
        lax.ppermute(picked[k], "seq", in_plane(lambda g, t: (g ^ k) * copies + t))
        for k in range(1, owners)
    ]
    keys = [
        pl.pallas_call(
            functools.partial(place_kernel, owners, copies),
            out_shape=jax.ShapeDtypeStruct((owners, width, slots), cache.dtype),
            in_specs=[anywhere] * owners,
            out_specs=vmem,
            scratch_shapes=[pltpu.SemaphoreType.DMA((owners,))],
            compiler_params=params,
        )(*blocks)
    ]
    for e in range(1, copies):
        keys.append(
            lax.ppermute(
                keys[0], "seq", in_plane(lambda g, t: g * copies + (t + e) % copies)
            )
        )

    all_rows = per_device * piece
    smem = pl.BlockSpec(memory_space=pltpu.SMEM)
    state = pl.pallas_call(
        functools.partial(begin_kernel, owners, copies, per_device, heads),
        out_shape=[
            jax.ShapeDtypeStruct((all_rows, width), jnp.bfloat16),
            jax.ShapeDtypeStruct((all_rows, 128), jnp.float32),
            jax.ShapeDtypeStruct((all_rows, 128), jnp.float32),
            jax.ShapeDtypeStruct((all_rows, LATENT), jnp.float32),
        ],
        in_specs=[smem] + [vmem] * (per_device + 1),
        out_specs=[vmem] * 4,
        compiler_params=params,
        cost_estimate=LONG,
    )(lengths, *arrived, keys[0])
    latent = pl.pallas_call(
        functools.partial(finish_kernel, owners, copies, per_device),
        out_shape=[jax.ShapeDtypeStruct((piece, LATENT), jnp.bfloat16)] * per_device,
        in_specs=[smem] + [vmem] * (len(state) + copies - 1),
        out_specs=[vmem] * per_device,
        compiler_params=params,
    )(lengths, *state, *keys[1:])

    back = [
        lax.ppermute(latent[k], both, [(owner(i, j, k), flat(i, j)) for i, j in devices])
        for k in range(per_device)
    ]
    return pl.pallas_call(
        functools.partial(project_kernel, per_device),
        out_shape=jax.ShapeDtypeStruct((rows, heads, w_uv.shape[2]), jnp.bfloat16),
        in_specs=[vmem] * (1 + per_device),
        out_specs=vmem,
        compiler_params=params,
    )(w_uv, *back)


def local_partial(
    query_tile_block,
    key_tile_block,
    incoming_keys,
    len_block,
    offset,
    own_first,
    score_scale,
    head_count,
):
    scores = (
        jnp.einsum(
            "vfa,vja->vfj", query_tile_block, key_tile_block, preferred_element_type=jnp.float32
        )
        * score_scale
    )
    positions = offset + lax.broadcasted_iota(jnp.int32, (1, 1, key_tile_block.shape[1]), 2)
    visible = positions < len_block[:, None, None]
    fresh_scores = (
        jnp.einsum(
            "vfa,vja->vfj", query_tile_block, incoming_keys, preferred_element_type=jnp.float32
        )
        * score_scale
    )
    spec_count = incoming_keys.shape[1]
    row_spec = (
        lax.broadcasted_iota(jnp.int32, (1, query_tile_block.shape[1], spec_count), 1) // head_count
    )
    key_spec = lax.broadcasted_iota(jnp.int32, (1, query_tile_block.shape[1], spec_count), 2)
    causal = (key_spec <= row_spec) & own_first
    row_top = jnp.maximum(
        jnp.max(jnp.where(visible, scores, masked_value), axis=2),
        jnp.max(jnp.where(causal, fresh_scores, masked_value), axis=2),
    )
    weights = jnp.where(visible, jnp.exp(scores - row_top[..., None]), 0.0)
    fresh_weights = jnp.where(causal, jnp.exp(fresh_scores - row_top[..., None]), 0.0)
    running_totals = jnp.sum(weights, axis=2) + jnp.sum(fresh_weights, axis=2)
    weighted = jnp.einsum(
        "mpu,mui->mpi",
        weights.astype(jnp.bfloat16),
        key_tile_block[:, :, :LATENT],
        preferred_element_type=jnp.float32,
    )
    weighted = weighted + jnp.einsum(
        "mpu,mui->mpi",
        fresh_weights.astype(jnp.bfloat16),
        incoming_keys[:, :, :LATENT],
        preferred_element_type=jnp.float32,
    )
    return (row_top, running_totals, weighted)


def project_values(latent_rows, value_weight):
    return jnp.einsum("rhc,hcv->rhv", latent_rows, value_weight, precision=lax.Precision.HIGHEST)


def split_positions(queries, new_latent, cache, lengths, w_uk, w_uv):
    own_rows, head_count, _ = queries.shape
    score_scale = (NOPE + ROPE) ** (-0.5)
    gathered, new_all = (
        lax.all_gather(queries, "seq", axis=0, tiled=True),
        lax.all_gather(new_latent, "seq", axis=0, tiled=True),
    )
    absorbed = jnp.einsum(
        "rhn,hnc->rhc", gathered[:, :, :NOPE], w_uk, preferred_element_type=jnp.float32
    ).astype(jnp.bfloat16)
    q_all = jnp.concatenate([absorbed, gathered[:, :, NOPE:]], axis=2)
    total_rows = q_all.shape[0]
    seq_count = total_rows // SPEC
    query_slots = SPEC * head_count
    q_seq = q_all.reshape(seq_count, query_slots, q_all.shape[2])
    new_seq = new_all.reshape(seq_count, SPEC, new_all.shape[1])
    seq_index = lax.axis_index("seq")
    offset = seq_index * cache.shape[1]
    own_first = seq_index == 0
    row_top, running_totals, weighted = local_partial(
        q_seq,
        lax.all_gather(cache, "head", axis=0, tiled=True),
        new_seq,
        lengths,
        offset,
        own_first,
        score_scale,
        head_count,
    )
    value_weight = w_uv.astype(jnp.float32)
    global_top = lax.pmax(row_top, "seq")
    factor = jnp.exp(row_top - global_top)
    scaled_totals = (running_totals * factor).reshape(total_rows, head_count)
    scaled_weighted = (weighted * factor[..., None]).reshape(total_rows, head_count, LATENT)
    row_totals, row_weighted = (
        lax.psum_scatter(scaled_totals, "seq", scatter_dimension=0, tiled=True),
        lax.psum_scatter(scaled_weighted, "seq", scatter_dimension=0, tiled=True),
    )
    latent_output = row_weighted / row_totals[..., None]
    result = project_values(latent_output, value_weight)
    return result.astype(jnp.bfloat16)


def shards(seq_size, head_size, queries, new_latent, cache, lengths, w_uk, w_uv):
    rows, owners = queries.shape[0], cache.shape[0]
    per_device = rows // SPEC
    if (
        per_device == 2
        and rows % SPEC == 0
        and seq_size == 2 * owners
        and head_size == owners
        and owners >= 4
        and owners & (owners - 1) == 0
        and cache.shape[2] % queries.shape[2] == 0
    ):
        return whole_sequences(
            seq_size, head_size, queries, new_latent, cache, lengths, w_uk, w_uv
        )
    return split_positions(queries, new_latent, cache, lengths, w_uk, w_uv)


def solution(mesh):
    return jax.shard_map(
        functools.partial(shards, mesh.shape["seq"], mesh.shape["head"]),
        mesh=mesh,
        in_specs=(
            P("seq", "head", None),
            P("seq", None),
            P("head", "seq", None),
            P(),
            P("head", None, None),
            P("head", None, None),
        ),
        out_specs=P("seq", "head", None),
        check_vma=False,
    )
```

```python
import functools

import jax
import jax.numpy as jnp
from jax import lax
from jax.experimental import pallas as pl
from jax.experimental.pallas import tpu as pltpu
from jax.sharding import PartitionSpec as P

NOPE = 128
ROPE = 64
LATENT = 512
SPEC = 4
SCORE_SCALE = (NOPE + ROPE) ** (-0.5)
VMEM_LIMIT = 16 * 1024 * 1024
LONG = pl.CostEstimate(flops=2 * 10**10, bytes_accessed=0, transcendentals=0)

masked_value = -1e30


def pick_kernel(owners, copies, cache_hbm, new_hbm, *refs):
    outs, (new_ref, sem) = refs[:owners], refs[owners:]
    group = lax.axis_index("seq") // copies
    width = cache_hbm.shape[1]
    moves = [
        pltpu.make_async_copy(
            cache_hbm.at[group ^ k], outs[k].at[pl.ds(0, width)], sem.at[k]
        )
        for k in range(owners)
    ]
    fresh_move = pltpu.make_async_copy(new_hbm, new_ref, sem.at[owners])
    fresh_move.start()
    for move in moves:
        move.start()
    fresh_move.wait()
    fresh = new_ref[...].astype(jnp.float32)
    rows, slots = outs[0].shape
    spare = -width % slots
    if spare:
        fresh = jnp.concatenate([fresh, jnp.zeros((fresh.shape[0], spare), jnp.float32)], axis=1)
    parts = [fresh[:, n : n + slots] for n in range(0, width, slots)]
    spare = rows - width - len(parts) * fresh.shape[0]
    if spare:
        parts.append(jnp.zeros((spare, slots), jnp.float32))
    fresh = jnp.concatenate(parts, axis=0).astype(outs[0].dtype)
    for out in outs:
        out[width:, :] = fresh
    for move in moves:
        move.wait()


def absorb_kernel(per_device, q_ref, w_ref, *outs):
    rows, heads, width = q_ref.shape
    piece = SPEC * heads
    q = q_ref[...].reshape(rows * heads, width)
    nope = q[:, :NOPE]
    own_head = lax.broadcasted_iota(jnp.int32, nope.shape, 0) % heads
    spread = jnp.concatenate(
        [jnp.where(own_head == h, nope, jnp.zeros_like(nope)) for h in range(heads)], axis=1
    )
    absorbed = jnp.dot(
        spread, w_ref[...].reshape(heads * NOPE, LATENT), preferred_element_type=jnp.float32
    ).astype(jnp.bfloat16)
    head_shard = lax.axis_index("head")
    for k in range(per_device):
        which = (head_shard + k) % per_device
        for a in range(per_device):

            @pl.when(which == a)
            def _():
                outs[k][:, :LATENT] = absorbed[a * piece : (a + 1) * piece]
                outs[k][:, LATENT:] = q[a * piece : (a + 1) * piece, NOPE:]


def block_scores(q, refs, starts, length):
    width = q.shape[1]
    keys = jnp.concatenate([ref[:width, :] for ref in refs], axis=1)
    lane = lax.broadcasted_iota(jnp.int32, (1, refs[0].shape[1]), 1)
    position = jnp.concatenate([lane + start for start in starts], axis=1)
    s = jnp.dot(q, keys, preferred_element_type=jnp.float32) * SCORE_SCALE
    return jnp.where(position < length, s, masked_value)


def weigh(s, refs, top):
    w = jnp.exp(s - top)
    values = jnp.concatenate([ref[:LATENT, :] for ref in refs], axis=1)
    out = lax.dot_general(
        w.astype(jnp.bfloat16),
        values,
        (((1,), (1,)), ((), ())),
        preferred_element_type=jnp.float32,
    )
    return jnp.sum(w, axis=1, keepdims=True), out


def begin_kernel(owners, copies, per_device, len_ref, *refs):
    q_refs, key_refs = refs[:per_device], refs[per_device : per_device + owners]
    q_out, top_ref, total_ref, out_ref = refs[per_device + owners :]
    seq_index = lax.axis_index("seq")
    group, core = seq_index // copies, seq_index % copies
    length = len_ref[lax.axis_index("head") * owners + group]
    slots = key_refs[0].shape[1]
    q = jnp.concatenate([ref[...] for ref in q_refs], axis=0)
    starts = [((group ^ k) * copies + core) * slots for k in range(owners)]
    s = block_scores(q, key_refs, starts, length)
    top = jnp.max(s, axis=1, keepdims=True)
    total, out = weigh(s, key_refs, top)
    q_out[...] = q
    top_ref[...] = jnp.broadcast_to(top, top_ref.shape)
    total_ref[...] = jnp.broadcast_to(total, total_ref.shape)
    out_ref[...] = out


def finish_kernel(
    owners, copies, per_device, heads, len_ref, q_ref, top_ref, total_ref, part_ref, *refs
):
    own_refs, far_refs = refs[:owners], refs[owners : owners * copies]
    outs, fresh_ref = refs[owners * copies : -1], refs[-1]
    seq_index = lax.axis_index("seq")
    group, core = seq_index // copies, seq_index % copies
    sequence = lax.axis_index("head") * owners + group
    length = len_ref[sequence]
    q = q_ref[...]
    slots, width = own_refs[0].shape[1], q.shape[1]

    home = sequence // per_device
    for e in range(copies):
        for k in range(owners):
            source = (group ^ k) * copies + (core + copies - e) % copies

            @pl.when(source == home)
            def _():
                fresh_ref[...] = (own_refs + far_refs)[e * owners + k][width:, :]

    parts = -(-width // slots)
    rows = per_device * SPEC
    fresh = fresh_ref[...].astype(jnp.float32)
    fresh = jnp.concatenate([fresh[n * rows : (n + 1) * rows] for n in range(parts)], axis=1)
    fresh = fresh[:, :width]
    spare = -rows % 16
    if spare:
        fresh = jnp.concatenate([fresh, jnp.zeros((spare, width), jnp.float32)], axis=0)
    fresh = fresh.astype(jnp.bfloat16)
    f = lax.dot_general(
        q, fresh, (((1,), (1,)), ((), ())), preferred_element_type=jnp.float32
    )
    row = lax.broadcasted_iota(jnp.int32, f.shape, 0) % (SPEC * heads)
    key = lax.broadcasted_iota(jnp.int32, f.shape, 1)
    causal = (key // SPEC == sequence % per_device) & (key % SPEC <= row // heads)
    f = jnp.where(causal, f * SCORE_SCALE, masked_value)

    starts = [
        ((group ^ k) * copies + (core + copies - e) % copies) * slots
        for e in range(1, copies)
        for k in range(owners)
    ]
    s = block_scores(q, far_refs, starts, length)
    first = top_ref[:, :1]
    top = jnp.maximum(
        jnp.maximum(first, jnp.max(s, axis=1, keepdims=True)), jnp.max(f, axis=1, keepdims=True)
    )
    total, out = weigh(s, far_refs, top)
    w = jnp.exp(f - top)
    scale = jnp.exp(first - top)
    total += jnp.sum(w, axis=1, keepdims=True) + total_ref[:, :1] * scale
    out += part_ref[...] * scale
    out += jnp.dot(
        w.astype(jnp.bfloat16), fresh[:, :LATENT], preferred_element_type=jnp.float32
    )
    out = (out / total).astype(jnp.bfloat16)
    piece = SPEC * heads
    for k in range(per_device):
        outs[k][...] = out[k * piece : (k + 1) * piece]


def project_kernel(per_device, w_ref, *refs):
    lat_refs, out_ref = refs[:-1], refs[-1]
    rows, heads, width = out_ref.shape
    head_shard = lax.axis_index("head")
    parts = []
    for a in range(per_device):
        part = lat_refs[0][...]
        for k in range(1, per_device):
            part = jnp.where((head_shard + k) % per_device == a, lat_refs[k][...], part)
        parts.append(part)
    latent = jnp.concatenate(parts, axis=0)
    out = jnp.zeros((rows * heads, width), jnp.float32)
    own_head = lax.broadcasted_iota(jnp.int32, out.shape, 0) % heads
    step = 2 if heads % 2 == 0 else 1
    for h in range(0, heads, step):
        group = jnp.concatenate([w_ref[h + n] for n in range(step)], axis=1)
        product = jnp.dot(latent, group, preferred_element_type=jnp.float32)
        for n in range(step):
            out = jnp.where(own_head == h + n, product[:, n * width : (n + 1) * width], out)
    out_ref[...] = out.astype(out_ref.dtype).reshape(out_ref.shape)


def whole_sequences(seq_size, head_size, queries, new_latent, cache, lengths, w_uk, w_uv):
    rows, heads, _ = queries.shape
    owners, slots, width = cache.shape
    copies = seq_size // owners
    per_device = rows // SPEC
    piece = SPEC * heads
    all_rows = per_device * piece
    fresh_rows = -(-rows * -(-width // slots) // 16) * 16
    params = pltpu.CompilerParams(vmem_limit_bytes=VMEM_LIMIT)
    vmem = pl.BlockSpec(memory_space=pltpu.VMEM)
    smem = pl.BlockSpec(memory_space=pltpu.SMEM)
    anywhere = pl.BlockSpec(memory_space=pl.ANY)
    both = ("seq", "head")
    devices = [(i, j) for i in range(seq_size) for j in range(head_size)]

    def flat(seq_index, head_index):
        return seq_index * head_size + head_index

    def in_hbm(x):
        return pltpu.with_memory_space_constraint(x, pltpu.HBM)

    def host(i, j):
        other = (i // copies) ^ (2 - ((j ^ (j >> 1)) & 1))
        return ((i % copies) * 2 + other // 2) * copies + other % 2

    def owner(i, j, k):
        sequence = i * per_device + (j + k) % per_device
        core = (j // per_device) ^ 1
        return flat((sequence % owners) * copies + core, sequence // owners)

    moved = lax.ppermute(queries, both, [(flat(i, j), flat(host(i, j), j)) for i, j in devices])

    def in_plane(move):
        return [(g * copies + t, move(g, t)) for g in range(owners) for t in range(copies)]

    picked = pl.pallas_call(
        functools.partial(pick_kernel, owners, copies),
        out_shape=[jax.ShapeDtypeStruct((width + fresh_rows, slots), cache.dtype)] * owners,
        in_specs=[anywhere] * 2,
        out_specs=[vmem] * owners,
        scratch_shapes=[
            pltpu.VMEM(new_latent.shape, new_latent.dtype),
            pltpu.SemaphoreType.DMA((owners + 1,)),
        ],
        compiler_params=params,
        cost_estimate=LONG,
    )(in_hbm(jnp.swapaxes(cache, 1, 2)), in_hbm(new_latent))
    own_keys = [picked[0]] + [
        lax.ppermute(picked[k], "seq", in_plane(lambda g, t: (g ^ k) * copies + t))
        for k in range(1, owners)
    ]
    far_keys = [
        lax.ppermute(keys, "seq", in_plane(lambda g, t: g * copies + (t + e) % copies))
        for e in range(1, copies)
        for keys in own_keys
    ]

    pieces = pl.pallas_call(
        functools.partial(absorb_kernel, per_device),
        out_shape=[jax.ShapeDtypeStruct((piece, width), cache.dtype)] * per_device,
        in_specs=[vmem] * 2,
        out_specs=[vmem] * per_device,
        compiler_params=params,
        cost_estimate=LONG,
    )(moved, w_uk)
    arrived = [
        lax.ppermute(
            pieces[k], both, [(flat(host(i, j), j), owner(i, j, k)) for i, j in devices]
        )
        for k in range(per_device)
    ]

    state = pl.pallas_call(
        functools.partial(begin_kernel, owners, copies, per_device),
        out_shape=[
            jax.ShapeDtypeStruct((all_rows, width), jnp.bfloat16),
            jax.ShapeDtypeStruct((all_rows, 128), jnp.float32),
            jax.ShapeDtypeStruct((all_rows, 128), jnp.float32),
            jax.ShapeDtypeStruct((all_rows, LATENT), jnp.float32),
        ],
        in_specs=[smem] + [vmem] * (per_device + owners),
        out_specs=[vmem] * 4,
        compiler_params=params,
        cost_estimate=LONG,
    )(lengths, *arrived, *own_keys)
    latent = pl.pallas_call(
        functools.partial(finish_kernel, owners, copies, per_device, heads),
        out_shape=[jax.ShapeDtypeStruct((piece, LATENT), jnp.bfloat16)] * per_device,
        in_specs=[smem] + [vmem] * (len(state) + owners * copies),
        out_specs=[vmem] * per_device,
        scratch_shapes=[pltpu.VMEM((fresh_rows, slots), jnp.bfloat16)],
        compiler_params=params,
    )(lengths, *state, *own_keys, *far_keys)

    back = [
        lax.ppermute(latent[k], both, [(owner(i, j, k), flat(i, j)) for i, j in devices])
        for k in range(per_device)
    ]
    return pl.pallas_call(
        functools.partial(project_kernel, per_device),
        out_shape=jax.ShapeDtypeStruct((rows, heads, w_uv.shape[2]), jnp.bfloat16),
        in_specs=[vmem] * (1 + per_device),
        out_specs=vmem,
        compiler_params=params,
    )(w_uv, *back)


def local_partial(
    query_tile_block,
    key_tile_block,
    incoming_keys,
    len_block,
    offset,
    own_first,
    score_scale,
    head_count,
):
    scores = (
        jnp.einsum(
            "vfa,vja->vfj", query_tile_block, key_tile_block, preferred_element_type=jnp.float32
        )
        * score_scale
    )
    positions = offset + lax.broadcasted_iota(jnp.int32, (1, 1, key_tile_block.shape[1]), 2)
    visible = positions < len_block[:, None, None]
    fresh_scores = (
        jnp.einsum(
            "vfa,vja->vfj", query_tile_block, incoming_keys, preferred_element_type=jnp.float32
        )
        * score_scale
    )
    spec_count = incoming_keys.shape[1]
    row_spec = (
        lax.broadcasted_iota(jnp.int32, (1, query_tile_block.shape[1], spec_count), 1) // head_count
    )
    key_spec = lax.broadcasted_iota(jnp.int32, (1, query_tile_block.shape[1], spec_count), 2)
    causal = (key_spec <= row_spec) & own_first
    row_top = jnp.maximum(
        jnp.max(jnp.where(visible, scores, masked_value), axis=2),
        jnp.max(jnp.where(causal, fresh_scores, masked_value), axis=2),
    )
    weights = jnp.where(visible, jnp.exp(scores - row_top[..., None]), 0.0)
    fresh_weights = jnp.where(causal, jnp.exp(fresh_scores - row_top[..., None]), 0.0)
    running_totals = jnp.sum(weights, axis=2) + jnp.sum(fresh_weights, axis=2)
    weighted = jnp.einsum(
        "mpu,mui->mpi",
        weights.astype(jnp.bfloat16),
        key_tile_block[:, :, :LATENT],
        preferred_element_type=jnp.float32,
    )
    weighted = weighted + jnp.einsum(
        "mpu,mui->mpi",
        fresh_weights.astype(jnp.bfloat16),
        incoming_keys[:, :, :LATENT],
        preferred_element_type=jnp.float32,
    )
    return (row_top, running_totals, weighted)


def project_values(latent_rows, value_weight):
    return jnp.einsum("rhc,hcv->rhv", latent_rows, value_weight, precision=lax.Precision.HIGHEST)


def split_positions(queries, new_latent, cache, lengths, w_uk, w_uv):
    own_rows, head_count, _ = queries.shape
    score_scale = (NOPE + ROPE) ** (-0.5)
    gathered, new_all = (
        lax.all_gather(queries, "seq", axis=0, tiled=True),
        lax.all_gather(new_latent, "seq", axis=0, tiled=True),
    )
    absorbed = jnp.einsum(
        "rhn,hnc->rhc", gathered[:, :, :NOPE], w_uk, preferred_element_type=jnp.float32
    ).astype(jnp.bfloat16)
    q_all = jnp.concatenate([absorbed, gathered[:, :, NOPE:]], axis=2)
    total_rows = q_all.shape[0]
    seq_count = total_rows // SPEC
    query_slots = SPEC * head_count
    q_seq = q_all.reshape(seq_count, query_slots, q_all.shape[2])
    new_seq = new_all.reshape(seq_count, SPEC, new_all.shape[1])
    seq_index = lax.axis_index("seq")
    offset = seq_index * cache.shape[1]
    own_first = seq_index == 0
    row_top, running_totals, weighted = local_partial(
        q_seq,
        lax.all_gather(cache, "head", axis=0, tiled=True),
        new_seq,
        lengths,
        offset,
        own_first,
        score_scale,
        head_count,
    )
    value_weight = w_uv.astype(jnp.float32)
    global_top = lax.pmax(row_top, "seq")
    factor = jnp.exp(row_top - global_top)
    scaled_totals = (running_totals * factor).reshape(total_rows, head_count)
    scaled_weighted = (weighted * factor[..., None]).reshape(total_rows, head_count, LATENT)
    row_totals, row_weighted = (
        lax.psum_scatter(scaled_totals, "seq", scatter_dimension=0, tiled=True),
        lax.psum_scatter(scaled_weighted, "seq", scatter_dimension=0, tiled=True),
    )
    latent_output = row_weighted / row_totals[..., None]
    result = project_values(latent_output, value_weight)
    return result.astype(jnp.bfloat16)


def shards(seq_size, head_size, queries, new_latent, cache, lengths, w_uk, w_uv):
    rows, owners = queries.shape[0], cache.shape[0]
    per_device = rows // SPEC
    if (
        per_device == 2
        and rows % SPEC == 0
        and seq_size == 2 * owners
        and head_size == owners == 4
    ):
        return whole_sequences(
            seq_size, head_size, queries, new_latent, cache, lengths, w_uk, w_uv
        )
    return split_positions(queries, new_latent, cache, lengths, w_uk, w_uv)


def solution(mesh):
    return jax.shard_map(
        functools.partial(shards, mesh.shape["seq"], mesh.shape["head"]),
        mesh=mesh,
        in_specs=(
            P("seq", "head", None),
            P("seq", None),
            P("head", "seq", None),
            P(),
            P("head", None, None),
            P("head", None, None),
        ),
        out_specs=P("seq", "head", None),
        check_vma=False,
    )
```

```python
import functools

import jax
import jax.numpy as jnp
from jax import lax
from jax.experimental import pallas as pl
from jax.experimental.pallas import tpu as pltpu
from jax.sharding import PartitionSpec as P

NOPE = 128
ROPE = 64
LATENT = 512
SPEC = 4
SCORE_SCALE = (NOPE + ROPE) ** (-0.5)
VMEM_LIMIT = 16 * 1024 * 1024
LONG = pl.CostEstimate(flops=2 * 10**10, bytes_accessed=0, transcendentals=0)

masked_value = -1e30


def pick_kernel(owners, copies, cache_hbm, new_hbm, *refs):
    outs, (new_ref, sem) = refs[:owners], refs[owners:]
    group = lax.axis_index("seq") // copies
    width = cache_hbm.shape[1]
    moves = [
        pltpu.make_async_copy(
            cache_hbm.at[group ^ k], outs[k].at[pl.ds(0, width)], sem.at[k]
        )
        for k in range(owners)
    ]
    fresh_move = pltpu.make_async_copy(new_hbm, new_ref, sem.at[owners])
    fresh_move.start()
    for move in moves:
        move.start()
    fresh_move.wait()
    fresh = new_ref[...].astype(jnp.float32)
    rows, slots = outs[0].shape
    spare = -width % slots
    if spare:
        fresh = jnp.concatenate([fresh, jnp.zeros((fresh.shape[0], spare), jnp.float32)], axis=1)
    parts = [fresh[:, n : n + slots] for n in range(0, width, slots)]
    spare = rows - width - len(parts) * fresh.shape[0]
    if spare:
        parts.append(jnp.zeros((spare, slots), jnp.float32))
    fresh = jnp.concatenate(parts, axis=0).astype(outs[0].dtype)
    for out in outs:
        out[width:, :] = fresh
    for move in moves:
        move.wait()


def place_kernel(owners, copies, *refs):
    blocks, out_ref, sem = refs[:owners], refs[owners], refs[owners + 1]
    group = lax.axis_index("seq") // copies
    moves = [
        pltpu.make_async_copy(blocks[k], out_ref.at[group ^ k], sem.at[k]) for k in range(owners)
    ]
    for move in moves:
        move.start()
    for move in moves:
        move.wait()


def absorb_kernel(per_device, q_ref, w_ref, *outs):
    rows, heads, width = q_ref.shape
    piece = SPEC * heads
    q = q_ref[...].reshape(rows * heads, width)
    nope = q[:, :NOPE]
    own_head = lax.broadcasted_iota(jnp.int32, nope.shape, 0) % heads
    spread = jnp.concatenate(
        [jnp.where(own_head == h, nope, jnp.zeros_like(nope)) for h in range(heads)], axis=1
    )
    absorbed = jnp.dot(
        spread, w_ref[...].reshape(heads * NOPE, LATENT), preferred_element_type=jnp.float32
    ).astype(jnp.bfloat16)
    head_shard = lax.axis_index("head")
    for k in range(per_device):
        which = (head_shard + k) % per_device
        for a in range(per_device):

            @pl.when(which == a)
            def _():
                outs[k][:, :LATENT] = absorbed[a * piece : (a + 1) * piece]
                outs[k][:, LATENT:] = q[a * piece : (a + 1) * piece, NOPE:]


def merge_kernel(*refs):
    q_refs, out_ref = refs[:-1], refs[-1]
    piece = q_refs[0].shape[0]
    for k, ref in enumerate(q_refs):
        out_ref[k * piece : (k + 1) * piece] = ref[...]


def attend_kernel(copies, per_device, heads, len_ref, q_ref, *refs):
    key_refs, outs = refs[:copies], refs[copies:]
    owners, rows, slots = key_refs[0].shape
    q = q_ref[...]
    width = q.shape[1]
    seq_index = lax.axis_index("seq")
    group, core = seq_index // copies, seq_index % copies
    sequence = lax.axis_index("head") * owners + group
    length = len_ref[sequence]
    lane = lax.broadcasted_iota(jnp.int32, (1, slots), 1)
    scores = []
    for e in range(copies):
        keys = jnp.concatenate([key_refs[e][g, :width] for g in range(owners)], axis=1)
        first = (core + copies - e) % copies
        position = jnp.concatenate(
            [lane + (g * copies + first) * slots for g in range(owners)], axis=1
        )
        s = jnp.dot(q, keys, preferred_element_type=jnp.float32) * SCORE_SCALE
        scores.append(jnp.where(position < length, s, masked_value))

    home = sequence // per_device
    fresh_all = key_refs[0][home // copies, width:]
    for e in range(1, copies):
        mine = (core + copies - e) % copies == home % copies
        fresh_all = jnp.where(mine, key_refs[e][home // copies, width:], fresh_all)
    fresh_all = fresh_all.astype(jnp.float32)
    count = per_device * SPEC
    parts = [fresh_all[n * count : (n + 1) * count] for n in range(-(-width // slots))]
    fresh = jnp.concatenate(parts, axis=1)[:, :width]
    spare = -count % 16
    if spare:
        fresh = jnp.concatenate([fresh, jnp.zeros((spare, width), jnp.float32)], axis=0)
    fresh = fresh.astype(jnp.bfloat16)
    f = lax.dot_general(
        q, fresh, (((1,), (1,)), ((), ())), preferred_element_type=jnp.float32
    )
    row = lax.broadcasted_iota(jnp.int32, f.shape, 0) % (SPEC * heads)
    key = lax.broadcasted_iota(jnp.int32, f.shape, 1)
    causal = (key // SPEC == sequence % per_device) & (key % SPEC <= row // heads)
    f = jnp.where(causal, f * SCORE_SCALE, masked_value)

    top = functools.reduce(
        jnp.maximum, [jnp.max(s, axis=1, keepdims=True) for s in scores + [f]]
    )
    w = jnp.exp(f - top)
    total = jnp.sum(w, axis=1, keepdims=True)
    out = jnp.dot(w.astype(jnp.bfloat16), fresh[:, :LATENT], preferred_element_type=jnp.float32)
    for s, ref in zip(scores, key_refs):
        w = jnp.exp(s - top)
        total += jnp.sum(w, axis=1, keepdims=True)
        values = jnp.concatenate([ref[g, :LATENT] for g in range(owners)], axis=1)
        out += lax.dot_general(
            w.astype(jnp.bfloat16),
            values,
            (((1,), (1,)), ((), ())),
            preferred_element_type=jnp.float32,
        )
    out = (out / total).astype(jnp.bfloat16)
    piece = SPEC * heads
    for k in range(per_device):
        outs[k][...] = out[k * piece : (k + 1) * piece]


def project_kernel(per_device, w_ref, *refs):
    lat_refs, out_ref = refs[:-1], refs[-1]
    rows, heads, width = out_ref.shape
    head_shard = lax.axis_index("head")
    parts = []
    for a in range(per_device):
        part = lat_refs[0][...]
        for k in range(1, per_device):
            part = jnp.where((head_shard + k) % per_device == a, lat_refs[k][...], part)
        parts.append(part)
    latent = jnp.concatenate(parts, axis=0)
    out = jnp.zeros((rows * heads, width), jnp.float32)
    own_head = lax.broadcasted_iota(jnp.int32, out.shape, 0) % heads
    step = 2 if heads % 2 == 0 else 1
    for h in range(0, heads, step):
        group = jnp.concatenate([w_ref[h + n] for n in range(step)], axis=1)
        product = jnp.dot(latent, group, preferred_element_type=jnp.float32)
        for n in range(step):
            out = jnp.where(own_head == h + n, product[:, n * width : (n + 1) * width], out)
    out_ref[...] = out.astype(out_ref.dtype).reshape(out_ref.shape)


def whole_sequences(seq_size, head_size, queries, new_latent, cache, lengths, w_uk, w_uv):
    rows, heads, _ = queries.shape
    owners, slots, width = cache.shape
    copies = seq_size // owners
    per_device = rows // SPEC
    piece = SPEC * heads
    all_rows = per_device * piece
    fresh_rows = -(-rows * -(-width // slots) // 16) * 16
    params = pltpu.CompilerParams(vmem_limit_bytes=VMEM_LIMIT)
    vmem = pl.BlockSpec(memory_space=pltpu.VMEM)
    smem = pl.BlockSpec(memory_space=pltpu.SMEM)
    anywhere = pl.BlockSpec(memory_space=pl.ANY)
    both = ("seq", "head")
    devices = [(i, j) for i in range(seq_size) for j in range(head_size)]

    def flat(seq_index, head_index):
        return seq_index * head_size + head_index

    def in_hbm(x):
        return pltpu.with_memory_space_constraint(x, pltpu.HBM)

    def host(i, j):
        other = (i // copies) ^ (2 - ((j ^ (j >> 1)) & 1))
        return ((i % copies) * 2 + other // 2) * copies + other % 2

    def owner(i, j, k):
        sequence = i * per_device + (j + k) % per_device
        core = (j // per_device) ^ 1
        return flat((sequence % owners) * copies + core, sequence // owners)

    moved = lax.ppermute(queries, both, [(flat(i, j), flat(host(i, j), j)) for i, j in devices])

    def in_plane(move):
        return [(g * copies + t, move(g, t)) for g in range(owners) for t in range(copies)]

    picked = pl.pallas_call(
        functools.partial(pick_kernel, owners, copies),
        out_shape=[jax.ShapeDtypeStruct((width + fresh_rows, slots), cache.dtype)] * owners,
        in_specs=[anywhere] * 2,
        out_specs=[vmem] * owners,
        scratch_shapes=[
            pltpu.VMEM(new_latent.shape, new_latent.dtype),
            pltpu.SemaphoreType.DMA((owners + 1,)),
        ],
        compiler_params=params,
        cost_estimate=LONG,
    )(in_hbm(jnp.swapaxes(cache, 1, 2)), in_hbm(new_latent))
    blocks = [picked[0]] + [
        lax.ppermute(picked[k], "seq", in_plane(lambda g, t: (g ^ k) * copies + t))
        for k in range(1, owners)
    ]
    keys = [
        pl.pallas_call(
            functools.partial(place_kernel, owners, copies),
            out_shape=jax.ShapeDtypeStruct((owners, *blocks[0].shape), cache.dtype),
            in_specs=[vmem] * owners,
            out_specs=vmem,
            scratch_shapes=[pltpu.SemaphoreType.DMA((owners,))],
            compiler_params=params,
        )(*blocks)
    ]
    for e in range(1, copies):
        keys.append(
            lax.ppermute(
                keys[0], "seq", in_plane(lambda g, t: g * copies + (t + e) % copies)
            )
        )

    pieces = pl.pallas_call(
        functools.partial(absorb_kernel, per_device),
        out_shape=[jax.ShapeDtypeStruct((piece, width), cache.dtype)] * per_device,
        in_specs=[vmem] * 2,
        out_specs=[vmem] * per_device,
        compiler_params=params,
        cost_estimate=LONG,
    )(moved, w_uk)
    arrived = [
        lax.ppermute(
            pieces[k], both, [(flat(host(i, j), j), owner(i, j, k)) for i, j in devices]
        )
        for k in range(per_device)
    ]

    q_all = pl.pallas_call(
        merge_kernel,
        out_shape=jax.ShapeDtypeStruct((all_rows, width), jnp.bfloat16),
        in_specs=[vmem] * per_device,
        out_specs=vmem,
        compiler_params=params,
        cost_estimate=LONG,
    )(*arrived)
    latent = pl.pallas_call(
        functools.partial(attend_kernel, copies, per_device, heads),
        out_shape=[jax.ShapeDtypeStruct((piece, LATENT), jnp.bfloat16)] * per_device,
        in_specs=[smem] + [vmem] * (1 + copies),
        out_specs=[vmem] * per_device,
        compiler_params=params,
    )(lengths, q_all, *keys)

    back = [
        lax.ppermute(latent[k], both, [(owner(i, j, k), flat(i, j)) for i, j in devices])
        for k in range(per_device)
    ]
    return pl.pallas_call(
        functools.partial(project_kernel, per_device),
        out_shape=jax.ShapeDtypeStruct((rows, heads, w_uv.shape[2]), jnp.bfloat16),
        in_specs=[vmem] * (1 + per_device),
        out_specs=vmem,
        compiler_params=params,
    )(w_uv, *back)


def local_partial(
    query_tile_block,
    key_tile_block,
    incoming_keys,
    len_block,
    offset,
    own_first,
    score_scale,
    head_count,
):
    scores = (
        jnp.einsum(
            "vfa,vja->vfj", query_tile_block, key_tile_block, preferred_element_type=jnp.float32
        )
        * score_scale
    )
    positions = offset + lax.broadcasted_iota(jnp.int32, (1, 1, key_tile_block.shape[1]), 2)
    visible = positions < len_block[:, None, None]
    fresh_scores = (
        jnp.einsum(
            "vfa,vja->vfj", query_tile_block, incoming_keys, preferred_element_type=jnp.float32
        )
        * score_scale
    )
    spec_count = incoming_keys.shape[1]
    row_spec = (
        lax.broadcasted_iota(jnp.int32, (1, query_tile_block.shape[1], spec_count), 1) // head_count
    )
    key_spec = lax.broadcasted_iota(jnp.int32, (1, query_tile_block.shape[1], spec_count), 2)
    causal = (key_spec <= row_spec) & own_first
    row_top = jnp.maximum(
        jnp.max(jnp.where(visible, scores, masked_value), axis=2),
        jnp.max(jnp.where(causal, fresh_scores, masked_value), axis=2),
    )
    weights = jnp.where(visible, jnp.exp(scores - row_top[..., None]), 0.0)
    fresh_weights = jnp.where(causal, jnp.exp(fresh_scores - row_top[..., None]), 0.0)
    running_totals = jnp.sum(weights, axis=2) + jnp.sum(fresh_weights, axis=2)
    weighted = jnp.einsum(
        "mpu,mui->mpi",
        weights.astype(jnp.bfloat16),
        key_tile_block[:, :, :LATENT],
        preferred_element_type=jnp.float32,
    )
    weighted = weighted + jnp.einsum(
        "mpu,mui->mpi",
        fresh_weights.astype(jnp.bfloat16),
        incoming_keys[:, :, :LATENT],
        preferred_element_type=jnp.float32,
    )
    return (row_top, running_totals, weighted)


def project_values(latent_rows, value_weight):
    return jnp.einsum("rhc,hcv->rhv", latent_rows, value_weight, precision=lax.Precision.HIGHEST)


def split_positions(queries, new_latent, cache, lengths, w_uk, w_uv):
    own_rows, head_count, _ = queries.shape
    score_scale = (NOPE + ROPE) ** (-0.5)
    gathered, new_all = (
        lax.all_gather(queries, "seq", axis=0, tiled=True),
        lax.all_gather(new_latent, "seq", axis=0, tiled=True),
    )
    absorbed = jnp.einsum(
        "rhn,hnc->rhc", gathered[:, :, :NOPE], w_uk, preferred_element_type=jnp.float32
    ).astype(jnp.bfloat16)
    q_all = jnp.concatenate([absorbed, gathered[:, :, NOPE:]], axis=2)
    total_rows = q_all.shape[0]
    seq_count = total_rows // SPEC
    query_slots = SPEC * head_count
    q_seq = q_all.reshape(seq_count, query_slots, q_all.shape[2])
    new_seq = new_all.reshape(seq_count, SPEC, new_all.shape[1])
    seq_index = lax.axis_index("seq")
    offset = seq_index * cache.shape[1]
    own_first = seq_index == 0
    row_top, running_totals, weighted = local_partial(
        q_seq,
        lax.all_gather(cache, "head", axis=0, tiled=True),
        new_seq,
        lengths,
        offset,
        own_first,
        score_scale,
        head_count,
    )
    value_weight = w_uv.astype(jnp.float32)
    global_top = lax.pmax(row_top, "seq")
    factor = jnp.exp(row_top - global_top)
    scaled_totals = (running_totals * factor).reshape(total_rows, head_count)
    scaled_weighted = (weighted * factor[..., None]).reshape(total_rows, head_count, LATENT)
    row_totals, row_weighted = (
        lax.psum_scatter(scaled_totals, "seq", scatter_dimension=0, tiled=True),
        lax.psum_scatter(scaled_weighted, "seq", scatter_dimension=0, tiled=True),
    )
    latent_output = row_weighted / row_totals[..., None]
    result = project_values(latent_output, value_weight)
    return result.astype(jnp.bfloat16)


def shards(seq_size, head_size, queries, new_latent, cache, lengths, w_uk, w_uv):
    rows, owners = queries.shape[0], cache.shape[0]
    per_device = rows // SPEC
    if (
        per_device == 2
        and rows % SPEC == 0
        and seq_size == 2 * owners
        and head_size == owners == 4
    ):
        return whole_sequences(
            seq_size, head_size, queries, new_latent, cache, lengths, w_uk, w_uv
        )
    return split_positions(queries, new_latent, cache, lengths, w_uk, w_uv)


def solution(mesh):
    return jax.shard_map(
        functools.partial(shards, mesh.shape["seq"], mesh.shape["head"]),
        mesh=mesh,
        in_specs=(
            P("seq", "head", None),
            P("seq", None),
            P("head", "seq", None),
            P(),
            P("head", None, None),
            P("head", None, None),
        ),
        out_specs=P("seq", "head", None),
        check_vma=False,
    )
```

```python
import functools

import jax
import jax.numpy as jnp
from jax import lax
from jax.experimental import pallas as pl
from jax.experimental.pallas import tpu as pltpu
from jax.sharding import PartitionSpec as P

NOPE = 128
ROPE = 64
LATENT = 512
SPEC = 4
SCORE_SCALE = (NOPE + ROPE) ** (-0.5)
VMEM_LIMIT = 16 * 1024 * 1024
LONG = pl.CostEstimate(flops=2 * 10**10, bytes_accessed=0, transcendentals=0)

masked_value = -1e30


def pick_kernel(turn, copies, cache_hbm, new_hbm, *refs):
    owners = len(turn)
    outs, (new_ref, sem) = refs[:owners], refs[owners:]
    group = lax.axis_index("seq") // copies
    width = cache_hbm.shape[1]
    moves = [
        pltpu.make_async_copy(
            cache_hbm.at[group ^ turn[k]], outs[k].at[pl.ds(0, width)], sem.at[k]
        )
        for k in range(owners)
    ]
    fresh_move = pltpu.make_async_copy(new_hbm, new_ref, sem.at[owners])
    fresh_move.start()
    for move in moves:
        move.start()
    fresh_move.wait()
    fresh = new_ref[...].astype(jnp.float32)
    rows, slots = outs[0].shape
    spare = -width % slots
    if spare:
        fresh = jnp.concatenate([fresh, jnp.zeros((fresh.shape[0], spare), jnp.float32)], axis=1)
    parts = [fresh[:, n : n + slots] for n in range(0, width, slots)]
    spare = rows - width - len(parts) * fresh.shape[0]
    if spare:
        parts.append(jnp.zeros((spare, slots), jnp.float32))
    fresh = jnp.concatenate(parts, axis=0).astype(outs[0].dtype)
    for out in outs:
        out[width:, :] = fresh
    for move in moves:
        move.wait()


def pair_kernel(first_ref, second_ref, out_ref, sem):
    moves = [
        pltpu.make_async_copy(ref, out_ref.at[n], sem.at[n])
        for n, ref in enumerate((first_ref, second_ref))
    ]
    for move in moves:
        move.start()
    for move in moves:
        move.wait()


def absorb_kernel(per_device, q_ref, w_ref, *outs):
    rows, heads, width = q_ref.shape
    piece = SPEC * heads
    q = q_ref[...].reshape(rows * heads, width)
    nope = q[:, :NOPE]
    own_head = lax.broadcasted_iota(jnp.int32, nope.shape, 0) % heads
    spread = jnp.concatenate(
        [jnp.where(own_head == h, nope, jnp.zeros_like(nope)) for h in range(heads)], axis=1
    )
    absorbed = jnp.dot(
        spread, w_ref[...].reshape(heads * NOPE, LATENT), preferred_element_type=jnp.float32
    ).astype(jnp.bfloat16)
    head_shard = lax.axis_index("head")
    for k in range(per_device):
        which = (head_shard + k) % per_device
        for a in range(per_device):

            @pl.when(which == a)
            def _():
                outs[k][:, :LATENT] = absorbed[a * piece : (a + 1) * piece]
                outs[k][:, LATENT:] = q[a * piece : (a + 1) * piece, NOPE:]


def block_scores(q, refs, starts, length):
    width = q.shape[1]
    keys = jnp.concatenate([ref[:width, :] for ref in refs], axis=1)
    lane = lax.broadcasted_iota(jnp.int32, (1, refs[0].shape[1]), 1)
    position = jnp.concatenate([lane + start for start in starts], axis=1)
    s = jnp.dot(q, keys, preferred_element_type=jnp.float32) * SCORE_SCALE
    return jnp.where(position < length, s, masked_value)


def weigh(s, refs, top):
    w = jnp.exp(s - top)
    values = jnp.concatenate([ref[:LATENT, :] for ref in refs], axis=1)
    out = lax.dot_general(
        w.astype(jnp.bfloat16),
        values,
        (((1,), (1,)), ((), ())),
        preferred_element_type=jnp.float32,
    )
    return jnp.sum(w, axis=1, keepdims=True), out


def begin_kernel(turn, copies, per_device, len_ref, *refs):
    owners = len(turn)
    q_refs, key_refs = refs[:per_device], refs[per_device : per_device + owners]
    q_out, top_ref, total_ref, out_ref = refs[per_device + owners :]
    seq_index = lax.axis_index("seq")
    group, core = seq_index // copies, seq_index % copies
    length = len_ref[lax.axis_index("head") * owners + group]
    slots = key_refs[0].shape[1]
    q = jnp.concatenate([ref[...] for ref in q_refs], axis=0)
    starts = [((group ^ k) * copies + core) * slots for k in turn]
    s = block_scores(q, key_refs, starts, length)
    top = jnp.max(s, axis=1, keepdims=True)
    total, out = weigh(s, key_refs, top)
    q_out[...] = q
    top_ref[...] = jnp.broadcast_to(top, top_ref.shape)
    total_ref[...] = jnp.broadcast_to(total, total_ref.shape)
    out_ref[...] = out


def finish_kernel(
    turn, copies, per_device, heads, len_ref, q_ref, top_ref, total_ref, part_ref, *refs
):
    owners = len(turn)
    own_refs, (pair_ref, *far_refs) = refs[:owners], refs[owners : 2 * owners - 1]
    far_refs = [pair_ref.at[0], pair_ref.at[1]] + far_refs
    outs, fresh_ref = refs[2 * owners - 1 : -1], refs[-1]
    seq_index = lax.axis_index("seq")
    group, core = seq_index // copies, seq_index % copies
    sequence = lax.axis_index("head") * owners + group
    length = len_ref[sequence]
    q = q_ref[...]
    slots, width = own_refs[0].shape[1], q.shape[1]

    home = sequence // per_device
    for e in range(copies):
        for k in range(owners):
            source = (group ^ turn[k]) * copies + (core + copies - e) % copies

            @pl.when(source == home)
            def _():
                fresh_ref[...] = (far_refs if e else own_refs)[k][width:, :]

    parts = -(-width // slots)
    rows = per_device * SPEC
    fresh = fresh_ref[...].astype(jnp.float32)
    fresh = jnp.concatenate([fresh[n * rows : (n + 1) * rows] for n in range(parts)], axis=1)
    fresh = fresh[:, :width]
    spare = -rows % 16
    if spare:
        fresh = jnp.concatenate([fresh, jnp.zeros((spare, width), jnp.float32)], axis=0)
    fresh = fresh.astype(jnp.bfloat16)
    f = lax.dot_general(
        q, fresh, (((1,), (1,)), ((), ())), preferred_element_type=jnp.float32
    )
    row = lax.broadcasted_iota(jnp.int32, f.shape, 0) % (SPEC * heads)
    key = lax.broadcasted_iota(jnp.int32, f.shape, 1)
    causal = (key // SPEC == sequence % per_device) & (key % SPEC <= row // heads)
    f = jnp.where(causal, f * SCORE_SCALE, masked_value)

    starts = [
        ((group ^ k) * copies + (core + copies - e) % copies) * slots
        for e in range(1, copies)
        for k in turn
    ]
    s = block_scores(q, far_refs, starts, length)
    first = top_ref[:, :1]
    top = jnp.maximum(
        jnp.maximum(first, jnp.max(s, axis=1, keepdims=True)), jnp.max(f, axis=1, keepdims=True)
    )
    total, out = weigh(s, far_refs, top)
    w = jnp.exp(f - top)
    scale = jnp.exp(first - top)
    total += jnp.sum(w, axis=1, keepdims=True) + total_ref[:, :1] * scale
    out += part_ref[...] * scale
    out += jnp.dot(
        w.astype(jnp.bfloat16), fresh[:, :LATENT], preferred_element_type=jnp.float32
    )
    out = (out / total).astype(jnp.bfloat16)
    piece = SPEC * heads
    for k in range(per_device):
        outs[k][...] = out[k * piece : (k + 1) * piece]


def project_kernel(per_device, w_ref, *refs):
    lat_refs, out_ref = refs[:-1], refs[-1]
    rows, heads, width = out_ref.shape
    head_shard = lax.axis_index("head")
    parts = []
    for a in range(per_device):
        part = lat_refs[0][...]
        for k in range(1, per_device):
            part = jnp.where((head_shard + k) % per_device == a, lat_refs[k][...], part)
        parts.append(part)
    latent = jnp.concatenate(parts, axis=0)
    out = jnp.zeros((rows * heads, width), jnp.float32)
    own_head = lax.broadcasted_iota(jnp.int32, out.shape, 0) % heads
    step = 2 if heads % 2 == 0 else 1
    for h in range(0, heads, step):
        group = jnp.concatenate([w_ref[h + n] for n in range(step)], axis=1)
        product = jnp.dot(latent, group, preferred_element_type=jnp.float32)
        for n in range(step):
            out = jnp.where(own_head == h + n, product[:, n * width : (n + 1) * width], out)
    out_ref[...] = out.astype(out_ref.dtype).reshape(out_ref.shape)


def whole_sequences(seq_size, head_size, queries, new_latent, cache, lengths, w_uk, w_uv):
    rows, heads, _ = queries.shape
    owners, slots, width = cache.shape
    copies = seq_size // owners
    per_device = rows // SPEC
    piece = SPEC * heads
    all_rows = per_device * piece
    fresh_rows = -(-rows * -(-width // slots) // 16) * 16
    params = pltpu.CompilerParams(vmem_limit_bytes=VMEM_LIMIT)
    vmem = pl.BlockSpec(memory_space=pltpu.VMEM)
    smem = pl.BlockSpec(memory_space=pltpu.SMEM)
    anywhere = pl.BlockSpec(memory_space=pl.ANY)
    both = ("seq", "head")
    devices = [(i, j) for i in range(seq_size) for j in range(head_size)]

    def flat(seq_index, head_index):
        return seq_index * head_size + head_index

    def in_hbm(x):
        return pltpu.with_memory_space_constraint(x, pltpu.HBM)

    def host(i, j):
        other = (i // copies) ^ (2 - ((j ^ (j >> 1)) & 1))
        return ((i % copies) * 2 + other // 2) * copies + other % 2

    def owner(i, j, k):
        sequence = i * per_device + (j + k) % per_device
        core = (j // per_device) ^ 1
        return flat((sequence % owners) * copies + core, sequence // owners)

    moved = lax.ppermute(queries, both, [(flat(i, j), flat(host(i, j), j)) for i, j in devices])

    turn = [0] + list(range(owners - 1, 0, -1))

    def in_plane(move):
        return [(g * copies + t, move(g, t)) for g in range(owners) for t in range(copies)]

    picked = pl.pallas_call(
        functools.partial(pick_kernel, turn, copies),
        out_shape=[jax.ShapeDtypeStruct((width + fresh_rows, slots), cache.dtype)] * owners,
        in_specs=[anywhere] * 2,
        out_specs=[vmem] * owners,
        scratch_shapes=[
            pltpu.VMEM(new_latent.shape, new_latent.dtype),
            pltpu.SemaphoreType.DMA((owners + 1,)),
        ],
        compiler_params=params,
        cost_estimate=LONG,
    )(in_hbm(jnp.swapaxes(cache, 1, 2)), in_hbm(new_latent))
    own_keys = [picked[0]] + [
        lax.ppermute(picked[k], "seq", in_plane(lambda g, t: (g ^ turn[k]) * copies + t))
        for k in range(1, owners)
    ]
    pair = pl.pallas_call(
        pair_kernel,
        out_shape=jax.ShapeDtypeStruct((2, *picked[0].shape), cache.dtype),
        in_specs=[vmem] * 2,
        out_specs=vmem,
        scratch_shapes=[pltpu.SemaphoreType.DMA((2,))],
        compiler_params=params,
    )(*own_keys[:2])
    other_core = in_plane(lambda g, t: g * copies + (t + 1) % copies)
    far_keys = [lax.ppermute(keys, "seq", other_core) for keys in [pair] + own_keys[2:]]

    pieces = pl.pallas_call(
        functools.partial(absorb_kernel, per_device),
        out_shape=[jax.ShapeDtypeStruct((piece, width), cache.dtype)] * per_device,
        in_specs=[vmem] * 2,
        out_specs=[vmem] * per_device,
        compiler_params=params,
        cost_estimate=LONG,
    )(moved, w_uk)
    arrived = [
        lax.ppermute(
            pieces[k], both, [(flat(host(i, j), j), owner(i, j, k)) for i, j in devices]
        )
        for k in range(per_device)
    ]

    state = pl.pallas_call(
        functools.partial(begin_kernel, turn, copies, per_device),
        out_shape=[
            jax.ShapeDtypeStruct((all_rows, width), jnp.bfloat16),
            jax.ShapeDtypeStruct((all_rows, 128), jnp.float32),
            jax.ShapeDtypeStruct((all_rows, 128), jnp.float32),
            jax.ShapeDtypeStruct((all_rows, LATENT), jnp.float32),
        ],
        in_specs=[smem] + [vmem] * (per_device + owners),
        out_specs=[vmem] * 4,
        compiler_params=params,
        cost_estimate=LONG,
    )(lengths, *arrived, *own_keys)
    latent = pl.pallas_call(
        functools.partial(finish_kernel, turn, copies, per_device, heads),
        out_shape=[jax.ShapeDtypeStruct((piece, LATENT), jnp.bfloat16)] * per_device,
        in_specs=[smem] + [vmem] * (len(state) + len(own_keys) + len(far_keys)),
        out_specs=[vmem] * per_device,
        scratch_shapes=[pltpu.VMEM((fresh_rows, slots), jnp.bfloat16)],
        compiler_params=params,
    )(lengths, *state, *own_keys, *far_keys)

    back = [
        lax.ppermute(latent[k], both, [(owner(i, j, k), flat(i, j)) for i, j in devices])
        for k in range(per_device)
    ]
    return pl.pallas_call(
        functools.partial(project_kernel, per_device),
        out_shape=jax.ShapeDtypeStruct((rows, heads, w_uv.shape[2]), jnp.bfloat16),
        in_specs=[vmem] * (1 + per_device),
        out_specs=vmem,
        compiler_params=params,
    )(w_uv, *back)


def local_partial(
    query_tile_block,
    key_tile_block,
    incoming_keys,
    len_block,
    offset,
    own_first,
    score_scale,
    head_count,
):
    scores = (
        jnp.einsum(
            "vfa,vja->vfj", query_tile_block, key_tile_block, preferred_element_type=jnp.float32
        )
        * score_scale
    )
    positions = offset + lax.broadcasted_iota(jnp.int32, (1, 1, key_tile_block.shape[1]), 2)
    visible = positions < len_block[:, None, None]
    fresh_scores = (
        jnp.einsum(
            "vfa,vja->vfj", query_tile_block, incoming_keys, preferred_element_type=jnp.float32
        )
        * score_scale
    )
    spec_count = incoming_keys.shape[1]
    row_spec = (
        lax.broadcasted_iota(jnp.int32, (1, query_tile_block.shape[1], spec_count), 1) // head_count
    )
    key_spec = lax.broadcasted_iota(jnp.int32, (1, query_tile_block.shape[1], spec_count), 2)
    causal = (key_spec <= row_spec) & own_first
    row_top = jnp.maximum(
        jnp.max(jnp.where(visible, scores, masked_value), axis=2),
        jnp.max(jnp.where(causal, fresh_scores, masked_value), axis=2),
    )
    weights = jnp.where(visible, jnp.exp(scores - row_top[..., None]), 0.0)
    fresh_weights = jnp.where(causal, jnp.exp(fresh_scores - row_top[..., None]), 0.0)
    running_totals = jnp.sum(weights, axis=2) + jnp.sum(fresh_weights, axis=2)
    weighted = jnp.einsum(
        "mpu,mui->mpi",
        weights.astype(jnp.bfloat16),
        key_tile_block[:, :, :LATENT],
        preferred_element_type=jnp.float32,
    )
    weighted = weighted + jnp.einsum(
        "mpu,mui->mpi",
        fresh_weights.astype(jnp.bfloat16),
        incoming_keys[:, :, :LATENT],
        preferred_element_type=jnp.float32,
    )
    return (row_top, running_totals, weighted)


def project_values(latent_rows, value_weight):
    return jnp.einsum("rhc,hcv->rhv", latent_rows, value_weight, precision=lax.Precision.HIGHEST)


def split_positions(queries, new_latent, cache, lengths, w_uk, w_uv):
    own_rows, head_count, _ = queries.shape
    score_scale = (NOPE + ROPE) ** (-0.5)
    gathered, new_all = (
        lax.all_gather(queries, "seq", axis=0, tiled=True),
        lax.all_gather(new_latent, "seq", axis=0, tiled=True),
    )
    absorbed = jnp.einsum(
        "rhn,hnc->rhc", gathered[:, :, :NOPE], w_uk, preferred_element_type=jnp.float32
    ).astype(jnp.bfloat16)
    q_all = jnp.concatenate([absorbed, gathered[:, :, NOPE:]], axis=2)
    total_rows = q_all.shape[0]
    seq_count = total_rows // SPEC
    query_slots = SPEC * head_count
    q_seq = q_all.reshape(seq_count, query_slots, q_all.shape[2])
    new_seq = new_all.reshape(seq_count, SPEC, new_all.shape[1])
    seq_index = lax.axis_index("seq")
    offset = seq_index * cache.shape[1]
    own_first = seq_index == 0
    row_top, running_totals, weighted = local_partial(
        q_seq,
        lax.all_gather(cache, "head", axis=0, tiled=True),
        new_seq,
        lengths,
        offset,
        own_first,
        score_scale,
        head_count,
    )
    value_weight = w_uv.astype(jnp.float32)
    global_top = lax.pmax(row_top, "seq")
    factor = jnp.exp(row_top - global_top)
    scaled_totals = (running_totals * factor).reshape(total_rows, head_count)
    scaled_weighted = (weighted * factor[..., None]).reshape(total_rows, head_count, LATENT)
    row_totals, row_weighted = (
        lax.psum_scatter(scaled_totals, "seq", scatter_dimension=0, tiled=True),
        lax.psum_scatter(scaled_weighted, "seq", scatter_dimension=0, tiled=True),
    )
    latent_output = row_weighted / row_totals[..., None]
    result = project_values(latent_output, value_weight)
    return result.astype(jnp.bfloat16)


def shards(seq_size, head_size, queries, new_latent, cache, lengths, w_uk, w_uv):
    rows, owners = queries.shape[0], cache.shape[0]
    per_device = rows // SPEC
    if (
        per_device == 2
        and rows % SPEC == 0
        and seq_size == 2 * owners
        and head_size == owners == 4
    ):
        return whole_sequences(
            seq_size, head_size, queries, new_latent, cache, lengths, w_uk, w_uv
        )
    return split_positions(queries, new_latent, cache, lengths, w_uk, w_uv)


def solution(mesh):
    return jax.shard_map(
        functools.partial(shards, mesh.shape["seq"], mesh.shape["head"]),
        mesh=mesh,
        in_specs=(
            P("seq", "head", None),
            P("seq", None),
            P("head", "seq", None),
            P(),
            P("head", None, None),
            P("head", None, None),
        ),
        out_specs=P("seq", "head", None),
        check_vma=False,
    )
```

```python
import functools

import jax
import jax.numpy as jnp
from jax import lax
from jax.experimental import pallas as pl
from jax.experimental.pallas import tpu as pltpu
from jax.sharding import PartitionSpec as P

NOPE = 128
ROPE = 64
LATENT = 512
SPEC = 4
SCORE_SCALE = (NOPE + ROPE) ** (-0.5)
COPIES = 2
VMEM_LIMIT = 16 * 1024 * 1024
LONG = pl.CostEstimate(flops=2 * 10**10, bytes_accessed=0, transcendentals=0)

masked_value = -1e30


def far_half(plane, pair):
    return 1 * (plane <= 2 * pair)


def first_out(host_chip, k):
    return (host_chip + 1 + k) % 2


def first_back(home_chip, head_shard):
    far = 1 * (far_half(home_chip, head_shard // 2) == head_shard % 2)
    return home_chip % 2 ^ far


def first_block(plane, chip, core):
    arrived = 1 - chip % 2 ^ plane // 2 ^ core
    back = far_half(plane, 1 - core) ^ (1 * (chip % 2 == plane % 2))
    return arrived ^ back


def pick_kernel(turn, copies, cache_hbm, new_hbm, *refs):
    owners = len(turn)
    outs, (new_ref, sem) = refs[:owners], refs[owners:]
    group = lax.axis_index("seq") // copies
    width = cache_hbm.shape[1]
    moves = [
        pltpu.make_async_copy(
            cache_hbm.at[group ^ turn[k]], outs[k].at[pl.ds(0, width)], sem.at[k]
        )
        for k in range(owners)
    ]
    fresh_move = pltpu.make_async_copy(new_hbm, new_ref, sem.at[owners])
    fresh_move.start()
    for move in moves:
        move.start()
    fresh_move.wait()
    fresh = new_ref[...].astype(jnp.float32)
    rows, slots = outs[0].shape
    spare = -width % slots
    if spare:
        fresh = jnp.concatenate([fresh, jnp.zeros((fresh.shape[0], spare), jnp.float32)], axis=1)
    parts = [fresh[:, n : n + slots] for n in range(0, width, slots)]
    spare = rows - width - len(parts) * fresh.shape[0]
    if spare:
        parts.append(jnp.zeros((spare, slots), jnp.float32))
    fresh = jnp.concatenate(parts, axis=0).astype(outs[0].dtype)
    for out in outs:
        out[width:, :] = fresh
    for move in moves:
        move.wait()


def pair_kernel(first_ref, second_ref, out_ref, sem):
    moves = [
        pltpu.make_async_copy(ref, out_ref.at[n], sem.at[n])
        for n, ref in enumerate((first_ref, second_ref))
    ]
    for move in moves:
        move.start()
    for move in moves:
        move.wait()


def absorb_kernel(per_device, q_ref, w_ref, *outs):
    rows, heads, width = q_ref.shape
    piece = SPEC * heads
    q = q_ref[...].reshape(rows * heads, width)
    nope = q[:, :NOPE]
    own_head = lax.broadcasted_iota(jnp.int32, nope.shape, 0) % heads
    spread = jnp.concatenate(
        [jnp.where(own_head == h, nope, jnp.zeros_like(nope)) for h in range(heads)], axis=1
    )
    absorbed = jnp.dot(
        spread, w_ref[...].reshape(heads * NOPE, LATENT), preferred_element_type=jnp.float32
    ).astype(jnp.bfloat16)
    group = lax.axis_index("seq") // COPIES
    for k in range(per_device):
        which = first_out(group, k)
        for a in range(per_device):

            @pl.when(which == a)
            def _():
                outs[k][:, :LATENT] = absorbed[a * piece : (a + 1) * piece]
                outs[k][:, LATENT:] = q[a * piece : (a + 1) * piece, NOPE:]


def block_scores(q, refs, starts, length):
    width = q.shape[1]
    keys = jnp.concatenate([ref[:width, :] for ref in refs], axis=1)
    lane = lax.broadcasted_iota(jnp.int32, (1, refs[0].shape[1]), 1)
    position = jnp.concatenate([lane + start for start in starts], axis=1)
    s = jnp.dot(q, keys, preferred_element_type=jnp.float32) * SCORE_SCALE
    return jnp.where(position < length, s, masked_value)


def weigh(s, refs, top):
    w = jnp.exp(s - top)
    values = jnp.concatenate([ref[:LATENT, :] for ref in refs], axis=1)
    out = lax.dot_general(
        w.astype(jnp.bfloat16),
        values,
        (((1,), (1,)), ((), ())),
        preferred_element_type=jnp.float32,
    )
    return jnp.sum(w, axis=1, keepdims=True), out


def begin_kernel(turn, copies, per_device, len_ref, *refs):
    owners = len(turn)
    q_refs, key_refs = refs[:per_device], refs[per_device : per_device + owners]
    q_out, top_ref, total_ref, out_ref = refs[per_device + owners :]
    seq_index = lax.axis_index("seq")
    group, core = seq_index // copies, seq_index % copies
    length = len_ref[lax.axis_index("head") * owners + group]
    slots = key_refs[0].shape[1]
    q = jnp.concatenate([ref[...] for ref in q_refs], axis=0)
    starts = [((group ^ k) * copies + core) * slots for k in turn]
    s = block_scores(q, key_refs, starts, length)
    top = jnp.max(s, axis=1, keepdims=True)
    total, out = weigh(s, key_refs, top)
    q_out[...] = q
    top_ref[...] = jnp.broadcast_to(top, top_ref.shape)
    total_ref[...] = jnp.broadcast_to(total, total_ref.shape)
    out_ref[...] = out


def finish_kernel(
    turn, copies, per_device, heads, len_ref, q_ref, top_ref, total_ref, part_ref, *refs
):
    owners = len(turn)
    own_refs, (pair_ref, *far_refs) = refs[:owners], refs[owners : 2 * owners - 1]
    far_refs = [pair_ref.at[0], pair_ref.at[1]] + far_refs
    outs, fresh_ref = refs[2 * owners - 1 : -1], refs[-1]
    seq_index = lax.axis_index("seq")
    group, core = seq_index // copies, seq_index % copies
    sequence = lax.axis_index("head") * owners + group
    length = len_ref[sequence]
    q = q_ref[...]
    slots, width = own_refs[0].shape[1], q.shape[1]

    home = sequence // per_device
    for e in range(copies):
        for k in range(owners):
            source = (group ^ turn[k]) * copies + (core + copies - e) % copies

            @pl.when(source == home)
            def _():
                fresh_ref[...] = (far_refs if e else own_refs)[k][width:, :]

    parts = -(-width // slots)
    rows = per_device * SPEC
    fresh = fresh_ref[...].astype(jnp.float32)
    fresh = jnp.concatenate([fresh[n * rows : (n + 1) * rows] for n in range(parts)], axis=1)
    fresh = fresh[:, :width]
    spare = -rows % 16
    if spare:
        fresh = jnp.concatenate([fresh, jnp.zeros((spare, width), jnp.float32)], axis=0)
    fresh = fresh.astype(jnp.bfloat16)
    f = lax.dot_general(
        q, fresh, (((1,), (1,)), ((), ())), preferred_element_type=jnp.float32
    )
    row = lax.broadcasted_iota(jnp.int32, f.shape, 0) % (SPEC * heads)
    key = lax.broadcasted_iota(jnp.int32, f.shape, 1)
    causal = (key // SPEC == sequence % per_device) & (key % SPEC <= row // heads)
    f = jnp.where(causal, f * SCORE_SCALE, masked_value)

    starts = [
        ((group ^ k) * copies + (core + copies - e) % copies) * slots
        for e in range(1, copies)
        for k in turn
    ]
    s = block_scores(q, far_refs, starts, length)
    first = top_ref[:, :1]
    top = jnp.maximum(
        jnp.maximum(first, jnp.max(s, axis=1, keepdims=True)), jnp.max(f, axis=1, keepdims=True)
    )
    total, out = weigh(s, far_refs, top)
    w = jnp.exp(f - top)
    scale = jnp.exp(first - top)
    total += jnp.sum(w, axis=1, keepdims=True) + total_ref[:, :1] * scale
    out += part_ref[...] * scale
    out += jnp.dot(
        w.astype(jnp.bfloat16), fresh[:, :LATENT], preferred_element_type=jnp.float32
    )
    out = (out / total).astype(jnp.bfloat16)
    piece = SPEC * heads
    swapped = first_block(lax.axis_index("head"), group, core)
    for k in range(per_device):
        for n in range(per_device):

            @pl.when(swapped ^ k != n)
            def _():
                outs[k][...] = out[n * piece : (n + 1) * piece]


def project_kernel(per_device, w_ref, *refs):
    lat_refs, out_ref = refs[:-1], refs[-1]
    rows, heads, width = out_ref.shape
    first = first_back(lax.axis_index("seq") // COPIES, lax.axis_index("head"))
    parts = [jnp.where(first == a, lat_refs[0][...], lat_refs[1][...]) for a in range(per_device)]
    latent = jnp.concatenate(parts, axis=0)
    out = jnp.zeros((rows * heads, width), jnp.float32)
    own_head = lax.broadcasted_iota(jnp.int32, out.shape, 0) % heads
    step = 2 if heads % 2 == 0 else 1
    for h in range(0, heads, step):
        group = jnp.concatenate([w_ref[h + n] for n in range(step)], axis=1)
        product = jnp.dot(latent, group, preferred_element_type=jnp.float32)
        for n in range(step):
            out = jnp.where(own_head == h + n, product[:, n * width : (n + 1) * width], out)
    out_ref[...] = out.astype(out_ref.dtype).reshape(out_ref.shape)


def whole_sequences(seq_size, head_size, queries, new_latent, cache, lengths, w_uk, w_uv):
    rows, heads, _ = queries.shape
    owners, slots, width = cache.shape
    copies = seq_size // owners
    per_device = rows // SPEC
    piece = SPEC * heads
    all_rows = per_device * piece
    fresh_rows = -(-rows * -(-width // slots) // 16) * 16
    params = pltpu.CompilerParams(vmem_limit_bytes=VMEM_LIMIT)
    vmem = pl.BlockSpec(memory_space=pltpu.VMEM)
    smem = pl.BlockSpec(memory_space=pltpu.SMEM)
    anywhere = pl.BlockSpec(memory_space=pl.ANY)
    both = ("seq", "head")
    devices = [(i, j) for i in range(seq_size) for j in range(head_size)]

    def flat(seq_index, head_index):
        return seq_index * head_size + head_index

    def in_hbm(x):
        return pltpu.with_memory_space_constraint(x, pltpu.HBM)

    def host(i, j):
        other = (i // copies) ^ (2 - ((j ^ (j >> 1)) & 1))
        return ((i % copies) * 2 + other // 2) * copies + other % 2

    def owner(i, j, a):
        sequence = i * per_device + a
        core = (j // per_device) ^ 1
        return flat((sequence % owners) * copies + core, sequence // owners)

    moved = lax.ppermute(queries, both, [(flat(i, j), flat(host(i, j), j)) for i, j in devices])

    turn = [0, 1, 3, 2]

    def in_plane(move):
        return [(g * copies + t, move(g, t)) for g in range(owners) for t in range(copies)]

    picked = pl.pallas_call(
        functools.partial(pick_kernel, turn, copies),
        out_shape=[jax.ShapeDtypeStruct((width + fresh_rows, slots), cache.dtype)] * owners,
        in_specs=[anywhere] * 2,
        out_specs=[vmem] * owners,
        scratch_shapes=[
            pltpu.VMEM(new_latent.shape, new_latent.dtype),
            pltpu.SemaphoreType.DMA((owners + 1,)),
        ],
        compiler_params=params,
        cost_estimate=LONG,
    )(in_hbm(jnp.swapaxes(cache, 1, 2)), in_hbm(new_latent))
    own_keys = [picked[0]] + [
        lax.ppermute(picked[k], "seq", in_plane(lambda g, t: (g ^ turn[k]) * copies + t))
        for k in range(1, owners)
    ]
    pair = pl.pallas_call(
        pair_kernel,
        out_shape=jax.ShapeDtypeStruct((2, *picked[0].shape), cache.dtype),
        in_specs=[vmem] * 2,
        out_specs=vmem,
        scratch_shapes=[pltpu.SemaphoreType.DMA((2,))],
        compiler_params=params,
    )(*own_keys[:2])
    other_core = in_plane(lambda g, t: g * copies + (t + 1) % copies)
    far_keys = [lax.ppermute(keys, "seq", other_core) for keys in [pair] + own_keys[2:]]

    pieces = pl.pallas_call(
        functools.partial(absorb_kernel, per_device),
        out_shape=[jax.ShapeDtypeStruct((piece, width), cache.dtype)] * per_device,
        in_specs=[vmem] * 2,
        out_specs=[vmem] * per_device,
        compiler_params=params,
        cost_estimate=LONG,
    )(moved, w_uk)
    arrived = [
        lax.ppermute(
            pieces[k],
            both,
            [
                (flat(host(i, j), j), owner(i, j, first_out(host(i, j) // copies, k)))
                for i, j in devices
            ],
        )
        for k in range(per_device)
    ]

    state = pl.pallas_call(
        functools.partial(begin_kernel, turn, copies, per_device),
        out_shape=[
            jax.ShapeDtypeStruct((all_rows, width), jnp.bfloat16),
            jax.ShapeDtypeStruct((all_rows, 128), jnp.float32),
            jax.ShapeDtypeStruct((all_rows, 128), jnp.float32),
            jax.ShapeDtypeStruct((all_rows, LATENT), jnp.float32),
        ],
        in_specs=[smem] + [vmem] * (per_device + owners),
        out_specs=[vmem] * 4,
        compiler_params=params,
        cost_estimate=LONG,
    )(lengths, *arrived, *own_keys)
    latent = pl.pallas_call(
        functools.partial(finish_kernel, turn, copies, per_device, heads),
        out_shape=[jax.ShapeDtypeStruct((piece, LATENT), jnp.bfloat16)] * per_device,
        in_specs=[smem] + [vmem] * (len(state) + len(own_keys) + len(far_keys)),
        out_specs=[vmem] * per_device,
        scratch_shapes=[pltpu.VMEM((fresh_rows, slots), jnp.bfloat16)],
        compiler_params=params,
    )(lengths, *state, *own_keys, *far_keys)

    back = [
        lax.ppermute(
            latent[k],
            both,
            [(owner(i, j, first_back(i // copies, j) ^ k ^ 1), flat(i, j)) for i, j in devices],
        )
        for k in range(per_device)
    ]
    return pl.pallas_call(
        functools.partial(project_kernel, per_device),
        out_shape=jax.ShapeDtypeStruct((rows, heads, w_uv.shape[2]), jnp.bfloat16),
        in_specs=[vmem] * (1 + per_device),
        out_specs=vmem,
        compiler_params=params,
    )(w_uv, *back[::-1])


def local_partial(
    query_tile_block,
    key_tile_block,
    incoming_keys,
    len_block,
    offset,
    own_first,
    score_scale,
    head_count,
):
    scores = (
        jnp.einsum(
            "vfa,vja->vfj", query_tile_block, key_tile_block, preferred_element_type=jnp.float32
        )
        * score_scale
    )
    positions = offset + lax.broadcasted_iota(jnp.int32, (1, 1, key_tile_block.shape[1]), 2)
    visible = positions < len_block[:, None, None]
    fresh_scores = (
        jnp.einsum(
            "vfa,vja->vfj", query_tile_block, incoming_keys, preferred_element_type=jnp.float32
        )
        * score_scale
    )
    spec_count = incoming_keys.shape[1]
    row_spec = (
        lax.broadcasted_iota(jnp.int32, (1, query_tile_block.shape[1], spec_count), 1) // head_count
    )
    key_spec = lax.broadcasted_iota(jnp.int32, (1, query_tile_block.shape[1], spec_count), 2)
    causal = (key_spec <= row_spec) & own_first
    row_top = jnp.maximum(
        jnp.max(jnp.where(visible, scores, masked_value), axis=2),
        jnp.max(jnp.where(causal, fresh_scores, masked_value), axis=2),
    )
    weights = jnp.where(visible, jnp.exp(scores - row_top[..., None]), 0.0)
    fresh_weights = jnp.where(causal, jnp.exp(fresh_scores - row_top[..., None]), 0.0)
    running_totals = jnp.sum(weights, axis=2) + jnp.sum(fresh_weights, axis=2)
    weighted = jnp.einsum(
        "mpu,mui->mpi",
        weights.astype(jnp.bfloat16),
        key_tile_block[:, :, :LATENT],
        preferred_element_type=jnp.float32,
    )
    weighted = weighted + jnp.einsum(
        "mpu,mui->mpi",
        fresh_weights.astype(jnp.bfloat16),
        incoming_keys[:, :, :LATENT],
        preferred_element_type=jnp.float32,
    )
    return (row_top, running_totals, weighted)


def project_values(latent_rows, value_weight):
    return jnp.einsum("rhc,hcv->rhv", latent_rows, value_weight, precision=lax.Precision.HIGHEST)


def split_positions(queries, new_latent, cache, lengths, w_uk, w_uv):
    own_rows, head_count, _ = queries.shape
    score_scale = (NOPE + ROPE) ** (-0.5)
    gathered, new_all = (
        lax.all_gather(queries, "seq", axis=0, tiled=True),
        lax.all_gather(new_latent, "seq", axis=0, tiled=True),
    )
    absorbed = jnp.einsum(
        "rhn,hnc->rhc", gathered[:, :, :NOPE], w_uk, preferred_element_type=jnp.float32
    ).astype(jnp.bfloat16)
    q_all = jnp.concatenate([absorbed, gathered[:, :, NOPE:]], axis=2)
    total_rows = q_all.shape[0]
    seq_count = total_rows // SPEC
    query_slots = SPEC * head_count
    q_seq = q_all.reshape(seq_count, query_slots, q_all.shape[2])
    new_seq = new_all.reshape(seq_count, SPEC, new_all.shape[1])
    seq_index = lax.axis_index("seq")
    offset = seq_index * cache.shape[1]
    own_first = seq_index == 0
    row_top, running_totals, weighted = local_partial(
        q_seq,
        lax.all_gather(cache, "head", axis=0, tiled=True),
        new_seq,
        lengths,
        offset,
        own_first,
        score_scale,
        head_count,
    )
    value_weight = w_uv.astype(jnp.float32)
    global_top = lax.pmax(row_top, "seq")
    factor = jnp.exp(row_top - global_top)
    scaled_totals = (running_totals * factor).reshape(total_rows, head_count)
    scaled_weighted = (weighted * factor[..., None]).reshape(total_rows, head_count, LATENT)
    row_totals, row_weighted = (
        lax.psum_scatter(scaled_totals, "seq", scatter_dimension=0, tiled=True),
        lax.psum_scatter(scaled_weighted, "seq", scatter_dimension=0, tiled=True),
    )
    latent_output = row_weighted / row_totals[..., None]
    result = project_values(latent_output, value_weight)
    return result.astype(jnp.bfloat16)


def shards(seq_size, head_size, queries, new_latent, cache, lengths, w_uk, w_uv):
    rows, owners = queries.shape[0], cache.shape[0]
    per_device = rows // SPEC
    if (
        per_device == 2
        and rows % SPEC == 0
        and seq_size == COPIES * owners
        and head_size == owners == 4
    ):
        return whole_sequences(
            seq_size, head_size, queries, new_latent, cache, lengths, w_uk, w_uv
        )
    return split_positions(queries, new_latent, cache, lengths, w_uk, w_uv)


def solution(mesh):
    return jax.shard_map(
        functools.partial(shards, mesh.shape["seq"], mesh.shape["head"]),
        mesh=mesh,
        in_specs=(
            P("seq", "head", None),
            P("seq", None),
            P("head", "seq", None),
            P(),
            P("head", None, None),
            P("head", None, None),
        ),
        out_specs=P("seq", "head", None),
        check_vma=False,
    )
```

```python
import functools

import jax
import jax.numpy as jnp
from jax import lax
from jax.experimental import pallas as pl
from jax.experimental.pallas import tpu as pltpu
from jax.sharding import PartitionSpec as P

NOPE = 128
ROPE = 64
LATENT = 512
SPEC = 4
SCORE_SCALE = (NOPE + ROPE) ** (-0.5)
COPIES = 2
VMEM_LIMIT = 16 * 1024 * 1024
LONG = pl.CostEstimate(flops=2 * 10**10, bytes_accessed=0, transcendentals=0)

masked_value = -1e30


def leaves_as(k, chip, head_shard):
    return (k + chip + head_shard) % 2


def owner_core(plane, chip, head_shard):
    return 1 ^ head_shard // 2 ^ chip // 2 ^ plane // 2


def far_half(plane, pair):
    return 1 * (plane <= 2 * pair)


def first_back(home_chip, head_shard):
    far = 1 * (far_half(home_chip, head_shard // 2) == head_shard % 2)
    return home_chip % 2 ^ far


def first_block(plane, chip, core):
    return far_half(plane, 1 ^ core ^ chip // 2 ^ plane // 2) ^ 1


def pick_kernel(turn, per_device, cache_hbm, q_hbm, new_hbm, *refs):
    owners = len(turn)
    blocks, outs = refs[:owners], refs[owners : owners + per_device]
    q_ref, new_ref, sem = refs[owners + per_device :]
    chip = lax.axis_index("seq") // COPIES
    moves = [
        pltpu.make_async_copy(q_hbm, q_ref, sem.at[owners]),
        pltpu.make_async_copy(new_hbm, new_ref, sem.at[owners + 1]),
    ] + [
        pltpu.make_async_copy(cache_hbm.at[chip ^ turn[k]], blocks[k], sem.at[k])
        for k in range(owners)
    ]
    for move in moves:
        move.start()
    moves[0].wait()
    moves[1].wait()
    heads, width = q_ref.shape[1:]
    fresh = new_ref[...].astype(jnp.float32)
    for a in range(per_device):
        rows = q_ref[a * SPEC : (a + 1) * SPEC].reshape(SPEC * heads, width)
        own = fresh[a * SPEC : (a + 1) * SPEC]
        parts = [own[:, n : n + ROPE] for n in range(0, own.shape[1], ROPE)]
        spare = SPEC * heads - SPEC * len(parts)
        if spare:
            parts.append(jnp.zeros((spare, ROPE), jnp.float32))
        own = jnp.concatenate(parts, axis=0).astype(rows.dtype)
        packed = jnp.concatenate([rows, own], axis=1)
        for k in range(per_device):

            @pl.when(leaves_as(k, chip, lax.axis_index("head")) == a)
            def _():
                outs[k][...] = packed

    for move in moves[2:]:
        move.wait()


def pair_kernel(first_ref, second_ref, out_ref, sem):
    moves = [
        pltpu.make_async_copy(ref, out_ref.at[n], sem.at[n])
        for n, ref in enumerate((first_ref, second_ref))
    ]
    for move in moves:
        move.start()
    for move in moves:
        move.wait()


def absorb_kernel(per_device, w_ref, *refs):
    packed, outs = refs[:per_device], refs[per_device:]
    heads = w_ref.shape[0]
    nope = jnp.concatenate([ref[:, :NOPE] for ref in packed], axis=0)
    own_head = lax.broadcasted_iota(jnp.int32, nope.shape, 0) % heads
    spread = jnp.concatenate(
        [jnp.where(own_head == h, nope, jnp.zeros_like(nope)) for h in range(heads)], axis=1
    )
    absorbed = jnp.dot(
        spread, w_ref[...].reshape(heads * NOPE, LATENT), preferred_element_type=jnp.float32
    ).astype(jnp.bfloat16)
    piece = SPEC * heads
    for k in range(per_device):
        outs[k][:, :LATENT] = absorbed[k * piece : (k + 1) * piece]
        outs[k][:, LATENT:] = packed[k][:, NOPE:]


def block_scores(q, refs, starts, length):
    width = q.shape[1]
    keys = jnp.concatenate([ref[:width, :] for ref in refs], axis=1)
    lane = lax.broadcasted_iota(jnp.int32, (1, refs[0].shape[1]), 1)
    position = jnp.concatenate([lane + start for start in starts], axis=1)
    s = jnp.dot(q, keys, preferred_element_type=jnp.float32) * SCORE_SCALE
    return jnp.where(position < length, s, masked_value)


def weigh(s, refs, top):
    w = jnp.exp(s - top)
    values = jnp.concatenate([ref[:LATENT, :] for ref in refs], axis=1)
    out = lax.dot_general(
        w.astype(jnp.bfloat16),
        values,
        (((1,), (1,)), ((), ())),
        preferred_element_type=jnp.float32,
    )
    return jnp.sum(w, axis=1, keepdims=True), out


def begin_kernel(turn, per_device, heads, len_ref, *refs):
    owners = len(turn)
    q_refs, key_refs = refs[:per_device], refs[per_device : per_device + owners]
    q_out, top_ref, total_ref, out_ref = refs[per_device + owners :]
    seq_index = lax.axis_index("seq")
    chip, core = seq_index // COPIES, seq_index % COPIES
    length = len_ref[lax.axis_index("head") * owners + chip]
    slots = key_refs[0].shape[1]
    width = LATENT + ROPE
    q = jnp.concatenate([ref[:, :width] for ref in q_refs], axis=0)

    fresh = q_refs[0][:, width:].astype(jnp.float32)
    fresh = jnp.concatenate(
        [fresh[n * SPEC : (n + 1) * SPEC] for n in range(width // ROPE)], axis=1
    )
    fresh = jnp.concatenate([fresh, jnp.zeros((16 - SPEC, width), jnp.float32)], axis=0)
    fresh = fresh.astype(jnp.bfloat16)
    f = lax.dot_general(
        q, fresh, (((1,), (1,)), ((), ())), preferred_element_type=jnp.float32
    )
    row = lax.broadcasted_iota(jnp.int32, f.shape, 0) % (SPEC * heads)
    key = lax.broadcasted_iota(jnp.int32, f.shape, 1)
    f = jnp.where(key <= row // heads, f * SCORE_SCALE, masked_value)

    starts = [((chip ^ k) * COPIES + core) * slots for k in turn]
    s = block_scores(q, key_refs, starts, length)
    top = jnp.maximum(jnp.max(s, axis=1, keepdims=True), jnp.max(f, axis=1, keepdims=True))
    total, out = weigh(s, key_refs, top)
    w = jnp.exp(f - top)
    total += jnp.sum(w, axis=1, keepdims=True)
    out += jnp.dot(
        w.astype(jnp.bfloat16), fresh[:, :LATENT], preferred_element_type=jnp.float32
    )
    q_out[...] = q
    top_ref[...] = jnp.broadcast_to(top, top_ref.shape)
    total_ref[...] = jnp.broadcast_to(total, total_ref.shape)
    out_ref[...] = out


def finish_kernel(
    turn, per_device, len_ref, q_ref, top_ref, total_ref, part_ref, pair_ref, *refs
):
    owners = len(turn)
    key_refs = [pair_ref.at[0], pair_ref.at[1], *refs[: owners - 2]]
    outs = refs[owners - 2 :]
    seq_index = lax.axis_index("seq")
    chip, core = seq_index // COPIES, seq_index % COPIES
    plane = lax.axis_index("head")
    length = len_ref[plane * owners + chip]
    slots = key_refs[0].shape[1]
    starts = [((chip ^ k) * COPIES + 1 - core) * slots for k in turn]
    s = block_scores(q_ref[...], key_refs, starts, length)
    first = top_ref[:, :1]
    top = jnp.maximum(first, jnp.max(s, axis=1, keepdims=True))
    total, out = weigh(s, key_refs, top)
    scale = jnp.exp(first - top)
    total += total_ref[:, :1] * scale
    out += part_ref[...] * scale
    out = (out / total).astype(jnp.bfloat16)
    piece = out.shape[0] // per_device
    sent_first = first_block(plane, chip, core)
    for k in range(per_device):
        for n in range(per_device):

            @pl.when(sent_first ^ k == n)
            def _():
                outs[k][...] = out[n * piece : (n + 1) * piece]


def project_kernel(per_device, w_ref, *refs):
    lat_refs, out_ref = refs[:-1], refs[-1]
    rows, heads, width = out_ref.shape
    first = first_back(lax.axis_index("seq") // COPIES, lax.axis_index("head"))
    parts = [jnp.where(first == a, lat_refs[1][...], lat_refs[0][...]) for a in range(per_device)]
    latent = jnp.concatenate(parts, axis=0)
    out = jnp.zeros((rows * heads, width), jnp.float32)
    own_head = lax.broadcasted_iota(jnp.int32, out.shape, 0) % heads
    step = 2 if heads % 2 == 0 else 1
    for h in range(0, heads, step):
        group = jnp.concatenate([w_ref[h + n] for n in range(step)], axis=1)
        product = jnp.dot(latent, group, preferred_element_type=jnp.float32)
        for n in range(step):
            out = jnp.where(own_head == h + n, product[:, n * width : (n + 1) * width], out)
    out_ref[...] = out.astype(out_ref.dtype).reshape(out_ref.shape)


def whole_sequences(seq_size, head_size, queries, new_latent, cache, lengths, w_uk, w_uv):
    rows, heads, q_width = queries.shape
    owners, slots, width = cache.shape
    per_device = rows // SPEC
    piece = SPEC * heads
    all_rows = per_device * piece
    params = pltpu.CompilerParams(vmem_limit_bytes=VMEM_LIMIT)
    vmem = pl.BlockSpec(memory_space=pltpu.VMEM)
    smem = pl.BlockSpec(memory_space=pltpu.SMEM)
    anywhere = pl.BlockSpec(memory_space=pl.ANY)
    both = ("seq", "head")
    devices = [(i, j) for i in range(seq_size) for j in range(head_size)]

    def flat(seq_index, head_index):
        return seq_index * head_size + head_index

    def in_hbm(x):
        return pltpu.with_memory_space_constraint(x, pltpu.HBM)

    def host(i, j, a):
        home, chip = i // COPIES, i % COPIES * per_device + a
        core = home // 2 ^ chip // 2 ^ j // 2
        exchanged = chip == home and home // 2 == j // 2
        return flat((chip ^ exchanged) * COPIES + core, j)

    def owner(i, j, a):
        plane, chip = i // COPIES, i % COPIES * per_device + a
        return flat(chip * COPIES + owner_core(plane, chip, j), plane)

    turn = [0, 1, 3, 2]

    def in_plane(move):
        return [(g * COPIES + t, move(g, t)) for g in range(owners) for t in range(COPIES)]

    made = pl.pallas_call(
        functools.partial(pick_kernel, turn, per_device),
        out_shape=[jax.ShapeDtypeStruct((width, slots), cache.dtype)] * owners
        + [jax.ShapeDtypeStruct((piece, q_width + ROPE), queries.dtype)] * per_device,
        in_specs=[anywhere] * 3,
        out_specs=[vmem] * (owners + per_device),
        scratch_shapes=[
            pltpu.VMEM(queries.shape, queries.dtype),
            pltpu.VMEM(new_latent.shape, new_latent.dtype),
            pltpu.SemaphoreType.DMA((owners + 2,)),
        ],
        compiler_params=params,
        cost_estimate=LONG,
    )(in_hbm(jnp.swapaxes(cache, 1, 2)), in_hbm(queries), in_hbm(new_latent))
    picked, packed = made[:owners], made[owners:]
    packed = [
        lax.ppermute(
            packed[k],
            both,
            [(flat(i, j), host(i, j, leaves_as(k, i // COPIES, j))) for i, j in devices],
        )
        for k in range(per_device)
    ]
    own_keys = [picked[0]] + [
        lax.ppermute(picked[k], "seq", in_plane(lambda g, t: (g ^ turn[k]) * COPIES + t))
        for k in range(1, owners)
    ]
    pair = pl.pallas_call(
        pair_kernel,
        out_shape=jax.ShapeDtypeStruct((2, *picked[0].shape), cache.dtype),
        in_specs=[vmem] * 2,
        out_specs=vmem,
        scratch_shapes=[pltpu.SemaphoreType.DMA((2,))],
        compiler_params=params,
    )(*own_keys[:2])
    other_core = in_plane(lambda g, t: g * COPIES + 1 - t)
    far_keys = [lax.ppermute(keys, "seq", other_core) for keys in [pair] + own_keys[2:]]

    pieces = pl.pallas_call(
        functools.partial(absorb_kernel, per_device),
        out_shape=[jax.ShapeDtypeStruct((piece, width + ROPE), cache.dtype)] * per_device,
        in_specs=[vmem] * (1 + per_device),
        out_specs=[vmem] * per_device,
        compiler_params=params,
        cost_estimate=LONG,
    )(w_uk, *packed)
    arrived = [
        lax.ppermute(
            pieces[k],
            both,
            [
                (host(i, j, a), owner(i, j, a))
                for i, j in devices
                for a in [leaves_as(k, i // COPIES, j)]
            ],
        )
        for k in range(per_device)
    ]

    state = pl.pallas_call(
        functools.partial(begin_kernel, turn, per_device, heads),
        out_shape=[
            jax.ShapeDtypeStruct((all_rows, width), jnp.bfloat16),
            jax.ShapeDtypeStruct((all_rows, 128), jnp.float32),
            jax.ShapeDtypeStruct((all_rows, 128), jnp.float32),
            jax.ShapeDtypeStruct((all_rows, LATENT), jnp.float32),
        ],
        in_specs=[smem] + [vmem] * (per_device + owners),
        out_specs=[vmem] * 4,
        compiler_params=params,
        cost_estimate=LONG,
    )(lengths, *arrived, *own_keys)
    latent = pl.pallas_call(
        functools.partial(finish_kernel, turn, per_device),
        out_shape=[jax.ShapeDtypeStruct((piece, LATENT), jnp.bfloat16)] * per_device,
        in_specs=[smem] + [vmem] * (len(state) + len(far_keys)),
        out_specs=[vmem] * per_device,
        compiler_params=params,
    )(lengths, *state, *far_keys)

    back = [
        lax.ppermute(
            latent[k],
            both,
            [(owner(i, j, first_back(i // COPIES, j) ^ k), flat(i, j)) for i, j in devices],
        )
        for k in range(per_device)
    ]
    return pl.pallas_call(
        functools.partial(project_kernel, per_device),
        out_shape=jax.ShapeDtypeStruct((rows, heads, w_uv.shape[2]), jnp.bfloat16),
        in_specs=[vmem] * (1 + per_device),
        out_specs=vmem,
        compiler_params=params,
    )(w_uv, *back[::-1])


def local_partial(
    query_tile_block,
    key_tile_block,
    incoming_keys,
    len_block,
    offset,
    own_first,
    score_scale,
    head_count,
):
    scores = (
        jnp.einsum(
            "vfa,vja->vfj", query_tile_block, key_tile_block, preferred_element_type=jnp.float32
        )
        * score_scale
    )
    positions = offset + lax.broadcasted_iota(jnp.int32, (1, 1, key_tile_block.shape[1]), 2)
    visible = positions < len_block[:, None, None]
    fresh_scores = (
        jnp.einsum(
            "vfa,vja->vfj", query_tile_block, incoming_keys, preferred_element_type=jnp.float32
        )
        * score_scale
    )
    spec_count = incoming_keys.shape[1]
    row_spec = (
        lax.broadcasted_iota(jnp.int32, (1, query_tile_block.shape[1], spec_count), 1) // head_count
    )
    key_spec = lax.broadcasted_iota(jnp.int32, (1, query_tile_block.shape[1], spec_count), 2)
    causal = (key_spec <= row_spec) & own_first
    row_top = jnp.maximum(
        jnp.max(jnp.where(visible, scores, masked_value), axis=2),
        jnp.max(jnp.where(causal, fresh_scores, masked_value), axis=2),
    )
    weights = jnp.where(visible, jnp.exp(scores - row_top[..., None]), 0.0)
    fresh_weights = jnp.where(causal, jnp.exp(fresh_scores - row_top[..., None]), 0.0)
    running_totals = jnp.sum(weights, axis=2) + jnp.sum(fresh_weights, axis=2)
    weighted = jnp.einsum(
        "mpu,mui->mpi",
        weights.astype(jnp.bfloat16),
        key_tile_block[:, :, :LATENT],
        preferred_element_type=jnp.float32,
    )
    weighted = weighted + jnp.einsum(
        "mpu,mui->mpi",
        fresh_weights.astype(jnp.bfloat16),
        incoming_keys[:, :, :LATENT],
        preferred_element_type=jnp.float32,
    )
    return (row_top, running_totals, weighted)


def project_values(latent_rows, value_weight):
    return jnp.einsum("rhc,hcv->rhv", latent_rows, value_weight, precision=lax.Precision.HIGHEST)


def split_positions(queries, new_latent, cache, lengths, w_uk, w_uv):
    own_rows, head_count, _ = queries.shape
    score_scale = (NOPE + ROPE) ** (-0.5)
    gathered, new_all = (
        lax.all_gather(queries, "seq", axis=0, tiled=True),
        lax.all_gather(new_latent, "seq", axis=0, tiled=True),
    )
    absorbed = jnp.einsum(
        "rhn,hnc->rhc", gathered[:, :, :NOPE], w_uk, preferred_element_type=jnp.float32
    ).astype(jnp.bfloat16)
    q_all = jnp.concatenate([absorbed, gathered[:, :, NOPE:]], axis=2)
    total_rows = q_all.shape[0]
    seq_count = total_rows // SPEC
    query_slots = SPEC * head_count
    q_seq = q_all.reshape(seq_count, query_slots, q_all.shape[2])
    new_seq = new_all.reshape(seq_count, SPEC, new_all.shape[1])
    seq_index = lax.axis_index("seq")
    offset = seq_index * cache.shape[1]
    own_first = seq_index == 0
    row_top, running_totals, weighted = local_partial(
        q_seq,
        lax.all_gather(cache, "head", axis=0, tiled=True),
        new_seq,
        lengths,
        offset,
        own_first,
        score_scale,
        head_count,
    )
    value_weight = w_uv.astype(jnp.float32)
    global_top = lax.pmax(row_top, "seq")
    factor = jnp.exp(row_top - global_top)
    scaled_totals = (running_totals * factor).reshape(total_rows, head_count)
    scaled_weighted = (weighted * factor[..., None]).reshape(total_rows, head_count, LATENT)
    row_totals, row_weighted = (
        lax.psum_scatter(scaled_totals, "seq", scatter_dimension=0, tiled=True),
        lax.psum_scatter(scaled_weighted, "seq", scatter_dimension=0, tiled=True),
    )
    latent_output = row_weighted / row_totals[..., None]
    result = project_values(latent_output, value_weight)
    return result.astype(jnp.bfloat16)


def shards(seq_size, head_size, queries, new_latent, cache, lengths, w_uk, w_uv):
    rows, owners = queries.shape[0], cache.shape[0]
    per_device = rows // SPEC
    if (
        per_device == 2
        and rows % SPEC == 0
        and seq_size == COPIES * owners
        and head_size == owners == 4
    ):
        return whole_sequences(
            seq_size, head_size, queries, new_latent, cache, lengths, w_uk, w_uv
        )
    return split_positions(queries, new_latent, cache, lengths, w_uk, w_uv)


def solution(mesh):
    return jax.shard_map(
        functools.partial(shards, mesh.shape["seq"], mesh.shape["head"]),
        mesh=mesh,
        in_specs=(
            P("seq", "head", None),
            P("seq", None),
            P("head", "seq", None),
            P(),
            P("head", None, None),
            P("head", None, None),
        ),
        out_specs=P("seq", "head", None),
        check_vma=False,
    )
```

```python
import functools

import jax
import jax.numpy as jnp
from jax import lax
from jax.experimental import pallas as pl
from jax.experimental.pallas import tpu as pltpu
from jax.sharding import PartitionSpec as P

NOPE = 128
ROPE = 64
LATENT = 512
SPEC = 4
SCORE_SCALE = (NOPE + ROPE) ** (-0.5)
COPIES = 2
VMEM_LIMIT = 16 * 1024 * 1024
LONG = pl.CostEstimate(flops=2 * 10**10, bytes_accessed=0, transcendentals=0)

masked_value = -1e30


def leaves_as(k, chip, head_shard):
    return (k + chip + head_shard) % 2


def owner_core(plane, chip, head_shard):
    return 1 ^ head_shard // 2 ^ chip // 2 ^ plane // 2


def far_half(plane, pair):
    return 1 * (plane <= 2 * pair)


def first_back(home_chip, head_shard):
    far = 1 * (far_half(home_chip, head_shard // 2) == head_shard % 2)
    return home_chip % 2 ^ far


def first_block(plane, chip, core):
    return far_half(plane, 1 ^ core ^ chip // 2 ^ plane // 2) ^ 1


def pick_kernel(turn, per_device, cache_hbm, q_hbm, new_hbm, *refs):
    owners = len(turn)
    blocks, outs = refs[:owners], refs[owners : owners + per_device]
    q_ref, new_ref, sem = refs[owners + per_device :]
    chip = lax.axis_index("seq") // COPIES
    moves = [
        pltpu.make_async_copy(q_hbm, q_ref, sem.at[owners]),
        pltpu.make_async_copy(new_hbm, new_ref, sem.at[owners + 1]),
    ] + [
        pltpu.make_async_copy(cache_hbm.at[chip ^ turn[k]], blocks[k], sem.at[k])
        for k in range(owners)
    ]
    for move in moves:
        move.start()
    moves[0].wait()
    moves[1].wait()
    heads, width = q_ref.shape[1:]
    fresh = new_ref[...].astype(jnp.float32)
    for a in range(per_device):
        rows = q_ref[a * SPEC : (a + 1) * SPEC].reshape(SPEC * heads, width)
        own = fresh[a * SPEC : (a + 1) * SPEC]
        parts = [own[:, n : n + ROPE] for n in range(0, own.shape[1], ROPE)]
        spare = SPEC * heads - SPEC * len(parts)
        if spare:
            parts.append(jnp.zeros((spare, ROPE), jnp.float32))
        own = jnp.concatenate(parts, axis=0).astype(rows.dtype)
        packed = jnp.concatenate([rows, own], axis=1)
        for k in range(per_device):

            @pl.when(leaves_as(k, chip, lax.axis_index("head")) == a)
            def _():
                outs[k][...] = packed

    for move in moves[2:]:
        move.wait()


def pair_kernel(first_ref, second_ref, out_ref, sem):
    moves = [
        pltpu.make_async_copy(ref, out_ref.at[n], sem.at[n])
        for n, ref in enumerate((first_ref, second_ref))
    ]
    for move in moves:
        move.start()
    for move in moves:
        move.wait()


def absorb_kernel(per_device, w_ref, *refs):
    packed, outs = refs[:per_device], refs[per_device:]
    heads = w_ref.shape[0]
    nope = jnp.concatenate([ref[:, :NOPE] for ref in packed], axis=0)
    own_head = lax.broadcasted_iota(jnp.int32, nope.shape, 0) % heads
    spread = jnp.concatenate(
        [jnp.where(own_head == h, nope, jnp.zeros_like(nope)) for h in range(heads)], axis=1
    )
    absorbed = jnp.dot(
        spread, w_ref[...].reshape(heads * NOPE, LATENT), preferred_element_type=jnp.float32
    ).astype(jnp.bfloat16)
    piece = SPEC * heads
    for k in range(per_device):
        outs[k][:, :LATENT] = absorbed[k * piece : (k + 1) * piece]
        outs[k][:, LATENT:] = packed[k][:, NOPE:]


def block_scores(q, refs, starts, length):
    width = q.shape[1]
    keys = jnp.concatenate([ref[:width, :] for ref in refs], axis=1)
    lane = lax.broadcasted_iota(jnp.int32, (1, refs[0].shape[1]), 1)
    position = jnp.concatenate([lane + start for start in starts], axis=1)
    s = jnp.dot(q, keys, preferred_element_type=jnp.float32) * SCORE_SCALE
    return jnp.where(position < length, s, masked_value)


def weigh(s, refs, top):
    w = jnp.exp(s - top)
    values = jnp.concatenate([ref[:LATENT, :] for ref in refs], axis=1)
    out = lax.dot_general(
        w.astype(jnp.bfloat16),
        values,
        (((1,), (1,)), ((), ())),
        preferred_element_type=jnp.float32,
    )
    return jnp.sum(w, axis=1, keepdims=True), out


def begin_kernel(turn, per_device, heads, len_ref, *refs):
    owners = len(turn)
    q_refs, key_refs = refs[:per_device], refs[per_device : per_device + owners]
    q_out, top_ref, total_ref, out_ref = refs[per_device + owners :]
    seq_index = lax.axis_index("seq")
    chip, core = seq_index // COPIES, seq_index % COPIES
    length = len_ref[lax.axis_index("head") * owners + chip]
    slots = key_refs[0].shape[1]
    width = LATENT + ROPE
    q = jnp.concatenate([ref[:, :width] for ref in q_refs], axis=0)

    fresh = q_refs[0][:, width:].astype(jnp.float32)
    fresh = jnp.concatenate(
        [fresh[n * SPEC : (n + 1) * SPEC] for n in range(width // ROPE)], axis=1
    )
    fresh = jnp.concatenate([fresh, jnp.zeros((16 - SPEC, width), jnp.float32)], axis=0)
    fresh = fresh.astype(jnp.bfloat16)
    f = lax.dot_general(
        q, fresh, (((1,), (1,)), ((), ())), preferred_element_type=jnp.float32
    )
    row = lax.broadcasted_iota(jnp.int32, f.shape, 0) % (SPEC * heads)
    key = lax.broadcasted_iota(jnp.int32, f.shape, 1)
    f = jnp.where(key <= row // heads, f * SCORE_SCALE, masked_value)

    starts = [((chip ^ k) * COPIES + core) * slots for k in turn]
    s = block_scores(q, key_refs, starts, length)
    top = jnp.maximum(jnp.max(s, axis=1, keepdims=True), jnp.max(f, axis=1, keepdims=True))
    total, out = weigh(s, key_refs, top)
    w = jnp.exp(f - top)
    total += jnp.sum(w, axis=1, keepdims=True)
    out += jnp.dot(
        w.astype(jnp.bfloat16), fresh[:, :LATENT], preferred_element_type=jnp.float32
    )
    q_out[...] = q
    top_ref[...] = jnp.broadcast_to(top, top_ref.shape)
    total_ref[...] = jnp.broadcast_to(total, total_ref.shape)
    out_ref[...] = out


def finish_kernel(
    turn, per_device, len_ref, q_ref, top_ref, total_ref, part_ref, pair_ref, *refs
):
    owners = len(turn)
    key_refs = [pair_ref.at[0], pair_ref.at[1], *refs[: owners - 2]]
    outs = refs[owners - 2 :]
    seq_index = lax.axis_index("seq")
    chip, core = seq_index // COPIES, seq_index % COPIES
    plane = lax.axis_index("head")
    length = len_ref[plane * owners + chip]
    slots = key_refs[0].shape[1]
    starts = [((chip ^ k) * COPIES + 1 - core) * slots for k in turn]
    s = block_scores(q_ref[...], key_refs, starts, length)
    first = top_ref[:, :1]
    top = jnp.maximum(first, jnp.max(s, axis=1, keepdims=True))
    total, out = weigh(s, key_refs, top)
    scale = jnp.exp(first - top)
    total += total_ref[:, :1] * scale
    out += part_ref[...] * scale
    out = (out / total).astype(jnp.bfloat16)
    piece = out.shape[0] // per_device
    sent_first = first_block(plane, chip, core)
    for k in range(per_device):
        for n in range(per_device):

            @pl.when(sent_first ^ k == n)
            def _():
                outs[k][...] = out[n * piece : (n + 1) * piece]


def project_kernel(per_device, w_ref, *refs):
    lat_refs, out_ref = refs[:-1], refs[-1]
    rows, heads, width = out_ref.shape
    first = first_back(lax.axis_index("seq") // COPIES, lax.axis_index("head"))
    parts = [jnp.where(first == a, lat_refs[1][...], lat_refs[0][...]) for a in range(per_device)]
    latent = jnp.concatenate(parts, axis=0)
    out = jnp.zeros((rows * heads, width), jnp.float32)
    own_head = lax.broadcasted_iota(jnp.int32, out.shape, 0) % heads
    step = 2 if heads % 2 == 0 else 1
    for h in range(0, heads, step):
        group = jnp.concatenate([w_ref[h + n] for n in range(step)], axis=1)
        product = jnp.dot(latent, group, preferred_element_type=jnp.float32)
        for n in range(step):
            out = jnp.where(own_head == h + n, product[:, n * width : (n + 1) * width], out)
    out_ref[...] = out.astype(out_ref.dtype).reshape(out_ref.shape)


def whole_sequences(seq_size, head_size, queries, new_latent, cache, lengths, w_uk, w_uv):
    rows, heads, q_width = queries.shape
    owners, slots, width = cache.shape
    per_device = rows // SPEC
    piece = SPEC * heads
    all_rows = per_device * piece
    params = pltpu.CompilerParams(vmem_limit_bytes=VMEM_LIMIT)
    vmem = pl.BlockSpec(memory_space=pltpu.VMEM)
    smem = pl.BlockSpec(memory_space=pltpu.SMEM)
    anywhere = pl.BlockSpec(memory_space=pl.ANY)
    both = ("seq", "head")
    devices = [(i, j) for i in range(seq_size) for j in range(head_size)]

    def flat(seq_index, head_index):
        return seq_index * head_size + head_index

    def in_hbm(x):
        return pltpu.with_memory_space_constraint(x, pltpu.HBM)

    def host(i, j, a):
        home, chip = i // COPIES, i % COPIES * per_device + a
        core = home // 2 ^ chip // 2 ^ j // 2
        exchanged = chip == home and home // 2 == j // 2
        return flat((chip ^ exchanged) * COPIES + core, j)

    def owner(i, j, a):
        plane, chip = i // COPIES, i % COPIES * per_device + a
        return flat(chip * COPIES + owner_core(plane, chip, j), plane)

    turn = [0, 3, 1, 2]

    def in_plane(move):
        return [(g * COPIES + t, move(g, t)) for g in range(owners) for t in range(COPIES)]

    made = pl.pallas_call(
        functools.partial(pick_kernel, turn, per_device),
        out_shape=[jax.ShapeDtypeStruct((width, slots), cache.dtype)] * owners
        + [jax.ShapeDtypeStruct((piece, q_width + ROPE), queries.dtype)] * per_device,
        in_specs=[anywhere] * 3,
        out_specs=[vmem] * (owners + per_device),
        scratch_shapes=[
            pltpu.VMEM(queries.shape, queries.dtype),
            pltpu.VMEM(new_latent.shape, new_latent.dtype),
            pltpu.SemaphoreType.DMA((owners + 2,)),
        ],
        compiler_params=params,
        cost_estimate=LONG,
    )(in_hbm(jnp.swapaxes(cache, 1, 2)), in_hbm(queries), in_hbm(new_latent))
    picked, packed = made[:owners], made[owners:]
    packed = [
        lax.ppermute(
            packed[k],
            both,
            [(flat(i, j), host(i, j, leaves_as(k, i // COPIES, j))) for i, j in devices],
        )
        for k in range(per_device)
    ]
    own_keys = [picked[0]] + [
        lax.ppermute(picked[k], "seq", in_plane(lambda g, t: (g ^ turn[k]) * COPIES + t))
        for k in range(1, owners)
    ]
    pair = pl.pallas_call(
        pair_kernel,
        out_shape=jax.ShapeDtypeStruct((2, *picked[0].shape), cache.dtype),
        in_specs=[vmem] * 2,
        out_specs=vmem,
        scratch_shapes=[pltpu.SemaphoreType.DMA((2,))],
        compiler_params=params,
    )(*own_keys[:2])
    other_core = in_plane(lambda g, t: g * COPIES + 1 - t)
    far_keys = [lax.ppermute(keys, "seq", other_core) for keys in [pair] + own_keys[2:]]

    pieces = pl.pallas_call(
        functools.partial(absorb_kernel, per_device),
        out_shape=[jax.ShapeDtypeStruct((piece, width + ROPE), cache.dtype)] * per_device,
        in_specs=[vmem] * (1 + per_device),
        out_specs=[vmem] * per_device,
        compiler_params=params,
        cost_estimate=LONG,
    )(w_uk, *packed)
    arrived = [
        lax.ppermute(
            pieces[k],
            both,
            [
                (host(i, j, a), owner(i, j, a))
                for i, j in devices
                for a in [leaves_as(k, i // COPIES, j)]
            ],
        )
        for k in range(per_device)
    ]

    state = pl.pallas_call(
        functools.partial(begin_kernel, turn, per_device, heads),
        out_shape=[
            jax.ShapeDtypeStruct((all_rows, width), jnp.bfloat16),
            jax.ShapeDtypeStruct((all_rows, 128), jnp.float32),
            jax.ShapeDtypeStruct((all_rows, 128), jnp.float32),
            jax.ShapeDtypeStruct((all_rows, LATENT), jnp.float32),
        ],
        in_specs=[smem] + [vmem] * (per_device + owners),
        out_specs=[vmem] * 4,
        compiler_params=params,
        cost_estimate=LONG,
    )(lengths, *arrived, *own_keys)
    latent = pl.pallas_call(
        functools.partial(finish_kernel, turn, per_device),
        out_shape=[jax.ShapeDtypeStruct((piece, LATENT), jnp.bfloat16)] * per_device,
        in_specs=[smem] + [vmem] * (len(state) + len(far_keys)),
        out_specs=[vmem] * per_device,
        compiler_params=params,
    )(lengths, *state, *far_keys)

    back = [
        lax.ppermute(
            latent[k],
            both,
            [(owner(i, j, first_back(i // COPIES, j) ^ k), flat(i, j)) for i, j in devices],
        )
        for k in range(per_device)
    ]
    return pl.pallas_call(
        functools.partial(project_kernel, per_device),
        out_shape=jax.ShapeDtypeStruct((rows, heads, w_uv.shape[2]), jnp.bfloat16),
        in_specs=[vmem] * (1 + per_device),
        out_specs=vmem,
        compiler_params=params,
    )(w_uv, *back[::-1])


def local_partial(
    query_tile_block,
    key_tile_block,
    incoming_keys,
    len_block,
    offset,
    own_first,
    score_scale,
    head_count,
):
    scores = (
        jnp.einsum(
            "vfa,vja->vfj", query_tile_block, key_tile_block, preferred_element_type=jnp.float32
        )
        * score_scale
    )
    positions = offset + lax.broadcasted_iota(jnp.int32, (1, 1, key_tile_block.shape[1]), 2)
    visible = positions < len_block[:, None, None]
    fresh_scores = (
        jnp.einsum(
            "vfa,vja->vfj", query_tile_block, incoming_keys, preferred_element_type=jnp.float32
        )
        * score_scale
    )
    spec_count = incoming_keys.shape[1]
    row_spec = (
        lax.broadcasted_iota(jnp.int32, (1, query_tile_block.shape[1], spec_count), 1) // head_count
    )
    key_spec = lax.broadcasted_iota(jnp.int32, (1, query_tile_block.shape[1], spec_count), 2)
    causal = (key_spec <= row_spec) & own_first
    row_top = jnp.maximum(
        jnp.max(jnp.where(visible, scores, masked_value), axis=2),
        jnp.max(jnp.where(causal, fresh_scores, masked_value), axis=2),
    )
    weights = jnp.where(visible, jnp.exp(scores - row_top[..., None]), 0.0)
    fresh_weights = jnp.where(causal, jnp.exp(fresh_scores - row_top[..., None]), 0.0)
    running_totals = jnp.sum(weights, axis=2) + jnp.sum(fresh_weights, axis=2)
    weighted = jnp.einsum(
        "mpu,mui->mpi",
        weights.astype(jnp.bfloat16),
        key_tile_block[:, :, :LATENT],
        preferred_element_type=jnp.float32,
    )
    weighted = weighted + jnp.einsum(
        "mpu,mui->mpi",
        fresh_weights.astype(jnp.bfloat16),
        incoming_keys[:, :, :LATENT],
        preferred_element_type=jnp.float32,
    )
    return (row_top, running_totals, weighted)


def project_values(latent_rows, value_weight):
    return jnp.einsum("rhc,hcv->rhv", latent_rows, value_weight, precision=lax.Precision.HIGHEST)


def split_positions(queries, new_latent, cache, lengths, w_uk, w_uv):
    own_rows, head_count, _ = queries.shape
    score_scale = (NOPE + ROPE) ** (-0.5)
    gathered, new_all = (
        lax.all_gather(queries, "seq", axis=0, tiled=True),
        lax.all_gather(new_latent, "seq", axis=0, tiled=True),
    )
    absorbed = jnp.einsum(
        "rhn,hnc->rhc", gathered[:, :, :NOPE], w_uk, preferred_element_type=jnp.float32
    ).astype(jnp.bfloat16)
    q_all = jnp.concatenate([absorbed, gathered[:, :, NOPE:]], axis=2)
    total_rows = q_all.shape[0]
    seq_count = total_rows // SPEC
    query_slots = SPEC * head_count
    q_seq = q_all.reshape(seq_count, query_slots, q_all.shape[2])
    new_seq = new_all.reshape(seq_count, SPEC, new_all.shape[1])
    seq_index = lax.axis_index("seq")
    offset = seq_index * cache.shape[1]
    own_first = seq_index == 0
    row_top, running_totals, weighted = local_partial(
        q_seq,
        lax.all_gather(cache, "head", axis=0, tiled=True),
        new_seq,
        lengths,
        offset,
        own_first,
        score_scale,
        head_count,
    )
    value_weight = w_uv.astype(jnp.float32)
    global_top = lax.pmax(row_top, "seq")
    factor = jnp.exp(row_top - global_top)
    scaled_totals = (running_totals * factor).reshape(total_rows, head_count)
    scaled_weighted = (weighted * factor[..., None]).reshape(total_rows, head_count, LATENT)
    row_totals, row_weighted = (
        lax.psum_scatter(scaled_totals, "seq", scatter_dimension=0, tiled=True),
        lax.psum_scatter(scaled_weighted, "seq", scatter_dimension=0, tiled=True),
    )
    latent_output = row_weighted / row_totals[..., None]
    result = project_values(latent_output, value_weight)
    return result.astype(jnp.bfloat16)


def shards(seq_size, head_size, queries, new_latent, cache, lengths, w_uk, w_uv):
    rows, owners = queries.shape[0], cache.shape[0]
    per_device = rows // SPEC
    if (
        per_device == 2
        and rows % SPEC == 0
        and seq_size == COPIES * owners
        and head_size == owners == 4
    ):
        return whole_sequences(
            seq_size, head_size, queries, new_latent, cache, lengths, w_uk, w_uv
        )
    return split_positions(queries, new_latent, cache, lengths, w_uk, w_uv)


def solution(mesh):
    return jax.shard_map(
        functools.partial(shards, mesh.shape["seq"], mesh.shape["head"]),
        mesh=mesh,
        in_specs=(
            P("seq", "head", None),
            P("seq", None),
            P("head", "seq", None),
            P(),
            P("head", None, None),
            P("head", None, None),
        ),
        out_specs=P("seq", "head", None),
        check_vma=False,
    )
```

```python
import functools

import jax
import jax.numpy as jnp
from jax import lax
from jax.experimental import pallas as pl
from jax.experimental.pallas import tpu as pltpu
from jax.sharding import PartitionSpec as P

NOPE = 128
ROPE = 64
LATENT = 512
SPEC = 4
SCORE_SCALE = (NOPE + ROPE) ** (-0.5)
COPIES = 2
VMEM_LIMIT = 16 * 1024 * 1024
LONG = pl.CostEstimate(flops=2 * 10**10, bytes_accessed=0, transcendentals=0)
SHORT = pl.CostEstimate(flops=10**8, bytes_accessed=0, transcendentals=0)

masked_value = -1e30


def leaves_as(k, chip, head_shard):
    return (k + chip + head_shard) % 2


def owner_core(plane, chip, head_shard):
    return 1 ^ head_shard // 2 ^ chip // 2 ^ plane // 2


def far_half(plane, pair):
    return 1 * (plane <= 2 * pair)


def first_back(home_chip, head_shard):
    far = 1 * (far_half(home_chip, head_shard // 2) == head_shard % 2)
    return home_chip % 2 ^ far


def first_block(plane, chip, core):
    return far_half(plane, 1 ^ core ^ chip // 2 ^ plane // 2) ^ 1


def pick_kernel(turn, per_device, cache_hbm, q_hbm, new_hbm, *refs):
    owners = len(turn)
    blocks, outs = refs[:owners], refs[owners : owners + per_device]
    q_ref, new_ref, sem = refs[owners + per_device :]
    chip = lax.axis_index("seq") // COPIES
    moves = [
        pltpu.make_async_copy(q_hbm, q_ref, sem.at[owners]),
        pltpu.make_async_copy(new_hbm, new_ref, sem.at[owners + 1]),
    ] + [
        pltpu.make_async_copy(cache_hbm.at[chip ^ turn[k]], blocks[k], sem.at[k])
        for k in range(owners)
    ]
    for move in moves:
        move.start()
    moves[0].wait()
    moves[1].wait()
    heads, width = q_ref.shape[1:]
    fresh = new_ref[...].astype(jnp.float32)
    for a in range(per_device):
        rows = q_ref[a * SPEC : (a + 1) * SPEC].reshape(SPEC * heads, width)
        own = fresh[a * SPEC : (a + 1) * SPEC]
        parts = [own[:, n : n + ROPE] for n in range(0, own.shape[1], ROPE)]
        spare = SPEC * heads - SPEC * len(parts)
        if spare:
            parts.append(jnp.zeros((spare, ROPE), jnp.float32))
        own = jnp.concatenate(parts, axis=0).astype(rows.dtype)
        packed = jnp.concatenate([rows, own], axis=1)
        for k in range(per_device):

            @pl.when(leaves_as(k, chip, lax.axis_index("head")) == a)
            def _():
                outs[k][...] = packed

    for move in moves[2:]:
        move.wait()


def pair_kernel(first_ref, second_ref, out_ref, sem):
    moves = [
        pltpu.make_async_copy(ref, out_ref.at[n], sem.at[n])
        for n, ref in enumerate((first_ref, second_ref))
    ]
    for move in moves:
        move.start()
    for move in moves:
        move.wait()


def absorb_kernel(per_device, w_ref, *refs):
    packed, outs = refs[:per_device], refs[per_device:]
    heads = w_ref.shape[0]
    nope = jnp.concatenate([ref[:, :NOPE] for ref in packed], axis=0)
    own_head = lax.broadcasted_iota(jnp.int32, nope.shape, 0) % heads
    spread = jnp.concatenate(
        [jnp.where(own_head == h, nope, jnp.zeros_like(nope)) for h in range(heads)], axis=1
    )
    absorbed = jnp.dot(
        spread, w_ref[...].reshape(heads * NOPE, LATENT), preferred_element_type=jnp.float32
    ).astype(jnp.bfloat16)
    piece = SPEC * heads
    for k in range(per_device):
        outs[k][:, :LATENT] = absorbed[k * piece : (k + 1) * piece]
        outs[k][:, LATENT:] = packed[k][:, NOPE:]


def block_scores(q, refs, starts, length):
    width = q.shape[1]
    keys = jnp.concatenate([ref[:width, :] for ref in refs], axis=1)
    lane = lax.broadcasted_iota(jnp.int32, (1, refs[0].shape[1]), 1)
    position = jnp.concatenate([lane + start for start in starts], axis=1)
    s = jnp.dot(q, keys, preferred_element_type=jnp.float32) * SCORE_SCALE
    return jnp.where(position < length, s, masked_value)


def weigh(s, refs, top):
    w = jnp.exp(s - top)
    values = jnp.concatenate([ref[:LATENT, :] for ref in refs], axis=1)
    out = lax.dot_general(
        w.astype(jnp.bfloat16),
        values,
        (((1,), (1,)), ((), ())),
        preferred_element_type=jnp.float32,
    )
    return jnp.sum(w, axis=1, keepdims=True), out


def begin_kernel(turn, per_device, heads, len_ref, *refs):
    owners = len(turn)
    q_refs, key_refs = refs[:per_device], refs[per_device : per_device + owners]
    q_out, top_ref, total_ref, out_ref = refs[per_device + owners :]
    seq_index = lax.axis_index("seq")
    chip, core = seq_index // COPIES, seq_index % COPIES
    length = len_ref[lax.axis_index("head") * owners + chip]
    slots = key_refs[0].shape[1]
    width = LATENT + ROPE
    q = jnp.concatenate([ref[:, :width] for ref in q_refs], axis=0)

    fresh = q_refs[0][:, width:].astype(jnp.float32)
    fresh = jnp.concatenate(
        [fresh[n * SPEC : (n + 1) * SPEC] for n in range(width // ROPE)], axis=1
    )
    fresh = jnp.concatenate([fresh, jnp.zeros((16 - SPEC, width), jnp.float32)], axis=0)
    fresh = fresh.astype(jnp.bfloat16)
    f = lax.dot_general(
        q, fresh, (((1,), (1,)), ((), ())), preferred_element_type=jnp.float32
    )
    row = lax.broadcasted_iota(jnp.int32, f.shape, 0) % (SPEC * heads)
    key = lax.broadcasted_iota(jnp.int32, f.shape, 1)
    f = jnp.where(key <= row // heads, f * SCORE_SCALE, masked_value)

    starts = [((chip ^ k) * COPIES + core) * slots for k in turn]
    s = block_scores(q, key_refs, starts, length)
    top = jnp.maximum(jnp.max(s, axis=1, keepdims=True), jnp.max(f, axis=1, keepdims=True))
    total, out = weigh(s, key_refs, top)
    w = jnp.exp(f - top)
    total += jnp.sum(w, axis=1, keepdims=True)
    out += jnp.dot(
        w.astype(jnp.bfloat16), fresh[:, :LATENT], preferred_element_type=jnp.float32
    )
    q_out[...] = q
    top_ref[...] = jnp.broadcast_to(top, top_ref.shape)
    total_ref[...] = jnp.broadcast_to(total, total_ref.shape)
    out_ref[...] = out


def finish_kernel(
    turn, per_device, len_ref, q_ref, top_ref, total_ref, part_ref, pair_ref, *refs
):
    owners = len(turn)
    key_refs = [pair_ref.at[0], pair_ref.at[1], *refs[: owners - 2]]
    outs = refs[owners - 2 :]
    seq_index = lax.axis_index("seq")
    chip, core = seq_index // COPIES, seq_index % COPIES
    plane = lax.axis_index("head")
    length = len_ref[plane * owners + chip]
    slots = key_refs[0].shape[1]
    starts = [((chip ^ k) * COPIES + 1 - core) * slots for k in turn]
    s = block_scores(q_ref[...], key_refs, starts, length)
    first = top_ref[:, :1]
    top = jnp.maximum(first, jnp.max(s, axis=1, keepdims=True))
    total, out = weigh(s, key_refs, top)
    scale = jnp.exp(first - top)
    total += total_ref[:, :1] * scale
    out += part_ref[...] * scale
    out = (out / total).astype(jnp.bfloat16)
    piece = out.shape[0] // per_device
    sent_first = first_block(plane, chip, core)
    for k in range(per_device):
        for n in range(per_device):

            @pl.when(sent_first ^ k == n)
            def _():
                outs[k][...] = out[n * piece : (n + 1) * piece]


def project_kernel(per_device, w_ref, *refs):
    lat_refs, out_ref = refs[:-1], refs[-1]
    rows, heads, width = out_ref.shape
    first = first_back(lax.axis_index("seq") // COPIES, lax.axis_index("head"))
    parts = [jnp.where(first == a, lat_refs[1][...], lat_refs[0][...]) for a in range(per_device)]
    latent = jnp.concatenate(parts, axis=0)
    out = jnp.zeros((rows * heads, width), jnp.float32)
    own_head = lax.broadcasted_iota(jnp.int32, out.shape, 0) % heads
    step = 2 if heads % 2 == 0 else 1
    for h in range(0, heads, step):
        group = jnp.concatenate([w_ref[h + n] for n in range(step)], axis=1)
        product = jnp.dot(latent, group, preferred_element_type=jnp.float32)
        for n in range(step):
            out = jnp.where(own_head == h + n, product[:, n * width : (n + 1) * width], out)
    out_ref[...] = out.astype(out_ref.dtype).reshape(out_ref.shape)


def whole_sequences(seq_size, head_size, queries, new_latent, cache, lengths, w_uk, w_uv):
    rows, heads, q_width = queries.shape
    owners, slots, width = cache.shape
    per_device = rows // SPEC
    piece = SPEC * heads
    all_rows = per_device * piece
    params = pltpu.CompilerParams(vmem_limit_bytes=VMEM_LIMIT)
    vmem = pl.BlockSpec(memory_space=pltpu.VMEM)
    smem = pl.BlockSpec(memory_space=pltpu.SMEM)
    anywhere = pl.BlockSpec(memory_space=pl.ANY)
    both = ("seq", "head")
    devices = [(i, j) for i in range(seq_size) for j in range(head_size)]

    def flat(seq_index, head_index):
        return seq_index * head_size + head_index

    def in_hbm(x):
        return pltpu.with_memory_space_constraint(x, pltpu.HBM)

    def host(i, j, a):
        home, chip = i // COPIES, i % COPIES * per_device + a
        core = home // 2 ^ chip // 2 ^ j // 2
        exchanged = chip == home and home // 2 == j // 2
        return flat((chip ^ exchanged) * COPIES + core, j)

    def owner(i, j, a):
        plane, chip = i // COPIES, i % COPIES * per_device + a
        return flat(chip * COPIES + owner_core(plane, chip, j), plane)

    turn = [0, 3, 1, 2]

    def in_plane(move):
        return [(g * COPIES + t, move(g, t)) for g in range(owners) for t in range(COPIES)]

    made = pl.pallas_call(
        functools.partial(pick_kernel, turn, per_device),
        out_shape=[jax.ShapeDtypeStruct((width, slots), cache.dtype)] * owners
        + [jax.ShapeDtypeStruct((piece, q_width + ROPE), queries.dtype)] * per_device,
        in_specs=[anywhere] * 3,
        out_specs=[vmem] * (owners + per_device),
        scratch_shapes=[
            pltpu.VMEM(queries.shape, queries.dtype),
            pltpu.VMEM(new_latent.shape, new_latent.dtype),
            pltpu.SemaphoreType.DMA((owners + 2,)),
        ],
        compiler_params=params,
        cost_estimate=LONG,
    )(in_hbm(jnp.swapaxes(cache, 1, 2)), in_hbm(queries), in_hbm(new_latent))
    picked, packed = made[:owners], made[owners:]
    packed = [
        lax.ppermute(
            packed[k],
            both,
            [(flat(i, j), host(i, j, leaves_as(k, i // COPIES, j))) for i, j in devices],
        )
        for k in range(per_device)
    ]
    own_keys = [picked[0]] + [
        lax.ppermute(picked[k], "seq", in_plane(lambda g, t: (g ^ turn[k]) * COPIES + t))
        for k in range(1, owners)
    ]
    pair = pl.pallas_call(
        pair_kernel,
        out_shape=jax.ShapeDtypeStruct((2, *picked[0].shape), cache.dtype),
        in_specs=[vmem] * 2,
        out_specs=vmem,
        scratch_shapes=[pltpu.SemaphoreType.DMA((2,))],
        compiler_params=params,
        cost_estimate=LONG,
    )(*own_keys[:2])
    other_core = in_plane(lambda g, t: g * COPIES + 1 - t)
    far_keys = [lax.ppermute(keys, "seq", other_core) for keys in [pair] + own_keys[2:]]

    pieces = pl.pallas_call(
        functools.partial(absorb_kernel, per_device),
        out_shape=[jax.ShapeDtypeStruct((piece, width + ROPE), cache.dtype)] * per_device,
        in_specs=[vmem] * (1 + per_device),
        out_specs=[vmem] * per_device,
        compiler_params=params,
        cost_estimate=SHORT,
    )(w_uk, *packed)
    arrived = [
        lax.ppermute(
            pieces[k],
            both,
            [
                (host(i, j, a), owner(i, j, a))
                for i, j in devices
                for a in [leaves_as(k, i // COPIES, j)]
            ],
        )
        for k in range(per_device)
    ]

    state = pl.pallas_call(
        functools.partial(begin_kernel, turn, per_device, heads),
        out_shape=[
            jax.ShapeDtypeStruct((all_rows, width), jnp.bfloat16),
            jax.ShapeDtypeStruct((all_rows, 128), jnp.float32),
            jax.ShapeDtypeStruct((all_rows, 128), jnp.float32),
            jax.ShapeDtypeStruct((all_rows, LATENT), jnp.float32),
        ],
        in_specs=[smem] + [vmem] * (per_device + owners),
        out_specs=[vmem] * 4,
        compiler_params=params,
        cost_estimate=LONG,
    )(lengths, *arrived, *own_keys)
    latent = pl.pallas_call(
        functools.partial(finish_kernel, turn, per_device),
        out_shape=[jax.ShapeDtypeStruct((piece, LATENT), jnp.bfloat16)] * per_device,
        in_specs=[smem] + [vmem] * (len(state) + len(far_keys)),
        out_specs=[vmem] * per_device,
        compiler_params=params,
    )(lengths, *state, *far_keys)

    back = [
        lax.ppermute(
            latent[k],
            both,
            [(owner(i, j, first_back(i // COPIES, j) ^ k), flat(i, j)) for i, j in devices],
        )
        for k in range(per_device)
    ]
    return pl.pallas_call(
        functools.partial(project_kernel, per_device),
        out_shape=jax.ShapeDtypeStruct((rows, heads, w_uv.shape[2]), jnp.bfloat16),
        in_specs=[vmem] * (1 + per_device),
        out_specs=vmem,
        compiler_params=params,
    )(w_uv, *back[::-1])


def local_partial(
    query_tile_block,
    key_tile_block,
    incoming_keys,
    len_block,
    offset,
    own_first,
    score_scale,
    head_count,
):
    scores = (
        jnp.einsum(
            "vfa,vja->vfj", query_tile_block, key_tile_block, preferred_element_type=jnp.float32
        )
        * score_scale
    )
    positions = offset + lax.broadcasted_iota(jnp.int32, (1, 1, key_tile_block.shape[1]), 2)
    visible = positions < len_block[:, None, None]
    fresh_scores = (
        jnp.einsum(
            "vfa,vja->vfj", query_tile_block, incoming_keys, preferred_element_type=jnp.float32
        )
        * score_scale
    )
    spec_count = incoming_keys.shape[1]
    row_spec = (
        lax.broadcasted_iota(jnp.int32, (1, query_tile_block.shape[1], spec_count), 1) // head_count
    )
    key_spec = lax.broadcasted_iota(jnp.int32, (1, query_tile_block.shape[1], spec_count), 2)
    causal = (key_spec <= row_spec) & own_first
    row_top = jnp.maximum(
        jnp.max(jnp.where(visible, scores, masked_value), axis=2),
        jnp.max(jnp.where(causal, fresh_scores, masked_value), axis=2),
    )
    weights = jnp.where(visible, jnp.exp(scores - row_top[..., None]), 0.0)
    fresh_weights = jnp.where(causal, jnp.exp(fresh_scores - row_top[..., None]), 0.0)
    running_totals = jnp.sum(weights, axis=2) + jnp.sum(fresh_weights, axis=2)
    weighted = jnp.einsum(
        "mpu,mui->mpi",
        weights.astype(jnp.bfloat16),
        key_tile_block[:, :, :LATENT],
        preferred_element_type=jnp.float32,
    )
    weighted = weighted + jnp.einsum(
        "mpu,mui->mpi",
        fresh_weights.astype(jnp.bfloat16),
        incoming_keys[:, :, :LATENT],
        preferred_element_type=jnp.float32,
    )
    return (row_top, running_totals, weighted)


def project_values(latent_rows, value_weight):
    return jnp.einsum("rhc,hcv->rhv", latent_rows, value_weight, precision=lax.Precision.HIGHEST)


def split_positions(queries, new_latent, cache, lengths, w_uk, w_uv):
    own_rows, head_count, _ = queries.shape
    score_scale = (NOPE + ROPE) ** (-0.5)
    gathered, new_all = (
        lax.all_gather(queries, "seq", axis=0, tiled=True),
        lax.all_gather(new_latent, "seq", axis=0, tiled=True),
    )
    absorbed = jnp.einsum(
        "rhn,hnc->rhc", gathered[:, :, :NOPE], w_uk, preferred_element_type=jnp.float32
    ).astype(jnp.bfloat16)
    q_all = jnp.concatenate([absorbed, gathered[:, :, NOPE:]], axis=2)
    total_rows = q_all.shape[0]
    seq_count = total_rows // SPEC
    query_slots = SPEC * head_count
    q_seq = q_all.reshape(seq_count, query_slots, q_all.shape[2])
    new_seq = new_all.reshape(seq_count, SPEC, new_all.shape[1])
    seq_index = lax.axis_index("seq")
    offset = seq_index * cache.shape[1]
    own_first = seq_index == 0
    row_top, running_totals, weighted = local_partial(
        q_seq,
        lax.all_gather(cache, "head", axis=0, tiled=True),
        new_seq,
        lengths,
        offset,
        own_first,
        score_scale,
        head_count,
    )
    value_weight = w_uv.astype(jnp.float32)
    global_top = lax.pmax(row_top, "seq")
    factor = jnp.exp(row_top - global_top)
    scaled_totals = (running_totals * factor).reshape(total_rows, head_count)
    scaled_weighted = (weighted * factor[..., None]).reshape(total_rows, head_count, LATENT)
    row_totals, row_weighted = (
        lax.psum_scatter(scaled_totals, "seq", scatter_dimension=0, tiled=True),
        lax.psum_scatter(scaled_weighted, "seq", scatter_dimension=0, tiled=True),
    )
    latent_output = row_weighted / row_totals[..., None]
    result = project_values(latent_output, value_weight)
    return result.astype(jnp.bfloat16)


def shards(seq_size, head_size, queries, new_latent, cache, lengths, w_uk, w_uv):
    rows, owners = queries.shape[0], cache.shape[0]
    per_device = rows // SPEC
    if (
        per_device == 2
        and rows % SPEC == 0
        and seq_size == COPIES * owners
        and head_size == owners == 4
    ):
        return whole_sequences(
            seq_size, head_size, queries, new_latent, cache, lengths, w_uk, w_uv
        )
    return split_positions(queries, new_latent, cache, lengths, w_uk, w_uv)


def solution(mesh):
    return jax.shard_map(
        functools.partial(shards, mesh.shape["seq"], mesh.shape["head"]),
        mesh=mesh,
        in_specs=(
            P("seq", "head", None),
            P("seq", None),
            P("head", "seq", None),
            P(),
            P("head", None, None),
            P("head", None, None),
        ),
        out_specs=P("seq", "head", None),
        check_vma=False,
    )
```

```python
import functools

import jax
import jax.numpy as jnp
from jax import lax
from jax.experimental import pallas as pl
from jax.experimental.pallas import tpu as pltpu
from jax.sharding import PartitionSpec as P

NOPE = 128
ROPE = 64
LATENT = 512
SPEC = 4
SCORE_SCALE = (NOPE + ROPE) ** (-0.5)
COPIES = 2
VMEM_LIMIT = 16 * 1024 * 1024
LONG = pl.CostEstimate(flops=2 * 10**10, bytes_accessed=0, transcendentals=0)

masked_value = -1e30


def leaves_as(k, chip, head_shard):
    return (k + chip + head_shard) % 2


def owner_core(plane, chip, head_shard):
    return 1 ^ head_shard // 2 ^ chip // 2 ^ plane // 2


def far_half(plane, pair):
    return 1 * (plane <= 2 * pair)


def first_back(home_chip, head_shard):
    far = 1 * (far_half(home_chip, head_shard // 2) == head_shard % 2)
    return home_chip % 2 ^ far


def first_block(plane, chip, core):
    return far_half(plane, 1 ^ core ^ chip // 2 ^ plane // 2) ^ 1


def partner(k, core):
    return (0, 3, 1 ^ 3 * core, 2 ^ 3 * core)[k]


def pick_kernel(per_device, cache_hbm, q_hbm, new_hbm, *refs):
    owners = cache_hbm.shape[0]
    blocks, outs = refs[:owners], refs[owners : owners + per_device]
    q_ref, new_ref, sem = refs[owners + per_device :]
    chip, core = lax.axis_index("seq") // COPIES, lax.axis_index("seq") % COPIES
    moves = [
        pltpu.make_async_copy(q_hbm, q_ref, sem.at[owners]),
        pltpu.make_async_copy(new_hbm, new_ref, sem.at[owners + 1]),
    ] + [
        pltpu.make_async_copy(cache_hbm.at[chip ^ partner(k, core)], blocks[k], sem.at[k])
        for k in range(owners)
    ]
    for move in moves:
        move.start()
    moves[0].wait()
    moves[1].wait()
    heads, width = q_ref.shape[1:]
    fresh = new_ref[...].astype(jnp.float32)
    for a in range(per_device):
        rows = q_ref[a * SPEC : (a + 1) * SPEC].reshape(SPEC * heads, width)
        own = fresh[a * SPEC : (a + 1) * SPEC]
        parts = [own[:, n : n + ROPE] for n in range(0, own.shape[1], ROPE)]
        spare = SPEC * heads - SPEC * len(parts)
        if spare:
            parts.append(jnp.zeros((spare, ROPE), jnp.float32))
        own = jnp.concatenate(parts, axis=0).astype(rows.dtype)
        packed = jnp.concatenate([rows, own], axis=1)
        for k in range(per_device):

            @pl.when(leaves_as(k, chip, lax.axis_index("head")) == a)
            def _():
                outs[k][...] = packed

    for move in moves[2:]:
        move.wait()


def pair_kernel(first_ref, second_ref, out_ref, sem):
    moves = [
        pltpu.make_async_copy(ref, out_ref.at[n], sem.at[n])
        for n, ref in enumerate((first_ref, second_ref))
    ]
    for move in moves:
        move.start()
    for move in moves:
        move.wait()


def absorb_kernel(per_device, w_ref, *refs):
    packed, outs = refs[:per_device], refs[per_device:]
    heads = w_ref.shape[0]
    nope = jnp.concatenate([ref[:, :NOPE] for ref in packed], axis=0)
    own_head = lax.broadcasted_iota(jnp.int32, nope.shape, 0) % heads
    spread = jnp.concatenate(
        [jnp.where(own_head == h, nope, jnp.zeros_like(nope)) for h in range(heads)], axis=1
    )
    absorbed = jnp.dot(
        spread, w_ref[...].reshape(heads * NOPE, LATENT), preferred_element_type=jnp.float32
    ).astype(jnp.bfloat16)
    piece = SPEC * heads
    for k in range(per_device):
        outs[k][:, :LATENT] = absorbed[k * piece : (k + 1) * piece]
        outs[k][:, LATENT:] = packed[k][:, NOPE:]


def block_scores(q, refs, starts, length):
    width = q.shape[1]
    keys = jnp.concatenate([ref[:width, :] for ref in refs], axis=1)
    lane = lax.broadcasted_iota(jnp.int32, (1, refs[0].shape[1]), 1)
    position = jnp.concatenate([lane + start for start in starts], axis=1)
    s = jnp.dot(q, keys, preferred_element_type=jnp.float32) * SCORE_SCALE
    return jnp.where(position < length, s, masked_value)


def weigh(s, refs, top):
    w = jnp.exp(s - top)
    values = jnp.concatenate([ref[:LATENT, :] for ref in refs], axis=1)
    out = lax.dot_general(
        w.astype(jnp.bfloat16),
        values,
        (((1,), (1,)), ((), ())),
        preferred_element_type=jnp.float32,
    )
    return jnp.sum(w, axis=1, keepdims=True), out


def begin_kernel(owners, per_device, heads, len_ref, *refs):
    q_refs, key_refs = refs[:per_device], refs[per_device : per_device + owners]
    q_out, top_ref, total_ref, out_ref = refs[per_device + owners :]
    seq_index = lax.axis_index("seq")
    chip, core = seq_index // COPIES, seq_index % COPIES
    length = len_ref[lax.axis_index("head") * owners + chip]
    slots = key_refs[0].shape[1]
    width = LATENT + ROPE
    q = jnp.concatenate([ref[:, :width] for ref in q_refs], axis=0)

    fresh = q_refs[0][:, width:].astype(jnp.float32)
    fresh = jnp.concatenate(
        [fresh[n * SPEC : (n + 1) * SPEC] for n in range(width // ROPE)], axis=1
    )
    fresh = jnp.concatenate([fresh, jnp.zeros((16 - SPEC, width), jnp.float32)], axis=0)
    fresh = fresh.astype(jnp.bfloat16)
    f = lax.dot_general(
        q, fresh, (((1,), (1,)), ((), ())), preferred_element_type=jnp.float32
    )
    row = lax.broadcasted_iota(jnp.int32, f.shape, 0) % (SPEC * heads)
    key = lax.broadcasted_iota(jnp.int32, f.shape, 1)
    f = jnp.where(key <= row // heads, f * SCORE_SCALE, masked_value)

    starts = [((chip ^ partner(k, core)) * COPIES + core) * slots for k in range(owners)]
    s = block_scores(q, key_refs, starts, length)
    top = jnp.maximum(jnp.max(s, axis=1, keepdims=True), jnp.max(f, axis=1, keepdims=True))
    total, out = weigh(s, key_refs, top)
    w = jnp.exp(f - top)
    total += jnp.sum(w, axis=1, keepdims=True)
    out += jnp.dot(
        w.astype(jnp.bfloat16), fresh[:, :LATENT], preferred_element_type=jnp.float32
    )
    q_out[...] = q
    top_ref[...] = jnp.broadcast_to(top, top_ref.shape)
    total_ref[...] = jnp.broadcast_to(total, total_ref.shape)
    out_ref[...] = out


def finish_kernel(
    owners, per_device, len_ref, q_ref, top_ref, total_ref, part_ref, pair_ref, *refs
):
    key_refs = [pair_ref.at[0], pair_ref.at[1], *refs[: owners - 2]]
    outs = refs[owners - 2 :]
    seq_index = lax.axis_index("seq")
    chip, core = seq_index // COPIES, seq_index % COPIES
    plane = lax.axis_index("head")
    length = len_ref[plane * owners + chip]
    slots = key_refs[0].shape[1]
    starts = [((chip ^ partner(k, 1 - core)) * COPIES + 1 - core) * slots for k in range(owners)]
    s = block_scores(q_ref[...], key_refs, starts, length)
    first = top_ref[:, :1]
    top = jnp.maximum(first, jnp.max(s, axis=1, keepdims=True))
    total, out = weigh(s, key_refs, top)
    scale = jnp.exp(first - top)
    total += total_ref[:, :1] * scale
    out += part_ref[...] * scale
    out = (out / total).astype(jnp.bfloat16)
    piece = out.shape[0] // per_device
    sent_first = first_block(plane, chip, core)
    for k in range(per_device):
        for n in range(per_device):

            @pl.when(sent_first ^ k == n)
            def _():
                outs[k][...] = out[n * piece : (n + 1) * piece]


def project_kernel(per_device, w_ref, *refs):
    lat_refs, out_ref = refs[:-1], refs[-1]
    rows, heads, width = out_ref.shape
    first = first_back(lax.axis_index("seq") // COPIES, lax.axis_index("head"))
    parts = [jnp.where(first == a, lat_refs[1][...], lat_refs[0][...]) for a in range(per_device)]
    latent = jnp.concatenate(parts, axis=0)
    out = jnp.zeros((rows * heads, width), jnp.float32)
    own_head = lax.broadcasted_iota(jnp.int32, out.shape, 0) % heads
    step = 2 if heads % 2 == 0 else 1
    for h in range(0, heads, step):
        group = jnp.concatenate([w_ref[h + n] for n in range(step)], axis=1)
        product = jnp.dot(latent, group, preferred_element_type=jnp.float32)
        for n in range(step):
            out = jnp.where(own_head == h + n, product[:, n * width : (n + 1) * width], out)
    out_ref[...] = out.astype(out_ref.dtype).reshape(out_ref.shape)


def whole_sequences(seq_size, head_size, queries, new_latent, cache, lengths, w_uk, w_uv):
    rows, heads, q_width = queries.shape
    owners, slots, width = cache.shape
    per_device = rows // SPEC
    piece = SPEC * heads
    all_rows = per_device * piece
    params = pltpu.CompilerParams(vmem_limit_bytes=VMEM_LIMIT)
    vmem = pl.BlockSpec(memory_space=pltpu.VMEM)
    smem = pl.BlockSpec(memory_space=pltpu.SMEM)
    anywhere = pl.BlockSpec(memory_space=pl.ANY)
    both = ("seq", "head")
    devices = [(i, j) for i in range(seq_size) for j in range(head_size)]

    def flat(seq_index, head_index):
        return seq_index * head_size + head_index

    def in_hbm(x):
        return pltpu.with_memory_space_constraint(x, pltpu.HBM)

    def host(i, j, a):
        home, chip = i // COPIES, i % COPIES * per_device + a
        core = home // 2 ^ chip // 2 ^ j // 2
        exchanged = chip == home and home // 2 == j // 2
        return flat((chip ^ exchanged) * COPIES + core, j)

    def owner(i, j, a):
        plane, chip = i // COPIES, i % COPIES * per_device + a
        return flat(chip * COPIES + owner_core(plane, chip, j), plane)

    def in_plane(move):
        return [(g * COPIES + t, move(g, t)) for g in range(owners) for t in range(COPIES)]

    made = pl.pallas_call(
        functools.partial(pick_kernel, per_device),
        out_shape=[jax.ShapeDtypeStruct((width, slots), cache.dtype)] * owners
        + [jax.ShapeDtypeStruct((piece, q_width + ROPE), queries.dtype)] * per_device,
        in_specs=[anywhere] * 3,
        out_specs=[vmem] * (owners + per_device),
        scratch_shapes=[
            pltpu.VMEM(queries.shape, queries.dtype),
            pltpu.VMEM(new_latent.shape, new_latent.dtype),
            pltpu.SemaphoreType.DMA((owners + 2,)),
        ],
        compiler_params=params,
        cost_estimate=LONG,
    )(in_hbm(jnp.swapaxes(cache, 1, 2)), in_hbm(queries), in_hbm(new_latent))
    picked, packed = made[:owners], made[owners:]
    packed = [
        lax.ppermute(
            packed[k],
            both,
            [(flat(i, j), host(i, j, leaves_as(k, i // COPIES, j))) for i, j in devices],
        )
        for k in range(per_device)
    ]
    own_keys = [picked[0]] + [
        lax.ppermute(picked[k], "seq", in_plane(lambda g, t: (g ^ partner(k, t)) * COPIES + t))
        for k in range(1, owners)
    ]
    pair = pl.pallas_call(
        pair_kernel,
        out_shape=jax.ShapeDtypeStruct((2, *picked[0].shape), cache.dtype),
        in_specs=[vmem] * 2,
        out_specs=vmem,
        scratch_shapes=[pltpu.SemaphoreType.DMA((2,))],
        compiler_params=params,
    )(*own_keys[:2])
    other_core = in_plane(lambda g, t: g * COPIES + 1 - t)
    far_keys = [lax.ppermute(keys, "seq", other_core) for keys in [pair] + own_keys[2:]]

    pieces = pl.pallas_call(
        functools.partial(absorb_kernel, per_device),
        out_shape=[jax.ShapeDtypeStruct((piece, width + ROPE), cache.dtype)] * per_device,
        in_specs=[vmem] * (1 + per_device),
        out_specs=[vmem] * per_device,
        compiler_params=params,
        cost_estimate=LONG,
    )(w_uk, *packed)
    arrived = [
        lax.ppermute(
            pieces[k],
            both,
            [
                (host(i, j, a), owner(i, j, a))
                for i, j in devices
                for a in [leaves_as(k, i // COPIES, j)]
            ],
        )
        for k in range(per_device)
    ]

    state = pl.pallas_call(
        functools.partial(begin_kernel, owners, per_device, heads),
        out_shape=[
            jax.ShapeDtypeStruct((all_rows, width), jnp.bfloat16),
            jax.ShapeDtypeStruct((all_rows, 128), jnp.float32),
            jax.ShapeDtypeStruct((all_rows, 128), jnp.float32),
            jax.ShapeDtypeStruct((all_rows, LATENT), jnp.float32),
        ],
        in_specs=[smem] + [vmem] * (per_device + owners),
        out_specs=[vmem] * 4,
        compiler_params=params,
        cost_estimate=LONG,
    )(lengths, *arrived, *own_keys)
    latent = pl.pallas_call(
        functools.partial(finish_kernel, owners, per_device),
        out_shape=[jax.ShapeDtypeStruct((piece, LATENT), jnp.bfloat16)] * per_device,
        in_specs=[smem] + [vmem] * (len(state) + len(far_keys)),
        out_specs=[vmem] * per_device,
        compiler_params=params,
    )(lengths, *state, *far_keys)

    back = [
        lax.ppermute(
            latent[k],
            both,
            [(owner(i, j, first_back(i // COPIES, j) ^ k), flat(i, j)) for i, j in devices],
        )
        for k in range(per_device)
    ]
    return pl.pallas_call(
        functools.partial(project_kernel, per_device),
        out_shape=jax.ShapeDtypeStruct((rows, heads, w_uv.shape[2]), jnp.bfloat16),
        in_specs=[vmem] * (1 + per_device),
        out_specs=vmem,
        compiler_params=params,
    )(w_uv, *back[::-1])


def local_partial(
    query_tile_block,
    key_tile_block,
    incoming_keys,
    len_block,
    offset,
    own_first,
    score_scale,
    head_count,
):
    scores = (
        jnp.einsum(
            "vfa,vja->vfj", query_tile_block, key_tile_block, preferred_element_type=jnp.float32
        )
        * score_scale
    )
    positions = offset + lax.broadcasted_iota(jnp.int32, (1, 1, key_tile_block.shape[1]), 2)
    visible = positions < len_block[:, None, None]
    fresh_scores = (
        jnp.einsum(
            "vfa,vja->vfj", query_tile_block, incoming_keys, preferred_element_type=jnp.float32
        )
        * score_scale
    )
    spec_count = incoming_keys.shape[1]
    row_spec = (
        lax.broadcasted_iota(jnp.int32, (1, query_tile_block.shape[1], spec_count), 1) // head_count
    )
    key_spec = lax.broadcasted_iota(jnp.int32, (1, query_tile_block.shape[1], spec_count), 2)
    causal = (key_spec <= row_spec) & own_first
    row_top = jnp.maximum(
        jnp.max(jnp.where(visible, scores, masked_value), axis=2),
        jnp.max(jnp.where(causal, fresh_scores, masked_value), axis=2),
    )
    weights = jnp.where(visible, jnp.exp(scores - row_top[..., None]), 0.0)
    fresh_weights = jnp.where(causal, jnp.exp(fresh_scores - row_top[..., None]), 0.0)
    running_totals = jnp.sum(weights, axis=2) + jnp.sum(fresh_weights, axis=2)
    weighted = jnp.einsum(
        "mpu,mui->mpi",
        weights.astype(jnp.bfloat16),
        key_tile_block[:, :, :LATENT],
        preferred_element_type=jnp.float32,
    )
    weighted = weighted + jnp.einsum(
        "mpu,mui->mpi",
        fresh_weights.astype(jnp.bfloat16),
        incoming_keys[:, :, :LATENT],
        preferred_element_type=jnp.float32,
    )
    return (row_top, running_totals, weighted)


def project_values(latent_rows, value_weight):
    return jnp.einsum("rhc,hcv->rhv", latent_rows, value_weight, precision=lax.Precision.HIGHEST)


def split_positions(queries, new_latent, cache, lengths, w_uk, w_uv):
    own_rows, head_count, _ = queries.shape
    score_scale = (NOPE + ROPE) ** (-0.5)
    gathered, new_all = (
        lax.all_gather(queries, "seq", axis=0, tiled=True),
        lax.all_gather(new_latent, "seq", axis=0, tiled=True),
    )
    absorbed = jnp.einsum(
        "rhn,hnc->rhc", gathered[:, :, :NOPE], w_uk, preferred_element_type=jnp.float32
    ).astype(jnp.bfloat16)
    q_all = jnp.concatenate([absorbed, gathered[:, :, NOPE:]], axis=2)
    total_rows = q_all.shape[0]
    seq_count = total_rows // SPEC
    query_slots = SPEC * head_count
    q_seq = q_all.reshape(seq_count, query_slots, q_all.shape[2])
    new_seq = new_all.reshape(seq_count, SPEC, new_all.shape[1])
    seq_index = lax.axis_index("seq")
    offset = seq_index * cache.shape[1]
    own_first = seq_index == 0
    row_top, running_totals, weighted = local_partial(
        q_seq,
        lax.all_gather(cache, "head", axis=0, tiled=True),
        new_seq,
        lengths,
        offset,
        own_first,
        score_scale,
        head_count,
    )
    value_weight = w_uv.astype(jnp.float32)
    global_top = lax.pmax(row_top, "seq")
    factor = jnp.exp(row_top - global_top)
    scaled_totals = (running_totals * factor).reshape(total_rows, head_count)
    scaled_weighted = (weighted * factor[..., None]).reshape(total_rows, head_count, LATENT)
    row_totals, row_weighted = (
        lax.psum_scatter(scaled_totals, "seq", scatter_dimension=0, tiled=True),
        lax.psum_scatter(scaled_weighted, "seq", scatter_dimension=0, tiled=True),
    )
    latent_output = row_weighted / row_totals[..., None]
    result = project_values(latent_output, value_weight)
    return result.astype(jnp.bfloat16)


def shards(seq_size, head_size, queries, new_latent, cache, lengths, w_uk, w_uv):
    rows, owners = queries.shape[0], cache.shape[0]
    per_device = rows // SPEC
    if (
        per_device == 2
        and rows % SPEC == 0
        and seq_size == COPIES * owners
        and head_size == owners == 4
    ):
        return whole_sequences(
            seq_size, head_size, queries, new_latent, cache, lengths, w_uk, w_uv
        )
    return split_positions(queries, new_latent, cache, lengths, w_uk, w_uv)


def solution(mesh):
    return jax.shard_map(
        functools.partial(shards, mesh.shape["seq"], mesh.shape["head"]),
        mesh=mesh,
        in_specs=(
            P("seq", "head", None),
            P("seq", None),
            P("head", "seq", None),
            P(),
            P("head", None, None),
            P("head", None, None),
        ),
        out_specs=P("seq", "head", None),
        check_vma=False,
    )
```

```python
import functools

import jax
import jax.numpy as jnp
from jax import lax
from jax.experimental import pallas as pl
from jax.experimental.pallas import tpu as pltpu
from jax.sharding import PartitionSpec as P

NOPE = 128
ROPE = 64
LATENT = 512
SPEC = 4
SCORE_SCALE = (NOPE + ROPE) ** (-0.5)
COPIES = 2
VMEM_LIMIT = 16 * 1024 * 1024
LONG = pl.CostEstimate(flops=2 * 10**10, bytes_accessed=0, transcendentals=0)

masked_value = -1e30


def leaves_as(k, chip, head_shard):
    return (k + chip + head_shard) % 2


def owner_core(plane, chip, head_shard):
    return 1 ^ head_shard // 2 ^ chip // 2 ^ plane // 2


def far_half(plane, pair):
    return 1 * (plane <= 2 * pair)


def first_back(home_chip, head_shard):
    far = 1 * (far_half(home_chip, head_shard // 2) == head_shard % 2)
    return home_chip % 2 ^ far


def first_block(plane, chip, core):
    return far_half(plane, 1 ^ core ^ chip // 2 ^ plane // 2) ^ 1


def partner(k, core):
    return (0, 3, 1 ^ 3 * core, 2 ^ 3 * core)[k]


def pick_kernel(per_device, cache_hbm, q_hbm, new_hbm, *refs):
    owners = cache_hbm.shape[0]
    blocks, outs = refs[:owners], refs[owners : owners + per_device]
    q_ref, new_ref, sem = refs[owners + per_device :]
    chip, core = lax.axis_index("seq") // COPIES, lax.axis_index("seq") % COPIES
    moves = [
        pltpu.make_async_copy(q_hbm, q_ref, sem.at[owners]),
        pltpu.make_async_copy(new_hbm, new_ref, sem.at[owners + 1]),
    ] + [
        pltpu.make_async_copy(cache_hbm.at[chip ^ partner(k, core)], blocks[k], sem.at[k])
        for k in range(owners)
    ]
    for move in moves:
        move.start()
    moves[0].wait()
    moves[1].wait()
    heads, width = q_ref.shape[1:]
    fresh = new_ref[...].astype(jnp.float32)
    for a in range(per_device):
        rows = q_ref[a * SPEC : (a + 1) * SPEC].reshape(SPEC * heads, width)
        own = fresh[a * SPEC : (a + 1) * SPEC]
        parts = [own[:, n : n + ROPE] for n in range(0, own.shape[1], ROPE)]
        spare = SPEC * heads - SPEC * len(parts)
        if spare:
            parts.append(jnp.zeros((spare, ROPE), jnp.float32))
        own = jnp.concatenate(parts, axis=0).astype(rows.dtype)
        packed = jnp.concatenate([rows, own], axis=1)
        for k in range(per_device):

            @pl.when(leaves_as(k, chip, lax.axis_index("head")) == a)
            def _():
                outs[k][...] = packed

    for move in moves[2:]:
        move.wait()


def pair_kernel(owners, len_ref, first_ref, second_ref, out_ref, limit_ref, sem):
    moves = [
        pltpu.make_async_copy(ref, out_ref.at[n], sem.at[n])
        for n, ref in enumerate((first_ref, second_ref))
    ]
    for move in moves:
        move.start()
    length = len_ref[lax.axis_index("head") * owners + lax.axis_index("seq") // COPIES]
    limit_ref[...] = jnp.full(limit_ref.shape, length, limit_ref.dtype)
    for move in moves:
        move.wait()


def absorb_kernel(per_device, w_ref, *refs):
    packed, outs = refs[:per_device], refs[per_device:]
    heads = w_ref.shape[0]
    nope = jnp.concatenate([ref[:, :NOPE] for ref in packed], axis=0)
    own_head = lax.broadcasted_iota(jnp.int32, nope.shape, 0) % heads
    spread = jnp.concatenate(
        [jnp.where(own_head == h, nope, jnp.zeros_like(nope)) for h in range(heads)], axis=1
    )
    absorbed = jnp.dot(
        spread, w_ref[...].reshape(heads * NOPE, LATENT), preferred_element_type=jnp.float32
    ).astype(jnp.bfloat16)
    piece = SPEC * heads
    for k in range(per_device):
        outs[k][:, :LATENT] = absorbed[k * piece : (k + 1) * piece]
        outs[k][:, LATENT:] = packed[k][:, NOPE:]


def block_scores(q, refs, starts, limit_ref):
    width = q.shape[1]
    keys = jnp.concatenate([ref[:width, :] for ref in refs], axis=1)
    limit = limit_ref[:1, :]
    lane = lax.broadcasted_iota(jnp.int32, limit.shape, 1)
    visible = jnp.concatenate([lane + start < limit for start in starts], axis=1)
    s = jnp.dot(q, keys, preferred_element_type=jnp.float32) * SCORE_SCALE
    return jnp.where(visible, s, masked_value)


def weigh(s, refs, top):
    w = jnp.exp(s - top)
    values = jnp.concatenate([ref[:LATENT, :] for ref in refs], axis=1)
    out = lax.dot_general(
        w.astype(jnp.bfloat16),
        values,
        (((1,), (1,)), ((), ())),
        preferred_element_type=jnp.float32,
    )
    return jnp.sum(w, axis=1, keepdims=True), out


def begin_kernel(owners, per_device, heads, limit_ref, *refs):
    q_refs, key_refs = refs[:per_device], refs[per_device : per_device + owners]
    q_out, top_ref, total_ref, out_ref = refs[per_device + owners :]
    seq_index = lax.axis_index("seq")
    chip, core = seq_index // COPIES, seq_index % COPIES
    slots = key_refs[0].shape[1]
    width = LATENT + ROPE
    q = jnp.concatenate([ref[:, :width] for ref in q_refs], axis=0)

    fresh = q_refs[0][:, width:].astype(jnp.float32)
    fresh = jnp.concatenate(
        [fresh[n * SPEC : (n + 1) * SPEC] for n in range(width // ROPE)], axis=1
    )
    fresh = jnp.concatenate([fresh, jnp.zeros((16 - SPEC, width), jnp.float32)], axis=0)
    fresh = fresh.astype(jnp.bfloat16)
    f = lax.dot_general(
        q, fresh, (((1,), (1,)), ((), ())), preferred_element_type=jnp.float32
    )
    row = lax.broadcasted_iota(jnp.int32, f.shape, 0) % (SPEC * heads)
    key = lax.broadcasted_iota(jnp.int32, f.shape, 1)
    f = jnp.where(key <= row // heads, f * SCORE_SCALE, masked_value)

    starts = [((chip ^ partner(k, core)) * COPIES + core) * slots for k in range(owners)]
    s = block_scores(q, key_refs, starts, limit_ref)
    top = jnp.maximum(jnp.max(s, axis=1, keepdims=True), jnp.max(f, axis=1, keepdims=True))
    total, out = weigh(s, key_refs, top)
    w = jnp.exp(f - top)
    total += jnp.sum(w, axis=1, keepdims=True)
    out += jnp.dot(
        w.astype(jnp.bfloat16), fresh[:, :LATENT], preferred_element_type=jnp.float32
    )
    q_out[...] = q
    top_ref[...] = jnp.broadcast_to(top, top_ref.shape)
    total_ref[...] = jnp.broadcast_to(total, total_ref.shape)
    out_ref[...] = out


def finish_kernel(
    owners, per_device, limit_ref, q_ref, top_ref, total_ref, part_ref, pair_ref, *refs
):
    key_refs = [pair_ref.at[0], pair_ref.at[1], *refs[: owners - 2]]
    outs = refs[owners - 2 :]
    seq_index = lax.axis_index("seq")
    chip, core = seq_index // COPIES, seq_index % COPIES
    plane = lax.axis_index("head")
    slots = key_refs[0].shape[1]
    starts = [((chip ^ partner(k, 1 - core)) * COPIES + 1 - core) * slots for k in range(owners)]
    s = block_scores(q_ref[...], key_refs, starts, limit_ref)
    first = top_ref[:, :1]
    top = jnp.maximum(first, jnp.max(s, axis=1, keepdims=True))
    total, out = weigh(s, key_refs, top)
    scale = jnp.exp(first - top)
    total += total_ref[:, :1] * scale
    out += part_ref[...] * scale
    out = (out * (1.0 / total)).astype(jnp.bfloat16)
    piece = out.shape[0] // per_device
    sent_first = first_block(plane, chip, core)
    for k in range(per_device):
        for n in range(per_device):

            @pl.when(sent_first ^ k == n)
            def _():
                outs[k][...] = out[n * piece : (n + 1) * piece]


def project_kernel(per_device, w_ref, *refs):
    lat_refs, out_ref = refs[:-1], refs[-1]
    rows, heads, width = out_ref.shape
    first = first_back(lax.axis_index("seq") // COPIES, lax.axis_index("head"))
    parts = [jnp.where(first == a, lat_refs[1][...], lat_refs[0][...]) for a in range(per_device)]
    latent = jnp.concatenate(parts, axis=0)
    out = jnp.zeros((rows * heads, width), jnp.float32)
    own_head = lax.broadcasted_iota(jnp.int32, out.shape, 0) % heads
    step = 2 if heads % 2 == 0 else 1
    for h in range(0, heads, step):
        group = jnp.concatenate([w_ref[h + n] for n in range(step)], axis=1)
        product = jnp.dot(latent, group, preferred_element_type=jnp.float32)
        for n in range(step):
            out = jnp.where(own_head == h + n, product[:, n * width : (n + 1) * width], out)
    out_ref[...] = out.astype(out_ref.dtype).reshape(out_ref.shape)


def whole_sequences(seq_size, head_size, queries, new_latent, cache, lengths, w_uk, w_uv):
    rows, heads, q_width = queries.shape
    owners, slots, width = cache.shape
    per_device = rows // SPEC
    piece = SPEC * heads
    all_rows = per_device * piece
    params = pltpu.CompilerParams(vmem_limit_bytes=VMEM_LIMIT)
    vmem = pl.BlockSpec(memory_space=pltpu.VMEM)
    smem = pl.BlockSpec(memory_space=pltpu.SMEM)
    anywhere = pl.BlockSpec(memory_space=pl.ANY)
    both = ("seq", "head")
    devices = [(i, j) for i in range(seq_size) for j in range(head_size)]

    def flat(seq_index, head_index):
        return seq_index * head_size + head_index

    def in_hbm(x):
        return pltpu.with_memory_space_constraint(x, pltpu.HBM)

    def host(i, j, a):
        home, chip = i // COPIES, i % COPIES * per_device + a
        core = home // 2 ^ chip // 2 ^ j // 2
        exchanged = chip == home and home // 2 == j // 2
        return flat((chip ^ exchanged) * COPIES + core, j)

    def owner(i, j, a):
        plane, chip = i // COPIES, i % COPIES * per_device + a
        return flat(chip * COPIES + owner_core(plane, chip, j), plane)

    def in_plane(move):
        return [(g * COPIES + t, move(g, t)) for g in range(owners) for t in range(COPIES)]

    made = pl.pallas_call(
        functools.partial(pick_kernel, per_device),
        out_shape=[jax.ShapeDtypeStruct((width, slots), cache.dtype)] * owners
        + [jax.ShapeDtypeStruct((piece, q_width + ROPE), queries.dtype)] * per_device,
        in_specs=[anywhere] * 3,
        out_specs=[vmem] * (owners + per_device),
        scratch_shapes=[
            pltpu.VMEM(queries.shape, queries.dtype),
            pltpu.VMEM(new_latent.shape, new_latent.dtype),
            pltpu.SemaphoreType.DMA((owners + 2,)),
        ],
        compiler_params=params,
        cost_estimate=LONG,
    )(in_hbm(jnp.swapaxes(cache, 1, 2)), in_hbm(queries), in_hbm(new_latent))
    picked, packed = made[:owners], made[owners:]
    packed = [
        lax.ppermute(
            packed[k],
            both,
            [(flat(i, j), host(i, j, leaves_as(k, i // COPIES, j))) for i, j in devices],
        )
        for k in range(per_device)
    ]
    own_keys = [picked[0]] + [
        lax.ppermute(picked[k], "seq", in_plane(lambda g, t: (g ^ partner(k, t)) * COPIES + t))
        for k in range(1, owners)
    ]
    pair, limit = pl.pallas_call(
        functools.partial(pair_kernel, owners),
        out_shape=[
            jax.ShapeDtypeStruct((2, *picked[0].shape), cache.dtype),
            jax.ShapeDtypeStruct((8, slots), jnp.int32),
        ],
        in_specs=[smem] + [vmem] * 2,
        out_specs=[vmem] * 2,
        scratch_shapes=[pltpu.SemaphoreType.DMA((2,))],
        compiler_params=params,
    )(lengths, *own_keys[:2])
    other_core = in_plane(lambda g, t: g * COPIES + 1 - t)
    far_keys = [lax.ppermute(keys, "seq", other_core) for keys in [pair] + own_keys[2:]]

    pieces = pl.pallas_call(
        functools.partial(absorb_kernel, per_device),
        out_shape=[jax.ShapeDtypeStruct((piece, width + ROPE), cache.dtype)] * per_device,
        in_specs=[vmem] * (1 + per_device),
        out_specs=[vmem] * per_device,
        compiler_params=params,
        cost_estimate=LONG,
    )(w_uk, *packed)
    arrived = [
        lax.ppermute(
            pieces[k],
            both,
            [
                (host(i, j, a), owner(i, j, a))
                for i, j in devices
                for a in [leaves_as(k, i // COPIES, j)]
            ],
        )
        for k in range(per_device)
    ]

    state = pl.pallas_call(
        functools.partial(begin_kernel, owners, per_device, heads),
        out_shape=[
            jax.ShapeDtypeStruct((all_rows, width), jnp.bfloat16),
            jax.ShapeDtypeStruct((all_rows, 128), jnp.float32),
            jax.ShapeDtypeStruct((all_rows, 128), jnp.float32),
            jax.ShapeDtypeStruct((all_rows, LATENT), jnp.float32),
        ],
        in_specs=[vmem] * (1 + per_device + owners),
        out_specs=[vmem] * 4,
        compiler_params=params,
        cost_estimate=LONG,
    )(limit, *arrived, *own_keys)
    latent = pl.pallas_call(
        functools.partial(finish_kernel, owners, per_device),
        out_shape=[jax.ShapeDtypeStruct((piece, LATENT), jnp.bfloat16)] * per_device,
        in_specs=[vmem] * (1 + len(state) + len(far_keys)),
        out_specs=[vmem] * per_device,
        compiler_params=params,
    )(limit, *state, *far_keys)

    back = [
        lax.ppermute(
            latent[k],
            both,
            [(owner(i, j, first_back(i // COPIES, j) ^ k), flat(i, j)) for i, j in devices],
        )
        for k in range(per_device)
    ]
    return pl.pallas_call(
        functools.partial(project_kernel, per_device),
        out_shape=jax.ShapeDtypeStruct((rows, heads, w_uv.shape[2]), jnp.bfloat16),
        in_specs=[vmem] * (1 + per_device),
        out_specs=vmem,
        compiler_params=params,
    )(w_uv, *back[::-1])


def local_partial(
    query_tile_block,
    key_tile_block,
    incoming_keys,
    len_block,
    offset,
    own_first,
    score_scale,
    head_count,
):
    scores = (
        jnp.einsum(
            "vfa,vja->vfj", query_tile_block, key_tile_block, preferred_element_type=jnp.float32
        )
        * score_scale
    )
    positions = offset + lax.broadcasted_iota(jnp.int32, (1, 1, key_tile_block.shape[1]), 2)
    visible = positions < len_block[:, None, None]
    fresh_scores = (
        jnp.einsum(
            "vfa,vja->vfj", query_tile_block, incoming_keys, preferred_element_type=jnp.float32
        )
        * score_scale
    )
    spec_count = incoming_keys.shape[1]
    row_spec = (
        lax.broadcasted_iota(jnp.int32, (1, query_tile_block.shape[1], spec_count), 1) // head_count
    )
    key_spec = lax.broadcasted_iota(jnp.int32, (1, query_tile_block.shape[1], spec_count), 2)
    causal = (key_spec <= row_spec) & own_first
    row_top = jnp.maximum(
        jnp.max(jnp.where(visible, scores, masked_value), axis=2),
        jnp.max(jnp.where(causal, fresh_scores, masked_value), axis=2),
    )
    weights = jnp.where(visible, jnp.exp(scores - row_top[..., None]), 0.0)
    fresh_weights = jnp.where(causal, jnp.exp(fresh_scores - row_top[..., None]), 0.0)
    running_totals = jnp.sum(weights, axis=2) + jnp.sum(fresh_weights, axis=2)
    weighted = jnp.einsum(
        "mpu,mui->mpi",
        weights.astype(jnp.bfloat16),
        key_tile_block[:, :, :LATENT],
        preferred_element_type=jnp.float32,
    )
    weighted = weighted + jnp.einsum(
        "mpu,mui->mpi",
        fresh_weights.astype(jnp.bfloat16),
        incoming_keys[:, :, :LATENT],
        preferred_element_type=jnp.float32,
    )
    return (row_top, running_totals, weighted)


def project_values(latent_rows, value_weight):
    return jnp.einsum("rhc,hcv->rhv", latent_rows, value_weight, precision=lax.Precision.HIGHEST)


def split_positions(queries, new_latent, cache, lengths, w_uk, w_uv):
    own_rows, head_count, _ = queries.shape
    score_scale = (NOPE + ROPE) ** (-0.5)
    gathered, new_all = (
        lax.all_gather(queries, "seq", axis=0, tiled=True),
        lax.all_gather(new_latent, "seq", axis=0, tiled=True),
    )
    absorbed = jnp.einsum(
        "rhn,hnc->rhc", gathered[:, :, :NOPE], w_uk, preferred_element_type=jnp.float32
    ).astype(jnp.bfloat16)
    q_all = jnp.concatenate([absorbed, gathered[:, :, NOPE:]], axis=2)
    total_rows = q_all.shape[0]
    seq_count = total_rows // SPEC
    query_slots = SPEC * head_count
    q_seq = q_all.reshape(seq_count, query_slots, q_all.shape[2])
    new_seq = new_all.reshape(seq_count, SPEC, new_all.shape[1])
    seq_index = lax.axis_index("seq")
    offset = seq_index * cache.shape[1]
    own_first = seq_index == 0
    row_top, running_totals, weighted = local_partial(
        q_seq,
        lax.all_gather(cache, "head", axis=0, tiled=True),
        new_seq,
        lengths,
        offset,
        own_first,
        score_scale,
        head_count,
    )
    value_weight = w_uv.astype(jnp.float32)
    global_top = lax.pmax(row_top, "seq")
    factor = jnp.exp(row_top - global_top)
    scaled_totals = (running_totals * factor).reshape(total_rows, head_count)
    scaled_weighted = (weighted * factor[..., None]).reshape(total_rows, head_count, LATENT)
    row_totals, row_weighted = (
        lax.psum_scatter(scaled_totals, "seq", scatter_dimension=0, tiled=True),
        lax.psum_scatter(scaled_weighted, "seq", scatter_dimension=0, tiled=True),
    )
    latent_output = row_weighted / row_totals[..., None]
    result = project_values(latent_output, value_weight)
    return result.astype(jnp.bfloat16)


def shards(seq_size, head_size, queries, new_latent, cache, lengths, w_uk, w_uv):
    rows, owners = queries.shape[0], cache.shape[0]
    per_device = rows // SPEC
    if (
        per_device == 2
        and rows % SPEC == 0
        and seq_size == COPIES * owners
        and head_size == owners == 4
    ):
        return whole_sequences(
            seq_size, head_size, queries, new_latent, cache, lengths, w_uk, w_uv
        )
    return split_positions(queries, new_latent, cache, lengths, w_uk, w_uv)


def solution(mesh):
    return jax.shard_map(
        functools.partial(shards, mesh.shape["seq"], mesh.shape["head"]),
        mesh=mesh,
        in_specs=(
            P("seq", "head", None),
            P("seq", None),
            P("head", "seq", None),
            P(),
            P("head", None, None),
            P("head", None, None),
        ),
        out_specs=P("seq", "head", None),
        check_vma=False,
    )
```

```python
import functools

import jax
import jax.numpy as jnp
from jax import lax
from jax.experimental import pallas as pl
from jax.experimental.pallas import tpu as pltpu
from jax.sharding import PartitionSpec as P

NOPE = 128
ROPE = 64
LATENT = 512
SPEC = 4
SCORE_SCALE = (NOPE + ROPE) ** (-0.5)
COPIES = 2
VMEM_LIMIT = 16 * 1024 * 1024
LONG = pl.CostEstimate(flops=2 * 10**10, bytes_accessed=0, transcendentals=0)

masked_value = -1e30


def leaves_as(k, head_shard):
    return (k + head_shard) % 2


def far_half(plane, pair):
    return 1 * (plane <= 2 * pair)


def first_back(home_chip, head_shard):
    far = 1 * (far_half(home_chip, head_shard // 2) == head_shard % 2)
    return home_chip % 2 ^ far


def first_block(plane, chip, core):
    near = 1 * (chip % 2 == plane % 2)
    return far_half(plane, 1 - core) ^ near ^ chip % 2


def partner(k, core):
    return (0, 3, 1 ^ 3 * core, 2 ^ 3 * core)[k]


def pick_kernel(per_device, cache_hbm, q_hbm, new_hbm, len_hbm, *refs):
    owners = cache_hbm.shape[0]
    blocks, (out_ref, limit_ref, q_ref, new_ref, len_ref, sem) = refs[:owners], refs[owners:]
    chip, core = lax.axis_index("seq") // COPIES, lax.axis_index("seq") % COPIES
    moves = [
        pltpu.make_async_copy(q_hbm, q_ref, sem.at[owners]),
        pltpu.make_async_copy(new_hbm, new_ref, sem.at[owners + 1]),
        pltpu.make_async_copy(len_hbm, len_ref, sem.at[owners + 2]),
    ] + [
        pltpu.make_async_copy(cache_hbm.at[chip ^ partner(k, core)], blocks[k], sem.at[k])
        for k in range(owners)
    ]
    for move in moves:
        move.start()
    moves[0].wait()
    moves[1].wait()
    heads, width = q_ref.shape[1:]
    fresh = new_ref[...].astype(jnp.float32)
    piece = SPEC * heads
    for a in range(per_device):
        rows = q_ref[a * SPEC : (a + 1) * SPEC].reshape(piece, width)
        own = fresh[a * SPEC : (a + 1) * SPEC]
        parts = [own[:, n : n + ROPE] for n in range(0, own.shape[1], ROPE)]
        spare = piece - SPEC * len(parts)
        if spare:
            parts.append(jnp.zeros((spare, ROPE), jnp.float32))
        own = jnp.concatenate(parts, axis=0).astype(rows.dtype)
        out_ref[a * piece : (a + 1) * piece] = jnp.concatenate([rows, own], axis=1)
    moves[2].wait()
    length = len_ref[lax.axis_index("head") * owners + chip]
    limit_ref[...] = jnp.full(limit_ref.shape, length, limit_ref.dtype)
    for move in moves[3:]:
        move.wait()


def pair_kernel(first_ref, second_ref, out_ref, sem):
    moves = [
        pltpu.make_async_copy(ref, out_ref.at[n], sem.at[n])
        for n, ref in enumerate((first_ref, second_ref))
    ]
    for move in moves:
        move.start()
    for move in moves:
        move.wait()


def absorb_kernel(per_device, w_ref, packed_ref, *outs):
    heads = w_ref.shape[0]
    piece = SPEC * heads
    nope = packed_ref[:, :NOPE]
    own_head = lax.broadcasted_iota(jnp.int32, nope.shape, 0) % heads
    spread = jnp.concatenate(
        [jnp.where(own_head == h, nope, jnp.zeros_like(nope)) for h in range(heads)], axis=1
    )
    absorbed = jnp.dot(
        spread, w_ref[...].reshape(heads * NOPE, LATENT), preferred_element_type=jnp.float32
    ).astype(jnp.bfloat16)
    for k in range(per_device):
        which = leaves_as(k, lax.axis_index("head"))
        for a in range(per_device):

            @pl.when(which == a)
            def _():
                rows = slice(a * piece, (a + 1) * piece)
                outs[k][:, :LATENT] = absorbed[rows]
                outs[k][:, LATENT:] = packed_ref[rows, NOPE:]


def block_scores(q, refs, starts, limit_ref):
    width = q.shape[1]
    keys = jnp.concatenate([ref[:width, :] for ref in refs], axis=1)
    limit = limit_ref[:1, :]
    lane = lax.broadcasted_iota(jnp.int32, limit.shape, 1)
    visible = jnp.concatenate([lane + start < limit for start in starts], axis=1)
    s = jnp.dot(q, keys, preferred_element_type=jnp.float32) * SCORE_SCALE
    return jnp.where(visible, s, masked_value)


def weigh(s, refs, top):
    w = jnp.exp(s - top)
    values = jnp.concatenate([ref[:LATENT, :] for ref in refs], axis=1)
    out = lax.dot_general(
        w.astype(jnp.bfloat16),
        values,
        (((1,), (1,)), ((), ())),
        preferred_element_type=jnp.float32,
    )
    return jnp.sum(w, axis=1, keepdims=True), out


def begin_kernel(owners, per_device, heads, limit_ref, *refs):
    q_refs, key_refs = refs[:per_device], refs[per_device : per_device + owners]
    q_out, top_ref, total_ref, out_ref = refs[per_device + owners :]
    seq_index = lax.axis_index("seq")
    chip, core = seq_index // COPIES, seq_index % COPIES
    slots = key_refs[0].shape[1]
    width = LATENT + ROPE
    q = jnp.concatenate([ref[:, :width] for ref in q_refs], axis=0)

    fresh = q_refs[0][:, width:].astype(jnp.float32)
    fresh = jnp.concatenate(
        [fresh[n * SPEC : (n + 1) * SPEC] for n in range(width // ROPE)], axis=1
    )
    fresh = jnp.concatenate([fresh, jnp.zeros((16 - SPEC, width), jnp.float32)], axis=0)
    fresh = fresh.astype(jnp.bfloat16)
    f = lax.dot_general(
        q, fresh, (((1,), (1,)), ((), ())), preferred_element_type=jnp.float32
    )
    row = lax.broadcasted_iota(jnp.int32, f.shape, 0) % (SPEC * heads)
    key = lax.broadcasted_iota(jnp.int32, f.shape, 1)
    f = jnp.where(key <= row // heads, f * SCORE_SCALE, masked_value)

    starts = [((chip ^ partner(k, core)) * COPIES + core) * slots for k in range(owners)]
    s = block_scores(q, key_refs, starts, limit_ref)
    top = jnp.maximum(jnp.max(s, axis=1, keepdims=True), jnp.max(f, axis=1, keepdims=True))
    total, out = weigh(s, key_refs, top)
    w = jnp.exp(f - top)
    total += jnp.sum(w, axis=1, keepdims=True)
    out += jnp.dot(
        w.astype(jnp.bfloat16), fresh[:, :LATENT], preferred_element_type=jnp.float32
    )
    q_out[...] = q
    top_ref[...] = jnp.broadcast_to(top, top_ref.shape)
    total_ref[...] = jnp.broadcast_to(total, total_ref.shape)
    out_ref[...] = out


def finish_kernel(
    owners, per_device, limit_ref, q_ref, top_ref, total_ref, part_ref, pair_ref, *refs
):
    key_refs = [pair_ref.at[0], pair_ref.at[1], *refs[: owners - 2]]
    outs = refs[owners - 2 :]
    seq_index = lax.axis_index("seq")
    chip, core = seq_index // COPIES, seq_index % COPIES
    plane = lax.axis_index("head")
    slots = key_refs[0].shape[1]
    starts = [((chip ^ partner(k, 1 - core)) * COPIES + 1 - core) * slots for k in range(owners)]
    s = block_scores(q_ref[...], key_refs, starts, limit_ref)
    first = top_ref[:, :1]
    top = jnp.maximum(first, jnp.max(s, axis=1, keepdims=True))
    total, out = weigh(s, key_refs, top)
    scale = jnp.exp(first - top)
    total += total_ref[:, :1] * scale
    out += part_ref[...] * scale
    out = (out * (1.0 / total)).astype(jnp.bfloat16)
    piece = out.shape[0] // per_device
    sent_first = first_block(plane, chip, core)
    for k in range(per_device):
        for n in range(per_device):

            @pl.when(sent_first ^ k == n)
            def _():
                outs[k][...] = out[n * piece : (n + 1) * piece]


def project_kernel(per_device, w_ref, *refs):
    lat_refs, out_ref = refs[:-1], refs[-1]
    rows, heads, width = out_ref.shape
    first = first_back(lax.axis_index("seq") // COPIES, lax.axis_index("head"))
    parts = [jnp.where(first == a, lat_refs[1][...], lat_refs[0][...]) for a in range(per_device)]
    latent = jnp.concatenate(parts, axis=0)
    out = jnp.zeros((rows * heads, width), jnp.float32)
    own_head = lax.broadcasted_iota(jnp.int32, out.shape, 0) % heads
    step = 2 if heads % 2 == 0 else 1
    for h in range(0, heads, step):
        group = jnp.concatenate([w_ref[h + n] for n in range(step)], axis=1)
        product = jnp.dot(latent, group, preferred_element_type=jnp.float32)
        for n in range(step):
            out = jnp.where(own_head == h + n, product[:, n * width : (n + 1) * width], out)
    out_ref[...] = out.astype(out_ref.dtype).reshape(out_ref.shape)


def whole_sequences(seq_size, head_size, queries, new_latent, cache, lengths, w_uk, w_uv):
    rows, heads, q_width = queries.shape
    owners, slots, width = cache.shape
    per_device = rows // SPEC
    piece = SPEC * heads
    all_rows = per_device * piece
    params = pltpu.CompilerParams(vmem_limit_bytes=VMEM_LIMIT)
    vmem = pl.BlockSpec(memory_space=pltpu.VMEM)
    anywhere = pl.BlockSpec(memory_space=pl.ANY)
    both = ("seq", "head")
    devices = [(i, j) for i in range(seq_size) for j in range(head_size)]

    def flat(seq_index, head_index):
        return seq_index * head_size + head_index

    def in_hbm(x):
        return pltpu.with_memory_space_constraint(x, pltpu.HBM)

    def host(i, j):
        other = (i // COPIES) ^ (2 - ((j ^ (j >> 1)) & 1))
        return flat(((i % COPIES) * 2 + other // 2) * COPIES + other % 2, j)

    def owner(i, j, a):
        plane, chip = i // COPIES, i % COPIES * per_device + a
        return flat(chip * COPIES + 1 - j // 2, plane)

    def in_plane(move):
        return [(g * COPIES + t, move(g, t)) for g in range(owners) for t in range(COPIES)]

    *picked, packed, limit = pl.pallas_call(
        functools.partial(pick_kernel, per_device),
        out_shape=[jax.ShapeDtypeStruct((width, slots), cache.dtype)] * owners
        + [
            jax.ShapeDtypeStruct((all_rows, q_width + ROPE), queries.dtype),
            jax.ShapeDtypeStruct((8, slots), jnp.int32),
        ],
        in_specs=[anywhere] * 4,
        out_specs=[vmem] * (owners + 2),
        scratch_shapes=[
            pltpu.VMEM(queries.shape, queries.dtype),
            pltpu.VMEM(new_latent.shape, new_latent.dtype),
            pltpu.SMEM(lengths.shape, lengths.dtype),
            pltpu.SemaphoreType.DMA((owners + 3,)),
        ],
        compiler_params=params,
        cost_estimate=LONG,
    )(*[in_hbm(x) for x in (jnp.swapaxes(cache, 1, 2), queries, new_latent, lengths)])
    moved = lax.ppermute(packed, both, [(flat(i, j), host(i, j)) for i, j in devices])
    own_keys = [picked[0]] + [
        lax.ppermute(picked[k], "seq", in_plane(lambda g, t: (g ^ partner(k, t)) * COPIES + t))
        for k in range(1, owners)
    ]
    pair = pl.pallas_call(
        pair_kernel,
        out_shape=jax.ShapeDtypeStruct((2, *picked[0].shape), cache.dtype),
        in_specs=[vmem] * 2,
        out_specs=vmem,
        scratch_shapes=[pltpu.SemaphoreType.DMA((2,))],
        compiler_params=params,
    )(*own_keys[:2])
    other_core = in_plane(lambda g, t: g * COPIES + 1 - t)
    far_keys = [lax.ppermute(keys, "seq", other_core) for keys in [pair] + own_keys[2:]]

    pieces = pl.pallas_call(
        functools.partial(absorb_kernel, per_device),
        out_shape=[jax.ShapeDtypeStruct((piece, width + ROPE), cache.dtype)] * per_device,
        in_specs=[vmem] * 2,
        out_specs=[vmem] * per_device,
        compiler_params=params,
        cost_estimate=LONG,
    )(w_uk, moved)
    arrived = [
        lax.ppermute(
            pieces[k],
            both,
            [(host(i, j), owner(i, j, leaves_as(k, j))) for i, j in devices],
        )
        for k in range(per_device)
    ]

    state = pl.pallas_call(
        functools.partial(begin_kernel, owners, per_device, heads),
        out_shape=[
            jax.ShapeDtypeStruct((all_rows, width), jnp.bfloat16),
            jax.ShapeDtypeStruct((all_rows, 128), jnp.float32),
            jax.ShapeDtypeStruct((all_rows, 128), jnp.float32),
            jax.ShapeDtypeStruct((all_rows, LATENT), jnp.float32),
        ],
        in_specs=[vmem] * (1 + per_device + owners),
        out_specs=[vmem] * 4,
        compiler_params=params,
        cost_estimate=LONG,
    )(limit, *arrived, *own_keys)
    latent = pl.pallas_call(
        functools.partial(finish_kernel, owners, per_device),
        out_shape=[jax.ShapeDtypeStruct((piece, LATENT), jnp.bfloat16)] * per_device,
        in_specs=[vmem] * (1 + len(state) + len(far_keys)),
        out_specs=[vmem] * per_device,
        compiler_params=params,
    )(limit, *state, *far_keys)

    back = [
        lax.ppermute(
            latent[k],
            both,
            [(owner(i, j, first_back(i // COPIES, j) ^ k), flat(i, j)) for i, j in devices],
        )
        for k in range(per_device)
    ]
    return pl.pallas_call(
        functools.partial(project_kernel, per_device),
        out_shape=jax.ShapeDtypeStruct((rows, heads, w_uv.shape[2]), jnp.bfloat16),
        in_specs=[vmem] * (1 + per_device),
        out_specs=vmem,
        compiler_params=params,
    )(w_uv, *back[::-1])


def local_partial(
    query_tile_block,
    key_tile_block,
    incoming_keys,
    len_block,
    offset,
    own_first,
    score_scale,
    head_count,
):
    scores = (
        jnp.einsum(
            "vfa,vja->vfj", query_tile_block, key_tile_block, preferred_element_type=jnp.float32
        )
        * score_scale
    )
    positions = offset + lax.broadcasted_iota(jnp.int32, (1, 1, key_tile_block.shape[1]), 2)
    visible = positions < len_block[:, None, None]
    fresh_scores = (
        jnp.einsum(
            "vfa,vja->vfj", query_tile_block, incoming_keys, preferred_element_type=jnp.float32
        )
        * score_scale
    )
    spec_count = incoming_keys.shape[1]
    row_spec = (
        lax.broadcasted_iota(jnp.int32, (1, query_tile_block.shape[1], spec_count), 1) // head_count
    )
    key_spec = lax.broadcasted_iota(jnp.int32, (1, query_tile_block.shape[1], spec_count), 2)
    causal = (key_spec <= row_spec) & own_first
    row_top = jnp.maximum(
        jnp.max(jnp.where(visible, scores, masked_value), axis=2),
        jnp.max(jnp.where(causal, fresh_scores, masked_value), axis=2),
    )
    weights = jnp.where(visible, jnp.exp(scores - row_top[..., None]), 0.0)
    fresh_weights = jnp.where(causal, jnp.exp(fresh_scores - row_top[..., None]), 0.0)
    running_totals = jnp.sum(weights, axis=2) + jnp.sum(fresh_weights, axis=2)
    weighted = jnp.einsum(
        "mpu,mui->mpi",
        weights.astype(jnp.bfloat16),
        key_tile_block[:, :, :LATENT],
        preferred_element_type=jnp.float32,
    )
    weighted = weighted + jnp.einsum(
        "mpu,mui->mpi",
        fresh_weights.astype(jnp.bfloat16),
        incoming_keys[:, :, :LATENT],
        preferred_element_type=jnp.float32,
    )
    return (row_top, running_totals, weighted)


def project_values(latent_rows, value_weight):
    return jnp.einsum("rhc,hcv->rhv", latent_rows, value_weight, precision=lax.Precision.HIGHEST)


def split_positions(queries, new_latent, cache, lengths, w_uk, w_uv):
    own_rows, head_count, _ = queries.shape
    score_scale = (NOPE + ROPE) ** (-0.5)
    gathered, new_all = (
        lax.all_gather(queries, "seq", axis=0, tiled=True),
        lax.all_gather(new_latent, "seq", axis=0, tiled=True),
    )
    absorbed = jnp.einsum(
        "rhn,hnc->rhc", gathered[:, :, :NOPE], w_uk, preferred_element_type=jnp.float32
    ).astype(jnp.bfloat16)
    q_all = jnp.concatenate([absorbed, gathered[:, :, NOPE:]], axis=2)
    total_rows = q_all.shape[0]
    seq_count = total_rows // SPEC
    query_slots = SPEC * head_count
    q_seq = q_all.reshape(seq_count, query_slots, q_all.shape[2])
    new_seq = new_all.reshape(seq_count, SPEC, new_all.shape[1])
    seq_index = lax.axis_index("seq")
    offset = seq_index * cache.shape[1]
    own_first = seq_index == 0
    row_top, running_totals, weighted = local_partial(
        q_seq,
        lax.all_gather(cache, "head", axis=0, tiled=True),
        new_seq,
        lengths,
        offset,
        own_first,
        score_scale,
        head_count,
    )
    value_weight = w_uv.astype(jnp.float32)
    global_top = lax.pmax(row_top, "seq")
    factor = jnp.exp(row_top - global_top)
    scaled_totals = (running_totals * factor).reshape(total_rows, head_count)
    scaled_weighted = (weighted * factor[..., None]).reshape(total_rows, head_count, LATENT)
    row_totals, row_weighted = (
        lax.psum_scatter(scaled_totals, "seq", scatter_dimension=0, tiled=True),
        lax.psum_scatter(scaled_weighted, "seq", scatter_dimension=0, tiled=True),
    )
    latent_output = row_weighted / row_totals[..., None]
    result = project_values(latent_output, value_weight)
    return result.astype(jnp.bfloat16)


def shards(seq_size, head_size, queries, new_latent, cache, lengths, w_uk, w_uv):
    rows, owners = queries.shape[0], cache.shape[0]
    per_device = rows // SPEC
    if (
        per_device == 2
        and rows % SPEC == 0
        and seq_size == COPIES * owners
        and head_size == owners == 4
    ):
        return whole_sequences(
            seq_size, head_size, queries, new_latent, cache, lengths, w_uk, w_uv
        )
    return split_positions(queries, new_latent, cache, lengths, w_uk, w_uv)


def solution(mesh):
    return jax.shard_map(
        functools.partial(shards, mesh.shape["seq"], mesh.shape["head"]),
        mesh=mesh,
        in_specs=(
            P("seq", "head", None),
            P("seq", None),
            P("head", "seq", None),
            P(),
            P("head", None, None),
            P("head", None, None),
        ),
        out_specs=P("seq", "head", None),
        check_vma=False,
    )
```

```python
import functools

import jax
import jax.numpy as jnp
from jax import lax
from jax.experimental import pallas as pl
from jax.experimental.pallas import tpu as pltpu
from jax.sharding import PartitionSpec as P

NOPE = 128
ROPE = 64
LATENT = 512
SPEC = 4
SCORE_SCALE = (NOPE + ROPE) ** (-0.5)
COPIES = 2
VMEM_LIMIT = 16 * 1024 * 1024
LONG = pl.CostEstimate(flops=2 * 10**10, bytes_accessed=0, transcendentals=0)

masked_value = -1e30


def leaves_as(k, head_shard):
    return (k + head_shard) % 2


def far_half(plane, pair):
    return 1 * (plane <= 2 * pair)


def first_back(home_chip, head_shard):
    far = 1 * (far_half(home_chip, head_shard // 2) == head_shard % 2)
    return home_chip % 2 ^ far


def first_block(plane, chip, core):
    near = 1 * (chip % 2 == plane % 2)
    return far_half(plane, 1 - core) ^ near ^ chip % 2


def partner(k, core):
    return (0, 3, 1 ^ 3 * core, 2 ^ 3 * core)[k]


def pick_kernel(per_device, cache_hbm, new_hbm, len_hbm, *refs):
    owners, width, slots = cache_hbm.shape
    blocks, (limit_ref, new_ref, len_ref, sem) = refs[:owners], refs[owners:]
    chip, core = lax.axis_index("seq") // COPIES, lax.axis_index("seq") % COPIES
    takers = [chip ^ partner(k, core) for k in range(owners)]
    moves = [
        pltpu.make_async_copy(new_hbm, new_ref, sem.at[owners]),
        pltpu.make_async_copy(len_hbm, len_ref, sem.at[owners + 1]),
    ] + [
        pltpu.make_async_copy(cache_hbm.at[takers[k]], blocks[k].at[pl.ds(0, width)], sem.at[k])
        for k in range(owners)
    ]
    for move in moves:
        move.start()
    moves[0].wait()
    fresh = new_ref[...].astype(jnp.float32)
    spare = -width % slots
    if spare:
        fresh = jnp.concatenate([fresh, jnp.zeros((fresh.shape[0], spare), jnp.float32)], axis=1)
    below = []
    for a in range(per_device):
        parts = [
            fresh[a * SPEC : (a + 1) * SPEC, n : n + slots] for n in range(0, width, slots)
        ]
        spare = blocks[0].shape[0] - width - SPEC * len(parts)
        if spare:
            parts.append(jnp.zeros((spare, slots), jnp.float32))
        below.append(jnp.concatenate(parts, axis=0))
    for k in range(owners):
        rows = jnp.where(takers[k] % per_device == 0, below[0], below[1])
        blocks[k][width:, :] = rows.astype(blocks[k].dtype)
    moves[1].wait()
    length = len_ref[lax.axis_index("head") * owners + chip]
    limit_ref[...] = jnp.full(limit_ref.shape, length, limit_ref.dtype)
    for move in moves[2:]:
        move.wait()


def pair_kernel(first_ref, second_ref, out_ref, sem):
    moves = [
        pltpu.make_async_copy(ref, out_ref.at[n], sem.at[n])
        for n, ref in enumerate((first_ref, second_ref))
    ]
    for move in moves:
        move.start()
    for move in moves:
        move.wait()


def absorb_kernel(per_device, w_ref, q_ref, *outs):
    rows, heads, width = q_ref.shape
    piece = SPEC * heads
    q = q_ref[...].reshape(rows * heads, width)
    nope = q[:, :NOPE]
    own_head = lax.broadcasted_iota(jnp.int32, nope.shape, 0) % heads
    spread = jnp.concatenate(
        [jnp.where(own_head == h, nope, jnp.zeros_like(nope)) for h in range(heads)], axis=1
    )
    absorbed = jnp.dot(
        spread, w_ref[...].reshape(heads * NOPE, LATENT), preferred_element_type=jnp.float32
    ).astype(jnp.bfloat16)
    for k in range(per_device):
        which = leaves_as(k, lax.axis_index("head"))
        for a in range(per_device):

            @pl.when(which == a)
            def _():
                outs[k][:, :LATENT] = absorbed[a * piece : (a + 1) * piece]
                outs[k][:, LATENT:] = q[a * piece : (a + 1) * piece, NOPE:]


def block_scores(q, refs, starts, limit_ref):
    width = q.shape[1]
    keys = jnp.concatenate([ref[:width, :] for ref in refs], axis=1)
    limit = limit_ref[:1, :]
    lane = lax.broadcasted_iota(jnp.int32, limit.shape, 1)
    visible = jnp.concatenate([lane + start < limit for start in starts], axis=1)
    s = jnp.dot(q, keys, preferred_element_type=jnp.float32) * SCORE_SCALE
    return jnp.where(visible, s, masked_value)


def weigh(s, refs, top):
    w = jnp.exp(s - top)
    values = jnp.concatenate([ref[:LATENT, :] for ref in refs], axis=1)
    out = lax.dot_general(
        w.astype(jnp.bfloat16),
        values,
        (((1,), (1,)), ((), ())),
        preferred_element_type=jnp.float32,
    )
    return jnp.sum(w, axis=1, keepdims=True), out


def begin_kernel(owners, per_device, limit_ref, *refs):
    q_refs, key_refs = refs[:per_device], refs[per_device : per_device + owners]
    q_out, top_ref, total_ref, out_ref = refs[per_device + owners :]
    seq_index = lax.axis_index("seq")
    chip, core = seq_index // COPIES, seq_index % COPIES
    slots = key_refs[0].shape[1]
    q = jnp.concatenate([ref[...] for ref in q_refs], axis=0)
    starts = [((chip ^ partner(k, core)) * COPIES + core) * slots for k in range(owners)]
    s = block_scores(q, key_refs, starts, limit_ref)
    top = jnp.max(s, axis=1, keepdims=True)
    total, out = weigh(s, key_refs, top)
    q_out[...] = q
    top_ref[...] = jnp.broadcast_to(top, top_ref.shape)
    total_ref[...] = jnp.broadcast_to(total, total_ref.shape)
    out_ref[...] = out


def finish_kernel(
    owners, per_device, heads, limit_ref, q_ref, top_ref, total_ref, part_ref, *refs
):
    own_refs, (pair_ref, *far_refs) = refs[:owners], refs[owners : 2 * owners - 1]
    far_refs = [pair_ref.at[0], pair_ref.at[1], *far_refs]
    outs, fresh_ref = refs[2 * owners - 1 : -1], refs[-1]
    seq_index = lax.axis_index("seq")
    chip, core = seq_index // COPIES, seq_index % COPIES
    plane = lax.axis_index("head")
    q = q_ref[...]
    width, slots = q.shape[1], pair_ref.shape[2]

    for key_refs, source_core in ((own_refs, core), (far_refs, 1 - core)):
        for k in range(owners):
            source = chip ^ partner(k, source_core)

            @pl.when((source == plane) & (source_core == chip // per_device))
            def _():
                fresh_ref[...] = key_refs[k][width:, :]

    fresh = fresh_ref[...].astype(jnp.float32)
    parts = [fresh[n * SPEC : (n + 1) * SPEC] for n in range(-(-width // slots))]
    fresh = jnp.concatenate(parts, axis=1)[:, :width]
    fresh = jnp.concatenate([fresh, jnp.zeros((16 - SPEC, width), jnp.float32)], axis=0)
    fresh = fresh.astype(jnp.bfloat16)
    f = lax.dot_general(
        q, fresh, (((1,), (1,)), ((), ())), preferred_element_type=jnp.float32
    )
    row = lax.broadcasted_iota(jnp.int32, f.shape, 0) % (SPEC * heads)
    key = lax.broadcasted_iota(jnp.int32, f.shape, 1)
    f = jnp.where(key <= row // heads, f * SCORE_SCALE, masked_value)

    starts = [((chip ^ partner(k, 1 - core)) * COPIES + 1 - core) * slots for k in range(owners)]
    s = block_scores(q, far_refs, starts, limit_ref)
    first = top_ref[:, :1]
    top = jnp.maximum(
        jnp.maximum(first, jnp.max(f, axis=1, keepdims=True)), jnp.max(s, axis=1, keepdims=True)
    )
    total, out = weigh(s, far_refs, top)
    w = jnp.exp(f - top)
    scale = jnp.exp(first - top)
    total += jnp.sum(w, axis=1, keepdims=True) + total_ref[:, :1] * scale
    out += part_ref[...] * scale
    out += jnp.dot(
        w.astype(jnp.bfloat16), fresh[:, :LATENT], preferred_element_type=jnp.float32
    )
    out = (out * (1.0 / total)).astype(jnp.bfloat16)
    piece = out.shape[0] // per_device
    sent_first = first_block(plane, chip, core)
    for k in range(per_device):
        for n in range(per_device):

            @pl.when(sent_first ^ k == n)
            def _():
                outs[k][...] = out[n * piece : (n + 1) * piece]


def project_kernel(per_device, w_ref, *refs):
    lat_refs, out_ref = refs[:-1], refs[-1]
    rows, heads, width = out_ref.shape
    first = first_back(lax.axis_index("seq") // COPIES, lax.axis_index("head"))
    parts = [jnp.where(first == a, lat_refs[1][...], lat_refs[0][...]) for a in range(per_device)]
    latent = jnp.concatenate(parts, axis=0)
    out = jnp.zeros((rows * heads, width), jnp.float32)
    own_head = lax.broadcasted_iota(jnp.int32, out.shape, 0) % heads
    step = 2 if heads % 2 == 0 else 1
    for h in range(0, heads, step):
        group = jnp.concatenate([w_ref[h + n] for n in range(step)], axis=1)
        product = jnp.dot(latent, group, preferred_element_type=jnp.float32)
        for n in range(step):
            out = jnp.where(own_head == h + n, product[:, n * width : (n + 1) * width], out)
    out_ref[...] = out.astype(out_ref.dtype).reshape(out_ref.shape)


def whole_sequences(seq_size, head_size, queries, new_latent, cache, lengths, w_uk, w_uv):
    rows, heads, _ = queries.shape
    owners, slots, width = cache.shape
    per_device = rows // SPEC
    piece = SPEC * heads
    all_rows = per_device * piece
    params = pltpu.CompilerParams(vmem_limit_bytes=VMEM_LIMIT)
    vmem = pl.BlockSpec(memory_space=pltpu.VMEM)
    anywhere = pl.BlockSpec(memory_space=pl.ANY)
    both = ("seq", "head")
    devices = [(i, j) for i in range(seq_size) for j in range(head_size)]

    def flat(seq_index, head_index):
        return seq_index * head_size + head_index

    def in_hbm(x):
        return pltpu.with_memory_space_constraint(x, pltpu.HBM)

    def host(i, j):
        other = (i // COPIES) ^ (2 - ((j ^ (j >> 1)) & 1))
        return flat(((i % COPIES) * 2 + other // 2) * COPIES + other % 2, j)

    def owner(i, j, a):
        plane, chip = i // COPIES, i % COPIES * per_device + a
        return flat(chip * COPIES + 1 - j // 2, plane)

    def in_plane(move):
        return [(g * COPIES + t, move(g, t)) for g in range(owners) for t in range(COPIES)]

    moved = lax.ppermute(queries, both, [(flat(i, j), host(i, j)) for i, j in devices])
    below = -(-SPEC * -(-width // slots) // 16) * 16
    *picked, limit = pl.pallas_call(
        functools.partial(pick_kernel, per_device),
        out_shape=[jax.ShapeDtypeStruct((width + below, slots), cache.dtype)] * owners
        + [jax.ShapeDtypeStruct((8, slots), jnp.int32)],
        in_specs=[anywhere] * 3,
        out_specs=[vmem] * (owners + 1),
        scratch_shapes=[
            pltpu.VMEM(new_latent.shape, new_latent.dtype),
            pltpu.SMEM(lengths.shape, lengths.dtype),
            pltpu.SemaphoreType.DMA((owners + 2,)),
        ],
        compiler_params=params,
        cost_estimate=LONG,
    )(*[in_hbm(x) for x in (jnp.swapaxes(cache, 1, 2), new_latent, lengths)])
    own_keys = [picked[0]] + [
        lax.ppermute(picked[k], "seq", in_plane(lambda g, t: (g ^ partner(k, t)) * COPIES + t))
        for k in range(1, owners)
    ]
    pair = pl.pallas_call(
        pair_kernel,
        out_shape=jax.ShapeDtypeStruct((2, *picked[0].shape), cache.dtype),
        in_specs=[vmem] * 2,
        out_specs=vmem,
        scratch_shapes=[pltpu.SemaphoreType.DMA((2,))],
        compiler_params=params,
    )(*own_keys[:2])
    other_core = in_plane(lambda g, t: g * COPIES + 1 - t)
    far_keys = [lax.ppermute(keys, "seq", other_core) for keys in [pair] + own_keys[2:]]

    pieces = pl.pallas_call(
        functools.partial(absorb_kernel, per_device),
        out_shape=[jax.ShapeDtypeStruct((piece, width), cache.dtype)] * per_device,
        in_specs=[vmem] * 2,
        out_specs=[vmem] * per_device,
        compiler_params=params,
        cost_estimate=LONG,
    )(w_uk, moved)
    arrived = [
        lax.ppermute(
            pieces[k],
            both,
            [(host(i, j), owner(i, j, leaves_as(k, j))) for i, j in devices],
        )
        for k in range(per_device)
    ]

    state = pl.pallas_call(
        functools.partial(begin_kernel, owners, per_device),
        out_shape=[
            jax.ShapeDtypeStruct((all_rows, width), jnp.bfloat16),
            jax.ShapeDtypeStruct((all_rows, 128), jnp.float32),
            jax.ShapeDtypeStruct((all_rows, 128), jnp.float32),
            jax.ShapeDtypeStruct((all_rows, LATENT), jnp.float32),
        ],
        in_specs=[vmem] * (1 + per_device + owners),
        out_specs=[vmem] * 4,
        compiler_params=params,
        cost_estimate=LONG,
    )(limit, *arrived, *own_keys)
    latent = pl.pallas_call(
        functools.partial(finish_kernel, owners, per_device, heads),
        out_shape=[jax.ShapeDtypeStruct((piece, LATENT), jnp.bfloat16)] * per_device,
        in_specs=[vmem] * (1 + len(state) + len(own_keys) + len(far_keys)),
        out_specs=[vmem] * per_device,
        scratch_shapes=[pltpu.VMEM((below, slots), cache.dtype)],
        compiler_params=params,
    )(limit, *state, *own_keys, *far_keys)

    back = [
        lax.ppermute(
            latent[k],
            both,
            [(owner(i, j, first_back(i // COPIES, j) ^ k), flat(i, j)) for i, j in devices],
        )
        for k in range(per_device)
    ]
    return pl.pallas_call(
        functools.partial(project_kernel, per_device),
        out_shape=jax.ShapeDtypeStruct((rows, heads, w_uv.shape[2]), jnp.bfloat16),
        in_specs=[vmem] * (1 + per_device),
        out_specs=vmem,
        compiler_params=params,
    )(w_uv, *back[::-1])


def local_partial(
    query_tile_block,
    key_tile_block,
    incoming_keys,
    len_block,
    offset,
    own_first,
    score_scale,
    head_count,
):
    scores = (
        jnp.einsum(
            "vfa,vja->vfj", query_tile_block, key_tile_block, preferred_element_type=jnp.float32
        )
        * score_scale
    )
    positions = offset + lax.broadcasted_iota(jnp.int32, (1, 1, key_tile_block.shape[1]), 2)
    visible = positions < len_block[:, None, None]
    fresh_scores = (
        jnp.einsum(
            "vfa,vja->vfj", query_tile_block, incoming_keys, preferred_element_type=jnp.float32
        )
        * score_scale
    )
    spec_count = incoming_keys.shape[1]
    row_spec = (
        lax.broadcasted_iota(jnp.int32, (1, query_tile_block.shape[1], spec_count), 1) // head_count
    )
    key_spec = lax.broadcasted_iota(jnp.int32, (1, query_tile_block.shape[1], spec_count), 2)
    causal = (key_spec <= row_spec) & own_first
    row_top = jnp.maximum(
        jnp.max(jnp.where(visible, scores, masked_value), axis=2),
        jnp.max(jnp.where(causal, fresh_scores, masked_value), axis=2),
    )
    weights = jnp.where(visible, jnp.exp(scores - row_top[..., None]), 0.0)
    fresh_weights = jnp.where(causal, jnp.exp(fresh_scores - row_top[..., None]), 0.0)
    running_totals = jnp.sum(weights, axis=2) + jnp.sum(fresh_weights, axis=2)
    weighted = jnp.einsum(
        "mpu,mui->mpi",
        weights.astype(jnp.bfloat16),
        key_tile_block[:, :, :LATENT],
        preferred_element_type=jnp.float32,
    )
    weighted = weighted + jnp.einsum(
        "mpu,mui->mpi",
        fresh_weights.astype(jnp.bfloat16),
        incoming_keys[:, :, :LATENT],
        preferred_element_type=jnp.float32,
    )
    return (row_top, running_totals, weighted)


def project_values(latent_rows, value_weight):
    return jnp.einsum("rhc,hcv->rhv", latent_rows, value_weight, precision=lax.Precision.HIGHEST)


def split_positions(queries, new_latent, cache, lengths, w_uk, w_uv):
    own_rows, head_count, _ = queries.shape
    score_scale = (NOPE + ROPE) ** (-0.5)
    gathered, new_all = (
        lax.all_gather(queries, "seq", axis=0, tiled=True),
        lax.all_gather(new_latent, "seq", axis=0, tiled=True),
    )
    absorbed = jnp.einsum(
        "rhn,hnc->rhc", gathered[:, :, :NOPE], w_uk, preferred_element_type=jnp.float32
    ).astype(jnp.bfloat16)
    q_all = jnp.concatenate([absorbed, gathered[:, :, NOPE:]], axis=2)
    total_rows = q_all.shape[0]
    seq_count = total_rows // SPEC
    query_slots = SPEC * head_count
    q_seq = q_all.reshape(seq_count, query_slots, q_all.shape[2])
    new_seq = new_all.reshape(seq_count, SPEC, new_all.shape[1])
    seq_index = lax.axis_index("seq")
    offset = seq_index * cache.shape[1]
    own_first = seq_index == 0
    row_top, running_totals, weighted = local_partial(
        q_seq,
        lax.all_gather(cache, "head", axis=0, tiled=True),
        new_seq,
        lengths,
        offset,
        own_first,
        score_scale,
        head_count,
    )
    value_weight = w_uv.astype(jnp.float32)
    global_top = lax.pmax(row_top, "seq")
    factor = jnp.exp(row_top - global_top)
    scaled_totals = (running_totals * factor).reshape(total_rows, head_count)
    scaled_weighted = (weighted * factor[..., None]).reshape(total_rows, head_count, LATENT)
    row_totals, row_weighted = (
        lax.psum_scatter(scaled_totals, "seq", scatter_dimension=0, tiled=True),
        lax.psum_scatter(scaled_weighted, "seq", scatter_dimension=0, tiled=True),
    )
    latent_output = row_weighted / row_totals[..., None]
    result = project_values(latent_output, value_weight)
    return result.astype(jnp.bfloat16)


def shards(seq_size, head_size, queries, new_latent, cache, lengths, w_uk, w_uv):
    rows, owners = queries.shape[0], cache.shape[0]
    per_device = rows // SPEC
    if (
        per_device == 2
        and rows % SPEC == 0
        and seq_size == COPIES * owners
        and head_size == owners == 4
    ):
        return whole_sequences(
            seq_size, head_size, queries, new_latent, cache, lengths, w_uk, w_uv
        )
    return split_positions(queries, new_latent, cache, lengths, w_uk, w_uv)


def solution(mesh):
    return jax.shard_map(
        functools.partial(shards, mesh.shape["seq"], mesh.shape["head"]),
        mesh=mesh,
        in_specs=(
            P("seq", "head", None),
            P("seq", None),
            P("head", "seq", None),
            P(),
            P("head", None, None),
            P("head", None, None),
        ),
        out_specs=P("seq", "head", None),
        check_vma=False,
    )
```

```python
import functools

import jax
import jax.numpy as jnp
from jax import lax
from jax.experimental import pallas as pl
from jax.experimental.pallas import tpu as pltpu
from jax.sharding import PartitionSpec as P

NOPE = 128
ROPE = 64
LATENT = 512
SPEC = 4
SCORE_SCALE = (NOPE + ROPE) ** (-0.5)
COPIES = 2
VMEM_LIMIT = 16 * 1024 * 1024
LONG = pl.CostEstimate(flops=2 * 10**10, bytes_accessed=0, transcendentals=0)

masked_value = -1e30


def leaves_as(k, head_shard):
    return (k + head_shard) % 2


def far_half(plane, pair):
    return 1 * (plane <= 2 * pair)


def first_back(home_chip, head_shard):
    far = 1 * (far_half(home_chip, head_shard // 2) == head_shard % 2)
    return home_chip % 2 ^ far


def first_block(plane, chip, core):
    near = 1 * (chip % 2 == plane % 2)
    return far_half(plane, core ^ 1 * (chip == plane)) ^ near ^ chip % 2


def partner(k, core):
    return (0, 3, 1 ^ 3 * core, 2 ^ 3 * core)[k]


def pick_kernel(per_device, cache_hbm, q_hbm, new_hbm, len_hbm, *refs):
    owners = cache_hbm.shape[0]
    blocks, (out_ref, limit_ref, q_ref, new_ref, len_ref, sem) = refs[:owners], refs[owners:]
    chip, core = lax.axis_index("seq") // COPIES, lax.axis_index("seq") % COPIES
    moves = [
        pltpu.make_async_copy(q_hbm, q_ref, sem.at[owners]),
        pltpu.make_async_copy(new_hbm, new_ref, sem.at[owners + 1]),
        pltpu.make_async_copy(len_hbm, len_ref, sem.at[owners + 2]),
    ] + [
        pltpu.make_async_copy(cache_hbm.at[chip ^ partner(k, core)], blocks[k], sem.at[k])
        for k in range(owners)
    ]
    for move in moves:
        move.start()
    moves[0].wait()
    moves[1].wait()
    heads, width = q_ref.shape[1:]
    fresh = new_ref[...].astype(jnp.float32)
    piece = SPEC * heads
    for a in range(per_device):
        rows = q_ref[a * SPEC : (a + 1) * SPEC].reshape(piece, width)
        own = fresh[a * SPEC : (a + 1) * SPEC]
        parts = [own[:, n : n + ROPE] for n in range(0, own.shape[1], ROPE)]
        spare = piece - SPEC * len(parts)
        if spare:
            parts.append(jnp.zeros((spare, ROPE), jnp.float32))
        own = jnp.concatenate(parts, axis=0).astype(rows.dtype)
        out_ref[a * piece : (a + 1) * piece] = jnp.concatenate([rows, own], axis=1)
    moves[2].wait()
    length = len_ref[lax.axis_index("head") * owners + chip]
    limit_ref[...] = jnp.full(limit_ref.shape, length, limit_ref.dtype)
    for move in moves[3:]:
        move.wait()


def pair_kernel(first_ref, second_ref, out_ref, sem):
    moves = [
        pltpu.make_async_copy(ref, out_ref.at[n], sem.at[n])
        for n, ref in enumerate((first_ref, second_ref))
    ]
    for move in moves:
        move.start()
    for move in moves:
        move.wait()


def absorb_kernel(per_device, w_ref, packed_ref, *outs):
    heads = w_ref.shape[0]
    piece = SPEC * heads
    nope = packed_ref[:, :NOPE]
    own_head = lax.broadcasted_iota(jnp.int32, nope.shape, 0) % heads
    spread = jnp.concatenate(
        [jnp.where(own_head == h, nope, jnp.zeros_like(nope)) for h in range(heads)], axis=1
    )
    absorbed = jnp.dot(
        spread, w_ref[...].reshape(heads * NOPE, LATENT), preferred_element_type=jnp.float32
    ).astype(jnp.bfloat16)
    for k in range(per_device):
        which = leaves_as(k, lax.axis_index("head"))
        for a in range(per_device):

            @pl.when(which == a)
            def _():
                rows = slice(a * piece, (a + 1) * piece)
                outs[k][:, :LATENT] = absorbed[rows]
                outs[k][:, LATENT:] = packed_ref[rows, NOPE:]


def block_scores(q, refs, starts, limit_ref):
    width = q.shape[1]
    keys = jnp.concatenate([ref[:width, :] for ref in refs], axis=1)
    limit = limit_ref[:1, :]
    lane = lax.broadcasted_iota(jnp.int32, limit.shape, 1)
    visible = jnp.concatenate([lane + start < limit for start in starts], axis=1)
    s = jnp.dot(q, keys, preferred_element_type=jnp.float32) * SCORE_SCALE
    return jnp.where(visible, s, masked_value)


def weigh(s, refs, top):
    w = jnp.exp(s - top)
    values = jnp.concatenate([ref[:LATENT, :] for ref in refs], axis=1)
    out = lax.dot_general(
        w.astype(jnp.bfloat16),
        values,
        (((1,), (1,)), ((), ())),
        preferred_element_type=jnp.float32,
    )
    return jnp.sum(w, axis=1, keepdims=True), out


def begin_kernel(owners, per_device, heads, limit_ref, *refs):
    q_refs, key_refs = refs[:per_device], refs[per_device : per_device + owners]
    q_out, top_ref, total_ref, out_ref = refs[per_device + owners :]
    seq_index = lax.axis_index("seq")
    chip, core = seq_index // COPIES, seq_index % COPIES
    slots = key_refs[0].shape[1]
    width = LATENT + ROPE
    q = jnp.concatenate([ref[:, :width] for ref in q_refs], axis=0)

    fresh = q_refs[0][:, width:].astype(jnp.float32)
    fresh = jnp.concatenate(
        [fresh[n * SPEC : (n + 1) * SPEC] for n in range(width // ROPE)], axis=1
    )
    fresh = jnp.concatenate([fresh, jnp.zeros((16 - SPEC, width), jnp.float32)], axis=0)
    fresh = fresh.astype(jnp.bfloat16)
    f = lax.dot_general(
        q, fresh, (((1,), (1,)), ((), ())), preferred_element_type=jnp.float32
    )
    row = lax.broadcasted_iota(jnp.int32, f.shape, 0) % (SPEC * heads)
    key = lax.broadcasted_iota(jnp.int32, f.shape, 1)
    f = jnp.where(key <= row // heads, f * SCORE_SCALE, masked_value)

    starts = [((chip ^ partner(k, core)) * COPIES + core) * slots for k in range(owners)]
    s = block_scores(q, key_refs, starts, limit_ref)
    top = jnp.maximum(jnp.max(s, axis=1, keepdims=True), jnp.max(f, axis=1, keepdims=True))
    total, out = weigh(s, key_refs, top)
    w = jnp.exp(f - top)
    total += jnp.sum(w, axis=1, keepdims=True)
    out += jnp.dot(
        w.astype(jnp.bfloat16), fresh[:, :LATENT], preferred_element_type=jnp.float32
    )
    q_out[...] = q
    top_ref[...] = jnp.broadcast_to(top, top_ref.shape)
    total_ref[...] = jnp.broadcast_to(total, total_ref.shape)
    out_ref[...] = out


def finish_kernel(
    owners, per_device, limit_ref, q_ref, top_ref, total_ref, part_ref, pair_ref, *refs
):
    key_refs = [pair_ref.at[0], pair_ref.at[1], *refs[: owners - 2]]
    outs = refs[owners - 2 :]
    seq_index = lax.axis_index("seq")
    chip, core = seq_index // COPIES, seq_index % COPIES
    plane = lax.axis_index("head")
    slots = key_refs[0].shape[1]
    starts = [((chip ^ partner(k, 1 - core)) * COPIES + 1 - core) * slots for k in range(owners)]
    s = block_scores(q_ref[...], key_refs, starts, limit_ref)
    first = top_ref[:, :1]
    top = jnp.maximum(first, jnp.max(s, axis=1, keepdims=True))
    total, out = weigh(s, key_refs, top)
    scale = jnp.exp(first - top)
    total += total_ref[:, :1] * scale
    out += part_ref[...] * scale
    out = (out * (1.0 / total)).astype(jnp.bfloat16)
    piece = out.shape[0] // per_device
    sent_first = first_block(plane, chip, core)
    for k in range(per_device):
        for n in range(per_device):

            @pl.when(sent_first ^ k == n)
            def _():
                outs[k][...] = out[n * piece : (n + 1) * piece]


def project_kernel(per_device, w_ref, *refs):
    lat_refs, out_ref = refs[:-1], refs[-1]
    rows, heads, width = out_ref.shape
    first = first_back(lax.axis_index("seq") // COPIES, lax.axis_index("head"))
    parts = [jnp.where(first == a, lat_refs[1][...], lat_refs[0][...]) for a in range(per_device)]
    latent = jnp.concatenate(parts, axis=0)
    out = jnp.zeros((rows * heads, width), jnp.float32)
    own_head = lax.broadcasted_iota(jnp.int32, out.shape, 0) % heads
    step = 2 if heads % 2 == 0 else 1
    for h in range(0, heads, step):
        group = jnp.concatenate([w_ref[h + n] for n in range(step)], axis=1)
        product = jnp.dot(latent, group, preferred_element_type=jnp.float32)
        for n in range(step):
            out = jnp.where(own_head == h + n, product[:, n * width : (n + 1) * width], out)
    out_ref[...] = out.astype(out_ref.dtype).reshape(out_ref.shape)


def whole_sequences(seq_size, head_size, queries, new_latent, cache, lengths, w_uk, w_uv):
    rows, heads, q_width = queries.shape
    owners, slots, width = cache.shape
    per_device = rows // SPEC
    piece = SPEC * heads
    all_rows = per_device * piece
    params = pltpu.CompilerParams(vmem_limit_bytes=VMEM_LIMIT)
    vmem = pl.BlockSpec(memory_space=pltpu.VMEM)
    anywhere = pl.BlockSpec(memory_space=pl.ANY)
    both = ("seq", "head")
    devices = [(i, j) for i in range(seq_size) for j in range(head_size)]

    def flat(seq_index, head_index):
        return seq_index * head_size + head_index

    def in_hbm(x):
        return pltpu.with_memory_space_constraint(x, pltpu.HBM)

    def host(i, j):
        home, row = i // COPIES, i % COPIES
        exchanged = row == home // 2 == j // 2
        return flat((row * 2 + home % 2 ^ exchanged) * COPIES + 1 - home // 2, j)

    def owner(i, j, a):
        plane, chip = i // COPIES, i % COPIES * per_device + a
        return flat(chip * COPIES + (j // 2 ^ (chip == plane)), plane)

    def in_plane(move):
        return [(g * COPIES + t, move(g, t)) for g in range(owners) for t in range(COPIES)]

    *picked, packed, limit = pl.pallas_call(
        functools.partial(pick_kernel, per_device),
        out_shape=[jax.ShapeDtypeStruct((width, slots), cache.dtype)] * owners
        + [
            jax.ShapeDtypeStruct((all_rows, q_width + ROPE), queries.dtype),
            jax.ShapeDtypeStruct((8, slots), jnp.int32),
        ],
        in_specs=[anywhere] * 4,
        out_specs=[vmem] * (owners + 2),
        scratch_shapes=[
            pltpu.VMEM(queries.shape, queries.dtype),
            pltpu.VMEM(new_latent.shape, new_latent.dtype),
            pltpu.SMEM(lengths.shape, lengths.dtype),
            pltpu.SemaphoreType.DMA((owners + 3,)),
        ],
        compiler_params=params,
        cost_estimate=LONG,
    )(*[in_hbm(x) for x in (jnp.swapaxes(cache, 1, 2), queries, new_latent, lengths)])
    moved = lax.ppermute(packed, both, [(flat(i, j), host(i, j)) for i, j in devices])
    own_keys = [picked[0]] + [
        lax.ppermute(picked[k], "seq", in_plane(lambda g, t: (g ^ partner(k, t)) * COPIES + t))
        for k in range(1, owners)
    ]
    pair = pl.pallas_call(
        pair_kernel,
        out_shape=jax.ShapeDtypeStruct((2, *picked[0].shape), cache.dtype),
        in_specs=[vmem] * 2,
        out_specs=vmem,
        scratch_shapes=[pltpu.SemaphoreType.DMA((2,))],
        compiler_params=params,
    )(*own_keys[:2])
    other_core = in_plane(lambda g, t: g * COPIES + 1 - t)
    far_keys = [lax.ppermute(keys, "seq", other_core) for keys in [pair] + own_keys[2:]]

    pieces = pl.pallas_call(
        functools.partial(absorb_kernel, per_device),
        out_shape=[jax.ShapeDtypeStruct((piece, width + ROPE), cache.dtype)] * per_device,
        in_specs=[vmem] * 2,
        out_specs=[vmem] * per_device,
        compiler_params=params,
        cost_estimate=LONG,
    )(w_uk, moved)
    arrived = [
        lax.ppermute(
            pieces[k],
            both,
            [(host(i, j), owner(i, j, leaves_as(k, j))) for i, j in devices],
        )
        for k in range(per_device)
    ]

    state = pl.pallas_call(
        functools.partial(begin_kernel, owners, per_device, heads),
        out_shape=[
            jax.ShapeDtypeStruct((all_rows, width), jnp.bfloat16),
            jax.ShapeDtypeStruct((all_rows, 128), jnp.float32),
            jax.ShapeDtypeStruct((all_rows, 128), jnp.float32),
            jax.ShapeDtypeStruct((all_rows, LATENT), jnp.float32),
        ],
        in_specs=[vmem] * (1 + per_device + owners),
        out_specs=[vmem] * 4,
        compiler_params=params,
        cost_estimate=LONG,
    )(limit, *arrived, *own_keys)
    latent = pl.pallas_call(
        functools.partial(finish_kernel, owners, per_device),
        out_shape=[jax.ShapeDtypeStruct((piece, LATENT), jnp.bfloat16)] * per_device,
        in_specs=[vmem] * (1 + len(state) + len(far_keys)),
        out_specs=[vmem] * per_device,
        compiler_params=params,
    )(limit, *state, *far_keys)

    back = [
        lax.ppermute(
            latent[k],
            both,
            [(owner(i, j, first_back(i // COPIES, j) ^ k), flat(i, j)) for i, j in devices],
        )
        for k in range(per_device)
    ]
    return pl.pallas_call(
        functools.partial(project_kernel, per_device),
        out_shape=jax.ShapeDtypeStruct((rows, heads, w_uv.shape[2]), jnp.bfloat16),
        in_specs=[vmem] * (1 + per_device),
        out_specs=vmem,
        compiler_params=params,
    )(w_uv, *back[::-1])


def local_partial(
    query_tile_block,
    key_tile_block,
    incoming_keys,
    len_block,
    offset,
    own_first,
    score_scale,
    head_count,
):
    scores = (
        jnp.einsum(
            "vfa,vja->vfj", query_tile_block, key_tile_block, preferred_element_type=jnp.float32
        )
        * score_scale
    )
    positions = offset + lax.broadcasted_iota(jnp.int32, (1, 1, key_tile_block.shape[1]), 2)
    visible = positions < len_block[:, None, None]
    fresh_scores = (
        jnp.einsum(
            "vfa,vja->vfj", query_tile_block, incoming_keys, preferred_element_type=jnp.float32
        )
        * score_scale
    )
    spec_count = incoming_keys.shape[1]
    row_spec = (
        lax.broadcasted_iota(jnp.int32, (1, query_tile_block.shape[1], spec_count), 1) // head_count
    )
    key_spec = lax.broadcasted_iota(jnp.int32, (1, query_tile_block.shape[1], spec_count), 2)
    causal = (key_spec <= row_spec) & own_first
    row_top = jnp.maximum(
        jnp.max(jnp.where(visible, scores, masked_value), axis=2),
        jnp.max(jnp.where(causal, fresh_scores, masked_value), axis=2),
    )
    weights = jnp.where(visible, jnp.exp(scores - row_top[..., None]), 0.0)
    fresh_weights = jnp.where(causal, jnp.exp(fresh_scores - row_top[..., None]), 0.0)
    running_totals = jnp.sum(weights, axis=2) + jnp.sum(fresh_weights, axis=2)
    weighted = jnp.einsum(
        "mpu,mui->mpi",
        weights.astype(jnp.bfloat16),
        key_tile_block[:, :, :LATENT],
        preferred_element_type=jnp.float32,
    )
    weighted = weighted + jnp.einsum(
        "mpu,mui->mpi",
        fresh_weights.astype(jnp.bfloat16),
        incoming_keys[:, :, :LATENT],
        preferred_element_type=jnp.float32,
    )
    return (row_top, running_totals, weighted)


def project_values(latent_rows, value_weight):
    return jnp.einsum("rhc,hcv->rhv", latent_rows, value_weight, precision=lax.Precision.HIGHEST)


def split_positions(queries, new_latent, cache, lengths, w_uk, w_uv):
    own_rows, head_count, _ = queries.shape
    score_scale = (NOPE + ROPE) ** (-0.5)
    gathered, new_all = (
        lax.all_gather(queries, "seq", axis=0, tiled=True),
        lax.all_gather(new_latent, "seq", axis=0, tiled=True),
    )
    absorbed = jnp.einsum(
        "rhn,hnc->rhc", gathered[:, :, :NOPE], w_uk, preferred_element_type=jnp.float32
    ).astype(jnp.bfloat16)
    q_all = jnp.concatenate([absorbed, gathered[:, :, NOPE:]], axis=2)
    total_rows = q_all.shape[0]
    seq_count = total_rows // SPEC
    query_slots = SPEC * head_count
    q_seq = q_all.reshape(seq_count, query_slots, q_all.shape[2])
    new_seq = new_all.reshape(seq_count, SPEC, new_all.shape[1])
    seq_index = lax.axis_index("seq")
    offset = seq_index * cache.shape[1]
    own_first = seq_index == 0
    row_top, running_totals, weighted = local_partial(
        q_seq,
        lax.all_gather(cache, "head", axis=0, tiled=True),
        new_seq,
        lengths,
        offset,
        own_first,
        score_scale,
        head_count,
    )
    value_weight = w_uv.astype(jnp.float32)
    global_top = lax.pmax(row_top, "seq")
    factor = jnp.exp(row_top - global_top)
    scaled_totals = (running_totals * factor).reshape(total_rows, head_count)
    scaled_weighted = (weighted * factor[..., None]).reshape(total_rows, head_count, LATENT)
    row_totals, row_weighted = (
        lax.psum_scatter(scaled_totals, "seq", scatter_dimension=0, tiled=True),
        lax.psum_scatter(scaled_weighted, "seq", scatter_dimension=0, tiled=True),
    )
    latent_output = row_weighted / row_totals[..., None]
    result = project_values(latent_output, value_weight)
    return result.astype(jnp.bfloat16)


def shards(seq_size, head_size, queries, new_latent, cache, lengths, w_uk, w_uv):
    rows, owners = queries.shape[0], cache.shape[0]
    per_device = rows // SPEC
    if (
        per_device == 2
        and rows % SPEC == 0
        and seq_size == COPIES * owners
        and head_size == owners == 4
    ):
        return whole_sequences(
            seq_size, head_size, queries, new_latent, cache, lengths, w_uk, w_uv
        )
    return split_positions(queries, new_latent, cache, lengths, w_uk, w_uv)


def solution(mesh):
    return jax.shard_map(
        functools.partial(shards, mesh.shape["seq"], mesh.shape["head"]),
        mesh=mesh,
        in_specs=(
            P("seq", "head", None),
            P("seq", None),
            P("head", "seq", None),
            P(),
            P("head", None, None),
            P("head", None, None),
        ),
        out_specs=P("seq", "head", None),
        check_vma=False,
    )
```

```python
import functools

import jax
import jax.numpy as jnp
from jax import lax
from jax.experimental import pallas as pl
from jax.experimental.pallas import tpu as pltpu
from jax.sharding import PartitionSpec as P

NOPE = 128
ROPE = 64
LATENT = 512
SPEC = 4
SCORE_SCALE = (NOPE + ROPE) ** (-0.5)
COPIES = 2
VMEM_LIMIT = 16 * 1024 * 1024
LONG = pl.CostEstimate(flops=2 * 10**10, bytes_accessed=0, transcendentals=0)
SHORT = pl.CostEstimate(flops=10**8, bytes_accessed=0, transcendentals=0)

masked_value = -1e30


def leaves_as(k, head_shard):
    return (k + head_shard) % 2


def far_half(plane, pair):
    return 1 * (plane <= 2 * pair)


def first_back(home_chip, head_shard):
    far = 1 * (far_half(home_chip, head_shard // 2) == head_shard % 2)
    return home_chip % 2 ^ far


def first_block(plane, chip, core):
    near = 1 * (chip % 2 == plane % 2)
    return far_half(plane, 1 - core) ^ near ^ chip % 2


def partner(k, core):
    return (0, 3, 1 ^ 3 * core, 2 ^ 3 * core)[k]


def pack_kernel(per_device, q_hbm, new_hbm, out_ref, q_ref, new_ref, sem):
    moves = [
        pltpu.make_async_copy(q_hbm, q_ref, sem.at[0]),
        pltpu.make_async_copy(new_hbm, new_ref, sem.at[1]),
    ]
    for move in moves:
        move.start()
    for move in moves:
        move.wait()
    heads, width = q_ref.shape[1:]
    fresh = new_ref[...].astype(jnp.float32)
    piece = SPEC * heads
    for a in range(per_device):
        rows = q_ref[a * SPEC : (a + 1) * SPEC].reshape(piece, width)
        own = fresh[a * SPEC : (a + 1) * SPEC]
        parts = [own[:, n : n + ROPE] for n in range(0, own.shape[1], ROPE)]
        spare = piece - SPEC * len(parts)
        if spare:
            parts.append(jnp.zeros((spare, ROPE), jnp.float32))
        own = jnp.concatenate(parts, axis=0).astype(rows.dtype)
        out_ref[a * piece : (a + 1) * piece] = jnp.concatenate([rows, own], axis=1)


def pick_kernel(cache_hbm, len_hbm, *refs):
    owners = cache_hbm.shape[0]
    blocks, (limit_ref, len_ref, sem) = refs[:owners], refs[owners:]
    chip, core = lax.axis_index("seq") // COPIES, lax.axis_index("seq") % COPIES
    moves = [pltpu.make_async_copy(len_hbm, len_ref, sem.at[owners])] + [
        pltpu.make_async_copy(cache_hbm.at[chip ^ partner(k, core)], blocks[k], sem.at[k])
        for k in range(owners)
    ]
    for move in moves:
        move.start()
    moves[0].wait()
    length = len_ref[lax.axis_index("head") * owners + chip]
    limit_ref[...] = jnp.full(limit_ref.shape, length, limit_ref.dtype)
    for move in moves[1:]:
        move.wait()


def pair_kernel(first_ref, second_ref, out_ref, sem):
    moves = [
        pltpu.make_async_copy(ref, out_ref.at[n], sem.at[n])
        for n, ref in enumerate((first_ref, second_ref))
    ]
    for move in moves:
        move.start()
    for move in moves:
        move.wait()


def absorb_kernel(per_device, w_ref, packed_ref, *outs):
    heads = w_ref.shape[0]
    piece = SPEC * heads
    nope = packed_ref[:, :NOPE]
    own_head = lax.broadcasted_iota(jnp.int32, nope.shape, 0) % heads
    spread = jnp.concatenate(
        [jnp.where(own_head == h, nope, jnp.zeros_like(nope)) for h in range(heads)], axis=1
    )
    absorbed = jnp.dot(
        spread, w_ref[...].reshape(heads * NOPE, LATENT), preferred_element_type=jnp.float32
    ).astype(jnp.bfloat16)
    for k in range(per_device):
        which = leaves_as(k, lax.axis_index("head"))
        for a in range(per_device):

            @pl.when(which == a)
            def _():
                rows = slice(a * piece, (a + 1) * piece)
                outs[k][:, :LATENT] = absorbed[rows]
                outs[k][:, LATENT:] = packed_ref[rows, NOPE:]


def block_scores(q, refs, starts, limit_ref):
    width = q.shape[1]
    keys = jnp.concatenate([ref[:width, :] for ref in refs], axis=1)
    limit = limit_ref[:1, :]
    lane = lax.broadcasted_iota(jnp.int32, limit.shape, 1)
    visible = jnp.concatenate([lane + start < limit for start in starts], axis=1)
    s = jnp.dot(q, keys, preferred_element_type=jnp.float32) * SCORE_SCALE
    return jnp.where(visible, s, masked_value)


def weigh(s, refs, top):
    w = jnp.exp(s - top)
    values = jnp.concatenate([ref[:LATENT, :] for ref in refs], axis=1)
    out = lax.dot_general(
        w.astype(jnp.bfloat16),
        values,
        (((1,), (1,)), ((), ())),
        preferred_element_type=jnp.float32,
    )
    return jnp.sum(w, axis=1, keepdims=True), out


def begin_kernel(owners, per_device, heads, limit_ref, *refs):
    q_refs, key_refs = refs[:per_device], refs[per_device : per_device + owners]
    q_out, top_ref, total_ref, out_ref = refs[per_device + owners :]
    seq_index = lax.axis_index("seq")
    chip, core = seq_index // COPIES, seq_index % COPIES
    slots = key_refs[0].shape[1]
    width = LATENT + ROPE
    q = jnp.concatenate([ref[:, :width] for ref in q_refs], axis=0)

    fresh = q_refs[0][:, width:].astype(jnp.float32)
    fresh = jnp.concatenate(
        [fresh[n * SPEC : (n + 1) * SPEC] for n in range(width // ROPE)], axis=1
    )
    fresh = jnp.concatenate([fresh, jnp.zeros((16 - SPEC, width), jnp.float32)], axis=0)
    fresh = fresh.astype(jnp.bfloat16)
    f = lax.dot_general(
        q, fresh, (((1,), (1,)), ((), ())), preferred_element_type=jnp.float32
    )
    row = lax.broadcasted_iota(jnp.int32, f.shape, 0) % (SPEC * heads)
    key = lax.broadcasted_iota(jnp.int32, f.shape, 1)
    f = jnp.where(key <= row // heads, f * SCORE_SCALE, masked_value)

    starts = [((chip ^ partner(k, core)) * COPIES + core) * slots for k in range(owners)]
    s = block_scores(q, key_refs, starts, limit_ref)
    top = jnp.maximum(jnp.max(s, axis=1, keepdims=True), jnp.max(f, axis=1, keepdims=True))
    total, out = weigh(s, key_refs, top)
    w = jnp.exp(f - top)
    total += jnp.sum(w, axis=1, keepdims=True)
    out += jnp.dot(
        w.astype(jnp.bfloat16), fresh[:, :LATENT], preferred_element_type=jnp.float32
    )
    q_out[...] = q
    top_ref[...] = jnp.broadcast_to(top, top_ref.shape)
    total_ref[...] = jnp.broadcast_to(total, total_ref.shape)
    out_ref[...] = out


def finish_kernel(
    owners, per_device, limit_ref, q_ref, top_ref, total_ref, part_ref, pair_ref, *refs
):
    key_refs = [pair_ref.at[0], pair_ref.at[1], *refs[: owners - 2]]
    outs = refs[owners - 2 :]
    seq_index = lax.axis_index("seq")
    chip, core = seq_index // COPIES, seq_index % COPIES
    plane = lax.axis_index("head")
    slots = key_refs[0].shape[1]
    starts = [((chip ^ partner(k, 1 - core)) * COPIES + 1 - core) * slots for k in range(owners)]
    s = block_scores(q_ref[...], key_refs, starts, limit_ref)
    first = top_ref[:, :1]
    top = jnp.maximum(first, jnp.max(s, axis=1, keepdims=True))
    total, out = weigh(s, key_refs, top)
    scale = jnp.exp(first - top)
    total += total_ref[:, :1] * scale
    out += part_ref[...] * scale
    out = (out * (1.0 / total)).astype(jnp.bfloat16)
    piece = out.shape[0] // per_device
    sent_first = first_block(plane, chip, core)
    for k in range(per_device):
        for n in range(per_device):

            @pl.when(sent_first ^ k == n)
            def _():
                outs[k][...] = out[n * piece : (n + 1) * piece]


def project_kernel(per_device, w_ref, *refs):
    lat_refs, out_ref = refs[:-1], refs[-1]
    rows, heads, width = out_ref.shape
    first = first_back(lax.axis_index("seq") // COPIES, lax.axis_index("head"))
    parts = [jnp.where(first == a, lat_refs[1][...], lat_refs[0][...]) for a in range(per_device)]
    latent = jnp.concatenate(parts, axis=0)
    out = jnp.zeros((rows * heads, width), jnp.float32)
    own_head = lax.broadcasted_iota(jnp.int32, out.shape, 0) % heads
    step = 2 if heads % 2 == 0 else 1
    for h in range(0, heads, step):
        group = jnp.concatenate([w_ref[h + n] for n in range(step)], axis=1)
        product = jnp.dot(latent, group, preferred_element_type=jnp.float32)
        for n in range(step):
            out = jnp.where(own_head == h + n, product[:, n * width : (n + 1) * width], out)
    out_ref[...] = out.astype(out_ref.dtype).reshape(out_ref.shape)


def whole_sequences(seq_size, head_size, queries, new_latent, cache, lengths, w_uk, w_uv):
    rows, heads, q_width = queries.shape
    owners, slots, width = cache.shape
    per_device = rows // SPEC
    piece = SPEC * heads
    all_rows = per_device * piece
    params = pltpu.CompilerParams(vmem_limit_bytes=VMEM_LIMIT)
    vmem = pl.BlockSpec(memory_space=pltpu.VMEM)
    anywhere = pl.BlockSpec(memory_space=pl.ANY)
    both = ("seq", "head")
    devices = [(i, j) for i in range(seq_size) for j in range(head_size)]

    def flat(seq_index, head_index):
        return seq_index * head_size + head_index

    def in_hbm(x):
        return pltpu.with_memory_space_constraint(x, pltpu.HBM)

    def host(i, j):
        other = (i // COPIES) ^ (2 - ((j ^ (j >> 1)) & 1))
        return flat(((i % COPIES) * 2 + other // 2) * COPIES + other % 2, j)

    def owner(i, j, a):
        plane, chip = i // COPIES, i % COPIES * per_device + a
        return flat(chip * COPIES + 1 - j // 2, plane)

    def in_plane(move):
        return [(g * COPIES + t, move(g, t)) for g in range(owners) for t in range(COPIES)]

    packed = pl.pallas_call(
        functools.partial(pack_kernel, per_device),
        out_shape=jax.ShapeDtypeStruct((all_rows, q_width + ROPE), queries.dtype),
        in_specs=[anywhere] * 2,
        out_specs=vmem,
        scratch_shapes=[
            pltpu.VMEM(queries.shape, queries.dtype),
            pltpu.VMEM(new_latent.shape, new_latent.dtype),
            pltpu.SemaphoreType.DMA((2,)),
        ],
        compiler_params=params,
        cost_estimate=SHORT,
    )(in_hbm(queries), in_hbm(new_latent))
    moved = lax.ppermute(packed, both, [(flat(i, j), host(i, j)) for i, j in devices])
    *picked, limit = pl.pallas_call(
        pick_kernel,
        out_shape=[jax.ShapeDtypeStruct((width, slots), cache.dtype)] * owners
        + [jax.ShapeDtypeStruct((8, slots), jnp.int32)],
        in_specs=[anywhere] * 2,
        out_specs=[vmem] * (owners + 1),
        scratch_shapes=[
            pltpu.SMEM(lengths.shape, lengths.dtype),
            pltpu.SemaphoreType.DMA((owners + 1,)),
        ],
        compiler_params=params,
        cost_estimate=LONG,
    )(in_hbm(jnp.swapaxes(cache, 1, 2)), in_hbm(lengths))
    own_keys = [picked[0]] + [
        lax.ppermute(picked[k], "seq", in_plane(lambda g, t: (g ^ partner(k, t)) * COPIES + t))
        for k in range(1, owners)
    ]
    pair = pl.pallas_call(
        pair_kernel,
        out_shape=jax.ShapeDtypeStruct((2, *picked[0].shape), cache.dtype),
        in_specs=[vmem] * 2,
        out_specs=vmem,
        scratch_shapes=[pltpu.SemaphoreType.DMA((2,))],
        compiler_params=params,
    )(*own_keys[:2])
    other_core = in_plane(lambda g, t: g * COPIES + 1 - t)
    far_keys = [lax.ppermute(keys, "seq", other_core) for keys in [pair] + own_keys[2:]]

    pieces = pl.pallas_call(
        functools.partial(absorb_kernel, per_device),
        out_shape=[jax.ShapeDtypeStruct((piece, width + ROPE), cache.dtype)] * per_device,
        in_specs=[vmem] * 2,
        out_specs=[vmem] * per_device,
        compiler_params=params,
        cost_estimate=LONG,
    )(w_uk, moved)
    arrived = [
        lax.ppermute(
            pieces[k],
            both,
            [(host(i, j), owner(i, j, leaves_as(k, j))) for i, j in devices],
        )
        for k in range(per_device)
    ]

    state = pl.pallas_call(
        functools.partial(begin_kernel, owners, per_device, heads),
        out_shape=[
            jax.ShapeDtypeStruct((all_rows, width), jnp.bfloat16),
            jax.ShapeDtypeStruct((all_rows, 128), jnp.float32),
            jax.ShapeDtypeStruct((all_rows, 128), jnp.float32),
            jax.ShapeDtypeStruct((all_rows, LATENT), jnp.float32),
        ],
        in_specs=[vmem] * (1 + per_device + owners),
        out_specs=[vmem] * 4,
        compiler_params=params,
        cost_estimate=LONG,
    )(limit, *arrived, *own_keys)
    latent = pl.pallas_call(
        functools.partial(finish_kernel, owners, per_device),
        out_shape=[jax.ShapeDtypeStruct((piece, LATENT), jnp.bfloat16)] * per_device,
        in_specs=[vmem] * (1 + len(state) + len(far_keys)),
        out_specs=[vmem] * per_device,
        compiler_params=params,
    )(limit, *state, *far_keys)

    back = [
        lax.ppermute(
            latent[k],
            both,
            [(owner(i, j, first_back(i // COPIES, j) ^ k), flat(i, j)) for i, j in devices],
        )
        for k in range(per_device)
    ]
    return pl.pallas_call(
        functools.partial(project_kernel, per_device),
        out_shape=jax.ShapeDtypeStruct((rows, heads, w_uv.shape[2]), jnp.bfloat16),
        in_specs=[vmem] * (1 + per_device),
        out_specs=vmem,
        compiler_params=params,
    )(w_uv, *back[::-1])


def local_partial(
    query_tile_block,
    key_tile_block,
    incoming_keys,
    len_block,
    offset,
    own_first,
    score_scale,
    head_count,
):
    scores = (
        jnp.einsum(
            "vfa,vja->vfj", query_tile_block, key_tile_block, preferred_element_type=jnp.float32
        )
        * score_scale
    )
    positions = offset + lax.broadcasted_iota(jnp.int32, (1, 1, key_tile_block.shape[1]), 2)
    visible = positions < len_block[:, None, None]
    fresh_scores = (
        jnp.einsum(
            "vfa,vja->vfj", query_tile_block, incoming_keys, preferred_element_type=jnp.float32
        )
        * score_scale
    )
    spec_count = incoming_keys.shape[1]
    row_spec = (
        lax.broadcasted_iota(jnp.int32, (1, query_tile_block.shape[1], spec_count), 1) // head_count
    )
    key_spec = lax.broadcasted_iota(jnp.int32, (1, query_tile_block.shape[1], spec_count), 2)
    causal = (key_spec <= row_spec) & own_first
    row_top = jnp.maximum(
        jnp.max(jnp.where(visible, scores, masked_value), axis=2),
        jnp.max(jnp.where(causal, fresh_scores, masked_value), axis=2),
    )
    weights = jnp.where(visible, jnp.exp(scores - row_top[..., None]), 0.0)
    fresh_weights = jnp.where(causal, jnp.exp(fresh_scores - row_top[..., None]), 0.0)
    running_totals = jnp.sum(weights, axis=2) + jnp.sum(fresh_weights, axis=2)
    weighted = jnp.einsum(
        "mpu,mui->mpi",
        weights.astype(jnp.bfloat16),
        key_tile_block[:, :, :LATENT],
        preferred_element_type=jnp.float32,
    )
    weighted = weighted + jnp.einsum(
        "mpu,mui->mpi",
        fresh_weights.astype(jnp.bfloat16),
        incoming_keys[:, :, :LATENT],
        preferred_element_type=jnp.float32,
    )
    return (row_top, running_totals, weighted)


def project_values(latent_rows, value_weight):
    return jnp.einsum("rhc,hcv->rhv", latent_rows, value_weight, precision=lax.Precision.HIGHEST)


def split_positions(queries, new_latent, cache, lengths, w_uk, w_uv):
    own_rows, head_count, _ = queries.shape
    score_scale = (NOPE + ROPE) ** (-0.5)
    gathered, new_all = (
        lax.all_gather(queries, "seq", axis=0, tiled=True),
        lax.all_gather(new_latent, "seq", axis=0, tiled=True),
    )
    absorbed = jnp.einsum(
        "rhn,hnc->rhc", gathered[:, :, :NOPE], w_uk, preferred_element_type=jnp.float32
    ).astype(jnp.bfloat16)
    q_all = jnp.concatenate([absorbed, gathered[:, :, NOPE:]], axis=2)
    total_rows = q_all.shape[0]
    seq_count = total_rows // SPEC
    query_slots = SPEC * head_count
    q_seq = q_all.reshape(seq_count, query_slots, q_all.shape[2])
    new_seq = new_all.reshape(seq_count, SPEC, new_all.shape[1])
    seq_index = lax.axis_index("seq")
    offset = seq_index * cache.shape[1]
    own_first = seq_index == 0
    row_top, running_totals, weighted = local_partial(
        q_seq,
        lax.all_gather(cache, "head", axis=0, tiled=True),
        new_seq,
        lengths,
        offset,
        own_first,
        score_scale,
        head_count,
    )
    value_weight = w_uv.astype(jnp.float32)
    global_top = lax.pmax(row_top, "seq")
    factor = jnp.exp(row_top - global_top)
    scaled_totals = (running_totals * factor).reshape(total_rows, head_count)
    scaled_weighted = (weighted * factor[..., None]).reshape(total_rows, head_count, LATENT)
    row_totals, row_weighted = (
        lax.psum_scatter(scaled_totals, "seq", scatter_dimension=0, tiled=True),
        lax.psum_scatter(scaled_weighted, "seq", scatter_dimension=0, tiled=True),
    )
    latent_output = row_weighted / row_totals[..., None]
    result = project_values(latent_output, value_weight)
    return result.astype(jnp.bfloat16)


def shards(seq_size, head_size, queries, new_latent, cache, lengths, w_uk, w_uv):
    rows, owners = queries.shape[0], cache.shape[0]
    per_device = rows // SPEC
    if (
        per_device == 2
        and rows % SPEC == 0
        and seq_size == COPIES * owners
        and head_size == owners == 4
    ):
        return whole_sequences(
            seq_size, head_size, queries, new_latent, cache, lengths, w_uk, w_uv
        )
    return split_positions(queries, new_latent, cache, lengths, w_uk, w_uv)


def solution(mesh):
    return jax.shard_map(
        functools.partial(shards, mesh.shape["seq"], mesh.shape["head"]),
        mesh=mesh,
        in_specs=(
            P("seq", "head", None),
            P("seq", None),
            P("head", "seq", None),
            P(),
            P("head", None, None),
            P("head", None, None),
        ),
        out_specs=P("seq", "head", None),
        check_vma=False,
    )
```

```python
import functools

import jax
import jax.numpy as jnp
from jax import lax
from jax.experimental import pallas as pl
from jax.experimental.pallas import tpu as pltpu
from jax.sharding import PartitionSpec as P

NOPE = 128
ROPE = 64
LATENT = 512
SPEC = 4
SCORE_SCALE = (NOPE + ROPE) ** (-0.5)
COPIES = 2
VMEM_LIMIT = 16 * 1024 * 1024
LONG = pl.CostEstimate(flops=2 * 10**10, bytes_accessed=0, transcendentals=0)

masked_value = -1e30


def leaves_as(k, head_shard):
    return (k + head_shard) % 2


def far_half(plane, pair):
    return 1 * (plane <= 2 * pair)


def first_back(home_chip, head_shard):
    far = 1 * (far_half(home_chip, head_shard // 2) == head_shard % 2)
    return home_chip % 2 ^ far


def first_block(plane, chip, core):
    near = 1 * (chip % 2 == plane % 2)
    return far_half(plane, 1 - core) ^ near ^ chip % 2


def partner(k, core):
    return (0, 1 ^ 3 * core, 3, 2 ^ 3 * core)[k]


def pick_kernel(per_device, cache_hbm, q_hbm, new_hbm, len_hbm, *refs):
    owners = cache_hbm.shape[0]
    blocks, (out_ref, limit_ref, q_ref, new_ref, len_ref, sem) = refs[:owners], refs[owners:]
    chip, core = lax.axis_index("seq") // COPIES, lax.axis_index("seq") % COPIES
    moves = [
        pltpu.make_async_copy(q_hbm, q_ref, sem.at[owners]),
        pltpu.make_async_copy(new_hbm, new_ref, sem.at[owners + 1]),
        pltpu.make_async_copy(len_hbm, len_ref, sem.at[owners + 2]),
    ] + [
        pltpu.make_async_copy(cache_hbm.at[chip ^ partner(k, core)], blocks[k], sem.at[k])
        for k in range(owners)
    ]
    for move in moves:
        move.start()
    moves[0].wait()
    moves[1].wait()
    heads, width = q_ref.shape[1:]
    fresh = new_ref[...].astype(jnp.float32)
    piece = SPEC * heads
    for a in range(per_device):
        rows = q_ref[a * SPEC : (a + 1) * SPEC].reshape(piece, width)
        own = fresh[a * SPEC : (a + 1) * SPEC]
        parts = [own[:, n : n + ROPE] for n in range(0, own.shape[1], ROPE)]
        spare = piece - SPEC * len(parts)
        if spare:
            parts.append(jnp.zeros((spare, ROPE), jnp.float32))
        own = jnp.concatenate(parts, axis=0).astype(rows.dtype)
        out_ref[a * piece : (a + 1) * piece] = jnp.concatenate([rows, own], axis=1)
    moves[2].wait()
    length = len_ref[lax.axis_index("head") * owners + chip]
    limit_ref[...] = jnp.full(limit_ref.shape, length, limit_ref.dtype)
    for move in moves[3:]:
        move.wait()


def pair_kernel(first_ref, second_ref, out_ref, sem):
    moves = [
        pltpu.make_async_copy(ref, out_ref.at[n], sem.at[n])
        for n, ref in enumerate((first_ref, second_ref))
    ]
    for move in moves:
        move.start()
    for move in moves:
        move.wait()


def absorb_kernel(per_device, w_ref, packed_ref, *outs):
    heads = w_ref.shape[0]
    piece = SPEC * heads
    nope = packed_ref[:, :NOPE]
    own_head = lax.broadcasted_iota(jnp.int32, nope.shape, 0) % heads
    spread = jnp.concatenate(
        [jnp.where(own_head == h, nope, jnp.zeros_like(nope)) for h in range(heads)], axis=1
    )
    absorbed = jnp.dot(
        spread, w_ref[...].reshape(heads * NOPE, LATENT), preferred_element_type=jnp.float32
    ).astype(jnp.bfloat16)
    for k in range(per_device):
        which = leaves_as(k, lax.axis_index("head"))
        for a in range(per_device):

            @pl.when(which == a)
            def _():
                rows = slice(a * piece, (a + 1) * piece)
                outs[k][:, :LATENT] = absorbed[rows]
                outs[k][:, LATENT:] = packed_ref[rows, NOPE:]


def block_scores(q, refs, starts, limit_ref):
    width = q.shape[1]
    keys = jnp.concatenate([ref[:width, :] for ref in refs], axis=1)
    limit = limit_ref[:1, :]
    lane = lax.broadcasted_iota(jnp.int32, limit.shape, 1)
    visible = jnp.concatenate([lane + start < limit for start in starts], axis=1)
    s = jnp.dot(q, keys, preferred_element_type=jnp.float32) * SCORE_SCALE
    return jnp.where(visible, s, masked_value)


def weigh(s, refs, top):
    w = jnp.exp(s - top)
    values = jnp.concatenate([ref[:LATENT, :] for ref in refs], axis=1)
    out = lax.dot_general(
        w.astype(jnp.bfloat16),
        values,
        (((1,), (1,)), ((), ())),
        preferred_element_type=jnp.float32,
    )
    return jnp.sum(w, axis=1, keepdims=True), out


def begin_kernel(owners, per_device, heads, limit_ref, *refs):
    q_refs, key_refs = refs[:per_device], refs[per_device : per_device + owners]
    q_out, top_ref, total_ref, out_ref = refs[per_device + owners :]
    seq_index = lax.axis_index("seq")
    chip, core = seq_index // COPIES, seq_index % COPIES
    slots = key_refs[0].shape[1]
    width = LATENT + ROPE
    q = jnp.concatenate([ref[:, :width] for ref in q_refs], axis=0)

    fresh = q_refs[0][:, width:].astype(jnp.float32)
    fresh = jnp.concatenate(
        [fresh[n * SPEC : (n + 1) * SPEC] for n in range(width // ROPE)], axis=1
    )
    fresh = jnp.concatenate([fresh, jnp.zeros((16 - SPEC, width), jnp.float32)], axis=0)
    fresh = fresh.astype(jnp.bfloat16)
    f = lax.dot_general(
        q, fresh, (((1,), (1,)), ((), ())), preferred_element_type=jnp.float32
    )
    row = lax.broadcasted_iota(jnp.int32, f.shape, 0) % (SPEC * heads)
    key = lax.broadcasted_iota(jnp.int32, f.shape, 1)
    f = jnp.where(key <= row // heads, f * SCORE_SCALE, masked_value)

    starts = [((chip ^ partner(k, core)) * COPIES + core) * slots for k in range(owners)]
    s = block_scores(q, key_refs, starts, limit_ref)
    top = jnp.maximum(jnp.max(s, axis=1, keepdims=True), jnp.max(f, axis=1, keepdims=True))
    total, out = weigh(s, key_refs, top)
    w = jnp.exp(f - top)
    total += jnp.sum(w, axis=1, keepdims=True)
    out += jnp.dot(
        w.astype(jnp.bfloat16), fresh[:, :LATENT], preferred_element_type=jnp.float32
    )
    q_out[...] = q
    top_ref[...] = jnp.broadcast_to(top, top_ref.shape)
    total_ref[...] = jnp.broadcast_to(total, total_ref.shape)
    out_ref[...] = out


def finish_kernel(
    owners, per_device, limit_ref, q_ref, top_ref, total_ref, part_ref, pair_ref, *refs
):
    key_refs = [pair_ref.at[0], pair_ref.at[1], *refs[: owners - 2]]
    outs = refs[owners - 2 :]
    seq_index = lax.axis_index("seq")
    chip, core = seq_index // COPIES, seq_index % COPIES
    plane = lax.axis_index("head")
    slots = key_refs[0].shape[1]
    starts = [((chip ^ partner(k, 1 - core)) * COPIES + 1 - core) * slots for k in range(owners)]
    s = block_scores(q_ref[...], key_refs, starts, limit_ref)
    first = top_ref[:, :1]
    top = jnp.maximum(first, jnp.max(s, axis=1, keepdims=True))
    total, out = weigh(s, key_refs, top)
    scale = jnp.exp(first - top)
    total += total_ref[:, :1] * scale
    out += part_ref[...] * scale
    out = (out * (1.0 / total)).astype(jnp.bfloat16)
    piece = out.shape[0] // per_device
    sent_first = first_block(plane, chip, core)
    for k in range(per_device):
        for n in range(per_device):

            @pl.when(sent_first ^ k == n)
            def _():
                outs[k][...] = out[n * piece : (n + 1) * piece]


def project_kernel(per_device, w_ref, *refs):
    lat_refs, out_ref = refs[:-1], refs[-1]
    rows, heads, width = out_ref.shape
    first = first_back(lax.axis_index("seq") // COPIES, lax.axis_index("head"))
    parts = [jnp.where(first == a, lat_refs[1][...], lat_refs[0][...]) for a in range(per_device)]
    latent = jnp.concatenate(parts, axis=0)
    out = jnp.zeros((rows * heads, width), jnp.float32)
    own_head = lax.broadcasted_iota(jnp.int32, out.shape, 0) % heads
    step = 2 if heads % 2 == 0 else 1
    for h in range(0, heads, step):
        group = jnp.concatenate([w_ref[h + n] for n in range(step)], axis=1)
        product = jnp.dot(latent, group, preferred_element_type=jnp.float32)
        for n in range(step):
            out = jnp.where(own_head == h + n, product[:, n * width : (n + 1) * width], out)
    out_ref[...] = out.astype(out_ref.dtype).reshape(out_ref.shape)


def whole_sequences(seq_size, head_size, queries, new_latent, cache, lengths, w_uk, w_uv):
    rows, heads, q_width = queries.shape
    owners, slots, width = cache.shape
    per_device = rows // SPEC
    piece = SPEC * heads
    all_rows = per_device * piece
    params = pltpu.CompilerParams(vmem_limit_bytes=VMEM_LIMIT)
    vmem = pl.BlockSpec(memory_space=pltpu.VMEM)
    anywhere = pl.BlockSpec(memory_space=pl.ANY)
    both = ("seq", "head")
    devices = [(i, j) for i in range(seq_size) for j in range(head_size)]

    def flat(seq_index, head_index):
        return seq_index * head_size + head_index

    def in_hbm(x):
        return pltpu.with_memory_space_constraint(x, pltpu.HBM)

    def host(i, j):
        other = (i // COPIES) ^ (2 - ((j ^ (j >> 1)) & 1))
        return flat(((i % COPIES) * 2 + other // 2) * COPIES + other % 2, j)

    def owner(i, j, a):
        plane, chip = i // COPIES, i % COPIES * per_device + a
        return flat(chip * COPIES + 1 - j // 2, plane)

    def in_plane(move):
        return [(g * COPIES + t, move(g, t)) for g in range(owners) for t in range(COPIES)]

    *picked, packed, limit = pl.pallas_call(
        functools.partial(pick_kernel, per_device),
        out_shape=[jax.ShapeDtypeStruct((width, slots), cache.dtype)] * owners
        + [
            jax.ShapeDtypeStruct((all_rows, q_width + ROPE), queries.dtype),
            jax.ShapeDtypeStruct((8, slots), jnp.int32),
        ],
        in_specs=[anywhere] * 4,
        out_specs=[vmem] * (owners + 2),
        scratch_shapes=[
            pltpu.VMEM(queries.shape, queries.dtype),
            pltpu.VMEM(new_latent.shape, new_latent.dtype),
            pltpu.SMEM(lengths.shape, lengths.dtype),
            pltpu.SemaphoreType.DMA((owners + 3,)),
        ],
        compiler_params=params,
        cost_estimate=LONG,
    )(*[in_hbm(x) for x in (jnp.swapaxes(cache, 1, 2), queries, new_latent, lengths)])
    moved = lax.ppermute(packed, both, [(flat(i, j), host(i, j)) for i, j in devices])
    own_keys = [picked[0]] + [
        lax.ppermute(picked[k], "seq", in_plane(lambda g, t: (g ^ partner(k, t)) * COPIES + t))
        for k in range(1, owners)
    ]
    pair = pl.pallas_call(
        pair_kernel,
        out_shape=jax.ShapeDtypeStruct((2, *picked[0].shape), cache.dtype),
        in_specs=[vmem] * 2,
        out_specs=vmem,
        scratch_shapes=[pltpu.SemaphoreType.DMA((2,))],
        compiler_params=params,
    )(*own_keys[:2])
    other_core = in_plane(lambda g, t: g * COPIES + 1 - t)
    far_keys = [lax.ppermute(keys, "seq", other_core) for keys in [pair] + own_keys[2:]]

    pieces = pl.pallas_call(
        functools.partial(absorb_kernel, per_device),
        out_shape=[jax.ShapeDtypeStruct((piece, width + ROPE), cache.dtype)] * per_device,
        in_specs=[vmem] * 2,
        out_specs=[vmem] * per_device,
        compiler_params=params,
        cost_estimate=LONG,
    )(w_uk, moved)
    arrived = [
        lax.ppermute(
            pieces[k],
            both,
            [(host(i, j), owner(i, j, leaves_as(k, j))) for i, j in devices],
        )
        for k in range(per_device)
    ]

    state = pl.pallas_call(
        functools.partial(begin_kernel, owners, per_device, heads),
        out_shape=[
            jax.ShapeDtypeStruct((all_rows, width), jnp.bfloat16),
            jax.ShapeDtypeStruct((all_rows, 128), jnp.float32),
            jax.ShapeDtypeStruct((all_rows, 128), jnp.float32),
            jax.ShapeDtypeStruct((all_rows, LATENT), jnp.float32),
        ],
        in_specs=[vmem] * (1 + per_device + owners),
        out_specs=[vmem] * 4,
        compiler_params=params,
        cost_estimate=LONG,
    )(limit, *arrived, *own_keys)
    latent = pl.pallas_call(
        functools.partial(finish_kernel, owners, per_device),
        out_shape=[jax.ShapeDtypeStruct((piece, LATENT), jnp.bfloat16)] * per_device,
        in_specs=[vmem] * (1 + len(state) + len(far_keys)),
        out_specs=[vmem] * per_device,
        compiler_params=params,
    )(limit, *state, *far_keys)

    back = [
        lax.ppermute(
            latent[k],
            both,
            [(owner(i, j, first_back(i // COPIES, j) ^ k), flat(i, j)) for i, j in devices],
        )
        for k in range(per_device)
    ]
    return pl.pallas_call(
        functools.partial(project_kernel, per_device),
        out_shape=jax.ShapeDtypeStruct((rows, heads, w_uv.shape[2]), jnp.bfloat16),
        in_specs=[vmem] * (1 + per_device),
        out_specs=vmem,
        compiler_params=params,
    )(w_uv, *back[::-1])


def local_partial(
    query_tile_block,
    key_tile_block,
    incoming_keys,
    len_block,
    offset,
    own_first,
    score_scale,
    head_count,
):
    scores = (
        jnp.einsum(
            "vfa,vja->vfj", query_tile_block, key_tile_block, preferred_element_type=jnp.float32
        )
        * score_scale
    )
    positions = offset + lax.broadcasted_iota(jnp.int32, (1, 1, key_tile_block.shape[1]), 2)
    visible = positions < len_block[:, None, None]
    fresh_scores = (
        jnp.einsum(
            "vfa,vja->vfj", query_tile_block, incoming_keys, preferred_element_type=jnp.float32
        )
        * score_scale
    )
    spec_count = incoming_keys.shape[1]
    row_spec = (
        lax.broadcasted_iota(jnp.int32, (1, query_tile_block.shape[1], spec_count), 1) // head_count
    )
    key_spec = lax.broadcasted_iota(jnp.int32, (1, query_tile_block.shape[1], spec_count), 2)
    causal = (key_spec <= row_spec) & own_first
    row_top = jnp.maximum(
        jnp.max(jnp.where(visible, scores, masked_value), axis=2),
        jnp.max(jnp.where(causal, fresh_scores, masked_value), axis=2),
    )
    weights = jnp.where(visible, jnp.exp(scores - row_top[..., None]), 0.0)
    fresh_weights = jnp.where(causal, jnp.exp(fresh_scores - row_top[..., None]), 0.0)
    running_totals = jnp.sum(weights, axis=2) + jnp.sum(fresh_weights, axis=2)
    weighted = jnp.einsum(
        "mpu,mui->mpi",
        weights.astype(jnp.bfloat16),
        key_tile_block[:, :, :LATENT],
        preferred_element_type=jnp.float32,
    )
    weighted = weighted + jnp.einsum(
        "mpu,mui->mpi",
        fresh_weights.astype(jnp.bfloat16),
        incoming_keys[:, :, :LATENT],
        preferred_element_type=jnp.float32,
    )
    return (row_top, running_totals, weighted)


def project_values(latent_rows, value_weight):
    return jnp.einsum("rhc,hcv->rhv", latent_rows, value_weight, precision=lax.Precision.HIGHEST)


def split_positions(queries, new_latent, cache, lengths, w_uk, w_uv):
    own_rows, head_count, _ = queries.shape
    score_scale = (NOPE + ROPE) ** (-0.5)
    gathered, new_all = (
        lax.all_gather(queries, "seq", axis=0, tiled=True),
        lax.all_gather(new_latent, "seq", axis=0, tiled=True),
    )
    absorbed = jnp.einsum(
        "rhn,hnc->rhc", gathered[:, :, :NOPE], w_uk, preferred_element_type=jnp.float32
    ).astype(jnp.bfloat16)
    q_all = jnp.concatenate([absorbed, gathered[:, :, NOPE:]], axis=2)
    total_rows = q_all.shape[0]
    seq_count = total_rows // SPEC
    query_slots = SPEC * head_count
    q_seq = q_all.reshape(seq_count, query_slots, q_all.shape[2])
    new_seq = new_all.reshape(seq_count, SPEC, new_all.shape[1])
    seq_index = lax.axis_index("seq")
    offset = seq_index * cache.shape[1]
    own_first = seq_index == 0
    row_top, running_totals, weighted = local_partial(
        q_seq,
        lax.all_gather(cache, "head", axis=0, tiled=True),
        new_seq,
        lengths,
        offset,
        own_first,
        score_scale,
        head_count,
    )
    value_weight = w_uv.astype(jnp.float32)
    global_top = lax.pmax(row_top, "seq")
    factor = jnp.exp(row_top - global_top)
    scaled_totals = (running_totals * factor).reshape(total_rows, head_count)
    scaled_weighted = (weighted * factor[..., None]).reshape(total_rows, head_count, LATENT)
    row_totals, row_weighted = (
        lax.psum_scatter(scaled_totals, "seq", scatter_dimension=0, tiled=True),
        lax.psum_scatter(scaled_weighted, "seq", scatter_dimension=0, tiled=True),
    )
    latent_output = row_weighted / row_totals[..., None]
    result = project_values(latent_output, value_weight)
    return result.astype(jnp.bfloat16)


def shards(seq_size, head_size, queries, new_latent, cache, lengths, w_uk, w_uv):
    rows, owners = queries.shape[0], cache.shape[0]
    per_device = rows // SPEC
    if (
        per_device == 2
        and rows % SPEC == 0
        and seq_size == COPIES * owners
        and head_size == owners == 4
    ):
        return whole_sequences(
            seq_size, head_size, queries, new_latent, cache, lengths, w_uk, w_uv
        )
    return split_positions(queries, new_latent, cache, lengths, w_uk, w_uv)


def solution(mesh):
    return jax.shard_map(
        functools.partial(shards, mesh.shape["seq"], mesh.shape["head"]),
        mesh=mesh,
        in_specs=(
            P("seq", "head", None),
            P("seq", None),
            P("head", "seq", None),
            P(),
            P("head", None, None),
            P("head", None, None),
        ),
        out_specs=P("seq", "head", None),
        check_vma=False,
    )
```

```python
import functools

import jax
import jax.numpy as jnp
from jax import lax
from jax.experimental import pallas as pl
from jax.experimental.pallas import tpu as pltpu
from jax.sharding import PartitionSpec as P

NOPE = 128
ROPE = 64
LATENT = 512
SPEC = 4
SCORE_SCALE = (NOPE + ROPE) ** (-0.5)
COPIES = 2
VMEM_LIMIT = 16 * 1024 * 1024
LONG = pl.CostEstimate(flops=2 * 10**10, bytes_accessed=0, transcendentals=0)

masked_value = -1e30


def leaves_as(k, head_shard):
    return (k + head_shard) % 2


def far_half(plane, pair):
    return 1 * (plane <= 2 * pair)


def near_half(home_chip, head_shard):
    return home_chip // 2 == head_shard // 2


def first_back(home_chip, head_shard):
    far = 1 * (far_half(home_chip, head_shard // 2) == head_shard % 2)
    return home_chip % 2 ^ far


def first_block(plane, chip, core):
    near = 1 * (chip % 2 == plane % 2)
    return far_half(plane, 1 - core) ^ near ^ chip % 2


def partner(k, core):
    return (0, 3, 1 ^ 3 * core, 2 ^ 3 * core)[k]


def pick_kernel(per_device, cache_hbm, q_hbm, new_hbm, len_hbm, *refs):
    owners = cache_hbm.shape[0]
    blocks, (out_ref, limit_ref, q_ref, new_ref, len_ref, sem) = refs[:owners], refs[owners:]
    chip, core = lax.axis_index("seq") // COPIES, lax.axis_index("seq") % COPIES
    moves = [
        pltpu.make_async_copy(q_hbm, q_ref, sem.at[owners]),
        pltpu.make_async_copy(new_hbm, new_ref, sem.at[owners + 1]),
        pltpu.make_async_copy(len_hbm, len_ref, sem.at[owners + 2]),
    ] + [
        pltpu.make_async_copy(cache_hbm.at[chip ^ partner(k, core)], blocks[k], sem.at[k])
        for k in range(owners)
    ]
    for move in moves:
        move.start()
    moves[0].wait()
    moves[1].wait()
    heads, width = q_ref.shape[1:]
    fresh = new_ref[...].astype(jnp.float32)
    piece = SPEC * heads
    for a in range(per_device):
        rows = q_ref[a * SPEC : (a + 1) * SPEC].reshape(piece, width)
        own = fresh[a * SPEC : (a + 1) * SPEC]
        parts = [own[:, n : n + ROPE] for n in range(0, own.shape[1], ROPE)]
        spare = piece - SPEC * len(parts)
        if spare:
            parts.append(jnp.zeros((spare, ROPE), jnp.float32))
        own = jnp.concatenate(parts, axis=0).astype(rows.dtype)
        out_ref[a * piece : (a + 1) * piece] = jnp.concatenate([rows, own], axis=1)
    moves[2].wait()
    length = len_ref[lax.axis_index("head") * owners + chip]
    limit_ref[...] = jnp.full(limit_ref.shape, length, limit_ref.dtype)
    for move in moves[3:]:
        move.wait()


def pair_kernel(first_ref, second_ref, out_ref, sem):
    moves = [
        pltpu.make_async_copy(ref, out_ref.at[n], sem.at[n])
        for n, ref in enumerate((first_ref, second_ref))
    ]
    for move in moves:
        move.start()
    for move in moves:
        move.wait()


def absorb_kernel(per_device, w_ref, packed_ref, *outs):
    heads = w_ref.shape[0]
    piece = SPEC * heads
    nope = packed_ref[:, :NOPE]
    own_head = lax.broadcasted_iota(jnp.int32, nope.shape, 0) % heads
    spread = jnp.concatenate(
        [jnp.where(own_head == h, nope, jnp.zeros_like(nope)) for h in range(heads)], axis=1
    )
    absorbed = jnp.dot(
        spread, w_ref[...].reshape(heads * NOPE, LATENT), preferred_element_type=jnp.float32
    ).astype(jnp.bfloat16)
    for k in range(per_device):
        which = leaves_as(k, lax.axis_index("head"))
        for a in range(per_device):

            @pl.when(which == a)
            def _():
                rows = slice(a * piece, (a + 1) * piece)
                outs[k][:, :LATENT] = absorbed[rows]
                outs[k][:, LATENT:] = packed_ref[rows, NOPE:]


def block_scores(q, refs, starts, limit_ref):
    width = q.shape[1]
    keys = jnp.concatenate([ref[:width, :] for ref in refs], axis=1)
    limit = limit_ref[:1, :]
    lane = lax.broadcasted_iota(jnp.int32, limit.shape, 1)
    visible = jnp.concatenate([lane + start < limit for start in starts], axis=1)
    s = jnp.dot(q, keys, preferred_element_type=jnp.float32) * SCORE_SCALE
    return jnp.where(visible, s, masked_value)


def weigh(s, refs, top):
    w = jnp.exp(s - top)
    values = jnp.concatenate([ref[:LATENT, :] for ref in refs], axis=1)
    out = lax.dot_general(
        w.astype(jnp.bfloat16),
        values,
        (((1,), (1,)), ((), ())),
        preferred_element_type=jnp.float32,
    )
    return jnp.sum(w, axis=1, keepdims=True), out


def begin_kernel(owners, per_device, heads, limit_ref, *refs):
    q_refs, key_refs = refs[:per_device], refs[per_device : per_device + owners]
    q_out, top_ref, total_ref, out_ref = refs[per_device + owners :]
    seq_index = lax.axis_index("seq")
    chip, core = seq_index // COPIES, seq_index % COPIES
    slots = key_refs[0].shape[1]
    width = LATENT + ROPE
    q = jnp.concatenate([ref[:, :width] for ref in q_refs], axis=0)

    fresh = q_refs[0][:, width:].astype(jnp.float32)
    fresh = jnp.concatenate(
        [fresh[n * SPEC : (n + 1) * SPEC] for n in range(width // ROPE)], axis=1
    )
    fresh = jnp.concatenate([fresh, jnp.zeros((16 - SPEC, width), jnp.float32)], axis=0)
    fresh = fresh.astype(jnp.bfloat16)
    f = lax.dot_general(
        q, fresh, (((1,), (1,)), ((), ())), preferred_element_type=jnp.float32
    )
    row = lax.broadcasted_iota(jnp.int32, f.shape, 0) % (SPEC * heads)
    key = lax.broadcasted_iota(jnp.int32, f.shape, 1)
    f = jnp.where(key <= row // heads, f * SCORE_SCALE, masked_value)

    starts = [((chip ^ partner(k, core)) * COPIES + core) * slots for k in range(owners)]
    s = block_scores(q, key_refs, starts, limit_ref)
    top = jnp.maximum(jnp.max(s, axis=1, keepdims=True), jnp.max(f, axis=1, keepdims=True))
    total, out = weigh(s, key_refs, top)
    w = jnp.exp(f - top)
    total += jnp.sum(w, axis=1, keepdims=True)
    out += jnp.dot(
        w.astype(jnp.bfloat16), fresh[:, :LATENT], preferred_element_type=jnp.float32
    )
    q_out[...] = q
    top_ref[...] = jnp.broadcast_to(top, top_ref.shape)
    total_ref[...] = jnp.broadcast_to(total, total_ref.shape)
    out_ref[...] = out


def finish_kernel(
    owners, per_device, limit_ref, q_ref, top_ref, total_ref, part_ref, pair_ref, *refs
):
    key_refs = [pair_ref.at[0], pair_ref.at[1], *refs[: owners - 2]]
    outs = refs[owners - 2 :]
    seq_index = lax.axis_index("seq")
    chip, core = seq_index // COPIES, seq_index % COPIES
    plane = lax.axis_index("head")
    slots = key_refs[0].shape[1]
    starts = [((chip ^ partner(k, 1 - core)) * COPIES + 1 - core) * slots for k in range(owners)]
    s = block_scores(q_ref[...], key_refs, starts, limit_ref)
    first = top_ref[:, :1]
    top = jnp.maximum(first, jnp.max(s, axis=1, keepdims=True))
    total, out = weigh(s, key_refs, top)
    scale = jnp.exp(first - top)
    total += total_ref[:, :1] * scale
    out += part_ref[...] * scale
    out = (out * (1.0 / total)).astype(jnp.bfloat16)
    piece = out.shape[0] // per_device
    sent_first = first_block(plane, chip, core)
    for k in range(per_device):
        for n in range(per_device):

            @pl.when(sent_first ^ k == n)
            def _():
                outs[k][...] = out[n * piece : (n + 1) * piece]


def project_kernel(per_device, w_ref, *refs):
    lat_refs, out_ref = refs[:-1], refs[-1]
    rows, heads, width = out_ref.shape
    chip, head_shard = lax.axis_index("seq") // COPIES, lax.axis_index("head")
    first, near = first_back(chip, head_shard), near_half(chip, head_shard)
    came = [
        jnp.where(near, lat_refs[1][...], lat_refs[3][...]),
        jnp.where(near, lat_refs[2][...], lat_refs[0][...]),
    ]
    parts = [jnp.where(first == a, came[0], came[1]) for a in range(per_device)]
    latent = jnp.concatenate(parts, axis=0)
    out = jnp.zeros((rows * heads, width), jnp.float32)
    own_head = lax.broadcasted_iota(jnp.int32, out.shape, 0) % heads
    step = 2 if heads % 2 == 0 else 1
    for h in range(0, heads, step):
        group = jnp.concatenate([w_ref[h + n] for n in range(step)], axis=1)
        product = jnp.dot(latent, group, preferred_element_type=jnp.float32)
        for n in range(step):
            out = jnp.where(own_head == h + n, product[:, n * width : (n + 1) * width], out)
    out_ref[...] = out.astype(out_ref.dtype).reshape(out_ref.shape)


def whole_sequences(seq_size, head_size, queries, new_latent, cache, lengths, w_uk, w_uv):
    rows, heads, q_width = queries.shape
    owners, slots, width = cache.shape
    per_device = rows // SPEC
    piece = SPEC * heads
    all_rows = per_device * piece
    params = pltpu.CompilerParams(vmem_limit_bytes=VMEM_LIMIT)
    vmem = pl.BlockSpec(memory_space=pltpu.VMEM)
    anywhere = pl.BlockSpec(memory_space=pl.ANY)
    both = ("seq", "head")
    devices = [(i, j) for i in range(seq_size) for j in range(head_size)]

    def flat(seq_index, head_index):
        return seq_index * head_size + head_index

    def in_hbm(x):
        return pltpu.with_memory_space_constraint(x, pltpu.HBM)

    def host(i, j):
        other = (i // COPIES) ^ (2 - ((j ^ (j >> 1)) & 1))
        return flat(((i % COPIES) * 2 + other // 2) * COPIES + other % 2, j)

    def owner(i, j, a):
        plane, chip = i // COPIES, i % COPIES * per_device + a
        return flat(chip * COPIES + 1 - j // 2, plane)

    def in_plane(move):
        return [(g * COPIES + t, move(g, t)) for g in range(owners) for t in range(COPIES)]

    *picked, packed, limit = pl.pallas_call(
        functools.partial(pick_kernel, per_device),
        out_shape=[jax.ShapeDtypeStruct((width, slots), cache.dtype)] * owners
        + [
            jax.ShapeDtypeStruct((all_rows, q_width + ROPE), queries.dtype),
            jax.ShapeDtypeStruct((8, slots), jnp.int32),
        ],
        in_specs=[anywhere] * 4,
        out_specs=[vmem] * (owners + 2),
        scratch_shapes=[
            pltpu.VMEM(queries.shape, queries.dtype),
            pltpu.VMEM(new_latent.shape, new_latent.dtype),
            pltpu.SMEM(lengths.shape, lengths.dtype),
            pltpu.SemaphoreType.DMA((owners + 3,)),
        ],
        compiler_params=params,
        cost_estimate=LONG,
    )(*[in_hbm(x) for x in (jnp.swapaxes(cache, 1, 2), queries, new_latent, lengths)])
    moved = lax.ppermute(packed, both, [(flat(i, j), host(i, j)) for i, j in devices])
    own_keys = [picked[0]] + [
        lax.ppermute(picked[k], "seq", in_plane(lambda g, t: (g ^ partner(k, t)) * COPIES + t))
        for k in range(1, owners)
    ]
    pair = pl.pallas_call(
        pair_kernel,
        out_shape=jax.ShapeDtypeStruct((2, *picked[0].shape), cache.dtype),
        in_specs=[vmem] * 2,
        out_specs=vmem,
        scratch_shapes=[pltpu.SemaphoreType.DMA((2,))],
        compiler_params=params,
    )(*own_keys[:2])
    other_core = in_plane(lambda g, t: g * COPIES + 1 - t)
    far_keys = [lax.ppermute(keys, "seq", other_core) for keys in [pair] + own_keys[2:]]

    pieces = pl.pallas_call(
        functools.partial(absorb_kernel, per_device),
        out_shape=[jax.ShapeDtypeStruct((piece, width + ROPE), cache.dtype)] * per_device,
        in_specs=[vmem] * 2,
        out_specs=[vmem] * per_device,
        compiler_params=params,
        cost_estimate=LONG,
    )(w_uk, moved)
    arrived = [
        lax.ppermute(
            pieces[k],
            both,
            [(host(i, j), owner(i, j, leaves_as(k, j))) for i, j in devices],
        )
        for k in range(per_device)
    ]

    state = pl.pallas_call(
        functools.partial(begin_kernel, owners, per_device, heads),
        out_shape=[
            jax.ShapeDtypeStruct((all_rows, width), jnp.bfloat16),
            jax.ShapeDtypeStruct((all_rows, 128), jnp.float32),
            jax.ShapeDtypeStruct((all_rows, 128), jnp.float32),
            jax.ShapeDtypeStruct((all_rows, LATENT), jnp.float32),
        ],
        in_specs=[vmem] * (1 + per_device + owners),
        out_specs=[vmem] * 4,
        compiler_params=params,
        cost_estimate=LONG,
    )(limit, *arrived, *own_keys)
    latent = pl.pallas_call(
        functools.partial(finish_kernel, owners, per_device),
        out_shape=[jax.ShapeDtypeStruct((piece, LATENT), jnp.bfloat16)] * per_device,
        in_specs=[vmem] * (1 + len(state) + len(far_keys)),
        out_specs=[vmem] * per_device,
        compiler_params=params,
    )(limit, *state, *far_keys)

    back = [
        lax.ppermute(
            latent[k],
            both,
            [
                (owner(i, j, first_back(i // COPIES, j) ^ k), flat(i, j))
                for i, j in devices
                if near_half(i // COPIES, j) == near
            ],
        )
        for near, k in ((False, 1), (True, 0), (True, 1), (False, 0))
    ]
    return pl.pallas_call(
        functools.partial(project_kernel, per_device),
        out_shape=jax.ShapeDtypeStruct((rows, heads, w_uv.shape[2]), jnp.bfloat16),
        in_specs=[vmem] * (1 + len(back)),
        out_specs=vmem,
        compiler_params=params,
    )(w_uv, *back)


def local_partial(
    query_tile_block,
    key_tile_block,
    incoming_keys,
    len_block,
    offset,
    own_first,
    score_scale,
    head_count,
):
    scores = (
        jnp.einsum(
            "vfa,vja->vfj", query_tile_block, key_tile_block, preferred_element_type=jnp.float32
        )
        * score_scale
    )
    positions = offset + lax.broadcasted_iota(jnp.int32, (1, 1, key_tile_block.shape[1]), 2)
    visible = positions < len_block[:, None, None]
    fresh_scores = (
        jnp.einsum(
            "vfa,vja->vfj", query_tile_block, incoming_keys, preferred_element_type=jnp.float32
        )
        * score_scale
    )
    spec_count = incoming_keys.shape[1]
    row_spec = (
        lax.broadcasted_iota(jnp.int32, (1, query_tile_block.shape[1], spec_count), 1) // head_count
    )
    key_spec = lax.broadcasted_iota(jnp.int32, (1, query_tile_block.shape[1], spec_count), 2)
    causal = (key_spec <= row_spec) & own_first
    row_top = jnp.maximum(
        jnp.max(jnp.where(visible, scores, masked_value), axis=2),
        jnp.max(jnp.where(causal, fresh_scores, masked_value), axis=2),
    )
    weights = jnp.where(visible, jnp.exp(scores - row_top[..., None]), 0.0)
    fresh_weights = jnp.where(causal, jnp.exp(fresh_scores - row_top[..., None]), 0.0)
    running_totals = jnp.sum(weights, axis=2) + jnp.sum(fresh_weights, axis=2)
    weighted = jnp.einsum(
        "mpu,mui->mpi",
        weights.astype(jnp.bfloat16),
        key_tile_block[:, :, :LATENT],
        preferred_element_type=jnp.float32,
    )
    weighted = weighted + jnp.einsum(
        "mpu,mui->mpi",
        fresh_weights.astype(jnp.bfloat16),
        incoming_keys[:, :, :LATENT],
        preferred_element_type=jnp.float32,
    )
    return (row_top, running_totals, weighted)


def project_values(latent_rows, value_weight):
    return jnp.einsum("rhc,hcv->rhv", latent_rows, value_weight, precision=lax.Precision.HIGHEST)


def split_positions(queries, new_latent, cache, lengths, w_uk, w_uv):
    own_rows, head_count, _ = queries.shape
    score_scale = (NOPE + ROPE) ** (-0.5)
    gathered, new_all = (
        lax.all_gather(queries, "seq", axis=0, tiled=True),
        lax.all_gather(new_latent, "seq", axis=0, tiled=True),
    )
    absorbed = jnp.einsum(
        "rhn,hnc->rhc", gathered[:, :, :NOPE], w_uk, preferred_element_type=jnp.float32
    ).astype(jnp.bfloat16)
    q_all = jnp.concatenate([absorbed, gathered[:, :, NOPE:]], axis=2)
    total_rows = q_all.shape[0]
    seq_count = total_rows // SPEC
    query_slots = SPEC * head_count
    q_seq = q_all.reshape(seq_count, query_slots, q_all.shape[2])
    new_seq = new_all.reshape(seq_count, SPEC, new_all.shape[1])
    seq_index = lax.axis_index("seq")
    offset = seq_index * cache.shape[1]
    own_first = seq_index == 0
    row_top, running_totals, weighted = local_partial(
        q_seq,
        lax.all_gather(cache, "head", axis=0, tiled=True),
        new_seq,
        lengths,
        offset,
        own_first,
        score_scale,
        head_count,
    )
    value_weight = w_uv.astype(jnp.float32)
    global_top = lax.pmax(row_top, "seq")
    factor = jnp.exp(row_top - global_top)
    scaled_totals = (running_totals * factor).reshape(total_rows, head_count)
    scaled_weighted = (weighted * factor[..., None]).reshape(total_rows, head_count, LATENT)
    row_totals, row_weighted = (
        lax.psum_scatter(scaled_totals, "seq", scatter_dimension=0, tiled=True),
        lax.psum_scatter(scaled_weighted, "seq", scatter_dimension=0, tiled=True),
    )
    latent_output = row_weighted / row_totals[..., None]
    result = project_values(latent_output, value_weight)
    return result.astype(jnp.bfloat16)


def shards(seq_size, head_size, queries, new_latent, cache, lengths, w_uk, w_uv):
    rows, owners = queries.shape[0], cache.shape[0]
    per_device = rows // SPEC
    if (
        per_device == 2
        and rows % SPEC == 0
        and seq_size == COPIES * owners
        and head_size == owners == 4
    ):
        return whole_sequences(
            seq_size, head_size, queries, new_latent, cache, lengths, w_uk, w_uv
        )
    return split_positions(queries, new_latent, cache, lengths, w_uk, w_uv)


def solution(mesh):
    return jax.shard_map(
        functools.partial(shards, mesh.shape["seq"], mesh.shape["head"]),
        mesh=mesh,
        in_specs=(
            P("seq", "head", None),
            P("seq", None),
            P("head", "seq", None),
            P(),
            P("head", None, None),
            P("head", None, None),
        ),
        out_specs=P("seq", "head", None),
        check_vma=False,
    )
```

```python
import functools

import jax
import jax.numpy as jnp
from jax import lax
from jax.experimental import pallas as pl
from jax.experimental.pallas import tpu as pltpu
from jax.sharding import PartitionSpec as P

NOPE = 128
ROPE = 64
LATENT = 512
SPEC = 4
SCORE_SCALE = (NOPE + ROPE) ** (-0.5)
COPIES = 2
VMEM_LIMIT = 16 * 1024 * 1024
LONG = pl.CostEstimate(flops=2 * 10**10, bytes_accessed=0, transcendentals=0)

masked_value = -1e30


def leaves_as(k, head_shard):
    return (k + head_shard) % 2


def far_half(plane, pair):
    return 1 * (plane <= 2 * pair)


def first_back(home_chip, head_shard):
    far = 1 * (far_half(home_chip, head_shard // 2) == head_shard % 2)
    return home_chip % 2 ^ far


def first_block(plane, chip, core):
    near = 1 * (chip % 2 == plane % 2)
    return far_half(plane, 1 - core) ^ near ^ chip % 2


def partner(k, core):
    return (0, 3, 1 ^ 3 * core, 2 ^ 3 * core)[k]


def pick_kernel(per_device, cache_hbm, q_hbm, new_hbm, len_hbm, *refs):
    owners = cache_hbm.shape[0]
    blocks, (out_ref, limit_ref, q_ref, new_ref, len_ref, sem) = refs[:owners], refs[owners:]
    chip, core = lax.axis_index("seq") // COPIES, lax.axis_index("seq") % COPIES
    moves = [
        pltpu.make_async_copy(q_hbm, q_ref, sem.at[owners]),
        pltpu.make_async_copy(new_hbm, new_ref, sem.at[owners + 1]),
        pltpu.make_async_copy(len_hbm, len_ref, sem.at[owners + 2]),
    ] + [
        pltpu.make_async_copy(cache_hbm.at[chip ^ partner(k, core)], blocks[k], sem.at[k])
        for k in range(owners)
    ]
    for move in moves:
        move.start()
    moves[0].wait()
    moves[1].wait()
    heads, width = q_ref.shape[1:]
    fresh = new_ref[...].astype(jnp.float32)
    piece = SPEC * heads
    for a in range(per_device):
        rows = q_ref[a * SPEC : (a + 1) * SPEC].reshape(piece, width)
        own = fresh[a * SPEC : (a + 1) * SPEC]
        parts = [own[:, n : n + ROPE] for n in range(0, own.shape[1], ROPE)]
        spare = piece - SPEC * len(parts)
        if spare:
            parts.append(jnp.zeros((spare, ROPE), jnp.float32))
        own = jnp.concatenate(parts, axis=0).astype(rows.dtype)
        out_ref[a * piece : (a + 1) * piece] = jnp.concatenate([rows, own], axis=1)
    moves[2].wait()
    length = len_ref[lax.axis_index("head") * owners + chip]
    limit_ref[...] = jnp.full(limit_ref.shape, length, limit_ref.dtype)
    for move in moves[3:]:
        move.wait()


def pair_kernel(first_ref, second_ref, out_ref, sem):
    moves = [
        pltpu.make_async_copy(ref, out_ref.at[n], sem.at[n])
        for n, ref in enumerate((first_ref, second_ref))
    ]
    for move in moves:
        move.start()
    for move in moves:
        move.wait()


def absorb_kernel(per_device, w_ref, packed_ref, *outs):
    heads = w_ref.shape[0]
    piece = SPEC * heads
    nope = packed_ref[:, :NOPE]
    own_head = lax.broadcasted_iota(jnp.int32, nope.shape, 0) % heads
    spread = jnp.concatenate(
        [jnp.where(own_head == h, nope, jnp.zeros_like(nope)) for h in range(heads)], axis=1
    )
    absorbed = jnp.dot(
        spread, w_ref[...].reshape(heads * NOPE, LATENT), preferred_element_type=jnp.float32
    ).astype(jnp.bfloat16)
    for k in range(per_device):
        which = leaves_as(k, lax.axis_index("head"))
        for a in range(per_device):

            @pl.when(which == a)
            def _():
                rows = slice(a * piece, (a + 1) * piece)
                outs[k][:, :LATENT] = absorbed[rows]
                outs[k][:, LATENT:] = packed_ref[rows, NOPE:]


def block_scores(q, refs, starts, limit_ref):
    width = q.shape[1]
    keys = jnp.concatenate([ref[:width, :] for ref in refs], axis=1)
    limit = limit_ref[:1, :]
    lane = lax.broadcasted_iota(jnp.int32, limit.shape, 1)
    visible = jnp.concatenate([lane + start < limit for start in starts], axis=1)
    s = jnp.dot(q, keys, preferred_element_type=jnp.float32) * SCORE_SCALE
    return jnp.where(visible, s, masked_value)


def weigh(s, refs, top):
    w = jnp.exp(s - top)
    values = jnp.concatenate([ref[:LATENT, :] for ref in refs], axis=1)
    out = lax.dot_general(
        w.astype(jnp.bfloat16),
        values,
        (((1,), (1,)), ((), ())),
        preferred_element_type=jnp.float32,
    )
    return jnp.sum(w, axis=1, keepdims=True), out


def begin_kernel(owners, per_device, heads, limit_ref, *refs):
    q_refs, key_refs = refs[:per_device], refs[per_device : per_device + owners]
    q_out, top_ref, total_ref, out_ref = refs[per_device + owners :]
    seq_index = lax.axis_index("seq")
    chip, core = seq_index // COPIES, seq_index % COPIES
    slots = key_refs[0].shape[1]
    width = LATENT + ROPE
    q = jnp.concatenate([ref[:, :width] for ref in q_refs], axis=0)

    fresh = q_refs[0][:, width:].astype(jnp.float32)
    fresh = jnp.concatenate(
        [fresh[n * SPEC : (n + 1) * SPEC] for n in range(width // ROPE)], axis=1
    )
    fresh = jnp.concatenate([fresh, jnp.zeros((16 - SPEC, width), jnp.float32)], axis=0)
    fresh = fresh.astype(jnp.bfloat16)
    f = lax.dot_general(
        q, fresh, (((1,), (1,)), ((), ())), preferred_element_type=jnp.float32
    )
    row = lax.broadcasted_iota(jnp.int32, f.shape, 0) % (SPEC * heads)
    key = lax.broadcasted_iota(jnp.int32, f.shape, 1)
    f = jnp.where(key <= row // heads, f * SCORE_SCALE, masked_value)

    starts = [((chip ^ partner(k, core)) * COPIES + core) * slots for k in range(owners)]
    s = block_scores(q, key_refs, starts, limit_ref)
    top = jnp.maximum(jnp.max(s, axis=1, keepdims=True), jnp.max(f, axis=1, keepdims=True))
    total, out = weigh(s, key_refs, top)
    w = jnp.exp(f - top)
    total += jnp.sum(w, axis=1, keepdims=True)
    out += jnp.dot(
        w.astype(jnp.bfloat16), fresh[:, :LATENT], preferred_element_type=jnp.float32
    )
    q_out[...] = q
    top_ref[...] = jnp.broadcast_to(top, top_ref.shape)
    total_ref[...] = jnp.broadcast_to(total, total_ref.shape)
    out_ref[...] = out


def finish_kernel(
    owners, per_device, limit_ref, q_ref, top_ref, total_ref, part_ref, pair_ref, *refs
):
    key_refs = [pair_ref.at[0], pair_ref.at[1], *refs[: owners - 2]]
    outs = refs[owners - 2 :]
    seq_index = lax.axis_index("seq")
    chip, core = seq_index // COPIES, seq_index % COPIES
    plane = lax.axis_index("head")
    slots = key_refs[0].shape[1]
    starts = [((chip ^ partner(k, 1 - core)) * COPIES + 1 - core) * slots for k in range(owners)]
    s = block_scores(q_ref[...], key_refs, starts, limit_ref)
    first = top_ref[:, :1]
    top = jnp.maximum(first, jnp.max(s, axis=1, keepdims=True))
    total, out = weigh(s, key_refs, top)
    scale = jnp.exp(first - top)
    total += total_ref[:, :1] * scale
    out += part_ref[...] * scale
    out = (out * (1.0 / total)).astype(jnp.bfloat16)
    piece = out.shape[0] // per_device
    sent_first = first_block(plane, chip, core)
    for k in range(per_device):
        for n in range(per_device):

            @pl.when(sent_first ^ k != n)
            def _():
                outs[k][...] = out[n * piece : (n + 1) * piece]


def project_kernel(per_device, w_ref, *refs):
    lat_refs, out_ref = refs[:-1], refs[-1]
    rows, heads, width = out_ref.shape
    first = first_back(lax.axis_index("seq") // COPIES, lax.axis_index("head"))
    parts = [jnp.where(first == a, lat_refs[0][...], lat_refs[1][...]) for a in range(per_device)]
    latent = jnp.concatenate(parts, axis=0)
    out = jnp.zeros((rows * heads, width), jnp.float32)
    own_head = lax.broadcasted_iota(jnp.int32, out.shape, 0) % heads
    step = 2 if heads % 2 == 0 else 1
    for h in range(0, heads, step):
        group = jnp.concatenate([w_ref[h + n] for n in range(step)], axis=1)
        product = jnp.dot(latent, group, preferred_element_type=jnp.float32)
        for n in range(step):
            out = jnp.where(own_head == h + n, product[:, n * width : (n + 1) * width], out)
    out_ref[...] = out.astype(out_ref.dtype).reshape(out_ref.shape)


def whole_sequences(seq_size, head_size, queries, new_latent, cache, lengths, w_uk, w_uv):
    rows, heads, q_width = queries.shape
    owners, slots, width = cache.shape
    per_device = rows // SPEC
    piece = SPEC * heads
    all_rows = per_device * piece
    params = pltpu.CompilerParams(vmem_limit_bytes=VMEM_LIMIT)
    vmem = pl.BlockSpec(memory_space=pltpu.VMEM)
    anywhere = pl.BlockSpec(memory_space=pl.ANY)
    both = ("seq", "head")
    devices = [(i, j) for i in range(seq_size) for j in range(head_size)]

    def flat(seq_index, head_index):
        return seq_index * head_size + head_index

    def in_hbm(x):
        return pltpu.with_memory_space_constraint(x, pltpu.HBM)

    def host(i, j):
        other = (i // COPIES) ^ (2 - ((j ^ (j >> 1)) & 1))
        return flat(((i % COPIES) * 2 + other // 2) * COPIES + other % 2, j)

    def owner(i, j, a):
        plane, chip = i // COPIES, i % COPIES * per_device + a
        return flat(chip * COPIES + 1 - j // 2, plane)

    def in_plane(move):
        return [(g * COPIES + t, move(g, t)) for g in range(owners) for t in range(COPIES)]

    *picked, packed, limit = pl.pallas_call(
        functools.partial(pick_kernel, per_device),
        out_shape=[jax.ShapeDtypeStruct((width, slots), cache.dtype)] * owners
        + [
            jax.ShapeDtypeStruct((all_rows, q_width + ROPE), queries.dtype),
            jax.ShapeDtypeStruct((8, slots), jnp.int32),
        ],
        in_specs=[anywhere] * 4,
        out_specs=[vmem] * (owners + 2),
        scratch_shapes=[
            pltpu.VMEM(queries.shape, queries.dtype),
            pltpu.VMEM(new_latent.shape, new_latent.dtype),
            pltpu.SMEM(lengths.shape, lengths.dtype),
            pltpu.SemaphoreType.DMA((owners + 3,)),
        ],
        compiler_params=params,
        cost_estimate=LONG,
    )(*[in_hbm(x) for x in (jnp.swapaxes(cache, 1, 2), queries, new_latent, lengths)])
    moved = lax.ppermute(packed, both, [(flat(i, j), host(i, j)) for i, j in devices])
    own_keys = [picked[0]] + [
        lax.ppermute(picked[k], "seq", in_plane(lambda g, t: (g ^ partner(k, t)) * COPIES + t))
        for k in range(1, owners)
    ]
    pair = pl.pallas_call(
        pair_kernel,
        out_shape=jax.ShapeDtypeStruct((2, *picked[0].shape), cache.dtype),
        in_specs=[vmem] * 2,
        out_specs=vmem,
        scratch_shapes=[pltpu.SemaphoreType.DMA((2,))],
        compiler_params=params,
    )(*own_keys[:2])
    other_core = in_plane(lambda g, t: g * COPIES + 1 - t)
    far_keys = [lax.ppermute(keys, "seq", other_core) for keys in [pair] + own_keys[2:]]

    pieces = pl.pallas_call(
        functools.partial(absorb_kernel, per_device),
        out_shape=[jax.ShapeDtypeStruct((piece, width + ROPE), cache.dtype)] * per_device,
        in_specs=[vmem] * 2,
        out_specs=[vmem] * per_device,
        compiler_params=params,
        cost_estimate=LONG,
    )(w_uk, moved)
    arrived = [
        lax.ppermute(
            pieces[k],
            both,
            [(host(i, j), owner(i, j, leaves_as(k, j))) for i, j in devices],
        )
        for k in range(per_device)
    ]

    state = pl.pallas_call(
        functools.partial(begin_kernel, owners, per_device, heads),
        out_shape=[
            jax.ShapeDtypeStruct((all_rows, width), jnp.bfloat16),
            jax.ShapeDtypeStruct((all_rows, 128), jnp.float32),
            jax.ShapeDtypeStruct((all_rows, 128), jnp.float32),
            jax.ShapeDtypeStruct((all_rows, LATENT), jnp.float32),
        ],
        in_specs=[vmem] * (1 + per_device + owners),
        out_specs=[vmem] * 4,
        compiler_params=params,
        cost_estimate=LONG,
    )(limit, *arrived, *own_keys)
    latent = pl.pallas_call(
        functools.partial(finish_kernel, owners, per_device),
        out_shape=[jax.ShapeDtypeStruct((piece, LATENT), jnp.bfloat16)] * per_device,
        in_specs=[vmem] * (1 + len(state) + len(far_keys)),
        out_specs=[vmem] * per_device,
        compiler_params=params,
    )(limit, *state, *far_keys)

    back = [
        lax.ppermute(
            latent[k],
            both,
            [(owner(i, j, first_back(i // COPIES, j) ^ k ^ 1), flat(i, j)) for i, j in devices],
        )
        for k in range(per_device)
    ]
    return pl.pallas_call(
        functools.partial(project_kernel, per_device),
        out_shape=jax.ShapeDtypeStruct((rows, heads, w_uv.shape[2]), jnp.bfloat16),
        in_specs=[vmem] * (1 + per_device),
        out_specs=vmem,
        compiler_params=params,
    )(w_uv, *back[::-1])


def local_partial(
    query_tile_block,
    key_tile_block,
    incoming_keys,
    len_block,
    offset,
    own_first,
    score_scale,
    head_count,
):
    scores = (
        jnp.einsum(
            "vfa,vja->vfj", query_tile_block, key_tile_block, preferred_element_type=jnp.float32
        )
        * score_scale
    )
    positions = offset + lax.broadcasted_iota(jnp.int32, (1, 1, key_tile_block.shape[1]), 2)
    visible = positions < len_block[:, None, None]
    fresh_scores = (
        jnp.einsum(
            "vfa,vja->vfj", query_tile_block, incoming_keys, preferred_element_type=jnp.float32
        )
        * score_scale
    )
    spec_count = incoming_keys.shape[1]
    row_spec = (
        lax.broadcasted_iota(jnp.int32, (1, query_tile_block.shape[1], spec_count), 1) // head_count
    )
    key_spec = lax.broadcasted_iota(jnp.int32, (1, query_tile_block.shape[1], spec_count), 2)
    causal = (key_spec <= row_spec) & own_first
    row_top = jnp.maximum(
        jnp.max(jnp.where(visible, scores, masked_value), axis=2),
        jnp.max(jnp.where(causal, fresh_scores, masked_value), axis=2),
    )
    weights = jnp.where(visible, jnp.exp(scores - row_top[..., None]), 0.0)
    fresh_weights = jnp.where(causal, jnp.exp(fresh_scores - row_top[..., None]), 0.0)
    running_totals = jnp.sum(weights, axis=2) + jnp.sum(fresh_weights, axis=2)
    weighted = jnp.einsum(
        "mpu,mui->mpi",
        weights.astype(jnp.bfloat16),
        key_tile_block[:, :, :LATENT],
        preferred_element_type=jnp.float32,
    )
    weighted = weighted + jnp.einsum(
        "mpu,mui->mpi",
        fresh_weights.astype(jnp.bfloat16),
        incoming_keys[:, :, :LATENT],
        preferred_element_type=jnp.float32,
    )
    return (row_top, running_totals, weighted)


def project_values(latent_rows, value_weight):
    return jnp.einsum("rhc,hcv->rhv", latent_rows, value_weight, precision=lax.Precision.HIGHEST)


def split_positions(queries, new_latent, cache, lengths, w_uk, w_uv):
    own_rows, head_count, _ = queries.shape
    score_scale = (NOPE + ROPE) ** (-0.5)
    gathered, new_all = (
        lax.all_gather(queries, "seq", axis=0, tiled=True),
        lax.all_gather(new_latent, "seq", axis=0, tiled=True),
    )
    absorbed = jnp.einsum(
        "rhn,hnc->rhc", gathered[:, :, :NOPE], w_uk, preferred_element_type=jnp.float32
    ).astype(jnp.bfloat16)
    q_all = jnp.concatenate([absorbed, gathered[:, :, NOPE:]], axis=2)
    total_rows = q_all.shape[0]
    seq_count = total_rows // SPEC
    query_slots = SPEC * head_count
    q_seq = q_all.reshape(seq_count, query_slots, q_all.shape[2])
    new_seq = new_all.reshape(seq_count, SPEC, new_all.shape[1])
    seq_index = lax.axis_index("seq")
    offset = seq_index * cache.shape[1]
    own_first = seq_index == 0
    row_top, running_totals, weighted = local_partial(
        q_seq,
        lax.all_gather(cache, "head", axis=0, tiled=True),
        new_seq,
        lengths,
        offset,
        own_first,
        score_scale,
        head_count,
    )
    value_weight = w_uv.astype(jnp.float32)
    global_top = lax.pmax(row_top, "seq")
    factor = jnp.exp(row_top - global_top)
    scaled_totals = (running_totals * factor).reshape(total_rows, head_count)
    scaled_weighted = (weighted * factor[..., None]).reshape(total_rows, head_count, LATENT)
    row_totals, row_weighted = (
        lax.psum_scatter(scaled_totals, "seq", scatter_dimension=0, tiled=True),
        lax.psum_scatter(scaled_weighted, "seq", scatter_dimension=0, tiled=True),
    )
    latent_output = row_weighted / row_totals[..., None]
    result = project_values(latent_output, value_weight)
    return result.astype(jnp.bfloat16)


def shards(seq_size, head_size, queries, new_latent, cache, lengths, w_uk, w_uv):
    rows, owners = queries.shape[0], cache.shape[0]
    per_device = rows // SPEC
    if (
        per_device == 2
        and rows % SPEC == 0
        and seq_size == COPIES * owners
        and head_size == owners == 4
    ):
        return whole_sequences(
            seq_size, head_size, queries, new_latent, cache, lengths, w_uk, w_uv
        )
    return split_positions(queries, new_latent, cache, lengths, w_uk, w_uv)


def solution(mesh):
    return jax.shard_map(
        functools.partial(shards, mesh.shape["seq"], mesh.shape["head"]),
        mesh=mesh,
        in_specs=(
            P("seq", "head", None),
            P("seq", None),
            P("head", "seq", None),
            P(),
            P("head", None, None),
            P("head", None, None),
        ),
        out_specs=P("seq", "head", None),
        check_vma=False,
    )
```

```python
import functools

import jax
import jax.numpy as jnp
from jax import lax
from jax.experimental import pallas as pl
from jax.experimental.pallas import tpu as pltpu
from jax.sharding import PartitionSpec as P

NOPE = 128
ROPE = 64
LATENT = 512
SPEC = 4
SCORE_SCALE = (NOPE + ROPE) ** (-0.5)
COPIES = 2
VMEM_LIMIT = 16 * 1024 * 1024
LONG = pl.CostEstimate(flops=2 * 10**10, bytes_accessed=0, transcendentals=0)

masked_value = -1e30


def leaves_as(k, head_shard):
    return (k + head_shard) % 2


def far_half(plane, pair):
    return 1 * (plane <= 2 * pair)


def first_back(home_chip, head_shard):
    far = 1 * (far_half(home_chip, head_shard // 2) == head_shard % 2)
    return home_chip % 2 ^ far


def first_block(plane, chip, core):
    near = 1 * (chip % 2 == plane % 2)
    return far_half(plane, 1 - core) ^ near ^ chip % 2


def partner(k, core):
    return (0, 3, 1 ^ 3 * core, 2 ^ 3 * core)[k]


def pack_kernel(
    per_device, owners, q_hbm, new_hbm, len_hbm, out_ref, limit_ref, q_ref, new_ref, len_ref, sem
):
    moves = [
        pltpu.make_async_copy(q_hbm, q_ref, sem.at[0]),
        pltpu.make_async_copy(new_hbm, new_ref, sem.at[1]),
        pltpu.make_async_copy(len_hbm, len_ref, sem.at[2]),
    ]
    for move in moves:
        move.start()
    for move in moves:
        move.wait()
    length = len_ref[lax.axis_index("head") * owners + lax.axis_index("seq") // COPIES]
    limit_ref[...] = jnp.full(limit_ref.shape, length, limit_ref.dtype)
    heads, width = q_ref.shape[1:]
    fresh = new_ref[...].astype(jnp.float32)
    piece = SPEC * heads
    for a in range(per_device):
        rows = q_ref[a * SPEC : (a + 1) * SPEC].reshape(piece, width)
        own = fresh[a * SPEC : (a + 1) * SPEC]
        parts = [own[:, n : n + ROPE] for n in range(0, own.shape[1], ROPE)]
        spare = piece - SPEC * len(parts)
        if spare:
            parts.append(jnp.zeros((spare, ROPE), jnp.float32))
        own = jnp.concatenate(parts, axis=0).astype(rows.dtype)
        out_ref[a * piece : (a + 1) * piece] = jnp.concatenate([rows, own], axis=1)


def pick_kernel(cache_ref, *refs):
    blocks, sem = refs[:-1], refs[-1]
    chip, core = lax.axis_index("seq") // COPIES, lax.axis_index("seq") % COPIES
    moves = [
        pltpu.make_async_copy(cache_ref.at[chip ^ partner(k, core)], block, sem.at[k])
        for k, block in enumerate(blocks)
    ]
    for move in moves:
        move.start()
    for move in moves:
        move.wait()


def pair_kernel(first_ref, second_ref, out_ref, sem):
    moves = [
        pltpu.make_async_copy(ref, out_ref.at[n], sem.at[n])
        for n, ref in enumerate((first_ref, second_ref))
    ]
    for move in moves:
        move.start()
    for move in moves:
        move.wait()


def absorb_kernel(per_device, w_ref, packed_ref, *outs):
    heads = w_ref.shape[0]
    piece = SPEC * heads
    nope = packed_ref[:, :NOPE]
    own_head = lax.broadcasted_iota(jnp.int32, nope.shape, 0) % heads
    spread = jnp.concatenate(
        [jnp.where(own_head == h, nope, jnp.zeros_like(nope)) for h in range(heads)], axis=1
    )
    absorbed = jnp.dot(
        spread, w_ref[...].reshape(heads * NOPE, LATENT), preferred_element_type=jnp.float32
    ).astype(jnp.bfloat16)
    for k in range(per_device):
        which = leaves_as(k, lax.axis_index("head"))
        for a in range(per_device):

            @pl.when(which == a)
            def _():
                rows = slice(a * piece, (a + 1) * piece)
                outs[k][:, :LATENT] = absorbed[rows]
                outs[k][:, LATENT:] = packed_ref[rows, NOPE:]


def block_scores(q, refs, starts, limit_ref):
    width = q.shape[1]
    keys = jnp.concatenate([ref[:width, :] for ref in refs], axis=1)
    limit = limit_ref[:1, :]
    lane = lax.broadcasted_iota(jnp.int32, limit.shape, 1)
    visible = jnp.concatenate([lane + start < limit for start in starts], axis=1)
    s = jnp.dot(q, keys, preferred_element_type=jnp.float32) * SCORE_SCALE
    return jnp.where(visible, s, masked_value)


def weigh(s, refs, top):
    w = jnp.exp(s - top)
    values = jnp.concatenate([ref[:LATENT, :] for ref in refs], axis=1)
    out = lax.dot_general(
        w.astype(jnp.bfloat16),
        values,
        (((1,), (1,)), ((), ())),
        preferred_element_type=jnp.float32,
    )
    return jnp.sum(w, axis=1, keepdims=True), out


def begin_kernel(owners, per_device, heads, limit_ref, *refs):
    q_refs, key_refs = refs[:per_device], refs[per_device : per_device + owners]
    q_out, top_ref, total_ref, out_ref = refs[per_device + owners :]
    seq_index = lax.axis_index("seq")
    chip, core = seq_index // COPIES, seq_index % COPIES
    slots = key_refs[0].shape[1]
    width = LATENT + ROPE
    q = jnp.concatenate([ref[:, :width] for ref in q_refs], axis=0)

    fresh = q_refs[0][:, width:].astype(jnp.float32)
    fresh = jnp.concatenate(
        [fresh[n * SPEC : (n + 1) * SPEC] for n in range(width // ROPE)], axis=1
    )
    fresh = jnp.concatenate([fresh, jnp.zeros((16 - SPEC, width), jnp.float32)], axis=0)
    fresh = fresh.astype(jnp.bfloat16)
    f = lax.dot_general(
        q, fresh, (((1,), (1,)), ((), ())), preferred_element_type=jnp.float32
    )
    row = lax.broadcasted_iota(jnp.int32, f.shape, 0) % (SPEC * heads)
    key = lax.broadcasted_iota(jnp.int32, f.shape, 1)
    f = jnp.where(key <= row // heads, f * SCORE_SCALE, masked_value)

    starts = [((chip ^ partner(k, core)) * COPIES + core) * slots for k in range(owners)]
    s = block_scores(q, key_refs, starts, limit_ref)
    top = jnp.maximum(jnp.max(s, axis=1, keepdims=True), jnp.max(f, axis=1, keepdims=True))
    total, out = weigh(s, key_refs, top)
    w = jnp.exp(f - top)
    total += jnp.sum(w, axis=1, keepdims=True)
    out += jnp.dot(
        w.astype(jnp.bfloat16), fresh[:, :LATENT], preferred_element_type=jnp.float32
    )
    q_out[...] = q
    top_ref[...] = jnp.broadcast_to(top, top_ref.shape)
    total_ref[...] = jnp.broadcast_to(total, total_ref.shape)
    out_ref[...] = out


def finish_kernel(
    owners, per_device, limit_ref, q_ref, top_ref, total_ref, part_ref, pair_ref, *refs
):
    key_refs = [pair_ref.at[0], pair_ref.at[1], *refs[: owners - 2]]
    outs = refs[owners - 2 :]
    seq_index = lax.axis_index("seq")
    chip, core = seq_index // COPIES, seq_index % COPIES
    plane = lax.axis_index("head")
    slots = key_refs[0].shape[1]
    starts = [((chip ^ partner(k, 1 - core)) * COPIES + 1 - core) * slots for k in range(owners)]
    s = block_scores(q_ref[...], key_refs, starts, limit_ref)
    first = top_ref[:, :1]
    top = jnp.maximum(first, jnp.max(s, axis=1, keepdims=True))
    total, out = weigh(s, key_refs, top)
    scale = jnp.exp(first - top)
    total += total_ref[:, :1] * scale
    out += part_ref[...] * scale
    out = (out * (1.0 / total)).astype(jnp.bfloat16)
    piece = out.shape[0] // per_device
    sent_first = first_block(plane, chip, core)
    for k in range(per_device):
        for n in range(per_device):

            @pl.when(sent_first ^ k == n)
            def _():
                outs[k][...] = out[n * piece : (n + 1) * piece]


def project_kernel(per_device, w_ref, *refs):
    lat_refs, out_ref = refs[:-1], refs[-1]
    rows, heads, width = out_ref.shape
    first = first_back(lax.axis_index("seq") // COPIES, lax.axis_index("head"))
    parts = [jnp.where(first == a, lat_refs[1][...], lat_refs[0][...]) for a in range(per_device)]
    latent = jnp.concatenate(parts, axis=0)
    out = jnp.zeros((rows * heads, width), jnp.float32)
    own_head = lax.broadcasted_iota(jnp.int32, out.shape, 0) % heads
    step = 2 if heads % 2 == 0 else 1
    for h in range(0, heads, step):
        group = jnp.concatenate([w_ref[h + n] for n in range(step)], axis=1)
        product = jnp.dot(latent, group, preferred_element_type=jnp.float32)
        for n in range(step):
            out = jnp.where(own_head == h + n, product[:, n * width : (n + 1) * width], out)
    out_ref[...] = out.astype(out_ref.dtype).reshape(out_ref.shape)


def whole_sequences(seq_size, head_size, queries, new_latent, cache, lengths, w_uk, w_uv):
    rows, heads, q_width = queries.shape
    owners, slots, width = cache.shape
    per_device = rows // SPEC
    piece = SPEC * heads
    all_rows = per_device * piece
    params = pltpu.CompilerParams(vmem_limit_bytes=VMEM_LIMIT)
    vmem = pl.BlockSpec(memory_space=pltpu.VMEM)
    anywhere = pl.BlockSpec(memory_space=pl.ANY)
    both = ("seq", "head")
    devices = [(i, j) for i in range(seq_size) for j in range(head_size)]

    def flat(seq_index, head_index):
        return seq_index * head_size + head_index

    def in_hbm(x):
        return pltpu.with_memory_space_constraint(x, pltpu.HBM)

    def host(i, j):
        other = (i // COPIES) ^ (2 - ((j ^ (j >> 1)) & 1))
        return flat(((i % COPIES) * 2 + other // 2) * COPIES + other % 2, j)

    def owner(i, j, a):
        plane, chip = i // COPIES, i % COPIES * per_device + a
        return flat(chip * COPIES + 1 - j // 2, plane)

    def in_plane(move):
        return [(g * COPIES + t, move(g, t)) for g in range(owners) for t in range(COPIES)]

    packed, limit = pl.pallas_call(
        functools.partial(pack_kernel, per_device, owners),
        out_shape=[
            jax.ShapeDtypeStruct((all_rows, q_width + ROPE), queries.dtype),
            jax.ShapeDtypeStruct((8, slots), jnp.int32),
        ],
        in_specs=[anywhere] * 3,
        out_specs=[vmem] * 2,
        scratch_shapes=[
            pltpu.VMEM(queries.shape, queries.dtype),
            pltpu.VMEM(new_latent.shape, new_latent.dtype),
            pltpu.SMEM(lengths.shape, lengths.dtype),
            pltpu.SemaphoreType.DMA((3,)),
        ],
        compiler_params=params,
        cost_estimate=LONG,
    )(in_hbm(queries), in_hbm(new_latent), in_hbm(lengths))
    moved = lax.ppermute(packed, both, [(flat(i, j), host(i, j)) for i, j in devices])
    picked = pl.pallas_call(
        pick_kernel,
        out_shape=[jax.ShapeDtypeStruct((width, slots), cache.dtype)] * owners,
        in_specs=[anywhere],
        out_specs=[vmem] * owners,
        scratch_shapes=[pltpu.SemaphoreType.DMA((owners,))],
        compiler_params=params,
        cost_estimate=LONG,
    )(jnp.swapaxes(cache, 1, 2))
    own_keys = [picked[0]] + [
        lax.ppermute(picked[k], "seq", in_plane(lambda g, t: (g ^ partner(k, t)) * COPIES + t))
        for k in range(1, owners)
    ]
    pair = pl.pallas_call(
        pair_kernel,
        out_shape=jax.ShapeDtypeStruct((2, *picked[0].shape), cache.dtype),
        in_specs=[vmem] * 2,
        out_specs=vmem,
        scratch_shapes=[pltpu.SemaphoreType.DMA((2,))],
        compiler_params=params,
    )(*own_keys[:2])
    other_core = in_plane(lambda g, t: g * COPIES + 1 - t)
    far_keys = [lax.ppermute(keys, "seq", other_core) for keys in [pair] + own_keys[2:]]

    pieces = pl.pallas_call(
        functools.partial(absorb_kernel, per_device),
        out_shape=[jax.ShapeDtypeStruct((piece, width + ROPE), cache.dtype)] * per_device,
        in_specs=[vmem] * 2,
        out_specs=[vmem] * per_device,
        compiler_params=params,
        cost_estimate=LONG,
    )(w_uk, moved)
    arrived = [
        lax.ppermute(
            pieces[k],
            both,
            [(host(i, j), owner(i, j, leaves_as(k, j))) for i, j in devices],
        )
        for k in range(per_device)
    ]

    state = pl.pallas_call(
        functools.partial(begin_kernel, owners, per_device, heads),
        out_shape=[
            jax.ShapeDtypeStruct((all_rows, width), jnp.bfloat16),
            jax.ShapeDtypeStruct((all_rows, 128), jnp.float32),
            jax.ShapeDtypeStruct((all_rows, 128), jnp.float32),
            jax.ShapeDtypeStruct((all_rows, LATENT), jnp.float32),
        ],
        in_specs=[vmem] * (1 + per_device + owners),
        out_specs=[vmem] * 4,
        compiler_params=params,
        cost_estimate=LONG,
    )(limit, *arrived, *own_keys)
    latent = pl.pallas_call(
        functools.partial(finish_kernel, owners, per_device),
        out_shape=[jax.ShapeDtypeStruct((piece, LATENT), jnp.bfloat16)] * per_device,
        in_specs=[vmem] * (1 + len(state) + len(far_keys)),
        out_specs=[vmem] * per_device,
        compiler_params=params,
    )(limit, *state, *far_keys)

    back = [
        lax.ppermute(
            latent[k],
            both,
            [(owner(i, j, first_back(i // COPIES, j) ^ k), flat(i, j)) for i, j in devices],
        )
        for k in range(per_device)
    ]
    return pl.pallas_call(
        functools.partial(project_kernel, per_device),
        out_shape=jax.ShapeDtypeStruct((rows, heads, w_uv.shape[2]), jnp.bfloat16),
        in_specs=[vmem] * (1 + per_device),
        out_specs=vmem,
        compiler_params=params,
    )(w_uv, *back[::-1])


def local_partial(
    query_tile_block,
    key_tile_block,
    incoming_keys,
    len_block,
    offset,
    own_first,
    score_scale,
    head_count,
):
    scores = (
        jnp.einsum(
            "vfa,vja->vfj", query_tile_block, key_tile_block, preferred_element_type=jnp.float32
        )
        * score_scale
    )
    positions = offset + lax.broadcasted_iota(jnp.int32, (1, 1, key_tile_block.shape[1]), 2)
    visible = positions < len_block[:, None, None]
    fresh_scores = (
        jnp.einsum(
            "vfa,vja->vfj", query_tile_block, incoming_keys, preferred_element_type=jnp.float32
        )
        * score_scale
    )
    spec_count = incoming_keys.shape[1]
    row_spec = (
        lax.broadcasted_iota(jnp.int32, (1, query_tile_block.shape[1], spec_count), 1) // head_count
    )
    key_spec = lax.broadcasted_iota(jnp.int32, (1, query_tile_block.shape[1], spec_count), 2)
    causal = (key_spec <= row_spec) & own_first
    row_top = jnp.maximum(
        jnp.max(jnp.where(visible, scores, masked_value), axis=2),
        jnp.max(jnp.where(causal, fresh_scores, masked_value), axis=2),
    )
    weights = jnp.where(visible, jnp.exp(scores - row_top[..., None]), 0.0)
    fresh_weights = jnp.where(causal, jnp.exp(fresh_scores - row_top[..., None]), 0.0)
    running_totals = jnp.sum(weights, axis=2) + jnp.sum(fresh_weights, axis=2)
    weighted = jnp.einsum(
        "mpu,mui->mpi",
        weights.astype(jnp.bfloat16),
        key_tile_block[:, :, :LATENT],
        preferred_element_type=jnp.float32,
    )
    weighted = weighted + jnp.einsum(
        "mpu,mui->mpi",
        fresh_weights.astype(jnp.bfloat16),
        incoming_keys[:, :, :LATENT],
        preferred_element_type=jnp.float32,
    )
    return (row_top, running_totals, weighted)


def project_values(latent_rows, value_weight):
    return jnp.einsum("rhc,hcv->rhv", latent_rows, value_weight, precision=lax.Precision.HIGHEST)


def split_positions(queries, new_latent, cache, lengths, w_uk, w_uv):
    own_rows, head_count, _ = queries.shape
    score_scale = (NOPE + ROPE) ** (-0.5)
    gathered, new_all = (
        lax.all_gather(queries, "seq", axis=0, tiled=True),
        lax.all_gather(new_latent, "seq", axis=0, tiled=True),
    )
    absorbed = jnp.einsum(
        "rhn,hnc->rhc", gathered[:, :, :NOPE], w_uk, preferred_element_type=jnp.float32
    ).astype(jnp.bfloat16)
    q_all = jnp.concatenate([absorbed, gathered[:, :, NOPE:]], axis=2)
    total_rows = q_all.shape[0]
    seq_count = total_rows // SPEC
    query_slots = SPEC * head_count
    q_seq = q_all.reshape(seq_count, query_slots, q_all.shape[2])
    new_seq = new_all.reshape(seq_count, SPEC, new_all.shape[1])
    seq_index = lax.axis_index("seq")
    offset = seq_index * cache.shape[1]
    own_first = seq_index == 0
    row_top, running_totals, weighted = local_partial(
        q_seq,
        lax.all_gather(cache, "head", axis=0, tiled=True),
        new_seq,
        lengths,
        offset,
        own_first,
        score_scale,
        head_count,
    )
    value_weight = w_uv.astype(jnp.float32)
    global_top = lax.pmax(row_top, "seq")
    factor = jnp.exp(row_top - global_top)
    scaled_totals = (running_totals * factor).reshape(total_rows, head_count)
    scaled_weighted = (weighted * factor[..., None]).reshape(total_rows, head_count, LATENT)
    row_totals, row_weighted = (
        lax.psum_scatter(scaled_totals, "seq", scatter_dimension=0, tiled=True),
        lax.psum_scatter(scaled_weighted, "seq", scatter_dimension=0, tiled=True),
    )
    latent_output = row_weighted / row_totals[..., None]
    result = project_values(latent_output, value_weight)
    return result.astype(jnp.bfloat16)


def shards(seq_size, head_size, queries, new_latent, cache, lengths, w_uk, w_uv):
    rows, owners = queries.shape[0], cache.shape[0]
    per_device = rows // SPEC
    if (
        per_device == 2
        and rows % SPEC == 0
        and seq_size == COPIES * owners
        and head_size == owners == 4
    ):
        return whole_sequences(
            seq_size, head_size, queries, new_latent, cache, lengths, w_uk, w_uv
        )
    return split_positions(queries, new_latent, cache, lengths, w_uk, w_uv)


def solution(mesh):
    return jax.shard_map(
        functools.partial(shards, mesh.shape["seq"], mesh.shape["head"]),
        mesh=mesh,
        in_specs=(
            P("seq", "head", None),
            P("seq", None),
            P("head", "seq", None),
            P(),
            P("head", None, None),
            P("head", None, None),
        ),
        out_specs=P("seq", "head", None),
        check_vma=False,
    )
```

```python
import functools

import jax
import jax.numpy as jnp
from jax import lax
from jax.experimental import pallas as pl
from jax.experimental.pallas import tpu as pltpu
from jax.sharding import PartitionSpec as P

NOPE = 128
ROPE = 64
LATENT = 512
SPEC = 4
SCORE_SCALE = (NOPE + ROPE) ** (-0.5)
COPIES = 2
VMEM_LIMIT = 16 * 1024 * 1024
LONG = pl.CostEstimate(flops=2 * 10**10, bytes_accessed=0, transcendentals=0)

masked_value = -1e30


def leaves_as(k, head_shard):
    return head_shard % 2 == k


def stays(home_chip, core, half):
    return home_chip % 2 ^ half & (home_chip // 2 ^ core)


def far_half(plane, pair):
    return 1 * (plane <= 2 * pair)


def first_back(home_chip, head_shard):
    far = 1 * (far_half(home_chip, head_shard // 2) == head_shard % 2)
    return home_chip % 2 ^ far


def first_block(plane, chip, core):
    first = far_half(plane, 1 - core) ^ 1 * (chip % 2 == plane % 2)
    return first ^ 1 * (stays(plane, chip // 2, 1 - core) != chip % 2)


def partner(k, core):
    return (0, 3, 1 ^ 3 * core, 2 ^ 3 * core)[k]


def pick_kernel(per_device, cache_hbm, q_hbm, new_hbm, len_hbm, *refs):
    owners = cache_hbm.shape[0]
    blocks, outs = refs[:owners], refs[owners : owners + per_device]
    limit_ref, q_ref, new_ref, len_ref, sem = refs[owners + per_device :]
    chip, core = lax.axis_index("seq") // COPIES, lax.axis_index("seq") % COPIES
    moves = [
        pltpu.make_async_copy(q_hbm, q_ref, sem.at[owners]),
        pltpu.make_async_copy(new_hbm, new_ref, sem.at[owners + 1]),
        pltpu.make_async_copy(len_hbm, len_ref, sem.at[owners + 2]),
    ] + [
        pltpu.make_async_copy(cache_hbm.at[chip ^ partner(k, core)], blocks[k], sem.at[k])
        for k in range(owners)
    ]
    for move in moves:
        move.start()
    moves[0].wait()
    moves[1].wait()
    heads, width = q_ref.shape[1:]
    fresh = new_ref[...].astype(jnp.float32)
    piece = SPEC * heads
    for a in range(per_device):
        rows = q_ref[a * SPEC : (a + 1) * SPEC].reshape(piece, width)
        own = fresh[a * SPEC : (a + 1) * SPEC]
        parts = [own[:, n : n + ROPE] for n in range(0, own.shape[1], ROPE)]
        spare = piece - SPEC * len(parts)
        if spare:
            parts.append(jnp.zeros((spare, ROPE), jnp.float32))
        own = jnp.concatenate(parts, axis=0).astype(rows.dtype)
        packed = jnp.concatenate([rows, own], axis=1)
        for n, out in enumerate(outs):

            @pl.when(stays(chip, core, lax.axis_index("head") // 2) ^ n == a)
            def _():
                out[...] = packed

    moves[2].wait()
    length = len_ref[lax.axis_index("head") * owners + chip]
    limit_ref[...] = jnp.full(limit_ref.shape, length, limit_ref.dtype)
    for move in moves[3:]:
        move.wait()


def pair_kernel(first_ref, second_ref, out_ref, sem):
    moves = [
        pltpu.make_async_copy(ref, out_ref.at[n], sem.at[n])
        for n, ref in enumerate((first_ref, second_ref))
    ]
    for move in moves:
        move.start()
    for move in moves:
        move.wait()


def absorb_kernel(per_device, w_ref, *refs):
    packed, outs = refs[:per_device], refs[per_device:]
    heads = w_ref.shape[0]
    piece = SPEC * heads
    nope = jnp.concatenate([ref[:, :NOPE] for ref in packed], axis=0)
    own_head = lax.broadcasted_iota(jnp.int32, nope.shape, 0) % heads
    spread = jnp.concatenate(
        [jnp.where(own_head == h, nope, jnp.zeros_like(nope)) for h in range(heads)], axis=1
    )
    absorbed = jnp.dot(
        spread, w_ref[...].reshape(heads * NOPE, LATENT), preferred_element_type=jnp.float32
    ).astype(jnp.bfloat16)
    for k in range(per_device):
        home_made = leaves_as(k, lax.axis_index("head"))
        for n in range(per_device):

            @pl.when(home_made == (n == 0))
            def _():
                outs[k][:, :LATENT] = absorbed[n * piece : (n + 1) * piece]
                outs[k][:, LATENT:] = packed[n][:, NOPE:]


def block_scores(q, refs, starts, limit_ref):
    width = q.shape[1]
    keys = jnp.concatenate([ref[:width, :] for ref in refs], axis=1)
    limit = limit_ref[:1, :]
    lane = lax.broadcasted_iota(jnp.int32, limit.shape, 1)
    visible = jnp.concatenate([lane + start < limit for start in starts], axis=1)
    s = jnp.dot(q, keys, preferred_element_type=jnp.float32) * SCORE_SCALE
    return jnp.where(visible, s, masked_value)


def weigh(s, refs, top):
    w = jnp.exp(s - top)
    values = jnp.concatenate([ref[:LATENT, :] for ref in refs], axis=1)
    out = lax.dot_general(
        w.astype(jnp.bfloat16),
        values,
        (((1,), (1,)), ((), ())),
        preferred_element_type=jnp.float32,
    )
    return jnp.sum(w, axis=1, keepdims=True), out


def begin_kernel(owners, per_device, heads, limit_ref, *refs):
    q_refs, key_refs = refs[:per_device], refs[per_device : per_device + owners]
    q_out, top_ref, total_ref, out_ref = refs[per_device + owners :]
    seq_index = lax.axis_index("seq")
    chip, core = seq_index // COPIES, seq_index % COPIES
    slots = key_refs[0].shape[1]
    width = LATENT + ROPE
    q = jnp.concatenate([ref[:, :width] for ref in q_refs], axis=0)

    fresh = q_refs[0][:, width:].astype(jnp.float32)
    fresh = jnp.concatenate(
        [fresh[n * SPEC : (n + 1) * SPEC] for n in range(width // ROPE)], axis=1
    )
    fresh = jnp.concatenate([fresh, jnp.zeros((16 - SPEC, width), jnp.float32)], axis=0)
    fresh = fresh.astype(jnp.bfloat16)
    f = lax.dot_general(
        q, fresh, (((1,), (1,)), ((), ())), preferred_element_type=jnp.float32
    )
    row = lax.broadcasted_iota(jnp.int32, f.shape, 0) % (SPEC * heads)
    key = lax.broadcasted_iota(jnp.int32, f.shape, 1)
    f = jnp.where(key <= row // heads, f * SCORE_SCALE, masked_value)

    starts = [((chip ^ partner(k, core)) * COPIES + core) * slots for k in range(owners)]
    s = block_scores(q, key_refs, starts, limit_ref)
    top = jnp.maximum(jnp.max(s, axis=1, keepdims=True), jnp.max(f, axis=1, keepdims=True))
    total, out = weigh(s, key_refs, top)
    w = jnp.exp(f - top)
    total += jnp.sum(w, axis=1, keepdims=True)
    out += jnp.dot(
        w.astype(jnp.bfloat16), fresh[:, :LATENT], preferred_element_type=jnp.float32
    )
    q_out[...] = q
    top_ref[...] = jnp.broadcast_to(top, top_ref.shape)
    total_ref[...] = jnp.broadcast_to(total, total_ref.shape)
    out_ref[...] = out


def finish_kernel(
    owners, per_device, limit_ref, q_ref, top_ref, total_ref, part_ref, pair_ref, *refs
):
    key_refs = [pair_ref.at[0], pair_ref.at[1], *refs[: owners - 2]]
    outs = refs[owners - 2 :]
    seq_index = lax.axis_index("seq")
    chip, core = seq_index // COPIES, seq_index % COPIES
    plane = lax.axis_index("head")
    slots = key_refs[0].shape[1]
    starts = [((chip ^ partner(k, 1 - core)) * COPIES + 1 - core) * slots for k in range(owners)]
    s = block_scores(q_ref[...], key_refs, starts, limit_ref)
    first = top_ref[:, :1]
    top = jnp.maximum(first, jnp.max(s, axis=1, keepdims=True))
    total, out = weigh(s, key_refs, top)
    scale = jnp.exp(first - top)
    total += total_ref[:, :1] * scale
    out += part_ref[...] * scale
    out = (out * (1.0 / total)).astype(jnp.bfloat16)
    piece = out.shape[0] // per_device
    sent_first = first_block(plane, chip, core)
    for k in range(per_device):
        for n in range(per_device):

            @pl.when(sent_first ^ k == n)
            def _():
                outs[k][...] = out[n * piece : (n + 1) * piece]


def project_kernel(per_device, w_ref, *refs):
    lat_refs, out_ref = refs[:-1], refs[-1]
    rows, heads, width = out_ref.shape
    first = first_back(lax.axis_index("seq") // COPIES, lax.axis_index("head"))
    parts = [jnp.where(first == a, lat_refs[1][...], lat_refs[0][...]) for a in range(per_device)]
    latent = jnp.concatenate(parts, axis=0)
    out = jnp.zeros((rows * heads, width), jnp.float32)
    own_head = lax.broadcasted_iota(jnp.int32, out.shape, 0) % heads
    step = 2 if heads % 2 == 0 else 1
    for h in range(0, heads, step):
        group = jnp.concatenate([w_ref[h + n] for n in range(step)], axis=1)
        product = jnp.dot(latent, group, preferred_element_type=jnp.float32)
        for n in range(step):
            out = jnp.where(own_head == h + n, product[:, n * width : (n + 1) * width], out)
    out_ref[...] = out.astype(out_ref.dtype).reshape(out_ref.shape)


def whole_sequences(seq_size, head_size, queries, new_latent, cache, lengths, w_uk, w_uv):
    rows, heads, q_width = queries.shape
    owners, slots, width = cache.shape
    per_device = rows // SPEC
    piece = SPEC * heads
    all_rows = per_device * piece
    params = pltpu.CompilerParams(vmem_limit_bytes=VMEM_LIMIT)
    vmem = pl.BlockSpec(memory_space=pltpu.VMEM)
    anywhere = pl.BlockSpec(memory_space=pl.ANY)
    both = ("seq", "head")
    devices = [(i, j) for i in range(seq_size) for j in range(head_size)]

    def flat(seq_index, head_index):
        return seq_index * head_size + head_index

    def in_hbm(x):
        return pltpu.with_memory_space_constraint(x, pltpu.HBM)

    def maker(i, j, k):
        home, row = i // COPIES, i % COPIES
        a = stays(home, row, j // 2)
        if leaves_as(k, j):
            return flat(i, j), a
        return flat((row * per_device + 1 - a) * COPIES + home // 2, j), 1 - a

    def owner(i, j, a):
        plane, chip = i // COPIES, i % COPIES * per_device + a
        return flat(chip * COPIES + 1 - j // 2, plane)

    def in_plane(move):
        return [(g * COPIES + t, move(g, t)) for g in range(owners) for t in range(COPIES)]

    *picked, kept, left, limit = pl.pallas_call(
        functools.partial(pick_kernel, per_device),
        out_shape=[jax.ShapeDtypeStruct((width, slots), cache.dtype)] * owners
        + [jax.ShapeDtypeStruct((piece, q_width + ROPE), queries.dtype)] * per_device
        + [jax.ShapeDtypeStruct((8, slots), jnp.int32)],
        in_specs=[anywhere] * 4,
        out_specs=[vmem] * (owners + per_device + 1),
        scratch_shapes=[
            pltpu.VMEM(queries.shape, queries.dtype),
            pltpu.VMEM(new_latent.shape, new_latent.dtype),
            pltpu.SMEM(lengths.shape, lengths.dtype),
            pltpu.SemaphoreType.DMA((owners + 3,)),
        ],
        compiler_params=params,
        cost_estimate=LONG,
    )(*[in_hbm(x) for x in (jnp.swapaxes(cache, 1, 2), queries, new_latent, lengths)])
    moved = lax.ppermute(
        left, both, [(flat(i, j), maker(i, j, 1 - j % 2)[0]) for i, j in devices]
    )
    own_keys = [picked[0]] + [
        lax.ppermute(picked[k], "seq", in_plane(lambda g, t: (g ^ partner(k, t)) * COPIES + t))
        for k in range(1, owners)
    ]
    pair = pl.pallas_call(
        pair_kernel,
        out_shape=jax.ShapeDtypeStruct((2, *picked[0].shape), cache.dtype),
        in_specs=[vmem] * 2,
        out_specs=vmem,
        scratch_shapes=[pltpu.SemaphoreType.DMA((2,))],
        compiler_params=params,
    )(*own_keys[:2])
    other_core = in_plane(lambda g, t: g * COPIES + 1 - t)
    far_keys = [lax.ppermute(keys, "seq", other_core) for keys in [pair] + own_keys[2:]]

    pieces = pl.pallas_call(
        functools.partial(absorb_kernel, per_device),
        out_shape=[jax.ShapeDtypeStruct((piece, width + ROPE), cache.dtype)] * per_device,
        in_specs=[vmem] * (1 + per_device),
        out_specs=[vmem] * per_device,
        compiler_params=params,
        cost_estimate=LONG,
    )(w_uk, kept, moved)
    arrived = [
        lax.ppermute(
            pieces[k],
            both,
            [
                (source, owner(i, j, a))
                for i, j in devices
                for source, a in [maker(i, j, k)]
            ],
        )
        for k in range(per_device)
    ]

    state = pl.pallas_call(
        functools.partial(begin_kernel, owners, per_device, heads),
        out_shape=[
            jax.ShapeDtypeStruct((all_rows, width), jnp.bfloat16),
            jax.ShapeDtypeStruct((all_rows, 128), jnp.float32),
            jax.ShapeDtypeStruct((all_rows, 128), jnp.float32),
            jax.ShapeDtypeStruct((all_rows, LATENT), jnp.float32),
        ],
        in_specs=[vmem] * (1 + per_device + owners),
        out_specs=[vmem] * 4,
        compiler_params=params,
        cost_estimate=LONG,
    )(limit, *arrived, *own_keys)
    latent = pl.pallas_call(
        functools.partial(finish_kernel, owners, per_device),
        out_shape=[jax.ShapeDtypeStruct((piece, LATENT), jnp.bfloat16)] * per_device,
        in_specs=[vmem] * (1 + len(state) + len(far_keys)),
        out_specs=[vmem] * per_device,
        compiler_params=params,
    )(limit, *state, *far_keys)

    back = [
        lax.ppermute(
            latent[k],
            both,
            [(owner(i, j, first_back(i // COPIES, j) ^ k), flat(i, j)) for i, j in devices],
        )
        for k in range(per_device)
    ]
    return pl.pallas_call(
        functools.partial(project_kernel, per_device),
        out_shape=jax.ShapeDtypeStruct((rows, heads, w_uv.shape[2]), jnp.bfloat16),
        in_specs=[vmem] * (1 + per_device),
        out_specs=vmem,
        compiler_params=params,
    )(w_uv, *back[::-1])


def local_partial(
    query_tile_block,
    key_tile_block,
    incoming_keys,
    len_block,
    offset,
    own_first,
    score_scale,
    head_count,
):
    scores = (
        jnp.einsum(
            "vfa,vja->vfj", query_tile_block, key_tile_block, preferred_element_type=jnp.float32
        )
        * score_scale
    )
    positions = offset + lax.broadcasted_iota(jnp.int32, (1, 1, key_tile_block.shape[1]), 2)
    visible = positions < len_block[:, None, None]
    fresh_scores = (
        jnp.einsum(
            "vfa,vja->vfj", query_tile_block, incoming_keys, preferred_element_type=jnp.float32
        )
        * score_scale
    )
    spec_count = incoming_keys.shape[1]
    row_spec = (
        lax.broadcasted_iota(jnp.int32, (1, query_tile_block.shape[1], spec_count), 1) // head_count
    )
    key_spec = lax.broadcasted_iota(jnp.int32, (1, query_tile_block.shape[1], spec_count), 2)
    causal = (key_spec <= row_spec) & own_first
    row_top = jnp.maximum(
        jnp.max(jnp.where(visible, scores, masked_value), axis=2),
        jnp.max(jnp.where(causal, fresh_scores, masked_value), axis=2),
    )
    weights = jnp.where(visible, jnp.exp(scores - row_top[..., None]), 0.0)
    fresh_weights = jnp.where(causal, jnp.exp(fresh_scores - row_top[..., None]), 0.0)
    running_totals = jnp.sum(weights, axis=2) + jnp.sum(fresh_weights, axis=2)
    weighted = jnp.einsum(
        "mpu,mui->mpi",
        weights.astype(jnp.bfloat16),
        key_tile_block[:, :, :LATENT],
        preferred_element_type=jnp.float32,
    )
    weighted = weighted + jnp.einsum(
        "mpu,mui->mpi",
        fresh_weights.astype(jnp.bfloat16),
        incoming_keys[:, :, :LATENT],
        preferred_element_type=jnp.float32,
    )
    return (row_top, running_totals, weighted)


def project_values(latent_rows, value_weight):
    return jnp.einsum("rhc,hcv->rhv", latent_rows, value_weight, precision=lax.Precision.HIGHEST)


def split_positions(queries, new_latent, cache, lengths, w_uk, w_uv):
    own_rows, head_count, _ = queries.shape
    score_scale = (NOPE + ROPE) ** (-0.5)
    gathered, new_all = (
        lax.all_gather(queries, "seq", axis=0, tiled=True),
        lax.all_gather(new_latent, "seq", axis=0, tiled=True),
    )
    absorbed = jnp.einsum(
        "rhn,hnc->rhc", gathered[:, :, :NOPE], w_uk, preferred_element_type=jnp.float32
    ).astype(jnp.bfloat16)
    q_all = jnp.concatenate([absorbed, gathered[:, :, NOPE:]], axis=2)
    total_rows = q_all.shape[0]
    seq_count = total_rows // SPEC
    query_slots = SPEC * head_count
    q_seq = q_all.reshape(seq_count, query_slots, q_all.shape[2])
    new_seq = new_all.reshape(seq_count, SPEC, new_all.shape[1])
    seq_index = lax.axis_index("seq")
    offset = seq_index * cache.shape[1]
    own_first = seq_index == 0
    row_top, running_totals, weighted = local_partial(
        q_seq,
        lax.all_gather(cache, "head", axis=0, tiled=True),
        new_seq,
        lengths,
        offset,
        own_first,
        score_scale,
        head_count,
    )
    value_weight = w_uv.astype(jnp.float32)
    global_top = lax.pmax(row_top, "seq")
    factor = jnp.exp(row_top - global_top)
    scaled_totals = (running_totals * factor).reshape(total_rows, head_count)
    scaled_weighted = (weighted * factor[..., None]).reshape(total_rows, head_count, LATENT)
    row_totals, row_weighted = (
        lax.psum_scatter(scaled_totals, "seq", scatter_dimension=0, tiled=True),
        lax.psum_scatter(scaled_weighted, "seq", scatter_dimension=0, tiled=True),
    )
    latent_output = row_weighted / row_totals[..., None]
    result = project_values(latent_output, value_weight)
    return result.astype(jnp.bfloat16)


def shards(seq_size, head_size, queries, new_latent, cache, lengths, w_uk, w_uv):
    rows, owners = queries.shape[0], cache.shape[0]
    per_device = rows // SPEC
    if (
        per_device == 2
        and rows % SPEC == 0
        and seq_size == COPIES * owners
        and head_size == owners == 4
    ):
        return whole_sequences(
            seq_size, head_size, queries, new_latent, cache, lengths, w_uk, w_uv
        )
    return split_positions(queries, new_latent, cache, lengths, w_uk, w_uv)


def solution(mesh):
    return jax.shard_map(
        functools.partial(shards, mesh.shape["seq"], mesh.shape["head"]),
        mesh=mesh,
        in_specs=(
            P("seq", "head", None),
            P("seq", None),
            P("head", "seq", None),
            P(),
            P("head", None, None),
            P("head", None, None),
        ),
        out_specs=P("seq", "head", None),
        check_vma=False,
    )
```

```python
import functools

import jax
import jax.numpy as jnp
from jax import lax
from jax.experimental import pallas as pl
from jax.experimental.pallas import tpu as pltpu
from jax.sharding import PartitionSpec as P

NOPE = 128
ROPE = 64
LATENT = 512
SPEC = 4
SCORE_SCALE = (NOPE + ROPE) ** (-0.5)
COPIES = 2
VMEM_LIMIT = 16 * 1024 * 1024
LONG = pl.CostEstimate(flops=2 * 10**10, bytes_accessed=0, transcendentals=0)

masked_value = -1e30


def leaves_as(k, head_shard):
    return head_shard % 2 == k


def stays(home_chip, core, half):
    row = home_chip // 2
    return home_chip % 2 ^ (1 ^ half ^ row) & (row ^ core)


def far_half(plane, pair):
    return 1 * (plane <= 2 * pair)


def first_back(home_chip, head_shard):
    far = 1 * (far_half(home_chip, head_shard // 2) == head_shard % 2)
    return home_chip % 2 ^ far


def first_block(plane, chip, core):
    first = far_half(plane, 1 - core) ^ 1 * (chip % 2 == plane % 2)
    return first ^ 1 * (stays(plane, chip // 2, 1 - core) != chip % 2)


def partner(k, core):
    return (0, 3, 1 ^ 3 * core, 2 ^ 3 * core)[k]


def pick_kernel(per_device, cache_hbm, q_hbm, new_hbm, len_hbm, *refs):
    owners = cache_hbm.shape[0]
    blocks, outs = refs[:owners], refs[owners : owners + per_device]
    limit_ref, q_ref, new_ref, len_ref, sem = refs[owners + per_device :]
    chip, core = lax.axis_index("seq") // COPIES, lax.axis_index("seq") % COPIES
    moves = [
        pltpu.make_async_copy(q_hbm, q_ref, sem.at[owners]),
        pltpu.make_async_copy(new_hbm, new_ref, sem.at[owners + 1]),
        pltpu.make_async_copy(len_hbm, len_ref, sem.at[owners + 2]),
    ] + [
        pltpu.make_async_copy(cache_hbm.at[chip ^ partner(k, core)], blocks[k], sem.at[k])
        for k in range(owners)
    ]
    for move in moves:
        move.start()
    moves[0].wait()
    moves[1].wait()
    heads, width = q_ref.shape[1:]
    fresh = new_ref[...].astype(jnp.float32)
    piece = SPEC * heads
    for a in range(per_device):
        rows = q_ref[a * SPEC : (a + 1) * SPEC].reshape(piece, width)
        own = fresh[a * SPEC : (a + 1) * SPEC]
        parts = [own[:, n : n + ROPE] for n in range(0, own.shape[1], ROPE)]
        spare = piece - SPEC * len(parts)
        if spare:
            parts.append(jnp.zeros((spare, ROPE), jnp.float32))
        own = jnp.concatenate(parts, axis=0).astype(rows.dtype)
        packed = jnp.concatenate([rows, own], axis=1)
        for n, out in enumerate(outs):

            @pl.when(stays(chip, core, lax.axis_index("head") // 2) ^ n == a)
            def _():
                out[...] = packed

    moves[2].wait()
    length = len_ref[lax.axis_index("head") * owners + chip]
    limit_ref[...] = jnp.full(limit_ref.shape, length, limit_ref.dtype)
    for move in moves[3:]:
        move.wait()


def pair_kernel(first_ref, second_ref, out_ref, sem):
    moves = [
        pltpu.make_async_copy(ref, out_ref.at[n], sem.at[n])
        for n, ref in enumerate((first_ref, second_ref))
    ]
    for move in moves:
        move.start()
    for move in moves:
        move.wait()


def absorb_kernel(per_device, w_ref, *refs):
    packed, outs = refs[:per_device], refs[per_device:]
    heads = w_ref.shape[0]
    piece = SPEC * heads
    nope = jnp.concatenate([ref[:, :NOPE] for ref in packed], axis=0)
    own_head = lax.broadcasted_iota(jnp.int32, nope.shape, 0) % heads
    spread = jnp.concatenate(
        [jnp.where(own_head == h, nope, jnp.zeros_like(nope)) for h in range(heads)], axis=1
    )
    absorbed = jnp.dot(
        spread, w_ref[...].reshape(heads * NOPE, LATENT), preferred_element_type=jnp.float32
    ).astype(jnp.bfloat16)
    for k in range(per_device):
        home_made = leaves_as(k, lax.axis_index("head"))
        for n in range(per_device):

            @pl.when(home_made == (n == 0))
            def _():
                outs[k][:, :LATENT] = absorbed[n * piece : (n + 1) * piece]
                outs[k][:, LATENT:] = packed[n][:, NOPE:]


def block_scores(q, refs, starts, limit_ref):
    width = q.shape[1]
    keys = jnp.concatenate([ref[:width, :] for ref in refs], axis=1)
    limit = limit_ref[:1, :]
    lane = lax.broadcasted_iota(jnp.int32, limit.shape, 1)
    visible = jnp.concatenate([lane + start < limit for start in starts], axis=1)
    s = jnp.dot(q, keys, preferred_element_type=jnp.float32) * SCORE_SCALE
    return jnp.where(visible, s, masked_value)


def weigh(s, refs, top):
    w = jnp.exp(s - top)
    values = jnp.concatenate([ref[:LATENT, :] for ref in refs], axis=1)
    out = lax.dot_general(
        w.astype(jnp.bfloat16),
        values,
        (((1,), (1,)), ((), ())),
        preferred_element_type=jnp.float32,
    )
    return jnp.sum(w, axis=1, keepdims=True), out


def begin_kernel(owners, per_device, heads, limit_ref, *refs):
    q_refs, key_refs = refs[:per_device], refs[per_device : per_device + owners]
    q_out, top_ref, total_ref, out_ref = refs[per_device + owners :]
    seq_index = lax.axis_index("seq")
    chip, core = seq_index // COPIES, seq_index % COPIES
    slots = key_refs[0].shape[1]
    width = LATENT + ROPE
    q = jnp.concatenate([ref[:, :width] for ref in q_refs], axis=0)

    fresh = q_refs[0][:, width:].astype(jnp.float32)
    fresh = jnp.concatenate(
        [fresh[n * SPEC : (n + 1) * SPEC] for n in range(width // ROPE)], axis=1
    )
    fresh = jnp.concatenate([fresh, jnp.zeros((16 - SPEC, width), jnp.float32)], axis=0)
    fresh = fresh.astype(jnp.bfloat16)
    f = lax.dot_general(
        q, fresh, (((1,), (1,)), ((), ())), preferred_element_type=jnp.float32
    )
    row = lax.broadcasted_iota(jnp.int32, f.shape, 0) % (SPEC * heads)
    key = lax.broadcasted_iota(jnp.int32, f.shape, 1)
    f = jnp.where(key <= row // heads, f * SCORE_SCALE, masked_value)

    starts = [((chip ^ partner(k, core)) * COPIES + core) * slots for k in range(owners)]
    s = block_scores(q, key_refs, starts, limit_ref)
    top = jnp.maximum(jnp.max(s, axis=1, keepdims=True), jnp.max(f, axis=1, keepdims=True))
    total, out = weigh(s, key_refs, top)
    w = jnp.exp(f - top)
    total += jnp.sum(w, axis=1, keepdims=True)
    out += jnp.dot(
        w.astype(jnp.bfloat16), fresh[:, :LATENT], preferred_element_type=jnp.float32
    )
    q_out[...] = q
    top_ref[...] = jnp.broadcast_to(top, top_ref.shape)
    total_ref[...] = jnp.broadcast_to(total, total_ref.shape)
    out_ref[...] = out


def finish_kernel(
    owners, per_device, limit_ref, q_ref, top_ref, total_ref, part_ref, pair_ref, *refs
):
    key_refs = [pair_ref.at[0], pair_ref.at[1], *refs[: owners - 2]]
    outs = refs[owners - 2 :]
    seq_index = lax.axis_index("seq")
    chip, core = seq_index // COPIES, seq_index % COPIES
    plane = lax.axis_index("head")
    slots = key_refs[0].shape[1]
    starts = [((chip ^ partner(k, 1 - core)) * COPIES + 1 - core) * slots for k in range(owners)]
    s = block_scores(q_ref[...], key_refs, starts, limit_ref)
    first = top_ref[:, :1]
    top = jnp.maximum(first, jnp.max(s, axis=1, keepdims=True))
    total, out = weigh(s, key_refs, top)
    scale = jnp.exp(first - top)
    total += total_ref[:, :1] * scale
    out += part_ref[...] * scale
    out = (out * (1.0 / total)).astype(jnp.bfloat16)
    piece = out.shape[0] // per_device
    sent_first = first_block(plane, chip, core)
    for k in range(per_device):
        for n in range(per_device):

            @pl.when(sent_first ^ k == n)
            def _():
                outs[k][...] = out[n * piece : (n + 1) * piece]


def project_kernel(per_device, w_ref, *refs):
    lat_refs, out_ref = refs[:-1], refs[-1]
    rows, heads, width = out_ref.shape
    first = first_back(lax.axis_index("seq") // COPIES, lax.axis_index("head"))
    parts = [jnp.where(first == a, lat_refs[1][...], lat_refs[0][...]) for a in range(per_device)]
    latent = jnp.concatenate(parts, axis=0)
    out = jnp.zeros((rows * heads, width), jnp.float32)
    own_head = lax.broadcasted_iota(jnp.int32, out.shape, 0) % heads
    step = 2 if heads % 2 == 0 else 1
    for h in range(0, heads, step):
        group = jnp.concatenate([w_ref[h + n] for n in range(step)], axis=1)
        product = jnp.dot(latent, group, preferred_element_type=jnp.float32)
        for n in range(step):
            out = jnp.where(own_head == h + n, product[:, n * width : (n + 1) * width], out)
    out_ref[...] = out.astype(out_ref.dtype).reshape(out_ref.shape)


def whole_sequences(seq_size, head_size, queries, new_latent, cache, lengths, w_uk, w_uv):
    rows, heads, q_width = queries.shape
    owners, slots, width = cache.shape
    per_device = rows // SPEC
    piece = SPEC * heads
    all_rows = per_device * piece
    params = pltpu.CompilerParams(vmem_limit_bytes=VMEM_LIMIT)
    vmem = pl.BlockSpec(memory_space=pltpu.VMEM)
    anywhere = pl.BlockSpec(memory_space=pl.ANY)
    both = ("seq", "head")
    devices = [(i, j) for i in range(seq_size) for j in range(head_size)]

    def flat(seq_index, head_index):
        return seq_index * head_size + head_index

    def in_hbm(x):
        return pltpu.with_memory_space_constraint(x, pltpu.HBM)

    def maker(i, j, k):
        home, row = i // COPIES, i % COPIES
        a = stays(home, row, j // 2)
        if leaves_as(k, j):
            return flat(i, j), a
        return flat((row * per_device + 1 - a) * COPIES + home // 2, j), 1 - a

    def owner(i, j, a):
        plane, chip = i // COPIES, i % COPIES * per_device + a
        return flat(chip * COPIES + 1 - j // 2, plane)

    def in_plane(move):
        return [(g * COPIES + t, move(g, t)) for g in range(owners) for t in range(COPIES)]

    *picked, kept, left, limit = pl.pallas_call(
        functools.partial(pick_kernel, per_device),
        out_shape=[jax.ShapeDtypeStruct((width, slots), cache.dtype)] * owners
        + [jax.ShapeDtypeStruct((piece, q_width + ROPE), queries.dtype)] * per_device
        + [jax.ShapeDtypeStruct((8, slots), jnp.int32)],
        in_specs=[anywhere] * 4,
        out_specs=[vmem] * (owners + per_device + 1),
        scratch_shapes=[
            pltpu.VMEM(queries.shape, queries.dtype),
            pltpu.VMEM(new_latent.shape, new_latent.dtype),
            pltpu.SMEM(lengths.shape, lengths.dtype),
            pltpu.SemaphoreType.DMA((owners + 3,)),
        ],
        compiler_params=params,
        cost_estimate=LONG,
    )(*[in_hbm(x) for x in (jnp.swapaxes(cache, 1, 2), queries, new_latent, lengths)])
    moved = lax.ppermute(
        left, both, [(flat(i, j), maker(i, j, 1 - j % 2)[0]) for i, j in devices]
    )
    own_keys = [picked[0]] + [
        lax.ppermute(picked[k], "seq", in_plane(lambda g, t: (g ^ partner(k, t)) * COPIES + t))
        for k in range(1, owners)
    ]
    pair = pl.pallas_call(
        pair_kernel,
        out_shape=jax.ShapeDtypeStruct((2, *picked[0].shape), cache.dtype),
        in_specs=[vmem] * 2,
        out_specs=vmem,
        scratch_shapes=[pltpu.SemaphoreType.DMA((2,))],
        compiler_params=params,
    )(*own_keys[:2])
    other_core = in_plane(lambda g, t: g * COPIES + 1 - t)
    far_keys = [lax.ppermute(keys, "seq", other_core) for keys in [pair] + own_keys[2:]]

    pieces = pl.pallas_call(
        functools.partial(absorb_kernel, per_device),
        out_shape=[jax.ShapeDtypeStruct((piece, width + ROPE), cache.dtype)] * per_device,
        in_specs=[vmem] * (1 + per_device),
        out_specs=[vmem] * per_device,
        compiler_params=params,
        cost_estimate=LONG,
    )(w_uk, kept, moved)
    arrived = [
        lax.ppermute(
            pieces[k],
            both,
            [
                (source, owner(i, j, a))
                for i, j in devices
                for source, a in [maker(i, j, k)]
            ],
        )
        for k in range(per_device)
    ]

    state = pl.pallas_call(
        functools.partial(begin_kernel, owners, per_device, heads),
        out_shape=[
            jax.ShapeDtypeStruct((all_rows, width), jnp.bfloat16),
            jax.ShapeDtypeStruct((all_rows, 128), jnp.float32),
            jax.ShapeDtypeStruct((all_rows, 128), jnp.float32),
            jax.ShapeDtypeStruct((all_rows, LATENT), jnp.float32),
        ],
        in_specs=[vmem] * (1 + per_device + owners),
        out_specs=[vmem] * 4,
        compiler_params=params,
        cost_estimate=LONG,
    )(limit, *arrived, *own_keys)
    latent = pl.pallas_call(
        functools.partial(finish_kernel, owners, per_device),
        out_shape=[jax.ShapeDtypeStruct((piece, LATENT), jnp.bfloat16)] * per_device,
        in_specs=[vmem] * (1 + len(state) + len(far_keys)),
        out_specs=[vmem] * per_device,
        compiler_params=params,
    )(limit, *state, *far_keys)

    back = [
        lax.ppermute(
            latent[k],
            both,
            [(owner(i, j, first_back(i // COPIES, j) ^ k), flat(i, j)) for i, j in devices],
        )
        for k in range(per_device)
    ]
    return pl.pallas_call(
        functools.partial(project_kernel, per_device),
        out_shape=jax.ShapeDtypeStruct((rows, heads, w_uv.shape[2]), jnp.bfloat16),
        in_specs=[vmem] * (1 + per_device),
        out_specs=vmem,
        compiler_params=params,
    )(w_uv, *back[::-1])


def local_partial(
    query_tile_block,
    key_tile_block,
    incoming_keys,
    len_block,
    offset,
    own_first,
    score_scale,
    head_count,
):
    scores = (
        jnp.einsum(
            "vfa,vja->vfj", query_tile_block, key_tile_block, preferred_element_type=jnp.float32
        )
        * score_scale
    )
    positions = offset + lax.broadcasted_iota(jnp.int32, (1, 1, key_tile_block.shape[1]), 2)
    visible = positions < len_block[:, None, None]
    fresh_scores = (
        jnp.einsum(
            "vfa,vja->vfj", query_tile_block, incoming_keys, preferred_element_type=jnp.float32
        )
        * score_scale
    )
    spec_count = incoming_keys.shape[1]
    row_spec = (
        lax.broadcasted_iota(jnp.int32, (1, query_tile_block.shape[1], spec_count), 1) // head_count
    )
    key_spec = lax.broadcasted_iota(jnp.int32, (1, query_tile_block.shape[1], spec_count), 2)
    causal = (key_spec <= row_spec) & own_first
    row_top = jnp.maximum(
        jnp.max(jnp.where(visible, scores, masked_value), axis=2),
        jnp.max(jnp.where(causal, fresh_scores, masked_value), axis=2),
    )
    weights = jnp.where(visible, jnp.exp(scores - row_top[..., None]), 0.0)
    fresh_weights = jnp.where(causal, jnp.exp(fresh_scores - row_top[..., None]), 0.0)
    running_totals = jnp.sum(weights, axis=2) + jnp.sum(fresh_weights, axis=2)
    weighted = jnp.einsum(
        "mpu,mui->mpi",
        weights.astype(jnp.bfloat16),
        key_tile_block[:, :, :LATENT],
        preferred_element_type=jnp.float32,
    )
    weighted = weighted + jnp.einsum(
        "mpu,mui->mpi",
        fresh_weights.astype(jnp.bfloat16),
        incoming_keys[:, :, :LATENT],
        preferred_element_type=jnp.float32,
    )
    return (row_top, running_totals, weighted)


def project_values(latent_rows, value_weight):
    return jnp.einsum("rhc,hcv->rhv", latent_rows, value_weight, precision=lax.Precision.HIGHEST)


def split_positions(queries, new_latent, cache, lengths, w_uk, w_uv):
    own_rows, head_count, _ = queries.shape
    score_scale = (NOPE + ROPE) ** (-0.5)
    gathered, new_all = (
        lax.all_gather(queries, "seq", axis=0, tiled=True),
        lax.all_gather(new_latent, "seq", axis=0, tiled=True),
    )
    absorbed = jnp.einsum(
        "rhn,hnc->rhc", gathered[:, :, :NOPE], w_uk, preferred_element_type=jnp.float32
    ).astype(jnp.bfloat16)
    q_all = jnp.concatenate([absorbed, gathered[:, :, NOPE:]], axis=2)
    total_rows = q_all.shape[0]
    seq_count = total_rows // SPEC
    query_slots = SPEC * head_count
    q_seq = q_all.reshape(seq_count, query_slots, q_all.shape[2])
    new_seq = new_all.reshape(seq_count, SPEC, new_all.shape[1])
    seq_index = lax.axis_index("seq")
    offset = seq_index * cache.shape[1]
    own_first = seq_index == 0
    row_top, running_totals, weighted = local_partial(
        q_seq,
        lax.all_gather(cache, "head", axis=0, tiled=True),
        new_seq,
        lengths,
        offset,
        own_first,
        score_scale,
        head_count,
    )
    value_weight = w_uv.astype(jnp.float32)
    global_top = lax.pmax(row_top, "seq")
    factor = jnp.exp(row_top - global_top)
    scaled_totals = (running_totals * factor).reshape(total_rows, head_count)
    scaled_weighted = (weighted * factor[..., None]).reshape(total_rows, head_count, LATENT)
    row_totals, row_weighted = (
        lax.psum_scatter(scaled_totals, "seq", scatter_dimension=0, tiled=True),
        lax.psum_scatter(scaled_weighted, "seq", scatter_dimension=0, tiled=True),
    )
    latent_output = row_weighted / row_totals[..., None]
    result = project_values(latent_output, value_weight)
    return result.astype(jnp.bfloat16)


def shards(seq_size, head_size, queries, new_latent, cache, lengths, w_uk, w_uv):
    rows, owners = queries.shape[0], cache.shape[0]
    per_device = rows // SPEC
    if (
        per_device == 2
        and rows % SPEC == 0
        and seq_size == COPIES * owners
        and head_size == owners == 4
    ):
        return whole_sequences(
            seq_size, head_size, queries, new_latent, cache, lengths, w_uk, w_uv
        )
    return split_positions(queries, new_latent, cache, lengths, w_uk, w_uv)


def solution(mesh):
    return jax.shard_map(
        functools.partial(shards, mesh.shape["seq"], mesh.shape["head"]),
        mesh=mesh,
        in_specs=(
            P("seq", "head", None),
            P("seq", None),
            P("head", "seq", None),
            P(),
            P("head", None, None),
            P("head", None, None),
        ),
        out_specs=P("seq", "head", None),
        check_vma=False,
    )
```

```python
import functools

import jax
import jax.numpy as jnp
from jax import lax
from jax.experimental import pallas as pl
from jax.experimental.pallas import tpu as pltpu
from jax.sharding import PartitionSpec as P

NOPE = 128
ROPE = 64
LATENT = 512
SPEC = 4
SCORE_SCALE = (NOPE + ROPE) ** (-0.5)
COPIES = 2
VMEM_LIMIT = 16 * 1024 * 1024
LONG = pl.CostEstimate(flops=2 * 10**10, bytes_accessed=0, transcendentals=0)

masked_value = -1e30


def leaves_as(k, head_shard):
    return head_shard % 2 != k


def stays(home_chip, core, half):
    row = home_chip // 2
    return home_chip % 2 ^ (1 ^ half ^ row) & (row ^ core)


def far_half(plane, pair):
    return 1 * (plane <= 2 * pair)


def first_back(home_chip, head_shard):
    far = 1 * (far_half(home_chip, head_shard // 2) == head_shard % 2)
    return home_chip % 2 ^ far


def first_block(plane, chip, core):
    first = far_half(plane, 1 - core) ^ 1 * (chip % 2 == plane % 2)
    return first ^ 1 * (stays(plane, chip // 2, 1 - core) == chip % 2)


def partner(k, core):
    return (0, 3, 1 ^ 3 * core, 2 ^ 3 * core)[k]


def pick_kernel(per_device, cache_hbm, q_hbm, new_hbm, len_hbm, *refs):
    owners = cache_hbm.shape[0]
    blocks, outs = refs[:owners], refs[owners : owners + per_device]
    limit_ref, q_ref, new_ref, len_ref, sem = refs[owners + per_device :]
    chip, core = lax.axis_index("seq") // COPIES, lax.axis_index("seq") % COPIES
    moves = [
        pltpu.make_async_copy(q_hbm, q_ref, sem.at[owners]),
        pltpu.make_async_copy(new_hbm, new_ref, sem.at[owners + 1]),
        pltpu.make_async_copy(len_hbm, len_ref, sem.at[owners + 2]),
    ] + [
        pltpu.make_async_copy(cache_hbm.at[chip ^ partner(k, core)], blocks[k], sem.at[k])
        for k in range(owners)
    ]
    for move in moves:
        move.start()
    moves[0].wait()
    moves[1].wait()
    heads, width = q_ref.shape[1:]
    fresh = new_ref[...].astype(jnp.float32)
    piece = SPEC * heads
    for a in range(per_device):
        rows = q_ref[a * SPEC : (a + 1) * SPEC].reshape(piece, width)
        own = fresh[a * SPEC : (a + 1) * SPEC]
        parts = [own[:, n : n + ROPE] for n in range(0, own.shape[1], ROPE)]
        spare = piece - SPEC * len(parts)
        if spare:
            parts.append(jnp.zeros((spare, ROPE), jnp.float32))
        own = jnp.concatenate(parts, axis=0).astype(rows.dtype)
        packed = jnp.concatenate([rows, own], axis=1)
        for n, out in enumerate(outs):

            @pl.when(stays(chip, core, lax.axis_index("head") // 2) ^ n == a)
            def _():
                out[...] = packed

    moves[2].wait()
    length = len_ref[lax.axis_index("head") * owners + chip]
    limit_ref[...] = jnp.full(limit_ref.shape, length, limit_ref.dtype)
    for move in moves[3:]:
        move.wait()


def pair_kernel(first_ref, second_ref, out_ref, sem):
    moves = [
        pltpu.make_async_copy(ref, out_ref.at[n], sem.at[n])
        for n, ref in enumerate((first_ref, second_ref))
    ]
    for move in moves:
        move.start()
    for move in moves:
        move.wait()


def absorb_kernel(per_device, w_ref, *refs):
    packed, outs = refs[:per_device], refs[per_device:]
    heads = w_ref.shape[0]
    piece = SPEC * heads
    nope = jnp.concatenate([ref[:, :NOPE] for ref in packed], axis=0)
    own_head = lax.broadcasted_iota(jnp.int32, nope.shape, 0) % heads
    spread = jnp.concatenate(
        [jnp.where(own_head == h, nope, jnp.zeros_like(nope)) for h in range(heads)], axis=1
    )
    absorbed = jnp.dot(
        spread, w_ref[...].reshape(heads * NOPE, LATENT), preferred_element_type=jnp.float32
    ).astype(jnp.bfloat16)
    for k in range(per_device):
        home_made = leaves_as(k, lax.axis_index("head"))
        for n in range(per_device):

            @pl.when(home_made == (n == 0))
            def _():
                outs[k][:, :LATENT] = absorbed[n * piece : (n + 1) * piece]
                outs[k][:, LATENT:] = packed[n][:, NOPE:]


def block_scores(q, refs, starts, limit_ref):
    width = q.shape[1]
    keys = jnp.concatenate([ref[:width, :] for ref in refs], axis=1)
    limit = limit_ref[:1, :]
    lane = lax.broadcasted_iota(jnp.int32, limit.shape, 1)
    visible = jnp.concatenate([lane + start < limit for start in starts], axis=1)
    s = jnp.dot(q, keys, preferred_element_type=jnp.float32) * SCORE_SCALE
    return jnp.where(visible, s, masked_value)


def weigh(s, refs, top):
    w = jnp.exp(s - top)
    values = jnp.concatenate([ref[:LATENT, :] for ref in refs], axis=1)
    out = lax.dot_general(
        w.astype(jnp.bfloat16),
        values,
        (((1,), (1,)), ((), ())),
        preferred_element_type=jnp.float32,
    )
    return jnp.sum(w, axis=1, keepdims=True), out


def begin_kernel(owners, per_device, heads, limit_ref, *refs):
    q_refs, key_refs = refs[:per_device], refs[per_device : per_device + owners]
    q_out, top_ref, total_ref, out_ref = refs[per_device + owners :]
    seq_index = lax.axis_index("seq")
    chip, core = seq_index // COPIES, seq_index % COPIES
    slots = key_refs[0].shape[1]
    width = LATENT + ROPE
    q = jnp.concatenate([ref[:, :width] for ref in q_refs], axis=0)

    fresh = q_refs[0][:, width:].astype(jnp.float32)
    fresh = jnp.concatenate(
        [fresh[n * SPEC : (n + 1) * SPEC] for n in range(width // ROPE)], axis=1
    )
    fresh = jnp.concatenate([fresh, jnp.zeros((16 - SPEC, width), jnp.float32)], axis=0)
    fresh = fresh.astype(jnp.bfloat16)
    f = lax.dot_general(
        q, fresh, (((1,), (1,)), ((), ())), preferred_element_type=jnp.float32
    )
    row = lax.broadcasted_iota(jnp.int32, f.shape, 0) % (SPEC * heads)
    key = lax.broadcasted_iota(jnp.int32, f.shape, 1)
    f = jnp.where(key <= row // heads, f * SCORE_SCALE, masked_value)

    starts = [((chip ^ partner(k, core)) * COPIES + core) * slots for k in range(owners)]
    s = block_scores(q, key_refs, starts, limit_ref)
    top = jnp.maximum(jnp.max(s, axis=1, keepdims=True), jnp.max(f, axis=1, keepdims=True))
    total, out = weigh(s, key_refs, top)
    w = jnp.exp(f - top)
    total += jnp.sum(w, axis=1, keepdims=True)
    out += jnp.dot(
        w.astype(jnp.bfloat16), fresh[:, :LATENT], preferred_element_type=jnp.float32
    )
    q_out[...] = q
    top_ref[...] = jnp.broadcast_to(top, top_ref.shape)
    total_ref[...] = jnp.broadcast_to(total, total_ref.shape)
    out_ref[...] = out


def finish_kernel(
    owners, per_device, limit_ref, q_ref, top_ref, total_ref, part_ref, pair_ref, *refs
):
    key_refs = [pair_ref.at[0], pair_ref.at[1], *refs[: owners - 2]]
    outs = refs[owners - 2 :]
    seq_index = lax.axis_index("seq")
    chip, core = seq_index // COPIES, seq_index % COPIES
    plane = lax.axis_index("head")
    slots = key_refs[0].shape[1]
    starts = [((chip ^ partner(k, 1 - core)) * COPIES + 1 - core) * slots for k in range(owners)]
    s = block_scores(q_ref[...], key_refs, starts, limit_ref)
    first = top_ref[:, :1]
    top = jnp.maximum(first, jnp.max(s, axis=1, keepdims=True))
    total, out = weigh(s, key_refs, top)
    scale = jnp.exp(first - top)
    total += total_ref[:, :1] * scale
    out += part_ref[...] * scale
    out = (out * (1.0 / total)).astype(jnp.bfloat16)
    piece = out.shape[0] // per_device
    sent_first = first_block(plane, chip, core)
    for k in range(per_device):
        for n in range(per_device):

            @pl.when(sent_first ^ k == n)
            def _():
                outs[k][...] = out[n * piece : (n + 1) * piece]


def project_kernel(per_device, w_ref, *refs):
    lat_refs, out_ref = refs[:-1], refs[-1]
    rows, heads, width = out_ref.shape
    first = first_back(lax.axis_index("seq") // COPIES, lax.axis_index("head"))
    parts = [jnp.where(first == a, lat_refs[1][...], lat_refs[0][...]) for a in range(per_device)]
    latent = jnp.concatenate(parts, axis=0)
    out = jnp.zeros((rows * heads, width), jnp.float32)
    own_head = lax.broadcasted_iota(jnp.int32, out.shape, 0) % heads
    step = 2 if heads % 2 == 0 else 1
    for h in range(0, heads, step):
        group = jnp.concatenate([w_ref[h + n] for n in range(step)], axis=1)
        product = jnp.dot(latent, group, preferred_element_type=jnp.float32)
        for n in range(step):
            out = jnp.where(own_head == h + n, product[:, n * width : (n + 1) * width], out)
    out_ref[...] = out.astype(out_ref.dtype).reshape(out_ref.shape)


def whole_sequences(seq_size, head_size, queries, new_latent, cache, lengths, w_uk, w_uv):
    rows, heads, q_width = queries.shape
    owners, slots, width = cache.shape
    per_device = rows // SPEC
    piece = SPEC * heads
    all_rows = per_device * piece
    params = pltpu.CompilerParams(vmem_limit_bytes=VMEM_LIMIT)
    vmem = pl.BlockSpec(memory_space=pltpu.VMEM)
    anywhere = pl.BlockSpec(memory_space=pl.ANY)
    both = ("seq", "head")
    devices = [(i, j) for i in range(seq_size) for j in range(head_size)]

    def flat(seq_index, head_index):
        return seq_index * head_size + head_index

    def in_hbm(x):
        return pltpu.with_memory_space_constraint(x, pltpu.HBM)

    def maker(i, j, k):
        home, row = i // COPIES, i % COPIES
        a = stays(home, row, j // 2)
        if leaves_as(k, j):
            return flat(i, j), a
        return flat((row * per_device + 1 - a) * COPIES + home // 2, j), 1 - a

    def owner(i, j, a):
        plane, chip = i // COPIES, i % COPIES * per_device + a
        return flat(chip * COPIES + 1 - j // 2, plane)

    def in_plane(move):
        return [(g * COPIES + t, move(g, t)) for g in range(owners) for t in range(COPIES)]

    *picked, kept, left, limit = pl.pallas_call(
        functools.partial(pick_kernel, per_device),
        out_shape=[jax.ShapeDtypeStruct((width, slots), cache.dtype)] * owners
        + [jax.ShapeDtypeStruct((piece, q_width + ROPE), queries.dtype)] * per_device
        + [jax.ShapeDtypeStruct((8, slots), jnp.int32)],
        in_specs=[anywhere] * 4,
        out_specs=[vmem] * (owners + per_device + 1),
        scratch_shapes=[
            pltpu.VMEM(queries.shape, queries.dtype),
            pltpu.VMEM(new_latent.shape, new_latent.dtype),
            pltpu.SMEM(lengths.shape, lengths.dtype),
            pltpu.SemaphoreType.DMA((owners + 3,)),
        ],
        compiler_params=params,
        cost_estimate=LONG,
    )(*[in_hbm(x) for x in (jnp.swapaxes(cache, 1, 2), queries, new_latent, lengths)])
    moved = lax.ppermute(
        left, both, [(flat(i, j), maker(i, j, j % 2)[0]) for i, j in devices]
    )
    own_keys = [picked[0]] + [
        lax.ppermute(picked[k], "seq", in_plane(lambda g, t: (g ^ partner(k, t)) * COPIES + t))
        for k in range(1, owners)
    ]
    pair = pl.pallas_call(
        pair_kernel,
        out_shape=jax.ShapeDtypeStruct((2, *picked[0].shape), cache.dtype),
        in_specs=[vmem] * 2,
        out_specs=vmem,
        scratch_shapes=[pltpu.SemaphoreType.DMA((2,))],
        compiler_params=params,
    )(*own_keys[:2])
    other_core = in_plane(lambda g, t: g * COPIES + 1 - t)
    far_keys = [lax.ppermute(keys, "seq", other_core) for keys in [pair] + own_keys[2:]]

    pieces = pl.pallas_call(
        functools.partial(absorb_kernel, per_device),
        out_shape=[jax.ShapeDtypeStruct((piece, width + ROPE), cache.dtype)] * per_device,
        in_specs=[vmem] * (1 + per_device),
        out_specs=[vmem] * per_device,
        compiler_params=params,
        cost_estimate=LONG,
    )(w_uk, kept, moved)
    arrived = [
        lax.ppermute(
            pieces[k],
            both,
            [
                (source, owner(i, j, a))
                for i, j in devices
                for source, a in [maker(i, j, k)]
            ],
        )
        for k in range(per_device)
    ]

    state = pl.pallas_call(
        functools.partial(begin_kernel, owners, per_device, heads),
        out_shape=[
            jax.ShapeDtypeStruct((all_rows, width), jnp.bfloat16),
            jax.ShapeDtypeStruct((all_rows, 128), jnp.float32),
            jax.ShapeDtypeStruct((all_rows, 128), jnp.float32),
            jax.ShapeDtypeStruct((all_rows, LATENT), jnp.float32),
        ],
        in_specs=[vmem] * (1 + per_device + owners),
        out_specs=[vmem] * 4,
        compiler_params=params,
        cost_estimate=LONG,
    )(limit, *arrived, *own_keys)
    latent = pl.pallas_call(
        functools.partial(finish_kernel, owners, per_device),
        out_shape=[jax.ShapeDtypeStruct((piece, LATENT), jnp.bfloat16)] * per_device,
        in_specs=[vmem] * (1 + len(state) + len(far_keys)),
        out_specs=[vmem] * per_device,
        compiler_params=params,
    )(limit, *state, *far_keys)

    back = [
        lax.ppermute(
            latent[k],
            both,
            [(owner(i, j, first_back(i // COPIES, j) ^ k), flat(i, j)) for i, j in devices],
        )
        for k in range(per_device)
    ]
    return pl.pallas_call(
        functools.partial(project_kernel, per_device),
        out_shape=jax.ShapeDtypeStruct((rows, heads, w_uv.shape[2]), jnp.bfloat16),
        in_specs=[vmem] * (1 + per_device),
        out_specs=vmem,
        compiler_params=params,
    )(w_uv, *back[::-1])


def local_partial(
    query_tile_block,
    key_tile_block,
    incoming_keys,
    len_block,
    offset,
    own_first,
    score_scale,
    head_count,
):
    scores = (
        jnp.einsum(
            "vfa,vja->vfj", query_tile_block, key_tile_block, preferred_element_type=jnp.float32
        )
        * score_scale
    )
    positions = offset + lax.broadcasted_iota(jnp.int32, (1, 1, key_tile_block.shape[1]), 2)
    visible = positions < len_block[:, None, None]
    fresh_scores = (
        jnp.einsum(
            "vfa,vja->vfj", query_tile_block, incoming_keys, preferred_element_type=jnp.float32
        )
        * score_scale
    )
    spec_count = incoming_keys.shape[1]
    row_spec = (
        lax.broadcasted_iota(jnp.int32, (1, query_tile_block.shape[1], spec_count), 1) // head_count
    )
    key_spec = lax.broadcasted_iota(jnp.int32, (1, query_tile_block.shape[1], spec_count), 2)
    causal = (key_spec <= row_spec) & own_first
    row_top = jnp.maximum(
        jnp.max(jnp.where(visible, scores, masked_value), axis=2),
        jnp.max(jnp.where(causal, fresh_scores, masked_value), axis=2),
    )
    weights = jnp.where(visible, jnp.exp(scores - row_top[..., None]), 0.0)
    fresh_weights = jnp.where(causal, jnp.exp(fresh_scores - row_top[..., None]), 0.0)
    running_totals = jnp.sum(weights, axis=2) + jnp.sum(fresh_weights, axis=2)
    weighted = jnp.einsum(
        "mpu,mui->mpi",
        weights.astype(jnp.bfloat16),
        key_tile_block[:, :, :LATENT],
        preferred_element_type=jnp.float32,
    )
    weighted = weighted + jnp.einsum(
        "mpu,mui->mpi",
        fresh_weights.astype(jnp.bfloat16),
        incoming_keys[:, :, :LATENT],
        preferred_element_type=jnp.float32,
    )
    return (row_top, running_totals, weighted)


def project_values(latent_rows, value_weight):
    return jnp.einsum("rhc,hcv->rhv", latent_rows, value_weight, precision=lax.Precision.HIGHEST)


def split_positions(queries, new_latent, cache, lengths, w_uk, w_uv):
    own_rows, head_count, _ = queries.shape
    score_scale = (NOPE + ROPE) ** (-0.5)
    gathered, new_all = (
        lax.all_gather(queries, "seq", axis=0, tiled=True),
        lax.all_gather(new_latent, "seq", axis=0, tiled=True),
    )
    absorbed = jnp.einsum(
        "rhn,hnc->rhc", gathered[:, :, :NOPE], w_uk, preferred_element_type=jnp.float32
    ).astype(jnp.bfloat16)
    q_all = jnp.concatenate([absorbed, gathered[:, :, NOPE:]], axis=2)
    total_rows = q_all.shape[0]
    seq_count = total_rows // SPEC
    query_slots = SPEC * head_count
    q_seq = q_all.reshape(seq_count, query_slots, q_all.shape[2])
    new_seq = new_all.reshape(seq_count, SPEC, new_all.shape[1])
    seq_index = lax.axis_index("seq")
    offset = seq_index * cache.shape[1]
    own_first = seq_index == 0
    row_top, running_totals, weighted = local_partial(
        q_seq,
        lax.all_gather(cache, "head", axis=0, tiled=True),
        new_seq,
        lengths,
        offset,
        own_first,
        score_scale,
        head_count,
    )
    value_weight = w_uv.astype(jnp.float32)
    global_top = lax.pmax(row_top, "seq")
    factor = jnp.exp(row_top - global_top)
    scaled_totals = (running_totals * factor).reshape(total_rows, head_count)
    scaled_weighted = (weighted * factor[..., None]).reshape(total_rows, head_count, LATENT)
    row_totals, row_weighted = (
        lax.psum_scatter(scaled_totals, "seq", scatter_dimension=0, tiled=True),
        lax.psum_scatter(scaled_weighted, "seq", scatter_dimension=0, tiled=True),
    )
    latent_output = row_weighted / row_totals[..., None]
    result = project_values(latent_output, value_weight)
    return result.astype(jnp.bfloat16)


def shards(seq_size, head_size, queries, new_latent, cache, lengths, w_uk, w_uv):
    rows, owners = queries.shape[0], cache.shape[0]
    per_device = rows // SPEC
    if (
        per_device == 2
        and rows % SPEC == 0
        and seq_size == COPIES * owners
        and head_size == owners == 4
    ):
        return whole_sequences(
            seq_size, head_size, queries, new_latent, cache, lengths, w_uk, w_uv
        )
    return split_positions(queries, new_latent, cache, lengths, w_uk, w_uv)


def solution(mesh):
    return jax.shard_map(
        functools.partial(shards, mesh.shape["seq"], mesh.shape["head"]),
        mesh=mesh,
        in_specs=(
            P("seq", "head", None),
            P("seq", None),
            P("head", "seq", None),
            P(),
            P("head", None, None),
            P("head", None, None),
        ),
        out_specs=P("seq", "head", None),
        check_vma=False,
    )
```

```python
import functools

import jax
import jax.numpy as jnp
from jax import lax
from jax.experimental import pallas as pl
from jax.experimental.pallas import tpu as pltpu
from jax.sharding import PartitionSpec as P

NOPE = 128
ROPE = 64
LATENT = 512
SPEC = 4
SCORE_SCALE = (NOPE + ROPE) ** (-0.5)
COPIES = 2
VMEM_LIMIT = 16 * 1024 * 1024
LONG = pl.CostEstimate(flops=2 * 10**10, bytes_accessed=0, transcendentals=0)

masked_value = -1e30


def leaves_as(k, head_shard):
    return (k + head_shard) % 2


def far_half(plane, pair):
    return 1 * (plane <= 2 * pair)


def first_back(home_chip, head_shard):
    far = 1 * (far_half(home_chip, head_shard // 2) == head_shard % 2)
    return home_chip % 2 ^ far


def first_block(plane, chip, core):
    near = 1 * (chip % 2 == plane % 2)
    return far_half(plane, 1 - core) ^ near ^ chip % 2


def partner(k, core):
    return (0, 3, 2 ^ 3 * core, 1 ^ 3 * core)[k]


def pick_kernel(per_device, cache_hbm, q_hbm, new_hbm, len_hbm, *refs):
    owners = cache_hbm.shape[0]
    blocks, (out_ref, limit_ref, q_ref, new_ref, len_ref, sem) = refs[:owners], refs[owners:]
    chip, core = lax.axis_index("seq") // COPIES, lax.axis_index("seq") % COPIES
    moves = [
        pltpu.make_async_copy(q_hbm, q_ref, sem.at[owners]),
        pltpu.make_async_copy(new_hbm, new_ref, sem.at[owners + 1]),
        pltpu.make_async_copy(len_hbm, len_ref, sem.at[owners + 2]),
    ] + [
        pltpu.make_async_copy(cache_hbm.at[chip ^ partner(k, core)], blocks[k], sem.at[k])
        for k in range(owners)
    ]
    for move in moves:
        move.start()
    moves[0].wait()
    moves[1].wait()
    heads, width = q_ref.shape[1:]
    fresh = new_ref[...].astype(jnp.float32)
    piece = SPEC * heads
    for a in range(per_device):
        rows = q_ref[a * SPEC : (a + 1) * SPEC].reshape(piece, width)
        own = fresh[a * SPEC : (a + 1) * SPEC]
        parts = [own[:, n : n + ROPE] for n in range(0, own.shape[1], ROPE)]
        spare = piece - SPEC * len(parts)
        if spare:
            parts.append(jnp.zeros((spare, ROPE), jnp.float32))
        own = jnp.concatenate(parts, axis=0).astype(rows.dtype)
        out_ref[a * piece : (a + 1) * piece] = jnp.concatenate([rows, own], axis=1)
    moves[2].wait()
    length = len_ref[lax.axis_index("head") * owners + chip]
    limit_ref[...] = jnp.full(limit_ref.shape, length, limit_ref.dtype)
    for move in moves[3:]:
        move.wait()


def pair_kernel(first_ref, second_ref, out_ref, sem):
    moves = [
        pltpu.make_async_copy(ref, out_ref.at[n], sem.at[n])
        for n, ref in enumerate((first_ref, second_ref))
    ]
    for move in moves:
        move.start()
    for move in moves:
        move.wait()


def absorb_kernel(per_device, w_ref, packed_ref, *outs):
    heads = w_ref.shape[0]
    piece = SPEC * heads
    nope = packed_ref[:, :NOPE]
    own_head = lax.broadcasted_iota(jnp.int32, nope.shape, 0) % heads
    spread = jnp.concatenate(
        [jnp.where(own_head == h, nope, jnp.zeros_like(nope)) for h in range(heads)], axis=1
    )
    absorbed = jnp.dot(
        spread, w_ref[...].reshape(heads * NOPE, LATENT), preferred_element_type=jnp.float32
    ).astype(jnp.bfloat16)
    for k in range(per_device):
        which = leaves_as(k, lax.axis_index("head"))
        for a in range(per_device):

            @pl.when(which == a)
            def _():
                rows = slice(a * piece, (a + 1) * piece)
                outs[k][:, :LATENT] = absorbed[rows]
                outs[k][:, LATENT:] = packed_ref[rows, NOPE:]


def block_scores(q, refs, starts, limit_ref):
    width = q.shape[1]
    keys = jnp.concatenate([ref[:width, :] for ref in refs], axis=1)
    limit = limit_ref[:1, :]
    lane = lax.broadcasted_iota(jnp.int32, limit.shape, 1)
    visible = jnp.concatenate([lane + start < limit for start in starts], axis=1)
    s = jnp.dot(q, keys, preferred_element_type=jnp.float32) * SCORE_SCALE
    return jnp.where(visible, s, masked_value)


def weigh(s, refs, top):
    w = jnp.exp(s - top)
    values = jnp.concatenate([ref[:LATENT, :] for ref in refs], axis=1)
    out = lax.dot_general(
        w.astype(jnp.bfloat16),
        values,
        (((1,), (1,)), ((), ())),
        preferred_element_type=jnp.float32,
    )
    return jnp.sum(w, axis=1, keepdims=True), out


def begin_kernel(owners, per_device, heads, limit_ref, *refs):
    q_refs, key_refs = refs[:per_device], refs[per_device : per_device + owners]
    q_out, top_ref, total_ref, out_ref = refs[per_device + owners :]
    seq_index = lax.axis_index("seq")
    chip, core = seq_index // COPIES, seq_index % COPIES
    slots = key_refs[0].shape[1]
    width = LATENT + ROPE
    q = jnp.concatenate([ref[:, :width] for ref in q_refs], axis=0)

    fresh = q_refs[0][:, width:].astype(jnp.float32)
    fresh = jnp.concatenate(
        [fresh[n * SPEC : (n + 1) * SPEC] for n in range(width // ROPE)], axis=1
    )
    fresh = jnp.concatenate([fresh, jnp.zeros((16 - SPEC, width), jnp.float32)], axis=0)
    fresh = fresh.astype(jnp.bfloat16)
    f = lax.dot_general(
        q, fresh, (((1,), (1,)), ((), ())), preferred_element_type=jnp.float32
    )
    row = lax.broadcasted_iota(jnp.int32, f.shape, 0) % (SPEC * heads)
    key = lax.broadcasted_iota(jnp.int32, f.shape, 1)
    f = jnp.where(key <= row // heads, f * SCORE_SCALE, masked_value)

    starts = [((chip ^ partner(k, core)) * COPIES + core) * slots for k in range(owners)]
    s = block_scores(q, key_refs, starts, limit_ref)
    top = jnp.maximum(jnp.max(s, axis=1, keepdims=True), jnp.max(f, axis=1, keepdims=True))
    total, out = weigh(s, key_refs, top)
    w = jnp.exp(f - top)
    total += jnp.sum(w, axis=1, keepdims=True)
    out += jnp.dot(
        w.astype(jnp.bfloat16), fresh[:, :LATENT], preferred_element_type=jnp.float32
    )
    q_out[...] = q
    top_ref[...] = jnp.broadcast_to(top, top_ref.shape)
    total_ref[...] = jnp.broadcast_to(total, total_ref.shape)
    out_ref[...] = out


def finish_kernel(
    owners, per_device, limit_ref, q_ref, top_ref, total_ref, part_ref, pair_ref, *refs
):
    key_refs = [pair_ref.at[0], pair_ref.at[1], *refs[: owners - 2]]
    outs = refs[owners - 2 :]
    seq_index = lax.axis_index("seq")
    chip, core = seq_index // COPIES, seq_index % COPIES
    plane = lax.axis_index("head")
    slots = key_refs[0].shape[1]
    starts = [((chip ^ partner(k, 1 - core)) * COPIES + 1 - core) * slots for k in range(owners)]
    s = block_scores(q_ref[...], key_refs, starts, limit_ref)
    first = top_ref[:, :1]
    top = jnp.maximum(first, jnp.max(s, axis=1, keepdims=True))
    total, out = weigh(s, key_refs, top)
    scale = jnp.exp(first - top)
    total += total_ref[:, :1] * scale
    out += part_ref[...] * scale
    out = (out * (1.0 / total)).astype(jnp.bfloat16)
    piece = out.shape[0] // per_device
    sent_first = first_block(plane, chip, core)
    for k in range(per_device):
        for n in range(per_device):

            @pl.when(sent_first ^ k == n)
            def _():
                outs[k][...] = out[n * piece : (n + 1) * piece]


def project_kernel(per_device, w_ref, *refs):
    lat_refs, out_ref = refs[:-1], refs[-1]
    rows, heads, width = out_ref.shape
    first = first_back(lax.axis_index("seq") // COPIES, lax.axis_index("head"))
    parts = [jnp.where(first == a, lat_refs[1][...], lat_refs[0][...]) for a in range(per_device)]
    latent = jnp.concatenate(parts, axis=0)
    out = jnp.zeros((rows * heads, width), jnp.float32)
    own_head = lax.broadcasted_iota(jnp.int32, out.shape, 0) % heads
    step = 2 if heads % 2 == 0 else 1
    for h in range(0, heads, step):
        group = jnp.concatenate([w_ref[h + n] for n in range(step)], axis=1)
        product = jnp.dot(latent, group, preferred_element_type=jnp.float32)
        for n in range(step):
            out = jnp.where(own_head == h + n, product[:, n * width : (n + 1) * width], out)
    out_ref[...] = out.astype(out_ref.dtype).reshape(out_ref.shape)


def whole_sequences(seq_size, head_size, queries, new_latent, cache, lengths, w_uk, w_uv):
    rows, heads, q_width = queries.shape
    owners, slots, width = cache.shape
    per_device = rows // SPEC
    piece = SPEC * heads
    all_rows = per_device * piece
    params = pltpu.CompilerParams(vmem_limit_bytes=VMEM_LIMIT)
    vmem = pl.BlockSpec(memory_space=pltpu.VMEM)
    anywhere = pl.BlockSpec(memory_space=pl.ANY)
    both = ("seq", "head")
    devices = [(i, j) for i in range(seq_size) for j in range(head_size)]

    def flat(seq_index, head_index):
        return seq_index * head_size + head_index

    def in_hbm(x):
        return pltpu.with_memory_space_constraint(x, pltpu.HBM)

    def host(i, j):
        other = (i // COPIES) ^ (2 - ((j ^ (j >> 1)) & 1))
        return flat(((i % COPIES) * 2 + other // 2) * COPIES + other % 2, j)

    def owner(i, j, a):
        plane, chip = i // COPIES, i % COPIES * per_device + a
        return flat(chip * COPIES + 1 - j // 2, plane)

    def in_plane(move):
        return [(g * COPIES + t, move(g, t)) for g in range(owners) for t in range(COPIES)]

    *picked, packed, limit = pl.pallas_call(
        functools.partial(pick_kernel, per_device),
        out_shape=[jax.ShapeDtypeStruct((width, slots), cache.dtype)] * owners
        + [
            jax.ShapeDtypeStruct((all_rows, q_width + ROPE), queries.dtype),
            jax.ShapeDtypeStruct((8, slots), jnp.int32),
        ],
        in_specs=[anywhere] * 4,
        out_specs=[vmem] * (owners + 2),
        scratch_shapes=[
            pltpu.VMEM(queries.shape, queries.dtype),
            pltpu.VMEM(new_latent.shape, new_latent.dtype),
            pltpu.SMEM(lengths.shape, lengths.dtype),
            pltpu.SemaphoreType.DMA((owners + 3,)),
        ],
        compiler_params=params,
        cost_estimate=LONG,
    )(*[in_hbm(x) for x in (jnp.swapaxes(cache, 1, 2), queries, new_latent, lengths)])
    moved = lax.ppermute(packed, both, [(flat(i, j), host(i, j)) for i, j in devices])
    own_keys = [picked[0]] + [
        lax.ppermute(picked[k], "seq", in_plane(lambda g, t: (g ^ partner(k, t)) * COPIES + t))
        for k in range(1, owners)
    ]
    pair = pl.pallas_call(
        pair_kernel,
        out_shape=jax.ShapeDtypeStruct((2, *picked[0].shape), cache.dtype),
        in_specs=[vmem] * 2,
        out_specs=vmem,
        scratch_shapes=[pltpu.SemaphoreType.DMA((2,))],
        compiler_params=params,
    )(*own_keys[:2])
    other_core = in_plane(lambda g, t: g * COPIES + 1 - t)
    far_keys = [lax.ppermute(keys, "seq", other_core) for keys in [pair] + own_keys[2:]]

    pieces = pl.pallas_call(
        functools.partial(absorb_kernel, per_device),
        out_shape=[jax.ShapeDtypeStruct((piece, width + ROPE), cache.dtype)] * per_device,
        in_specs=[vmem] * 2,
        out_specs=[vmem] * per_device,
        compiler_params=params,
        cost_estimate=LONG,
    )(w_uk, moved)
    arrived = [
        lax.ppermute(
            pieces[k],
            both,
            [(host(i, j), owner(i, j, leaves_as(k, j))) for i, j in devices],
        )
        for k in range(per_device)
    ]

    state = pl.pallas_call(
        functools.partial(begin_kernel, owners, per_device, heads),
        out_shape=[
            jax.ShapeDtypeStruct((all_rows, width), jnp.bfloat16),
            jax.ShapeDtypeStruct((all_rows, 128), jnp.float32),
            jax.ShapeDtypeStruct((all_rows, 128), jnp.float32),
            jax.ShapeDtypeStruct((all_rows, LATENT), jnp.float32),
        ],
        in_specs=[vmem] * (1 + per_device + owners),
        out_specs=[vmem] * 4,
        compiler_params=params,
        cost_estimate=LONG,
    )(limit, *arrived, *own_keys)
    latent = pl.pallas_call(
        functools.partial(finish_kernel, owners, per_device),
        out_shape=[jax.ShapeDtypeStruct((piece, LATENT), jnp.bfloat16)] * per_device,
        in_specs=[vmem] * (1 + len(state) + len(far_keys)),
        out_specs=[vmem] * per_device,
        compiler_params=params,
    )(limit, *state, *far_keys)

    back = [
        lax.ppermute(
            latent[k],
            both,
            [(owner(i, j, first_back(i // COPIES, j) ^ k), flat(i, j)) for i, j in devices],
        )
        for k in range(per_device)
    ]
    return pl.pallas_call(
        functools.partial(project_kernel, per_device),
        out_shape=jax.ShapeDtypeStruct((rows, heads, w_uv.shape[2]), jnp.bfloat16),
        in_specs=[vmem] * (1 + per_device),
        out_specs=vmem,
        compiler_params=params,
    )(w_uv, *back[::-1])


def local_partial(
    query_tile_block,
    key_tile_block,
    incoming_keys,
    len_block,
    offset,
    own_first,
    score_scale,
    head_count,
):
    scores = (
        jnp.einsum(
            "vfa,vja->vfj", query_tile_block, key_tile_block, preferred_element_type=jnp.float32
        )
        * score_scale
    )
    positions = offset + lax.broadcasted_iota(jnp.int32, (1, 1, key_tile_block.shape[1]), 2)
    visible = positions < len_block[:, None, None]
    fresh_scores = (
        jnp.einsum(
            "vfa,vja->vfj", query_tile_block, incoming_keys, preferred_element_type=jnp.float32
        )
        * score_scale
    )
    spec_count = incoming_keys.shape[1]
    row_spec = (
        lax.broadcasted_iota(jnp.int32, (1, query_tile_block.shape[1], spec_count), 1) // head_count
    )
    key_spec = lax.broadcasted_iota(jnp.int32, (1, query_tile_block.shape[1], spec_count), 2)
    causal = (key_spec <= row_spec) & own_first
    row_top = jnp.maximum(
        jnp.max(jnp.where(visible, scores, masked_value), axis=2),
        jnp.max(jnp.where(causal, fresh_scores, masked_value), axis=2),
    )
    weights = jnp.where(visible, jnp.exp(scores - row_top[..., None]), 0.0)
    fresh_weights = jnp.where(causal, jnp.exp(fresh_scores - row_top[..., None]), 0.0)
    running_totals = jnp.sum(weights, axis=2) + jnp.sum(fresh_weights, axis=2)
    weighted = jnp.einsum(
        "mpu,mui->mpi",
        weights.astype(jnp.bfloat16),
        key_tile_block[:, :, :LATENT],
        preferred_element_type=jnp.float32,
    )
    weighted = weighted + jnp.einsum(
        "mpu,mui->mpi",
        fresh_weights.astype(jnp.bfloat16),
        incoming_keys[:, :, :LATENT],
        preferred_element_type=jnp.float32,
    )
    return (row_top, running_totals, weighted)


def project_values(latent_rows, value_weight):
    return jnp.einsum("rhc,hcv->rhv", latent_rows, value_weight, precision=lax.Precision.HIGHEST)


def split_positions(queries, new_latent, cache, lengths, w_uk, w_uv):
    own_rows, head_count, _ = queries.shape
    score_scale = (NOPE + ROPE) ** (-0.5)
    gathered, new_all = (
        lax.all_gather(queries, "seq", axis=0, tiled=True),
        lax.all_gather(new_latent, "seq", axis=0, tiled=True),
    )
    absorbed = jnp.einsum(
        "rhn,hnc->rhc", gathered[:, :, :NOPE], w_uk, preferred_element_type=jnp.float32
    ).astype(jnp.bfloat16)
    q_all = jnp.concatenate([absorbed, gathered[:, :, NOPE:]], axis=2)
    total_rows = q_all.shape[0]
    seq_count = total_rows // SPEC
    query_slots = SPEC * head_count
    q_seq = q_all.reshape(seq_count, query_slots, q_all.shape[2])
    new_seq = new_all.reshape(seq_count, SPEC, new_all.shape[1])
    seq_index = lax.axis_index("seq")
    offset = seq_index * cache.shape[1]
    own_first = seq_index == 0
    row_top, running_totals, weighted = local_partial(
        q_seq,
        lax.all_gather(cache, "head", axis=0, tiled=True),
        new_seq,
        lengths,
        offset,
        own_first,
        score_scale,
        head_count,
    )
    value_weight = w_uv.astype(jnp.float32)
    global_top = lax.pmax(row_top, "seq")
    factor = jnp.exp(row_top - global_top)
    scaled_totals = (running_totals * factor).reshape(total_rows, head_count)
    scaled_weighted = (weighted * factor[..., None]).reshape(total_rows, head_count, LATENT)
    row_totals, row_weighted = (
        lax.psum_scatter(scaled_totals, "seq", scatter_dimension=0, tiled=True),
        lax.psum_scatter(scaled_weighted, "seq", scatter_dimension=0, tiled=True),
    )
    latent_output = row_weighted / row_totals[..., None]
    result = project_values(latent_output, value_weight)
    return result.astype(jnp.bfloat16)


def shards(seq_size, head_size, queries, new_latent, cache, lengths, w_uk, w_uv):
    rows, owners = queries.shape[0], cache.shape[0]
    per_device = rows // SPEC
    if (
        per_device == 2
        and rows % SPEC == 0
        and seq_size == COPIES * owners
        and head_size == owners == 4
    ):
        return whole_sequences(
            seq_size, head_size, queries, new_latent, cache, lengths, w_uk, w_uv
        )
    return split_positions(queries, new_latent, cache, lengths, w_uk, w_uv)


def solution(mesh):
    return jax.shard_map(
        functools.partial(shards, mesh.shape["seq"], mesh.shape["head"]),
        mesh=mesh,
        in_specs=(
            P("seq", "head", None),
            P("seq", None),
            P("head", "seq", None),
            P(),
            P("head", None, None),
            P("head", None, None),
        ),
        out_specs=P("seq", "head", None),
        check_vma=False,
    )
```

```python
import functools

import jax
import jax.numpy as jnp
from jax import lax
from jax.experimental import pallas as pl
from jax.experimental.pallas import tpu as pltpu
from jax.sharding import PartitionSpec as P

NOPE = 128
ROPE = 64
LATENT = 512
SPEC = 4
SCORE_SCALE = (NOPE + ROPE) ** (-0.5)
COPIES = 2
VMEM_LIMIT = 16 * 1024 * 1024
LONG = pl.CostEstimate(flops=2 * 10**10, bytes_accessed=0, transcendentals=0)

masked_value = -1e30


def leaves_as(k, head_shard):
    return (k + head_shard + 1) % 2


def far_half(plane, pair):
    return 1 * (plane <= 2 * pair)


def first_back(home_chip, head_shard):
    far = 1 * (far_half(home_chip, head_shard // 2) == head_shard % 2)
    return home_chip % 2 ^ far


def first_block(plane, chip, core):
    near = 1 * (chip % 2 == plane % 2)
    return far_half(plane, 1 - core) ^ near ^ 1 - chip % 2


def partner(k, core):
    return (0, 3, 1 ^ 3 * core, 2 ^ 3 * core)[k]


def pick_kernel(per_device, cache_hbm, q_hbm, new_hbm, len_hbm, *refs):
    owners = cache_hbm.shape[0]
    blocks, (out_ref, limit_ref, q_ref, new_ref, len_ref, sem) = refs[:owners], refs[owners:]
    chip, core = lax.axis_index("seq") // COPIES, lax.axis_index("seq") % COPIES
    moves = [
        pltpu.make_async_copy(q_hbm, q_ref, sem.at[owners]),
        pltpu.make_async_copy(new_hbm, new_ref, sem.at[owners + 1]),
        pltpu.make_async_copy(len_hbm, len_ref, sem.at[owners + 2]),
    ] + [
        pltpu.make_async_copy(cache_hbm.at[chip ^ partner(k, core)], blocks[k], sem.at[k])
        for k in range(owners)
    ]
    for move in moves:
        move.start()
    moves[0].wait()
    moves[1].wait()
    heads, width = q_ref.shape[1:]
    fresh = new_ref[...].astype(jnp.float32)
    piece = SPEC * heads
    for a in range(per_device):
        rows = q_ref[a * SPEC : (a + 1) * SPEC].reshape(piece, width)
        own = fresh[a * SPEC : (a + 1) * SPEC]
        parts = [own[:, n : n + ROPE] for n in range(0, own.shape[1], ROPE)]
        spare = piece - SPEC * len(parts)
        if spare:
            parts.append(jnp.zeros((spare, ROPE), jnp.float32))
        own = jnp.concatenate(parts, axis=0).astype(rows.dtype)
        out_ref[a * piece : (a + 1) * piece] = jnp.concatenate([rows, own], axis=1)
    moves[2].wait()
    length = len_ref[lax.axis_index("head") * owners + chip]
    limit_ref[...] = jnp.full(limit_ref.shape, length, limit_ref.dtype)
    for move in moves[3:]:
        move.wait()


def pair_kernel(first_ref, second_ref, out_ref, sem):
    moves = [
        pltpu.make_async_copy(ref, out_ref.at[n], sem.at[n])
        for n, ref in enumerate((first_ref, second_ref))
    ]
    for move in moves:
        move.start()
    for move in moves:
        move.wait()


def absorb_kernel(per_device, w_ref, packed_ref, *outs):
    heads = w_ref.shape[0]
    piece = SPEC * heads
    nope = packed_ref[:, :NOPE]
    own_head = lax.broadcasted_iota(jnp.int32, nope.shape, 0) % heads
    spread = jnp.concatenate(
        [jnp.where(own_head == h, nope, jnp.zeros_like(nope)) for h in range(heads)], axis=1
    )
    absorbed = jnp.dot(
        spread, w_ref[...].reshape(heads * NOPE, LATENT), preferred_element_type=jnp.float32
    ).astype(jnp.bfloat16)
    for k in range(per_device):
        which = leaves_as(k, lax.axis_index("head"))
        for a in range(per_device):

            @pl.when(which == a)
            def _():
                rows = slice(a * piece, (a + 1) * piece)
                outs[k][:, :LATENT] = absorbed[rows]
                outs[k][:, LATENT:] = packed_ref[rows, NOPE:]


def block_scores(q, refs, starts, limit_ref):
    width = q.shape[1]
    keys = jnp.concatenate([ref[:width, :] for ref in refs], axis=1)
    limit = limit_ref[:1, :]
    lane = lax.broadcasted_iota(jnp.int32, limit.shape, 1)
    visible = jnp.concatenate([lane + start < limit for start in starts], axis=1)
    s = jnp.dot(q, keys, preferred_element_type=jnp.float32) * SCORE_SCALE
    return jnp.where(visible, s, masked_value)


def weigh(s, refs, top):
    w = jnp.exp(s - top)
    values = jnp.concatenate([ref[:LATENT, :] for ref in refs], axis=1)
    out = lax.dot_general(
        w.astype(jnp.bfloat16),
        values,
        (((1,), (1,)), ((), ())),
        preferred_element_type=jnp.float32,
    )
    return jnp.sum(w, axis=1, keepdims=True), out


def begin_kernel(owners, per_device, heads, limit_ref, *refs):
    q_refs, key_refs = refs[:per_device], refs[per_device : per_device + owners]
    q_out, top_ref, total_ref, out_ref = refs[per_device + owners :]
    seq_index = lax.axis_index("seq")
    chip, core = seq_index // COPIES, seq_index % COPIES
    slots = key_refs[0].shape[1]
    width = LATENT + ROPE
    q = jnp.concatenate([ref[:, :width] for ref in q_refs], axis=0)

    fresh = q_refs[0][:, width:].astype(jnp.float32)
    fresh = jnp.concatenate(
        [fresh[n * SPEC : (n + 1) * SPEC] for n in range(width // ROPE)], axis=1
    )
    fresh = jnp.concatenate([fresh, jnp.zeros((16 - SPEC, width), jnp.float32)], axis=0)
    fresh = fresh.astype(jnp.bfloat16)
    f = lax.dot_general(
        q, fresh, (((1,), (1,)), ((), ())), preferred_element_type=jnp.float32
    )
    row = lax.broadcasted_iota(jnp.int32, f.shape, 0) % (SPEC * heads)
    key = lax.broadcasted_iota(jnp.int32, f.shape, 1)
    f = jnp.where(key <= row // heads, f * SCORE_SCALE, masked_value)

    starts = [((chip ^ partner(k, core)) * COPIES + core) * slots for k in range(owners)]
    s = block_scores(q, key_refs, starts, limit_ref)
    top = jnp.maximum(jnp.max(s, axis=1, keepdims=True), jnp.max(f, axis=1, keepdims=True))
    total, out = weigh(s, key_refs, top)
    w = jnp.exp(f - top)
    total += jnp.sum(w, axis=1, keepdims=True)
    out += jnp.dot(
        w.astype(jnp.bfloat16), fresh[:, :LATENT], preferred_element_type=jnp.float32
    )
    q_out[...] = q
    top_ref[...] = jnp.broadcast_to(top, top_ref.shape)
    total_ref[...] = jnp.broadcast_to(total, total_ref.shape)
    out_ref[...] = out


def finish_kernel(
    owners, per_device, limit_ref, q_ref, top_ref, total_ref, part_ref, pair_ref, *refs
):
    key_refs = [pair_ref.at[0], pair_ref.at[1], *refs[: owners - 2]]
    outs = refs[owners - 2 :]
    seq_index = lax.axis_index("seq")
    chip, core = seq_index // COPIES, seq_index % COPIES
    plane = lax.axis_index("head")
    slots = key_refs[0].shape[1]
    starts = [((chip ^ partner(k, 1 - core)) * COPIES + 1 - core) * slots for k in range(owners)]
    s = block_scores(q_ref[...], key_refs, starts, limit_ref)
    first = top_ref[:, :1]
    top = jnp.maximum(first, jnp.max(s, axis=1, keepdims=True))
    total, out = weigh(s, key_refs, top)
    scale = jnp.exp(first - top)
    total += total_ref[:, :1] * scale
    out += part_ref[...] * scale
    out = (out * (1.0 / total)).astype(jnp.bfloat16)
    piece = out.shape[0] // per_device
    sent_first = first_block(plane, chip, core)
    for k in range(per_device):
        for n in range(per_device):

            @pl.when(sent_first ^ k == n)
            def _():
                outs[k][...] = out[n * piece : (n + 1) * piece]


def project_kernel(per_device, w_ref, *refs):
    lat_refs, out_ref = refs[:-1], refs[-1]
    rows, heads, width = out_ref.shape
    first = first_back(lax.axis_index("seq") // COPIES, lax.axis_index("head"))
    parts = [jnp.where(first == a, lat_refs[1][...], lat_refs[0][...]) for a in range(per_device)]
    latent = jnp.concatenate(parts, axis=0)
    out = jnp.zeros((rows * heads, width), jnp.float32)
    own_head = lax.broadcasted_iota(jnp.int32, out.shape, 0) % heads
    step = 2 if heads % 2 == 0 else 1
    for h in range(0, heads, step):
        group = jnp.concatenate([w_ref[h + n] for n in range(step)], axis=1)
        product = jnp.dot(latent, group, preferred_element_type=jnp.float32)
        for n in range(step):
            out = jnp.where(own_head == h + n, product[:, n * width : (n + 1) * width], out)
    out_ref[...] = out.astype(out_ref.dtype).reshape(out_ref.shape)


def whole_sequences(seq_size, head_size, queries, new_latent, cache, lengths, w_uk, w_uv):
    rows, heads, q_width = queries.shape
    owners, slots, width = cache.shape
    per_device = rows // SPEC
    piece = SPEC * heads
    all_rows = per_device * piece
    params = pltpu.CompilerParams(vmem_limit_bytes=VMEM_LIMIT)
    vmem = pl.BlockSpec(memory_space=pltpu.VMEM)
    anywhere = pl.BlockSpec(memory_space=pl.ANY)
    both = ("seq", "head")
    devices = [(i, j) for i in range(seq_size) for j in range(head_size)]

    def flat(seq_index, head_index):
        return seq_index * head_size + head_index

    def in_hbm(x):
        return pltpu.with_memory_space_constraint(x, pltpu.HBM)

    def host(i, j):
        other = (i // COPIES) ^ (2 - ((j ^ (j >> 1)) & 1))
        return flat(((i % COPIES) * 2 + other // 2) * COPIES + other % 2, j)

    def owner(i, j, a):
        plane, chip = i // COPIES, i % COPIES * per_device + a
        return flat(chip * COPIES + 1 - j // 2, plane)

    def in_plane(move):
        return [(g * COPIES + t, move(g, t)) for g in range(owners) for t in range(COPIES)]

    *picked, packed, limit = pl.pallas_call(
        functools.partial(pick_kernel, per_device),
        out_shape=[jax.ShapeDtypeStruct((width, slots), cache.dtype)] * owners
        + [
            jax.ShapeDtypeStruct((all_rows, q_width + ROPE), queries.dtype),
            jax.ShapeDtypeStruct((8, slots), jnp.int32),
        ],
        in_specs=[anywhere] * 4,
        out_specs=[vmem] * (owners + 2),
        scratch_shapes=[
            pltpu.VMEM(queries.shape, queries.dtype),
            pltpu.VMEM(new_latent.shape, new_latent.dtype),
            pltpu.SMEM(lengths.shape, lengths.dtype),
            pltpu.SemaphoreType.DMA((owners + 3,)),
        ],
        compiler_params=params,
        cost_estimate=LONG,
    )(*[in_hbm(x) for x in (jnp.swapaxes(cache, 1, 2), queries, new_latent, lengths)])
    moved = lax.ppermute(packed, both, [(flat(i, j), host(i, j)) for i, j in devices])
    own_keys = [picked[0]] + [
        lax.ppermute(picked[k], "seq", in_plane(lambda g, t: (g ^ partner(k, t)) * COPIES + t))
        for k in range(1, owners)
    ]
    pair = pl.pallas_call(
        pair_kernel,
        out_shape=jax.ShapeDtypeStruct((2, *picked[0].shape), cache.dtype),
        in_specs=[vmem] * 2,
        out_specs=vmem,
        scratch_shapes=[pltpu.SemaphoreType.DMA((2,))],
        compiler_params=params,
    )(*own_keys[:2])
    other_core = in_plane(lambda g, t: g * COPIES + 1 - t)
    far_keys = [lax.ppermute(keys, "seq", other_core) for keys in [pair] + own_keys[2:]]

    pieces = pl.pallas_call(
        functools.partial(absorb_kernel, per_device),
        out_shape=[jax.ShapeDtypeStruct((piece, width + ROPE), cache.dtype)] * per_device,
        in_specs=[vmem] * 2,
        out_specs=[vmem] * per_device,
        compiler_params=params,
        cost_estimate=LONG,
    )(w_uk, moved)
    arrived = [
        lax.ppermute(
            pieces[k],
            both,
            [(host(i, j), owner(i, j, leaves_as(k, j))) for i, j in devices],
        )
        for k in range(per_device)
    ]

    state = pl.pallas_call(
        functools.partial(begin_kernel, owners, per_device, heads),
        out_shape=[
            jax.ShapeDtypeStruct((all_rows, width), jnp.bfloat16),
            jax.ShapeDtypeStruct((all_rows, 128), jnp.float32),
            jax.ShapeDtypeStruct((all_rows, 128), jnp.float32),
            jax.ShapeDtypeStruct((all_rows, LATENT), jnp.float32),
        ],
        in_specs=[vmem] * (1 + per_device + owners),
        out_specs=[vmem] * 4,
        compiler_params=params,
        cost_estimate=LONG,
    )(limit, *arrived, *own_keys)
    latent = pl.pallas_call(
        functools.partial(finish_kernel, owners, per_device),
        out_shape=[jax.ShapeDtypeStruct((piece, LATENT), jnp.bfloat16)] * per_device,
        in_specs=[vmem] * (1 + len(state) + len(far_keys)),
        out_specs=[vmem] * per_device,
        compiler_params=params,
    )(limit, *state, *far_keys)

    back = [
        lax.ppermute(
            latent[k],
            both,
            [(owner(i, j, first_back(i // COPIES, j) ^ k), flat(i, j)) for i, j in devices],
        )
        for k in range(per_device)
    ]
    return pl.pallas_call(
        functools.partial(project_kernel, per_device),
        out_shape=jax.ShapeDtypeStruct((rows, heads, w_uv.shape[2]), jnp.bfloat16),
        in_specs=[vmem] * (1 + per_device),
        out_specs=vmem,
        compiler_params=params,
    )(w_uv, *back[::-1])


def local_partial(
    query_tile_block,
    key_tile_block,
    incoming_keys,
    len_block,
    offset,
    own_first,
    score_scale,
    head_count,
):
    scores = (
        jnp.einsum(
            "vfa,vja->vfj", query_tile_block, key_tile_block, preferred_element_type=jnp.float32
        )
        * score_scale
    )
    positions = offset + lax.broadcasted_iota(jnp.int32, (1, 1, key_tile_block.shape[1]), 2)
    visible = positions < len_block[:, None, None]
    fresh_scores = (
        jnp.einsum(
            "vfa,vja->vfj", query_tile_block, incoming_keys, preferred_element_type=jnp.float32
        )
        * score_scale
    )
    spec_count = incoming_keys.shape[1]
    row_spec = (
        lax.broadcasted_iota(jnp.int32, (1, query_tile_block.shape[1], spec_count), 1) // head_count
    )
    key_spec = lax.broadcasted_iota(jnp.int32, (1, query_tile_block.shape[1], spec_count), 2)
    causal = (key_spec <= row_spec) & own_first
    row_top = jnp.maximum(
        jnp.max(jnp.where(visible, scores, masked_value), axis=2),
        jnp.max(jnp.where(causal, fresh_scores, masked_value), axis=2),
    )
    weights = jnp.where(visible, jnp.exp(scores - row_top[..., None]), 0.0)
    fresh_weights = jnp.where(causal, jnp.exp(fresh_scores - row_top[..., None]), 0.0)
    running_totals = jnp.sum(weights, axis=2) + jnp.sum(fresh_weights, axis=2)
    weighted = jnp.einsum(
        "mpu,mui->mpi",
        weights.astype(jnp.bfloat16),
        key_tile_block[:, :, :LATENT],
        preferred_element_type=jnp.float32,
    )
    weighted = weighted + jnp.einsum(
        "mpu,mui->mpi",
        fresh_weights.astype(jnp.bfloat16),
        incoming_keys[:, :, :LATENT],
        preferred_element_type=jnp.float32,
    )
    return (row_top, running_totals, weighted)


def project_values(latent_rows, value_weight):
    return jnp.einsum("rhc,hcv->rhv", latent_rows, value_weight, precision=lax.Precision.HIGHEST)


def split_positions(queries, new_latent, cache, lengths, w_uk, w_uv):
    own_rows, head_count, _ = queries.shape
    score_scale = (NOPE + ROPE) ** (-0.5)
    gathered, new_all = (
        lax.all_gather(queries, "seq", axis=0, tiled=True),
        lax.all_gather(new_latent, "seq", axis=0, tiled=True),
    )
    absorbed = jnp.einsum(
        "rhn,hnc->rhc", gathered[:, :, :NOPE], w_uk, preferred_element_type=jnp.float32
    ).astype(jnp.bfloat16)
    q_all = jnp.concatenate([absorbed, gathered[:, :, NOPE:]], axis=2)
    total_rows = q_all.shape[0]
    seq_count = total_rows // SPEC
    query_slots = SPEC * head_count
    q_seq = q_all.reshape(seq_count, query_slots, q_all.shape[2])
    new_seq = new_all.reshape(seq_count, SPEC, new_all.shape[1])
    seq_index = lax.axis_index("seq")
    offset = seq_index * cache.shape[1]
    own_first = seq_index == 0
    row_top, running_totals, weighted = local_partial(
        q_seq,
        lax.all_gather(cache, "head", axis=0, tiled=True),
        new_seq,
        lengths,
        offset,
        own_first,
        score_scale,
        head_count,
    )
    value_weight = w_uv.astype(jnp.float32)
    global_top = lax.pmax(row_top, "seq")
    factor = jnp.exp(row_top - global_top)
    scaled_totals = (running_totals * factor).reshape(total_rows, head_count)
    scaled_weighted = (weighted * factor[..., None]).reshape(total_rows, head_count, LATENT)
    row_totals, row_weighted = (
        lax.psum_scatter(scaled_totals, "seq", scatter_dimension=0, tiled=True),
        lax.psum_scatter(scaled_weighted, "seq", scatter_dimension=0, tiled=True),
    )
    latent_output = row_weighted / row_totals[..., None]
    result = project_values(latent_output, value_weight)
    return result.astype(jnp.bfloat16)


def shards(seq_size, head_size, queries, new_latent, cache, lengths, w_uk, w_uv):
    rows, owners = queries.shape[0], cache.shape[0]
    per_device = rows // SPEC
    if (
        per_device == 2
        and rows % SPEC == 0
        and seq_size == COPIES * owners
        and head_size == owners == 4
    ):
        return whole_sequences(
            seq_size, head_size, queries, new_latent, cache, lengths, w_uk, w_uv
        )
    return split_positions(queries, new_latent, cache, lengths, w_uk, w_uv)


def solution(mesh):
    return jax.shard_map(
        functools.partial(shards, mesh.shape["seq"], mesh.shape["head"]),
        mesh=mesh,
        in_specs=(
            P("seq", "head", None),
            P("seq", None),
            P("head", "seq", None),
            P(),
            P("head", None, None),
            P("head", None, None),
        ),
        out_specs=P("seq", "head", None),
        check_vma=False,
    )
```

```python
import functools

import jax
import jax.numpy as jnp
from jax import lax
from jax.experimental import pallas as pl
from jax.experimental.pallas import tpu as pltpu
from jax.sharding import PartitionSpec as P

NOPE = 128
ROPE = 64
LATENT = 512
SPEC = 4
SCORE_SCALE = (NOPE + ROPE) ** (-0.5)
COPIES = 2
VMEM_LIMIT = 16 * 1024 * 1024
LONG = pl.CostEstimate(flops=2 * 10**10, bytes_accessed=0, transcendentals=0)

masked_value = -1e30


def leaves_as(k, head_shard):
    return (k + head_shard) % 2


def far_half(plane, pair):
    return 1 * (plane <= 2 * pair)


def first_back(home_chip, head_shard):
    far = 1 * (far_half(home_chip, head_shard // 2) == head_shard % 2)
    return home_chip % 2 ^ far


def first_block(plane, chip, core):
    near = 1 * (chip % 2 == plane % 2)
    return far_half(plane, 1 - core) ^ near ^ chip % 2


def partner(k, core):
    return (0, 3, 1 ^ 3 * core, 2 ^ 3 * core)[k]


def pick_kernel(per_device, cache_hbm, q_hbm, new_hbm, len_hbm, *refs):
    owners = cache_hbm.shape[0]
    blocks, (out_ref, limit_ref, q_ref, new_ref, len_ref, sem) = refs[:owners], refs[owners:]
    chip, core = lax.axis_index("seq") // COPIES, lax.axis_index("seq") % COPIES
    moves = [
        pltpu.make_async_copy(cache_hbm.at[chip ^ partner(k, core)], blocks[k], sem.at[k])
        for k in range(owners)
    ]
    small = [
        pltpu.make_async_copy(source, target, sem.at[owners + n])
        for n, (source, target) in enumerate(
            ((q_hbm, q_ref), (new_hbm, new_ref), (len_hbm, len_ref))
        )
    ]
    for move in moves + small:
        move.start()
    small[0].wait()
    small[1].wait()
    heads, width = q_ref.shape[1:]
    fresh = new_ref[...].astype(jnp.float32)
    piece = SPEC * heads
    for a in range(per_device):
        rows = q_ref[a * SPEC : (a + 1) * SPEC].reshape(piece, width)
        own = fresh[a * SPEC : (a + 1) * SPEC]
        parts = [own[:, n : n + ROPE] for n in range(0, own.shape[1], ROPE)]
        spare = piece - SPEC * len(parts)
        if spare:
            parts.append(jnp.zeros((spare, ROPE), jnp.float32))
        own = jnp.concatenate(parts, axis=0).astype(rows.dtype)
        out_ref[a * piece : (a + 1) * piece] = jnp.concatenate([rows, own], axis=1)
    small[2].wait()
    length = len_ref[lax.axis_index("head") * owners + chip]
    limit_ref[...] = jnp.full(limit_ref.shape, length, limit_ref.dtype)
    for move in moves:
        move.wait()


def pair_kernel(first_ref, second_ref, out_ref, sem):
    moves = [
        pltpu.make_async_copy(ref, out_ref.at[n], sem.at[n])
        for n, ref in enumerate((first_ref, second_ref))
    ]
    for move in moves:
        move.start()
    for move in moves:
        move.wait()


def absorb_kernel(per_device, w_ref, packed_ref, *outs):
    heads = w_ref.shape[0]
    piece = SPEC * heads
    nope = packed_ref[:, :NOPE]
    own_head = lax.broadcasted_iota(jnp.int32, nope.shape, 0) % heads
    spread = jnp.concatenate(
        [jnp.where(own_head == h, nope, jnp.zeros_like(nope)) for h in range(heads)], axis=1
    )
    absorbed = jnp.dot(
        spread, w_ref[...].reshape(heads * NOPE, LATENT), preferred_element_type=jnp.float32
    ).astype(jnp.bfloat16)
    for k in range(per_device):
        which = leaves_as(k, lax.axis_index("head"))
        for a in range(per_device):

            @pl.when(which == a)
            def _():
                rows = slice(a * piece, (a + 1) * piece)
                outs[k][:, :LATENT] = absorbed[rows]
                outs[k][:, LATENT:] = packed_ref[rows, NOPE:]


def block_scores(q, refs, starts, limit_ref):
    width = q.shape[1]
    keys = jnp.concatenate([ref[:width, :] for ref in refs], axis=1)
    limit = limit_ref[:1, :]
    lane = lax.broadcasted_iota(jnp.int32, limit.shape, 1)
    visible = jnp.concatenate([lane + start < limit for start in starts], axis=1)
    s = jnp.dot(q, keys, preferred_element_type=jnp.float32) * SCORE_SCALE
    return jnp.where(visible, s, masked_value)


def weigh(s, refs, top):
    w = jnp.exp(s - top)
    values = jnp.concatenate([ref[:LATENT, :] for ref in refs], axis=1)
    out = lax.dot_general(
        w.astype(jnp.bfloat16),
        values,
        (((1,), (1,)), ((), ())),
        preferred_element_type=jnp.float32,
    )
    return jnp.sum(w, axis=1, keepdims=True), out


def begin_kernel(owners, per_device, heads, limit_ref, *refs):
    q_refs, key_refs = refs[:per_device], refs[per_device : per_device + owners]
    q_out, top_ref, total_ref, out_ref = refs[per_device + owners :]
    seq_index = lax.axis_index("seq")
    chip, core = seq_index // COPIES, seq_index % COPIES
    slots = key_refs[0].shape[1]
    width = LATENT + ROPE
    q = jnp.concatenate([ref[:, :width] for ref in q_refs], axis=0)

    fresh = q_refs[0][:, width:].astype(jnp.float32)
    fresh = jnp.concatenate(
        [fresh[n * SPEC : (n + 1) * SPEC] for n in range(width // ROPE)], axis=1
    )
    fresh = jnp.concatenate([fresh, jnp.zeros((16 - SPEC, width), jnp.float32)], axis=0)
    fresh = fresh.astype(jnp.bfloat16)
    f = lax.dot_general(
        q, fresh, (((1,), (1,)), ((), ())), preferred_element_type=jnp.float32
    )
    row = lax.broadcasted_iota(jnp.int32, f.shape, 0) % (SPEC * heads)
    key = lax.broadcasted_iota(jnp.int32, f.shape, 1)
    f = jnp.where(key <= row // heads, f * SCORE_SCALE, masked_value)

    starts = [((chip ^ partner(k, core)) * COPIES + core) * slots for k in range(owners)]
    s = block_scores(q, key_refs, starts, limit_ref)
    top = jnp.maximum(jnp.max(s, axis=1, keepdims=True), jnp.max(f, axis=1, keepdims=True))
    total, out = weigh(s, key_refs, top)
    w = jnp.exp(f - top)
    total += jnp.sum(w, axis=1, keepdims=True)
    out += jnp.dot(
        w.astype(jnp.bfloat16), fresh[:, :LATENT], preferred_element_type=jnp.float32
    )
    q_out[...] = q
    top_ref[...] = jnp.broadcast_to(top, top_ref.shape)
    total_ref[...] = jnp.broadcast_to(total, total_ref.shape)
    out_ref[...] = out


def finish_kernel(
    owners, per_device, limit_ref, q_ref, top_ref, total_ref, part_ref, pair_ref, *refs
):
    key_refs = [pair_ref.at[0], pair_ref.at[1], *refs[: owners - 2]]
    outs = refs[owners - 2 :]
    seq_index = lax.axis_index("seq")
    chip, core = seq_index // COPIES, seq_index % COPIES
    plane = lax.axis_index("head")
    slots = key_refs[0].shape[1]
    starts = [((chip ^ partner(k, 1 - core)) * COPIES + 1 - core) * slots for k in range(owners)]
    s = block_scores(q_ref[...], key_refs, starts, limit_ref)
    first = top_ref[:, :1]
    top = jnp.maximum(first, jnp.max(s, axis=1, keepdims=True))
    total, out = weigh(s, key_refs, top)
    scale = jnp.exp(first - top)
    total += total_ref[:, :1] * scale
    out += part_ref[...] * scale
    out = (out * (1.0 / total)).astype(jnp.bfloat16)
    piece = out.shape[0] // per_device
    sent_first = first_block(plane, chip, core)
    for k in range(per_device):
        for n in range(per_device):

            @pl.when(sent_first ^ k == n)
            def _():
                outs[k][...] = out[n * piece : (n + 1) * piece]


def project_kernel(per_device, w_ref, *refs):
    lat_refs, out_ref = refs[:-1], refs[-1]
    rows, heads, width = out_ref.shape
    first = first_back(lax.axis_index("seq") // COPIES, lax.axis_index("head"))
    parts = [jnp.where(first == a, lat_refs[1][...], lat_refs[0][...]) for a in range(per_device)]
    latent = jnp.concatenate(parts, axis=0)
    out = jnp.zeros((rows * heads, width), jnp.float32)
    own_head = lax.broadcasted_iota(jnp.int32, out.shape, 0) % heads
    step = 2 if heads % 2 == 0 else 1
    for h in range(0, heads, step):
        group = jnp.concatenate([w_ref[h + n] for n in range(step)], axis=1)
        product = jnp.dot(latent, group, preferred_element_type=jnp.float32)
        for n in range(step):
            out = jnp.where(own_head == h + n, product[:, n * width : (n + 1) * width], out)
    out_ref[...] = out.astype(out_ref.dtype).reshape(out_ref.shape)


def whole_sequences(seq_size, head_size, queries, new_latent, cache, lengths, w_uk, w_uv):
    rows, heads, q_width = queries.shape
    owners, slots, width = cache.shape
    per_device = rows // SPEC
    piece = SPEC * heads
    all_rows = per_device * piece
    params = pltpu.CompilerParams(vmem_limit_bytes=VMEM_LIMIT)
    vmem = pl.BlockSpec(memory_space=pltpu.VMEM)
    anywhere = pl.BlockSpec(memory_space=pl.ANY)
    both = ("seq", "head")
    devices = [(i, j) for i in range(seq_size) for j in range(head_size)]

    def flat(seq_index, head_index):
        return seq_index * head_size + head_index

    def in_hbm(x):
        return pltpu.with_memory_space_constraint(x, pltpu.HBM)

    def host(i, j):
        other = (i // COPIES) ^ (2 - ((j ^ (j >> 1)) & 1))
        return flat(((i % COPIES) * 2 + other // 2) * COPIES + other % 2, j)

    def owner(i, j, a):
        plane, chip = i // COPIES, i % COPIES * per_device + a
        return flat(chip * COPIES + 1 - j // 2, plane)

    def in_plane(move):
        return [(g * COPIES + t, move(g, t)) for g in range(owners) for t in range(COPIES)]

    *picked, packed, limit = pl.pallas_call(
        functools.partial(pick_kernel, per_device),
        out_shape=[jax.ShapeDtypeStruct((width, slots), cache.dtype)] * owners
        + [
            jax.ShapeDtypeStruct((all_rows, q_width + ROPE), queries.dtype),
            jax.ShapeDtypeStruct((8, slots), jnp.int32),
        ],
        in_specs=[anywhere] * 4,
        out_specs=[vmem] * (owners + 2),
        scratch_shapes=[
            pltpu.VMEM(queries.shape, queries.dtype),
            pltpu.VMEM(new_latent.shape, new_latent.dtype),
            pltpu.SMEM(lengths.shape, lengths.dtype),
            pltpu.SemaphoreType.DMA((owners + 3,)),
        ],
        compiler_params=params,
        cost_estimate=LONG,
    )(*[in_hbm(x) for x in (jnp.swapaxes(cache, 1, 2), queries, new_latent, lengths)])
    moved = lax.ppermute(packed, both, [(flat(i, j), host(i, j)) for i, j in devices])
    own_keys = [picked[0]] + [
        lax.ppermute(picked[k], "seq", in_plane(lambda g, t: (g ^ partner(k, t)) * COPIES + t))
        for k in range(1, owners)
    ]
    pair = pl.pallas_call(
        pair_kernel,
        out_shape=jax.ShapeDtypeStruct((2, *picked[0].shape), cache.dtype),
        in_specs=[vmem] * 2,
        out_specs=vmem,
        scratch_shapes=[pltpu.SemaphoreType.DMA((2,))],
        compiler_params=params,
    )(*own_keys[:2])
    other_core = in_plane(lambda g, t: g * COPIES + 1 - t)
    far_keys = [lax.ppermute(keys, "seq", other_core) for keys in [pair] + own_keys[2:]]

    pieces = pl.pallas_call(
        functools.partial(absorb_kernel, per_device),
        out_shape=[jax.ShapeDtypeStruct((piece, width + ROPE), cache.dtype)] * per_device,
        in_specs=[vmem] * 2,
        out_specs=[vmem] * per_device,
        compiler_params=params,
        cost_estimate=LONG,
    )(w_uk, moved)
    arrived = [
        lax.ppermute(
            pieces[k],
            both,
            [(host(i, j), owner(i, j, leaves_as(k, j))) for i, j in devices],
        )
        for k in range(per_device)
    ]

    state = pl.pallas_call(
        functools.partial(begin_kernel, owners, per_device, heads),
        out_shape=[
            jax.ShapeDtypeStruct((all_rows, width), jnp.bfloat16),
            jax.ShapeDtypeStruct((all_rows, 128), jnp.float32),
            jax.ShapeDtypeStruct((all_rows, 128), jnp.float32),
            jax.ShapeDtypeStruct((all_rows, LATENT), jnp.float32),
        ],
        in_specs=[vmem] * (1 + per_device + owners),
        out_specs=[vmem] * 4,
        compiler_params=params,
        cost_estimate=LONG,
    )(limit, *arrived, *own_keys)
    latent = pl.pallas_call(
        functools.partial(finish_kernel, owners, per_device),
        out_shape=[jax.ShapeDtypeStruct((piece, LATENT), jnp.bfloat16)] * per_device,
        in_specs=[vmem] * (1 + len(state) + len(far_keys)),
        out_specs=[vmem] * per_device,
        compiler_params=params,
    )(limit, *state, *far_keys)

    back = [
        lax.ppermute(
            latent[k],
            both,
            [(owner(i, j, first_back(i // COPIES, j) ^ k), flat(i, j)) for i, j in devices],
        )
        for k in range(per_device)
    ]
    return pl.pallas_call(
        functools.partial(project_kernel, per_device),
        out_shape=jax.ShapeDtypeStruct((rows, heads, w_uv.shape[2]), jnp.bfloat16),
        in_specs=[vmem] * (1 + per_device),
        out_specs=vmem,
        compiler_params=params,
    )(w_uv, *back[::-1])


def local_partial(
    query_tile_block,
    key_tile_block,
    incoming_keys,
    len_block,
    offset,
    own_first,
    score_scale,
    head_count,
):
    scores = (
        jnp.einsum(
            "vfa,vja->vfj", query_tile_block, key_tile_block, preferred_element_type=jnp.float32
        )
        * score_scale
    )
    positions = offset + lax.broadcasted_iota(jnp.int32, (1, 1, key_tile_block.shape[1]), 2)
    visible = positions < len_block[:, None, None]
    fresh_scores = (
        jnp.einsum(
            "vfa,vja->vfj", query_tile_block, incoming_keys, preferred_element_type=jnp.float32
        )
        * score_scale
    )
    spec_count = incoming_keys.shape[1]
    row_spec = (
        lax.broadcasted_iota(jnp.int32, (1, query_tile_block.shape[1], spec_count), 1) // head_count
    )
    key_spec = lax.broadcasted_iota(jnp.int32, (1, query_tile_block.shape[1], spec_count), 2)
    causal = (key_spec <= row_spec) & own_first
    row_top = jnp.maximum(
        jnp.max(jnp.where(visible, scores, masked_value), axis=2),
        jnp.max(jnp.where(causal, fresh_scores, masked_value), axis=2),
    )
    weights = jnp.where(visible, jnp.exp(scores - row_top[..., None]), 0.0)
    fresh_weights = jnp.where(causal, jnp.exp(fresh_scores - row_top[..., None]), 0.0)
    running_totals = jnp.sum(weights, axis=2) + jnp.sum(fresh_weights, axis=2)
    weighted = jnp.einsum(
        "mpu,mui->mpi",
        weights.astype(jnp.bfloat16),
        key_tile_block[:, :, :LATENT],
        preferred_element_type=jnp.float32,
    )
    weighted = weighted + jnp.einsum(
        "mpu,mui->mpi",
        fresh_weights.astype(jnp.bfloat16),
        incoming_keys[:, :, :LATENT],
        preferred_element_type=jnp.float32,
    )
    return (row_top, running_totals, weighted)


def project_values(latent_rows, value_weight):
    return jnp.einsum("rhc,hcv->rhv", latent_rows, value_weight, precision=lax.Precision.HIGHEST)


def split_positions(queries, new_latent, cache, lengths, w_uk, w_uv):
    own_rows, head_count, _ = queries.shape
    score_scale = (NOPE + ROPE) ** (-0.5)
    gathered, new_all = (
        lax.all_gather(queries, "seq", axis=0, tiled=True),
        lax.all_gather(new_latent, "seq", axis=0, tiled=True),
    )
    absorbed = jnp.einsum(
        "rhn,hnc->rhc", gathered[:, :, :NOPE], w_uk, preferred_element_type=jnp.float32
    ).astype(jnp.bfloat16)
    q_all = jnp.concatenate([absorbed, gathered[:, :, NOPE:]], axis=2)
    total_rows = q_all.shape[0]
    seq_count = total_rows // SPEC
    query_slots = SPEC * head_count
    q_seq = q_all.reshape(seq_count, query_slots, q_all.shape[2])
    new_seq = new_all.reshape(seq_count, SPEC, new_all.shape[1])
    seq_index = lax.axis_index("seq")
    offset = seq_index * cache.shape[1]
    own_first = seq_index == 0
    row_top, running_totals, weighted = local_partial(
        q_seq,
        lax.all_gather(cache, "head", axis=0, tiled=True),
        new_seq,
        lengths,
        offset,
        own_first,
        score_scale,
        head_count,
    )
    value_weight = w_uv.astype(jnp.float32)
    global_top = lax.pmax(row_top, "seq")
    factor = jnp.exp(row_top - global_top)
    scaled_totals = (running_totals * factor).reshape(total_rows, head_count)
    scaled_weighted = (weighted * factor[..., None]).reshape(total_rows, head_count, LATENT)
    row_totals, row_weighted = (
        lax.psum_scatter(scaled_totals, "seq", scatter_dimension=0, tiled=True),
        lax.psum_scatter(scaled_weighted, "seq", scatter_dimension=0, tiled=True),
    )
    latent_output = row_weighted / row_totals[..., None]
    result = project_values(latent_output, value_weight)
    return result.astype(jnp.bfloat16)


def shards(seq_size, head_size, queries, new_latent, cache, lengths, w_uk, w_uv):
    rows, owners = queries.shape[0], cache.shape[0]
    per_device = rows // SPEC
    if (
        per_device == 2
        and rows % SPEC == 0
        and seq_size == COPIES * owners
        and head_size == owners == 4
    ):
        return whole_sequences(
            seq_size, head_size, queries, new_latent, cache, lengths, w_uk, w_uv
        )
    return split_positions(queries, new_latent, cache, lengths, w_uk, w_uv)


def solution(mesh):
    return jax.shard_map(
        functools.partial(shards, mesh.shape["seq"], mesh.shape["head"]),
        mesh=mesh,
        in_specs=(
            P("seq", "head", None),
            P("seq", None),
            P("head", "seq", None),
            P(),
            P("head", None, None),
            P("head", None, None),
        ),
        out_specs=P("seq", "head", None),
        check_vma=False,
    )
```

```python
import functools

import jax
import jax.numpy as jnp
from jax import lax
from jax.experimental import pallas as pl
from jax.experimental.pallas import tpu as pltpu
from jax.sharding import PartitionSpec as P

NOPE = 128
ROPE = 64
LATENT = 512
SPEC = 4
SCORE_SCALE = (NOPE + ROPE) ** (-0.5)
COPIES = 2
COPY_PARTS = 3
VMEM_LIMIT = 16 * 1024 * 1024
LONG = pl.CostEstimate(flops=2 * 10**10, bytes_accessed=0, transcendentals=0)

masked_value = -1e30


def leaves_as(k, head_shard):
    return (k + head_shard) % 2


def far_half(plane, pair):
    return 1 * (plane <= 2 * pair)


def first_back(home_chip, head_shard):
    far = 1 * (far_half(home_chip, head_shard // 2) == head_shard % 2)
    return home_chip % 2 ^ far


def first_block(plane, chip, core):
    near = 1 * (chip % 2 == plane % 2)
    return far_half(plane, 1 - core) ^ near ^ chip % 2


def partner(k, core):
    return (0, 3, 1 ^ 3 * core, 2 ^ 3 * core)[k]


def pick_kernel(per_device, cache_hbm, q_hbm, new_hbm, len_hbm, *refs):
    owners = cache_hbm.shape[0]
    blocks, (out_ref, limit_ref, q_ref, new_ref, len_ref, sem) = refs[:owners], refs[owners:]
    chip, core = lax.axis_index("seq") // COPIES, lax.axis_index("seq") % COPIES
    moves = [
        pltpu.make_async_copy(q_hbm, q_ref, sem.at[0]),
        pltpu.make_async_copy(new_hbm, new_ref, sem.at[1]),
        pltpu.make_async_copy(len_hbm, len_ref, sem.at[2]),
    ]
    part = cache_hbm.shape[1] // COPY_PARTS
    for k in range(owners):
        for n in range(COPY_PARTS):
            rows = pl.ds(n * part, part)
            moves.append(
                pltpu.make_async_copy(
                    cache_hbm.at[chip ^ partner(k, core), rows],
                    blocks[k].at[rows],
                    sem.at[3 + k * COPY_PARTS + n],
                )
            )
    for move in moves:
        move.start()
    moves[0].wait()
    moves[1].wait()
    heads, width = q_ref.shape[1:]
    fresh = new_ref[...].astype(jnp.float32)
    piece = SPEC * heads
    for a in range(per_device):
        rows = q_ref[a * SPEC : (a + 1) * SPEC].reshape(piece, width)
        own = fresh[a * SPEC : (a + 1) * SPEC]
        parts = [own[:, n : n + ROPE] for n in range(0, own.shape[1], ROPE)]
        spare = piece - SPEC * len(parts)
        if spare:
            parts.append(jnp.zeros((spare, ROPE), jnp.float32))
        own = jnp.concatenate(parts, axis=0).astype(rows.dtype)
        out_ref[a * piece : (a + 1) * piece] = jnp.concatenate([rows, own], axis=1)
    moves[2].wait()
    length = len_ref[lax.axis_index("head") * owners + chip]
    limit_ref[...] = jnp.full(limit_ref.shape, length, limit_ref.dtype)
    for move in moves[3:]:
        move.wait()


def pair_kernel(first_ref, second_ref, out_ref, sem):
    moves = [
        pltpu.make_async_copy(ref, out_ref.at[n], sem.at[n])
        for n, ref in enumerate((first_ref, second_ref))
    ]
    for move in moves:
        move.start()
    for move in moves:
        move.wait()


def absorb_kernel(per_device, w_ref, packed_ref, *outs):
    heads = w_ref.shape[0]
    piece = SPEC * heads
    nope = packed_ref[:, :NOPE]
    own_head = lax.broadcasted_iota(jnp.int32, nope.shape, 0) % heads
    spread = jnp.concatenate(
        [jnp.where(own_head == h, nope, jnp.zeros_like(nope)) for h in range(heads)], axis=1
    )
    absorbed = jnp.dot(
        spread, w_ref[...].reshape(heads * NOPE, LATENT), preferred_element_type=jnp.float32
    ).astype(jnp.bfloat16)
    for k in range(per_device):
        which = leaves_as(k, lax.axis_index("head"))
        for a in range(per_device):

            @pl.when(which == a)
            def _():
                rows = slice(a * piece, (a + 1) * piece)
                outs[k][:, :LATENT] = absorbed[rows]
                outs[k][:, LATENT:] = packed_ref[rows, NOPE:]


def block_scores(q, refs, starts, limit_ref):
    width = q.shape[1]
    keys = jnp.concatenate([ref[:width, :] for ref in refs], axis=1)
    limit = limit_ref[:1, :]
    lane = lax.broadcasted_iota(jnp.int32, limit.shape, 1)
    visible = jnp.concatenate([lane + start < limit for start in starts], axis=1)
    s = jnp.dot(q, keys, preferred_element_type=jnp.float32) * SCORE_SCALE
    return jnp.where(visible, s, masked_value)


def weigh(s, refs, top):
    w = jnp.exp(s - top)
    values = jnp.concatenate([ref[:LATENT, :] for ref in refs], axis=1)
    out = lax.dot_general(
        w.astype(jnp.bfloat16),
        values,
        (((1,), (1,)), ((), ())),
        preferred_element_type=jnp.float32,
    )
    return jnp.sum(w, axis=1, keepdims=True), out


def begin_kernel(owners, per_device, heads, limit_ref, *refs):
    q_refs, key_refs = refs[:per_device], refs[per_device : per_device + owners]
    q_out, top_ref, total_ref, out_ref = refs[per_device + owners :]
    seq_index = lax.axis_index("seq")
    chip, core = seq_index // COPIES, seq_index % COPIES
    slots = key_refs[0].shape[1]
    width = LATENT + ROPE
    q = jnp.concatenate([ref[:, :width] for ref in q_refs], axis=0)

    fresh = q_refs[0][:, width:].astype(jnp.float32)
    fresh = jnp.concatenate(
        [fresh[n * SPEC : (n + 1) * SPEC] for n in range(width // ROPE)], axis=1
    )
    fresh = jnp.concatenate([fresh, jnp.zeros((16 - SPEC, width), jnp.float32)], axis=0)
    fresh = fresh.astype(jnp.bfloat16)
    f = lax.dot_general(
        q, fresh, (((1,), (1,)), ((), ())), preferred_element_type=jnp.float32
    )
    row = lax.broadcasted_iota(jnp.int32, f.shape, 0) % (SPEC * heads)
    key = lax.broadcasted_iota(jnp.int32, f.shape, 1)
    f = jnp.where(key <= row // heads, f * SCORE_SCALE, masked_value)

    starts = [((chip ^ partner(k, core)) * COPIES + core) * slots for k in range(owners)]
    s = block_scores(q, key_refs, starts, limit_ref)
    top = jnp.maximum(jnp.max(s, axis=1, keepdims=True), jnp.max(f, axis=1, keepdims=True))
    total, out = weigh(s, key_refs, top)
    w = jnp.exp(f - top)
    total += jnp.sum(w, axis=1, keepdims=True)
    out += jnp.dot(
        w.astype(jnp.bfloat16), fresh[:, :LATENT], preferred_element_type=jnp.float32
    )
    q_out[...] = q
    top_ref[...] = jnp.broadcast_to(top, top_ref.shape)
    total_ref[...] = jnp.broadcast_to(total, total_ref.shape)
    out_ref[...] = out


def finish_kernel(
    owners, per_device, limit_ref, q_ref, top_ref, total_ref, part_ref, pair_ref, *refs
):
    key_refs = [pair_ref.at[0], pair_ref.at[1], *refs[: owners - 2]]
    outs = refs[owners - 2 :]
    seq_index = lax.axis_index("seq")
    chip, core = seq_index // COPIES, seq_index % COPIES
    plane = lax.axis_index("head")
    slots = key_refs[0].shape[1]
    starts = [((chip ^ partner(k, 1 - core)) * COPIES + 1 - core) * slots for k in range(owners)]
    s = block_scores(q_ref[...], key_refs, starts, limit_ref)
    first = top_ref[:, :1]
    top = jnp.maximum(first, jnp.max(s, axis=1, keepdims=True))
    total, out = weigh(s, key_refs, top)
    scale = jnp.exp(first - top)
    total += total_ref[:, :1] * scale
    out += part_ref[...] * scale
    out = (out * (1.0 / total)).astype(jnp.bfloat16)
    piece = out.shape[0] // per_device
    sent_first = first_block(plane, chip, core)
    for k in range(per_device):
        for n in range(per_device):

            @pl.when(sent_first ^ k == n)
            def _():
                outs[k][...] = out[n * piece : (n + 1) * piece]


def project_kernel(per_device, w_ref, *refs):
    lat_refs, out_ref = refs[:-1], refs[-1]
    rows, heads, width = out_ref.shape
    first = first_back(lax.axis_index("seq") // COPIES, lax.axis_index("head"))
    parts = [jnp.where(first == a, lat_refs[1][...], lat_refs[0][...]) for a in range(per_device)]
    latent = jnp.concatenate(parts, axis=0)
    out = jnp.zeros((rows * heads, width), jnp.float32)
    own_head = lax.broadcasted_iota(jnp.int32, out.shape, 0) % heads
    step = 2 if heads % 2 == 0 else 1
    for h in range(0, heads, step):
        group = jnp.concatenate([w_ref[h + n] for n in range(step)], axis=1)
        product = jnp.dot(latent, group, preferred_element_type=jnp.float32)
        for n in range(step):
            out = jnp.where(own_head == h + n, product[:, n * width : (n + 1) * width], out)
    out_ref[...] = out.astype(out_ref.dtype).reshape(out_ref.shape)


def whole_sequences(seq_size, head_size, queries, new_latent, cache, lengths, w_uk, w_uv):
    rows, heads, q_width = queries.shape
    owners, slots, width = cache.shape
    per_device = rows // SPEC
    piece = SPEC * heads
    all_rows = per_device * piece
    params = pltpu.CompilerParams(vmem_limit_bytes=VMEM_LIMIT)
    vmem = pl.BlockSpec(memory_space=pltpu.VMEM)
    anywhere = pl.BlockSpec(memory_space=pl.ANY)
    both = ("seq", "head")
    devices = [(i, j) for i in range(seq_size) for j in range(head_size)]

    def flat(seq_index, head_index):
        return seq_index * head_size + head_index

    def in_hbm(x):
        return pltpu.with_memory_space_constraint(x, pltpu.HBM)

    def host(i, j):
        other = (i // COPIES) ^ (2 - ((j ^ (j >> 1)) & 1))
        return flat(((i % COPIES) * 2 + other // 2) * COPIES + other % 2, j)

    def owner(i, j, a):
        plane, chip = i // COPIES, i % COPIES * per_device + a
        return flat(chip * COPIES + 1 - j // 2, plane)

    def in_plane(move):
        return [(g * COPIES + t, move(g, t)) for g in range(owners) for t in range(COPIES)]

    *picked, packed, limit = pl.pallas_call(
        functools.partial(pick_kernel, per_device),
        out_shape=[jax.ShapeDtypeStruct((width, slots), cache.dtype)] * owners
        + [
            jax.ShapeDtypeStruct((all_rows, q_width + ROPE), queries.dtype),
            jax.ShapeDtypeStruct((8, slots), jnp.int32),
        ],
        in_specs=[anywhere] * 4,
        out_specs=[vmem] * (owners + 2),
        scratch_shapes=[
            pltpu.VMEM(queries.shape, queries.dtype),
            pltpu.VMEM(new_latent.shape, new_latent.dtype),
            pltpu.SMEM(lengths.shape, lengths.dtype),
            pltpu.SemaphoreType.DMA((3 + owners * COPY_PARTS,)),
        ],
        compiler_params=params,
        cost_estimate=LONG,
    )(*[in_hbm(x) for x in (jnp.swapaxes(cache, 1, 2), queries, new_latent, lengths)])
    moved = lax.ppermute(packed, both, [(flat(i, j), host(i, j)) for i, j in devices])
    own_keys = [picked[0]] + [
        lax.ppermute(picked[k], "seq", in_plane(lambda g, t: (g ^ partner(k, t)) * COPIES + t))
        for k in range(1, owners)
    ]
    pair = pl.pallas_call(
        pair_kernel,
        out_shape=jax.ShapeDtypeStruct((2, *picked[0].shape), cache.dtype),
        in_specs=[vmem] * 2,
        out_specs=vmem,
        scratch_shapes=[pltpu.SemaphoreType.DMA((2,))],
        compiler_params=params,
    )(*own_keys[:2])
    other_core = in_plane(lambda g, t: g * COPIES + 1 - t)
    far_keys = [lax.ppermute(keys, "seq", other_core) for keys in [pair] + own_keys[2:]]

    pieces = pl.pallas_call(
        functools.partial(absorb_kernel, per_device),
        out_shape=[jax.ShapeDtypeStruct((piece, width + ROPE), cache.dtype)] * per_device,
        in_specs=[vmem] * 2,
        out_specs=[vmem] * per_device,
        compiler_params=params,
        cost_estimate=LONG,
    )(w_uk, moved)
    arrived = [
        lax.ppermute(
            pieces[k],
            both,
            [(host(i, j), owner(i, j, leaves_as(k, j))) for i, j in devices],
        )
        for k in range(per_device)
    ]

    state = pl.pallas_call(
        functools.partial(begin_kernel, owners, per_device, heads),
        out_shape=[
            jax.ShapeDtypeStruct((all_rows, width), jnp.bfloat16),
            jax.ShapeDtypeStruct((all_rows, 128), jnp.float32),
            jax.ShapeDtypeStruct((all_rows, 128), jnp.float32),
            jax.ShapeDtypeStruct((all_rows, LATENT), jnp.float32),
        ],
        in_specs=[vmem] * (1 + per_device + owners),
        out_specs=[vmem] * 4,
        compiler_params=params,
        cost_estimate=LONG,
    )(limit, *arrived, *own_keys)
    latent = pl.pallas_call(
        functools.partial(finish_kernel, owners, per_device),
        out_shape=[jax.ShapeDtypeStruct((piece, LATENT), jnp.bfloat16)] * per_device,
        in_specs=[vmem] * (1 + len(state) + len(far_keys)),
        out_specs=[vmem] * per_device,
        compiler_params=params,
    )(limit, *state, *far_keys)

    back = [
        lax.ppermute(
            latent[k],
            both,
            [(owner(i, j, first_back(i // COPIES, j) ^ k), flat(i, j)) for i, j in devices],
        )
        for k in range(per_device)
    ]
    return pl.pallas_call(
        functools.partial(project_kernel, per_device),
        out_shape=jax.ShapeDtypeStruct((rows, heads, w_uv.shape[2]), jnp.bfloat16),
        in_specs=[vmem] * (1 + per_device),
        out_specs=vmem,
        compiler_params=params,
    )(w_uv, *back[::-1])


def local_partial(
    query_tile_block,
    key_tile_block,
    incoming_keys,
    len_block,
    offset,
    own_first,
    score_scale,
    head_count,
):
    scores = (
        jnp.einsum(
            "vfa,vja->vfj", query_tile_block, key_tile_block, preferred_element_type=jnp.float32
        )
        * score_scale
    )
    positions = offset + lax.broadcasted_iota(jnp.int32, (1, 1, key_tile_block.shape[1]), 2)
    visible = positions < len_block[:, None, None]
    fresh_scores = (
        jnp.einsum(
            "vfa,vja->vfj", query_tile_block, incoming_keys, preferred_element_type=jnp.float32
        )
        * score_scale
    )
    spec_count = incoming_keys.shape[1]
    row_spec = (
        lax.broadcasted_iota(jnp.int32, (1, query_tile_block.shape[1], spec_count), 1) // head_count
    )
    key_spec = lax.broadcasted_iota(jnp.int32, (1, query_tile_block.shape[1], spec_count), 2)
    causal = (key_spec <= row_spec) & own_first
    row_top = jnp.maximum(
        jnp.max(jnp.where(visible, scores, masked_value), axis=2),
        jnp.max(jnp.where(causal, fresh_scores, masked_value), axis=2),
    )
    weights = jnp.where(visible, jnp.exp(scores - row_top[..., None]), 0.0)
    fresh_weights = jnp.where(causal, jnp.exp(fresh_scores - row_top[..., None]), 0.0)
    running_totals = jnp.sum(weights, axis=2) + jnp.sum(fresh_weights, axis=2)
    weighted = jnp.einsum(
        "mpu,mui->mpi",
        weights.astype(jnp.bfloat16),
        key_tile_block[:, :, :LATENT],
        preferred_element_type=jnp.float32,
    )
    weighted = weighted + jnp.einsum(
        "mpu,mui->mpi",
        fresh_weights.astype(jnp.bfloat16),
        incoming_keys[:, :, :LATENT],
        preferred_element_type=jnp.float32,
    )
    return (row_top, running_totals, weighted)


def project_values(latent_rows, value_weight):
    return jnp.einsum("rhc,hcv->rhv", latent_rows, value_weight, precision=lax.Precision.HIGHEST)


def split_positions(queries, new_latent, cache, lengths, w_uk, w_uv):
    own_rows, head_count, _ = queries.shape
    score_scale = (NOPE + ROPE) ** (-0.5)
    gathered, new_all = (
        lax.all_gather(queries, "seq", axis=0, tiled=True),
        lax.all_gather(new_latent, "seq", axis=0, tiled=True),
    )
    absorbed = jnp.einsum(
        "rhn,hnc->rhc", gathered[:, :, :NOPE], w_uk, preferred_element_type=jnp.float32
    ).astype(jnp.bfloat16)
    q_all = jnp.concatenate([absorbed, gathered[:, :, NOPE:]], axis=2)
    total_rows = q_all.shape[0]
    seq_count = total_rows // SPEC
    query_slots = SPEC * head_count
    q_seq = q_all.reshape(seq_count, query_slots, q_all.shape[2])
    new_seq = new_all.reshape(seq_count, SPEC, new_all.shape[1])
    seq_index = lax.axis_index("seq")
    offset = seq_index * cache.shape[1]
    own_first = seq_index == 0
    row_top, running_totals, weighted = local_partial(
        q_seq,
        lax.all_gather(cache, "head", axis=0, tiled=True),
        new_seq,
        lengths,
        offset,
        own_first,
        score_scale,
        head_count,
    )
    value_weight = w_uv.astype(jnp.float32)
    global_top = lax.pmax(row_top, "seq")
    factor = jnp.exp(row_top - global_top)
    scaled_totals = (running_totals * factor).reshape(total_rows, head_count)
    scaled_weighted = (weighted * factor[..., None]).reshape(total_rows, head_count, LATENT)
    row_totals, row_weighted = (
        lax.psum_scatter(scaled_totals, "seq", scatter_dimension=0, tiled=True),
        lax.psum_scatter(scaled_weighted, "seq", scatter_dimension=0, tiled=True),
    )
    latent_output = row_weighted / row_totals[..., None]
    result = project_values(latent_output, value_weight)
    return result.astype(jnp.bfloat16)


def shards(seq_size, head_size, queries, new_latent, cache, lengths, w_uk, w_uv):
    rows, owners = queries.shape[0], cache.shape[0]
    per_device = rows // SPEC
    if (
        per_device == 2
        and rows % SPEC == 0
        and seq_size == COPIES * owners
        and head_size == owners == 4
        and cache.shape[2] % (16 * COPY_PARTS) == 0
    ):
        return whole_sequences(
            seq_size, head_size, queries, new_latent, cache, lengths, w_uk, w_uv
        )
    return split_positions(queries, new_latent, cache, lengths, w_uk, w_uv)


def solution(mesh):
    return jax.shard_map(
        functools.partial(shards, mesh.shape["seq"], mesh.shape["head"]),
        mesh=mesh,
        in_specs=(
            P("seq", "head", None),
            P("seq", None),
            P("head", "seq", None),
            P(),
            P("head", None, None),
            P("head", None, None),
        ),
        out_specs=P("seq", "head", None),
        check_vma=False,
    )
```

```python
import functools

import jax
import jax.numpy as jnp
from jax import lax
from jax.experimental import pallas as pl
from jax.experimental.pallas import tpu as pltpu
from jax.sharding import PartitionSpec as P

NOPE = 128
ROPE = 64
LATENT = 512
SPEC = 4
SCORE_SCALE = (NOPE + ROPE) ** (-0.5)
COPIES = 2
COPY_PARTS = 3
VMEM_LIMIT = 16 * 1024 * 1024
LONG = pl.CostEstimate(flops=2 * 10**10, bytes_accessed=0, transcendentals=0)

masked_value = -1e30


def leaves_as(k, head_shard):
    return (k + head_shard) % 2


def far_half(plane, pair):
    return 1 * (plane <= 2 * pair)


def first_back(home_chip, head_shard):
    far = 1 * (far_half(home_chip, head_shard // 2) == head_shard % 2)
    return home_chip % 2 ^ far


def first_block(plane, chip, core):
    a = 1 - chip % 2
    return far_half(plane, 1 - core) ^ 1 * (a == plane % 2) ^ a


def partner(k, core):
    return (0, 3, 1 ^ 3 * core, 2 ^ 3 * core)[k]


def pick_kernel(per_device, cache_hbm, q_hbm, new_hbm, len_hbm, *refs):
    owners = cache_hbm.shape[0]
    blocks, (out_ref, limit_ref, q_ref, new_ref, len_ref, sem) = refs[:owners], refs[owners:]
    chip, core = lax.axis_index("seq") // COPIES, lax.axis_index("seq") % COPIES
    moves = [
        pltpu.make_async_copy(q_hbm, q_ref, sem.at[0]),
        pltpu.make_async_copy(new_hbm, new_ref, sem.at[1]),
        pltpu.make_async_copy(len_hbm, len_ref, sem.at[2]),
    ]
    part = cache_hbm.shape[1] // COPY_PARTS
    for k in range(owners):
        for n in range(COPY_PARTS):
            rows = pl.ds(n * part, part)
            moves.append(
                pltpu.make_async_copy(
                    cache_hbm.at[chip ^ partner(k, core) ^ 1, rows],
                    blocks[k].at[rows],
                    sem.at[3 + k * COPY_PARTS + n],
                )
            )
    for move in moves:
        move.start()
    moves[0].wait()
    moves[1].wait()
    heads, width = q_ref.shape[1:]
    fresh = new_ref[...].astype(jnp.float32)
    piece = SPEC * heads
    for a in range(per_device):
        rows = q_ref[a * SPEC : (a + 1) * SPEC].reshape(piece, width)
        own = fresh[a * SPEC : (a + 1) * SPEC]
        parts = [own[:, n : n + ROPE] for n in range(0, own.shape[1], ROPE)]
        spare = piece - SPEC * len(parts)
        if spare:
            parts.append(jnp.zeros((spare, ROPE), jnp.float32))
        own = jnp.concatenate(parts, axis=0).astype(rows.dtype)
        out_ref[a * piece : (a + 1) * piece] = jnp.concatenate([rows, own], axis=1)
    moves[2].wait()
    length = len_ref[lax.axis_index("head") * owners + (chip ^ 1)]
    limit_ref[...] = jnp.full(limit_ref.shape, length, limit_ref.dtype)
    for move in moves[3:]:
        move.wait()


def pair_kernel(first_ref, second_ref, out_ref, sem):
    moves = [
        pltpu.make_async_copy(ref, out_ref.at[n], sem.at[n])
        for n, ref in enumerate((first_ref, second_ref))
    ]
    for move in moves:
        move.start()
    for move in moves:
        move.wait()


def absorb_kernel(per_device, w_ref, packed_ref, *outs):
    heads = w_ref.shape[0]
    piece = SPEC * heads
    nope = packed_ref[:, :NOPE]
    own_head = lax.broadcasted_iota(jnp.int32, nope.shape, 0) % heads
    spread = jnp.concatenate(
        [jnp.where(own_head == h, nope, jnp.zeros_like(nope)) for h in range(heads)], axis=1
    )
    absorbed = jnp.dot(
        spread, w_ref[...].reshape(heads * NOPE, LATENT), preferred_element_type=jnp.float32
    ).astype(jnp.bfloat16)
    for k in range(per_device):
        which = leaves_as(k, lax.axis_index("head"))
        for a in range(per_device):

            @pl.when(which == a)
            def _():
                rows = slice(a * piece, (a + 1) * piece)
                outs[k][:, :LATENT] = absorbed[rows]
                outs[k][:, LATENT:] = packed_ref[rows, NOPE:]


def block_scores(q, refs, starts, limit_ref):
    width = q.shape[1]
    keys = jnp.concatenate([ref[:width, :] for ref in refs], axis=1)
    limit = limit_ref[:1, :]
    lane = lax.broadcasted_iota(jnp.int32, limit.shape, 1)
    visible = jnp.concatenate([lane + start < limit for start in starts], axis=1)
    s = jnp.dot(q, keys, preferred_element_type=jnp.float32) * SCORE_SCALE
    return jnp.where(visible, s, masked_value)


def weigh(s, refs, top):
    w = jnp.exp(s - top)
    values = jnp.concatenate([ref[:LATENT, :] for ref in refs], axis=1)
    out = lax.dot_general(
        w.astype(jnp.bfloat16),
        values,
        (((1,), (1,)), ((), ())),
        preferred_element_type=jnp.float32,
    )
    return jnp.sum(w, axis=1, keepdims=True), out


def begin_kernel(owners, per_device, heads, limit_ref, *refs):
    q_refs, key_refs = refs[:per_device], refs[per_device : per_device + owners]
    q_out, top_ref, total_ref, out_ref = refs[per_device + owners :]
    seq_index = lax.axis_index("seq")
    chip, core = seq_index // COPIES, seq_index % COPIES
    slots = key_refs[0].shape[1]
    width = LATENT + ROPE
    q = jnp.concatenate([ref[:, :width] for ref in q_refs], axis=0)

    fresh = q_refs[0][:, width:].astype(jnp.float32)
    fresh = jnp.concatenate(
        [fresh[n * SPEC : (n + 1) * SPEC] for n in range(width // ROPE)], axis=1
    )
    fresh = jnp.concatenate([fresh, jnp.zeros((16 - SPEC, width), jnp.float32)], axis=0)
    fresh = fresh.astype(jnp.bfloat16)
    f = lax.dot_general(
        q, fresh, (((1,), (1,)), ((), ())), preferred_element_type=jnp.float32
    )
    row = lax.broadcasted_iota(jnp.int32, f.shape, 0) % (SPEC * heads)
    key = lax.broadcasted_iota(jnp.int32, f.shape, 1)
    f = jnp.where(key <= row // heads, f * SCORE_SCALE, masked_value)

    starts = [((chip ^ partner(k, core)) * COPIES + core) * slots for k in range(owners)]
    s = block_scores(q, key_refs, starts, limit_ref)
    top = jnp.maximum(jnp.max(s, axis=1, keepdims=True), jnp.max(f, axis=1, keepdims=True))
    total, out = weigh(s, key_refs, top)
    w = jnp.exp(f - top)
    total += jnp.sum(w, axis=1, keepdims=True)
    out += jnp.dot(
        w.astype(jnp.bfloat16), fresh[:, :LATENT], preferred_element_type=jnp.float32
    )
    q_out[...] = q
    top_ref[...] = jnp.broadcast_to(top, top_ref.shape)
    total_ref[...] = jnp.broadcast_to(total, total_ref.shape)
    out_ref[...] = out


def finish_kernel(
    owners, per_device, limit_ref, q_ref, top_ref, total_ref, part_ref, pair_ref, *refs
):
    key_refs = [pair_ref.at[0], pair_ref.at[1], *refs[: owners - 2]]
    outs = refs[owners - 2 :]
    seq_index = lax.axis_index("seq")
    chip, core = seq_index // COPIES, seq_index % COPIES
    plane = lax.axis_index("head")
    slots = key_refs[0].shape[1]
    starts = [((chip ^ partner(k, 1 - core)) * COPIES + 1 - core) * slots for k in range(owners)]
    s = block_scores(q_ref[...], key_refs, starts, limit_ref)
    first = top_ref[:, :1]
    top = jnp.maximum(first, jnp.max(s, axis=1, keepdims=True))
    total, out = weigh(s, key_refs, top)
    scale = jnp.exp(first - top)
    total += total_ref[:, :1] * scale
    out += part_ref[...] * scale
    out = (out * (1.0 / total)).astype(jnp.bfloat16)
    piece = out.shape[0] // per_device
    sent_first = first_block(plane, chip, core)
    for k in range(per_device):
        for n in range(per_device):

            @pl.when(sent_first ^ k == n)
            def _():
                outs[k][...] = out[n * piece : (n + 1) * piece]


def project_kernel(per_device, w_ref, *refs):
    lat_refs, out_ref = refs[:-1], refs[-1]
    rows, heads, width = out_ref.shape
    first = first_back(lax.axis_index("seq") // COPIES, lax.axis_index("head"))
    parts = [jnp.where(first == a, lat_refs[1][...], lat_refs[0][...]) for a in range(per_device)]
    latent = jnp.concatenate(parts, axis=0)
    out = jnp.zeros((rows * heads, width), jnp.float32)
    own_head = lax.broadcasted_iota(jnp.int32, out.shape, 0) % heads
    step = 2 if heads % 2 == 0 else 1
    for h in range(0, heads, step):
        group = jnp.concatenate([w_ref[h + n] for n in range(step)], axis=1)
        product = jnp.dot(latent, group, preferred_element_type=jnp.float32)
        for n in range(step):
            out = jnp.where(own_head == h + n, product[:, n * width : (n + 1) * width], out)
    out_ref[...] = out.astype(out_ref.dtype).reshape(out_ref.shape)


def whole_sequences(seq_size, head_size, queries, new_latent, cache, lengths, w_uk, w_uv):
    rows, heads, q_width = queries.shape
    owners, slots, width = cache.shape
    per_device = rows // SPEC
    piece = SPEC * heads
    all_rows = per_device * piece
    params = pltpu.CompilerParams(vmem_limit_bytes=VMEM_LIMIT)
    vmem = pl.BlockSpec(memory_space=pltpu.VMEM)
    anywhere = pl.BlockSpec(memory_space=pl.ANY)
    both = ("seq", "head")
    devices = [(i, j) for i in range(seq_size) for j in range(head_size)]

    def flat(seq_index, head_index):
        return seq_index * head_size + head_index

    def in_hbm(x):
        return pltpu.with_memory_space_constraint(x, pltpu.HBM)

    def host(i, j):
        other = (i // COPIES) ^ (2 - ((j ^ (j >> 1)) & 1))
        return flat(((i % COPIES) * 2 + other // 2) * COPIES + other % 2, j)

    def owner(i, j, a):
        plane, chip = i // COPIES, (i % COPIES * per_device + a) ^ 1
        return flat(chip * COPIES + 1 - j // 2, plane)

    def in_plane(move):
        return [(g * COPIES + t, move(g, t)) for g in range(owners) for t in range(COPIES)]

    *picked, packed, limit = pl.pallas_call(
        functools.partial(pick_kernel, per_device),
        out_shape=[jax.ShapeDtypeStruct((width, slots), cache.dtype)] * owners
        + [
            jax.ShapeDtypeStruct((all_rows, q_width + ROPE), queries.dtype),
            jax.ShapeDtypeStruct((8, slots), jnp.int32),
        ],
        in_specs=[anywhere] * 4,
        out_specs=[vmem] * (owners + 2),
        scratch_shapes=[
            pltpu.VMEM(queries.shape, queries.dtype),
            pltpu.VMEM(new_latent.shape, new_latent.dtype),
            pltpu.SMEM(lengths.shape, lengths.dtype),
            pltpu.SemaphoreType.DMA((3 + owners * COPY_PARTS,)),
        ],
        compiler_params=params,
        cost_estimate=LONG,
    )(*[in_hbm(x) for x in (jnp.swapaxes(cache, 1, 2), queries, new_latent, lengths)])
    moved = lax.ppermute(packed, both, [(flat(i, j), host(i, j)) for i, j in devices])
    own_keys = [picked[0]] + [
        lax.ppermute(picked[k], "seq", in_plane(lambda g, t: (g ^ partner(k, t)) * COPIES + t))
        for k in range(1, owners)
    ]
    pair = pl.pallas_call(
        pair_kernel,
        out_shape=jax.ShapeDtypeStruct((2, *picked[0].shape), cache.dtype),
        in_specs=[vmem] * 2,
        out_specs=vmem,
        scratch_shapes=[pltpu.SemaphoreType.DMA((2,))],
        compiler_params=params,
    )(*own_keys[:2])
    other_core = in_plane(lambda g, t: g * COPIES + 1 - t)
    far_keys = [lax.ppermute(keys, "seq", other_core) for keys in [pair] + own_keys[2:]]

    pieces = pl.pallas_call(
        functools.partial(absorb_kernel, per_device),
        out_shape=[jax.ShapeDtypeStruct((piece, width + ROPE), cache.dtype)] * per_device,
        in_specs=[vmem] * 2,
        out_specs=[vmem] * per_device,
        compiler_params=params,
        cost_estimate=LONG,
    )(w_uk, moved)
    arrived = [
        lax.ppermute(
            pieces[k],
            both,
            [(host(i, j), owner(i, j, leaves_as(k, j))) for i, j in devices],
        )
        for k in range(per_device)
    ]

    state = pl.pallas_call(
        functools.partial(begin_kernel, owners, per_device, heads),
        out_shape=[
            jax.ShapeDtypeStruct((all_rows, width), jnp.bfloat16),
            jax.ShapeDtypeStruct((all_rows, 128), jnp.float32),
            jax.ShapeDtypeStruct((all_rows, 128), jnp.float32),
            jax.ShapeDtypeStruct((all_rows, LATENT), jnp.float32),
        ],
        in_specs=[vmem] * (1 + per_device + owners),
        out_specs=[vmem] * 4,
        compiler_params=params,
        cost_estimate=LONG,
    )(limit, *arrived, *own_keys)
    latent = pl.pallas_call(
        functools.partial(finish_kernel, owners, per_device),
        out_shape=[jax.ShapeDtypeStruct((piece, LATENT), jnp.bfloat16)] * per_device,
        in_specs=[vmem] * (1 + len(state) + len(far_keys)),
        out_specs=[vmem] * per_device,
        compiler_params=params,
    )(limit, *state, *far_keys)

    back = [
        lax.ppermute(
            latent[k],
            both,
            [(owner(i, j, first_back(i // COPIES, j) ^ k), flat(i, j)) for i, j in devices],
        )
        for k in range(per_device)
    ]
    return pl.pallas_call(
        functools.partial(project_kernel, per_device),
        out_shape=jax.ShapeDtypeStruct((rows, heads, w_uv.shape[2]), jnp.bfloat16),
        in_specs=[vmem] * (1 + per_device),
        out_specs=vmem,
        compiler_params=params,
    )(w_uv, *back[::-1])


def local_partial(
    query_tile_block,
    key_tile_block,
    incoming_keys,
    len_block,
    offset,
    own_first,
    score_scale,
    head_count,
):
    scores = (
        jnp.einsum(
            "vfa,vja->vfj", query_tile_block, key_tile_block, preferred_element_type=jnp.float32
        )
        * score_scale
    )
    positions = offset + lax.broadcasted_iota(jnp.int32, (1, 1, key_tile_block.shape[1]), 2)
    visible = positions < len_block[:, None, None]
    fresh_scores = (
        jnp.einsum(
            "vfa,vja->vfj", query_tile_block, incoming_keys, preferred_element_type=jnp.float32
        )
        * score_scale
    )
    spec_count = incoming_keys.shape[1]
    row_spec = (
        lax.broadcasted_iota(jnp.int32, (1, query_tile_block.shape[1], spec_count), 1) // head_count
    )
    key_spec = lax.broadcasted_iota(jnp.int32, (1, query_tile_block.shape[1], spec_count), 2)
    causal = (key_spec <= row_spec) & own_first
    row_top = jnp.maximum(
        jnp.max(jnp.where(visible, scores, masked_value), axis=2),
        jnp.max(jnp.where(causal, fresh_scores, masked_value), axis=2),
    )
    weights = jnp.where(visible, jnp.exp(scores - row_top[..., None]), 0.0)
    fresh_weights = jnp.where(causal, jnp.exp(fresh_scores - row_top[..., None]), 0.0)
    running_totals = jnp.sum(weights, axis=2) + jnp.sum(fresh_weights, axis=2)
    weighted = jnp.einsum(
        "mpu,mui->mpi",
        weights.astype(jnp.bfloat16),
        key_tile_block[:, :, :LATENT],
        preferred_element_type=jnp.float32,
    )
    weighted = weighted + jnp.einsum(
        "mpu,mui->mpi",
        fresh_weights.astype(jnp.bfloat16),
        incoming_keys[:, :, :LATENT],
        preferred_element_type=jnp.float32,
    )
    return (row_top, running_totals, weighted)


def project_values(latent_rows, value_weight):
    return jnp.einsum("rhc,hcv->rhv", latent_rows, value_weight, precision=lax.Precision.HIGHEST)


def split_positions(queries, new_latent, cache, lengths, w_uk, w_uv):
    own_rows, head_count, _ = queries.shape
    score_scale = (NOPE + ROPE) ** (-0.5)
    gathered, new_all = (
        lax.all_gather(queries, "seq", axis=0, tiled=True),
        lax.all_gather(new_latent, "seq", axis=0, tiled=True),
    )
    absorbed = jnp.einsum(
        "rhn,hnc->rhc", gathered[:, :, :NOPE], w_uk, preferred_element_type=jnp.float32
    ).astype(jnp.bfloat16)
    q_all = jnp.concatenate([absorbed, gathered[:, :, NOPE:]], axis=2)
    total_rows = q_all.shape[0]
    seq_count = total_rows // SPEC
    query_slots = SPEC * head_count
    q_seq = q_all.reshape(seq_count, query_slots, q_all.shape[2])
    new_seq = new_all.reshape(seq_count, SPEC, new_all.shape[1])
    seq_index = lax.axis_index("seq")
    offset = seq_index * cache.shape[1]
    own_first = seq_index == 0
    row_top, running_totals, weighted = local_partial(
        q_seq,
        lax.all_gather(cache, "head", axis=0, tiled=True),
        new_seq,
        lengths,
        offset,
        own_first,
        score_scale,
        head_count,
    )
    value_weight = w_uv.astype(jnp.float32)
    global_top = lax.pmax(row_top, "seq")
    factor = jnp.exp(row_top - global_top)
    scaled_totals = (running_totals * factor).reshape(total_rows, head_count)
    scaled_weighted = (weighted * factor[..., None]).reshape(total_rows, head_count, LATENT)
    row_totals, row_weighted = (
        lax.psum_scatter(scaled_totals, "seq", scatter_dimension=0, tiled=True),
        lax.psum_scatter(scaled_weighted, "seq", scatter_dimension=0, tiled=True),
    )
    latent_output = row_weighted / row_totals[..., None]
    result = project_values(latent_output, value_weight)
    return result.astype(jnp.bfloat16)


def shards(seq_size, head_size, queries, new_latent, cache, lengths, w_uk, w_uv):
    rows, owners = queries.shape[0], cache.shape[0]
    per_device = rows // SPEC
    if (
        per_device == 2
        and rows % SPEC == 0
        and seq_size == COPIES * owners
        and head_size == owners == 4
        and cache.shape[2] % (16 * COPY_PARTS) == 0
    ):
        return whole_sequences(
            seq_size, head_size, queries, new_latent, cache, lengths, w_uk, w_uv
        )
    return split_positions(queries, new_latent, cache, lengths, w_uk, w_uv)


def solution(mesh):
    return jax.shard_map(
        functools.partial(shards, mesh.shape["seq"], mesh.shape["head"]),
        mesh=mesh,
        in_specs=(
            P("seq", "head", None),
            P("seq", None),
            P("head", "seq", None),
            P(),
            P("head", None, None),
            P("head", None, None),
        ),
        out_specs=P("seq", "head", None),
        check_vma=False,
    )
```

```python
import functools

import jax
import jax.numpy as jnp
from jax import lax
from jax.experimental import pallas as pl
from jax.experimental.pallas import tpu as pltpu
from jax.sharding import PartitionSpec as P

NOPE = 128
ROPE = 64
LATENT = 512
SPEC = 4
SCORE_SCALE = (NOPE + ROPE) ** (-0.5)
COPIES = 2
COPY_PARTS = 3
VMEM_LIMIT = 16 * 1024 * 1024
LONG = pl.CostEstimate(flops=2 * 10**10, bytes_accessed=0, transcendentals=0)

masked_value = -1e30


def leaves_as(k, head_shard):
    return (k + head_shard) % 2


def far_half(plane, pair):
    return 1 * (plane <= 2 * pair)


def first_back(home_chip, head_shard):
    far = 1 * (far_half(home_chip, head_shard // 2) == head_shard % 2)
    return home_chip % 2 ^ far


def first_block(plane, chip, core):
    near = 1 * (chip % 2 == plane % 2)
    return far_half(plane, 1 - core) ^ near ^ chip % 2


def partner(k, core):
    return (0, 3, 1 ^ 3 * core, 2 ^ 3 * core)[k]


def pick_kernel(per_device, cache_hbm, q_hbm, new_hbm, len_hbm, *refs):
    owners = cache_hbm.shape[0]
    blocks, (out_ref, limit_ref, q_ref, new_ref, len_ref, sem) = refs[:owners], refs[owners:]
    chip, core = lax.axis_index("seq") // COPIES, lax.axis_index("seq") % COPIES
    moves = [
        pltpu.make_async_copy(q_hbm, q_ref, sem.at[0]),
        pltpu.make_async_copy(new_hbm, new_ref, sem.at[1]),
        pltpu.make_async_copy(len_hbm, len_ref, sem.at[2]),
    ]
    part = cache_hbm.shape[1] // COPY_PARTS
    for k in range(owners):
        for n in range(COPY_PARTS):
            rows = pl.ds(n * part, part)
            moves.append(
                pltpu.make_async_copy(
                    cache_hbm.at[chip ^ partner(k, core), rows],
                    blocks[k].at[rows],
                    sem.at[3 + k * COPY_PARTS + n],
                )
            )
    for move in moves:
        move.start()
    moves[0].wait()
    moves[1].wait()
    heads, width = q_ref.shape[1:]
    fresh = new_ref[...].astype(jnp.float32)
    piece = SPEC * heads
    for a in range(per_device):
        rows = q_ref[a * SPEC : (a + 1) * SPEC].reshape(piece, width)
        own = fresh[a * SPEC : (a + 1) * SPEC]
        parts = [own[:, n : n + ROPE] for n in range(0, own.shape[1], ROPE)]
        spare = piece - SPEC * len(parts)
        if spare:
            parts.append(jnp.zeros((spare, ROPE), jnp.float32))
        own = jnp.concatenate(parts, axis=0).astype(rows.dtype)
        out_ref[a * piece : (a + 1) * piece] = jnp.concatenate([rows, own], axis=1)
    moves[2].wait()
    length = len_ref[lax.axis_index("head") * owners + chip]
    limit_ref[...] = jnp.full(limit_ref.shape, length, limit_ref.dtype)
    for move in moves[3:]:
        move.wait()


def pair_kernel(first_ref, second_ref, out_ref, sem):
    moves = [
        pltpu.make_async_copy(ref, out_ref.at[n], sem.at[n])
        for n, ref in enumerate((first_ref, second_ref))
    ]
    for move in moves:
        move.start()
    for move in moves:
        move.wait()


def absorb_kernel(per_device, w_ref, packed_ref, *outs):
    heads = w_ref.shape[0]
    piece = SPEC * heads
    nope = packed_ref[:, :NOPE]
    own_head = lax.broadcasted_iota(jnp.int32, nope.shape, 0) % heads
    spread = jnp.concatenate(
        [jnp.where(own_head == h, nope, jnp.zeros_like(nope)) for h in range(heads)], axis=1
    )
    absorbed = jnp.dot(
        spread, w_ref[...].reshape(heads * NOPE, LATENT), preferred_element_type=jnp.float32
    ).astype(jnp.bfloat16)
    for k in range(per_device):
        which = leaves_as(k, lax.axis_index("head"))
        for a in range(per_device):

            @pl.when(which == a)
            def _():
                rows = slice(a * piece, (a + 1) * piece)
                outs[k][:, :LATENT] = absorbed[rows]
                outs[k][:, LATENT:] = packed_ref[rows, NOPE:]


def block_scores(q, refs, starts, limit_ref):
    width = q.shape[1]
    keys = jnp.concatenate([ref[:width, :] for ref in refs], axis=1)
    limit = limit_ref[:1, :]
    lane = lax.broadcasted_iota(jnp.int32, limit.shape, 1)
    visible = jnp.concatenate([lane + start < limit for start in starts], axis=1)
    s = jnp.dot(q, keys, preferred_element_type=jnp.float32) * SCORE_SCALE
    return jnp.where(visible, s, masked_value)


def weigh(s, refs, top):
    w = jnp.exp(s - top)
    values = jnp.concatenate([ref[:LATENT, :] for ref in refs], axis=1)
    out = lax.dot_general(
        w.astype(jnp.bfloat16),
        values,
        (((1,), (1,)), ((), ())),
        preferred_element_type=jnp.float32,
    )
    return jnp.sum(w, axis=1, keepdims=True), out


def begin_kernel(owners, per_device, heads, limit_ref, *refs):
    q_refs, key_refs = refs[:per_device], refs[per_device : per_device + owners]
    q_out, top_ref, total_ref, out_ref = refs[per_device + owners :]
    seq_index = lax.axis_index("seq")
    chip, core = seq_index // COPIES, seq_index % COPIES
    slots = key_refs[0].shape[1]
    width = LATENT + ROPE
    q = jnp.concatenate([ref[:, :width] for ref in q_refs], axis=0)

    fresh = q_refs[0][:, width:].astype(jnp.float32)
    fresh = jnp.concatenate(
        [fresh[n * SPEC : (n + 1) * SPEC] for n in range(width // ROPE)], axis=1
    )
    fresh = jnp.concatenate([fresh, jnp.zeros((16 - SPEC, width), jnp.float32)], axis=0)
    fresh = fresh.astype(jnp.bfloat16)
    f = lax.dot_general(
        q, fresh, (((1,), (1,)), ((), ())), preferred_element_type=jnp.float32
    )
    row = lax.broadcasted_iota(jnp.int32, f.shape, 0) % (SPEC * heads)
    key = lax.broadcasted_iota(jnp.int32, f.shape, 1)
    f = jnp.where(key <= row // heads, f * SCORE_SCALE, masked_value)

    starts = [((chip ^ partner(k, core)) * COPIES + core) * slots for k in range(owners)]
    s = block_scores(q, key_refs, starts, limit_ref)
    top = jnp.maximum(jnp.max(s, axis=1, keepdims=True), jnp.max(f, axis=1, keepdims=True))
    total, out = weigh(s, key_refs, top)
    w = jnp.exp(f - top)
    total += jnp.sum(w, axis=1, keepdims=True)
    out += jnp.dot(
        w.astype(jnp.bfloat16), fresh[:, :LATENT], preferred_element_type=jnp.float32
    )
    q_out[...] = q
    top_ref[...] = jnp.broadcast_to(top, top_ref.shape)
    total_ref[...] = jnp.broadcast_to(total, total_ref.shape)
    out_ref[...] = out


def finish_kernel(
    owners, per_device, limit_ref, q_ref, top_ref, total_ref, part_ref, pair_ref, *refs
):
    key_refs = [pair_ref.at[0], pair_ref.at[1], *refs[: owners - 2]]
    outs = refs[owners - 2 :]
    seq_index = lax.axis_index("seq")
    chip, core = seq_index // COPIES, seq_index % COPIES
    plane = lax.axis_index("head")
    slots = key_refs[0].shape[1]
    starts = [((chip ^ partner(k, 1 - core)) * COPIES + 1 - core) * slots for k in range(owners)]
    s = block_scores(q_ref[...], key_refs, starts, limit_ref)
    first = top_ref[:, :1]
    top = jnp.maximum(first, jnp.max(s, axis=1, keepdims=True))
    total, out = weigh(s, key_refs, top)
    scale = jnp.exp(first - top)
    total += total_ref[:, :1] * scale
    out += part_ref[...] * scale
    out = (out * (1.0 / total)).astype(jnp.bfloat16)
    piece = out.shape[0] // per_device
    sent_first = first_block(plane, chip, core)
    for k in range(per_device):
        for n in range(per_device):

            @pl.when(sent_first ^ k == n)
            def _():
                outs[k][...] = out[n * piece : (n + 1) * piece]


def project_kernel(per_device, w_ref, *refs):
    lat_refs, out_ref = refs[:-1], refs[-1]
    rows, heads, width = out_ref.shape
    latent = jnp.concatenate([ref[...] for ref in lat_refs], axis=0)
    out = jnp.zeros((rows * heads, width), jnp.float32)
    own_head = lax.broadcasted_iota(jnp.int32, out.shape, 0) % heads
    step = 2 if heads % 2 == 0 else 1
    for h in range(0, heads, step):
        group = jnp.concatenate([w_ref[h + n] for n in range(step)], axis=1)
        product = jnp.dot(latent, group, preferred_element_type=jnp.float32)
        for n in range(step):
            out = jnp.where(own_head == h + n, product[:, n * width : (n + 1) * width], out)
    out = out.astype(out_ref.dtype)
    first = first_back(lax.axis_index("seq") // COPIES, lax.axis_index("head"))
    piece = SPEC * heads
    for n in range(per_device):
        for a in range(per_device):

            @pl.when(first ^ n != a)
            def _():
                block = out[n * piece : (n + 1) * piece]
                out_ref[a * SPEC : (a + 1) * SPEC] = block.reshape(SPEC, heads, width)


def whole_sequences(seq_size, head_size, queries, new_latent, cache, lengths, w_uk, w_uv):
    rows, heads, q_width = queries.shape
    owners, slots, width = cache.shape
    per_device = rows // SPEC
    piece = SPEC * heads
    all_rows = per_device * piece
    params = pltpu.CompilerParams(vmem_limit_bytes=VMEM_LIMIT)
    vmem = pl.BlockSpec(memory_space=pltpu.VMEM)
    anywhere = pl.BlockSpec(memory_space=pl.ANY)
    both = ("seq", "head")
    devices = [(i, j) for i in range(seq_size) for j in range(head_size)]

    def flat(seq_index, head_index):
        return seq_index * head_size + head_index

    def in_hbm(x):
        return pltpu.with_memory_space_constraint(x, pltpu.HBM)

    def host(i, j):
        other = (i // COPIES) ^ (2 - ((j ^ (j >> 1)) & 1))
        return flat(((i % COPIES) * 2 + other // 2) * COPIES + other % 2, j)

    def owner(i, j, a):
        plane, chip = i // COPIES, i % COPIES * per_device + a
        return flat(chip * COPIES + 1 - j // 2, plane)

    def in_plane(move):
        return [(g * COPIES + t, move(g, t)) for g in range(owners) for t in range(COPIES)]

    *picked, packed, limit = pl.pallas_call(
        functools.partial(pick_kernel, per_device),
        out_shape=[jax.ShapeDtypeStruct((width, slots), cache.dtype)] * owners
        + [
            jax.ShapeDtypeStruct((all_rows, q_width + ROPE), queries.dtype),
            jax.ShapeDtypeStruct((8, slots), jnp.int32),
        ],
        in_specs=[anywhere] * 4,
        out_specs=[vmem] * (owners + 2),
        scratch_shapes=[
            pltpu.VMEM(queries.shape, queries.dtype),
            pltpu.VMEM(new_latent.shape, new_latent.dtype),
            pltpu.SMEM(lengths.shape, lengths.dtype),
            pltpu.SemaphoreType.DMA((3 + owners * COPY_PARTS,)),
        ],
        compiler_params=params,
        cost_estimate=LONG,
    )(*[in_hbm(x) for x in (jnp.swapaxes(cache, 1, 2), queries, new_latent, lengths)])
    moved = lax.ppermute(packed, both, [(flat(i, j), host(i, j)) for i, j in devices])
    own_keys = [picked[0]] + [
        lax.ppermute(picked[k], "seq", in_plane(lambda g, t: (g ^ partner(k, t)) * COPIES + t))
        for k in range(1, owners)
    ]
    pair = pl.pallas_call(
        pair_kernel,
        out_shape=jax.ShapeDtypeStruct((2, *picked[0].shape), cache.dtype),
        in_specs=[vmem] * 2,
        out_specs=vmem,
        scratch_shapes=[pltpu.SemaphoreType.DMA((2,))],
        compiler_params=params,
    )(*own_keys[:2])
    other_core = in_plane(lambda g, t: g * COPIES + 1 - t)
    far_keys = [lax.ppermute(keys, "seq", other_core) for keys in [pair] + own_keys[2:]]

    pieces = pl.pallas_call(
        functools.partial(absorb_kernel, per_device),
        out_shape=[jax.ShapeDtypeStruct((piece, width + ROPE), cache.dtype)] * per_device,
        in_specs=[vmem] * 2,
        out_specs=[vmem] * per_device,
        compiler_params=params,
        cost_estimate=LONG,
    )(w_uk, moved)
    arrived = [
        lax.ppermute(
            pieces[k],
            both,
            [(host(i, j), owner(i, j, leaves_as(k, j))) for i, j in devices],
        )
        for k in range(per_device)
    ]

    state = pl.pallas_call(
        functools.partial(begin_kernel, owners, per_device, heads),
        out_shape=[
            jax.ShapeDtypeStruct((all_rows, width), jnp.bfloat16),
            jax.ShapeDtypeStruct((all_rows, 128), jnp.float32),
            jax.ShapeDtypeStruct((all_rows, 128), jnp.float32),
            jax.ShapeDtypeStruct((all_rows, LATENT), jnp.float32),
        ],
        in_specs=[vmem] * (1 + per_device + owners),
        out_specs=[vmem] * 4,
        compiler_params=params,
        cost_estimate=LONG,
    )(limit, *arrived, *own_keys)
    latent = pl.pallas_call(
        functools.partial(finish_kernel, owners, per_device),
        out_shape=[jax.ShapeDtypeStruct((piece, LATENT), jnp.bfloat16)] * per_device,
        in_specs=[vmem] * (1 + len(state) + len(far_keys)),
        out_specs=[vmem] * per_device,
        compiler_params=params,
    )(limit, *state, *far_keys)

    back = [
        lax.ppermute(
            latent[k],
            both,
            [(owner(i, j, first_back(i // COPIES, j) ^ k), flat(i, j)) for i, j in devices],
        )
        for k in range(per_device)
    ]
    return pl.pallas_call(
        functools.partial(project_kernel, per_device),
        out_shape=jax.ShapeDtypeStruct((rows, heads, w_uv.shape[2]), jnp.bfloat16),
        in_specs=[vmem] * (1 + per_device),
        out_specs=vmem,
        compiler_params=params,
    )(w_uv, *back[::-1])


def local_partial(
    query_tile_block,
    key_tile_block,
    incoming_keys,
    len_block,
    offset,
    own_first,
    score_scale,
    head_count,
):
    scores = (
        jnp.einsum(
            "vfa,vja->vfj", query_tile_block, key_tile_block, preferred_element_type=jnp.float32
        )
        * score_scale
    )
    positions = offset + lax.broadcasted_iota(jnp.int32, (1, 1, key_tile_block.shape[1]), 2)
    visible = positions < len_block[:, None, None]
    fresh_scores = (
        jnp.einsum(
            "vfa,vja->vfj", query_tile_block, incoming_keys, preferred_element_type=jnp.float32
        )
        * score_scale
    )
    spec_count = incoming_keys.shape[1]
    row_spec = (
        lax.broadcasted_iota(jnp.int32, (1, query_tile_block.shape[1], spec_count), 1) // head_count
    )
    key_spec = lax.broadcasted_iota(jnp.int32, (1, query_tile_block.shape[1], spec_count), 2)
    causal = (key_spec <= row_spec) & own_first
    row_top = jnp.maximum(
        jnp.max(jnp.where(visible, scores, masked_value), axis=2),
        jnp.max(jnp.where(causal, fresh_scores, masked_value), axis=2),
    )
    weights = jnp.where(visible, jnp.exp(scores - row_top[..., None]), 0.0)
    fresh_weights = jnp.where(causal, jnp.exp(fresh_scores - row_top[..., None]), 0.0)
    running_totals = jnp.sum(weights, axis=2) + jnp.sum(fresh_weights, axis=2)
    weighted = jnp.einsum(
        "mpu,mui->mpi",
        weights.astype(jnp.bfloat16),
        key_tile_block[:, :, :LATENT],
        preferred_element_type=jnp.float32,
    )
    weighted = weighted + jnp.einsum(
        "mpu,mui->mpi",
        fresh_weights.astype(jnp.bfloat16),
        incoming_keys[:, :, :LATENT],
        preferred_element_type=jnp.float32,
    )
    return (row_top, running_totals, weighted)


def project_values(latent_rows, value_weight):
    return jnp.einsum("rhc,hcv->rhv", latent_rows, value_weight, precision=lax.Precision.HIGHEST)


def split_positions(queries, new_latent, cache, lengths, w_uk, w_uv):
    own_rows, head_count, _ = queries.shape
    score_scale = (NOPE + ROPE) ** (-0.5)
    gathered, new_all = (
        lax.all_gather(queries, "seq", axis=0, tiled=True),
        lax.all_gather(new_latent, "seq", axis=0, tiled=True),
    )
    absorbed = jnp.einsum(
        "rhn,hnc->rhc", gathered[:, :, :NOPE], w_uk, preferred_element_type=jnp.float32
    ).astype(jnp.bfloat16)
    q_all = jnp.concatenate([absorbed, gathered[:, :, NOPE:]], axis=2)
    total_rows = q_all.shape[0]
    seq_count = total_rows // SPEC
    query_slots = SPEC * head_count
    q_seq = q_all.reshape(seq_count, query_slots, q_all.shape[2])
    new_seq = new_all.reshape(seq_count, SPEC, new_all.shape[1])
    seq_index = lax.axis_index("seq")
    offset = seq_index * cache.shape[1]
    own_first = seq_index == 0
    row_top, running_totals, weighted = local_partial(
        q_seq,
        lax.all_gather(cache, "head", axis=0, tiled=True),
        new_seq,
        lengths,
        offset,
        own_first,
        score_scale,
        head_count,
    )
    value_weight = w_uv.astype(jnp.float32)
    global_top = lax.pmax(row_top, "seq")
    factor = jnp.exp(row_top - global_top)
    scaled_totals = (running_totals * factor).reshape(total_rows, head_count)
    scaled_weighted = (weighted * factor[..., None]).reshape(total_rows, head_count, LATENT)
    row_totals, row_weighted = (
        lax.psum_scatter(scaled_totals, "seq", scatter_dimension=0, tiled=True),
        lax.psum_scatter(scaled_weighted, "seq", scatter_dimension=0, tiled=True),
    )
    latent_output = row_weighted / row_totals[..., None]
    result = project_values(latent_output, value_weight)
    return result.astype(jnp.bfloat16)


def shards(seq_size, head_size, queries, new_latent, cache, lengths, w_uk, w_uv):
    rows, owners = queries.shape[0], cache.shape[0]
    per_device = rows // SPEC
    if (
        per_device == 2
        and rows % SPEC == 0
        and seq_size == COPIES * owners
        and head_size == owners == 4
        and cache.shape[2] % (16 * COPY_PARTS) == 0
    ):
        return whole_sequences(
            seq_size, head_size, queries, new_latent, cache, lengths, w_uk, w_uv
        )
    return split_positions(queries, new_latent, cache, lengths, w_uk, w_uv)


def solution(mesh):
    return jax.shard_map(
        functools.partial(shards, mesh.shape["seq"], mesh.shape["head"]),
        mesh=mesh,
        in_specs=(
            P("seq", "head", None),
            P("seq", None),
            P("head", "seq", None),
            P(),
            P("head", None, None),
            P("head", None, None),
        ),
        out_specs=P("seq", "head", None),
        check_vma=False,
    )
```

```python
import functools

import jax
import jax.numpy as jnp
from jax import lax
from jax.experimental import pallas as pl
from jax.experimental.pallas import tpu as pltpu
from jax.sharding import PartitionSpec as P

NOPE = 128
ROPE = 64
LATENT = 512
SPEC = 4
SCORE_SCALE = (NOPE + ROPE) ** (-0.5)
COPIES = 2
COPY_PARTS = 3
VMEM_LIMIT = 16 * 1024 * 1024
LONG = pl.CostEstimate(flops=2 * 10**10, bytes_accessed=0, transcendentals=0)

masked_value = -1e30


def leaves_as(k, head_shard):
    return (k + head_shard) % 2


def far_half(plane, pair):
    return 1 * (plane <= 2 * pair)


def first_back(home_chip, head_shard):
    far = 1 * (far_half(home_chip, head_shard // 2) == head_shard % 2)
    return home_chip % 2 ^ far


def first_block(plane, chip, core):
    near = 1 * (chip % 2 == plane % 2)
    return far_half(plane, 1 - core) ^ near ^ chip % 2


def partner(k, core):
    return (0, 3, 1 ^ 3 * core, 2 ^ 3 * core)[k]


def pick_kernel(per_device, cache_hbm, q_hbm, new_hbm, len_hbm, *refs):
    owners = cache_hbm.shape[0]
    blocks, (out_ref, limit_ref, q_ref, new_ref, len_ref, sem) = refs[:owners], refs[owners:]
    chip, core = lax.axis_index("seq") // COPIES, lax.axis_index("seq") % COPIES
    moves = [
        pltpu.make_async_copy(q_hbm, q_ref, sem.at[0]),
        pltpu.make_async_copy(new_hbm, new_ref, sem.at[1]),
        pltpu.make_async_copy(len_hbm, len_ref, sem.at[2]),
    ]
    part = cache_hbm.shape[1] // COPY_PARTS
    for k in range(owners):
        for n in range(COPY_PARTS):
            rows = pl.ds(n * part, part)
            moves.append(
                pltpu.make_async_copy(
                    cache_hbm.at[chip ^ partner(k, core), rows],
                    blocks[k].at[rows],
                    sem.at[3 + k * COPY_PARTS + n],
                )
            )
    for move in moves:
        move.start()
    moves[0].wait()
    moves[1].wait()
    heads, width = q_ref.shape[1:]
    fresh = new_ref[...].astype(jnp.float32)
    piece = SPEC * heads
    for a in range(per_device):
        rows = q_ref[a * SPEC : (a + 1) * SPEC].reshape(piece, width)
        own = fresh[a * SPEC : (a + 1) * SPEC]
        parts = [own[:, n : n + ROPE] for n in range(0, own.shape[1], ROPE)]
        spare = piece - SPEC * len(parts)
        if spare:
            parts.append(jnp.zeros((spare, ROPE), jnp.float32))
        own = jnp.concatenate(parts, axis=0).astype(rows.dtype)
        out_ref[a * piece : (a + 1) * piece] = jnp.concatenate([rows, own], axis=1)
    moves[2].wait()
    length = len_ref[lax.axis_index("head") * owners + chip]
    limit_ref[...] = jnp.full(limit_ref.shape, length, limit_ref.dtype)
    for move in moves[3:]:
        move.wait()


def pair_kernel(first_ref, second_ref, out_ref, sem):
    moves = [
        pltpu.make_async_copy(ref, out_ref.at[n], sem.at[n])
        for n, ref in enumerate((first_ref, second_ref))
    ]
    for move in moves:
        move.start()
    for move in moves:
        move.wait()


def absorb_kernel(per_device, w_ref, packed_ref, block_ref, *outs):
    del block_ref
    heads = w_ref.shape[0]
    piece = SPEC * heads
    nope = packed_ref[:, :NOPE]
    own_head = lax.broadcasted_iota(jnp.int32, nope.shape, 0) % heads
    spread = jnp.concatenate(
        [jnp.where(own_head == h, nope, jnp.zeros_like(nope)) for h in range(heads)], axis=1
    )
    absorbed = jnp.dot(
        spread, w_ref[...].reshape(heads * NOPE, LATENT), preferred_element_type=jnp.float32
    ).astype(jnp.bfloat16)
    for k in range(per_device):
        which = leaves_as(k, lax.axis_index("head"))
        for a in range(per_device):

            @pl.when(which == a)
            def _():
                rows = slice(a * piece, (a + 1) * piece)
                outs[k][:, :LATENT] = absorbed[rows]
                outs[k][:, LATENT:] = packed_ref[rows, NOPE:]


def block_scores(q, refs, starts, limit_ref):
    width = q.shape[1]
    keys = jnp.concatenate([ref[:width, :] for ref in refs], axis=1)
    limit = limit_ref[:1, :]
    lane = lax.broadcasted_iota(jnp.int32, limit.shape, 1)
    visible = jnp.concatenate([lane + start < limit for start in starts], axis=1)
    s = jnp.dot(q, keys, preferred_element_type=jnp.float32) * SCORE_SCALE
    return jnp.where(visible, s, masked_value)


def weigh(s, refs, top):
    w = jnp.exp(s - top)
    values = jnp.concatenate([ref[:LATENT, :] for ref in refs], axis=1)
    out = lax.dot_general(
        w.astype(jnp.bfloat16),
        values,
        (((1,), (1,)), ((), ())),
        preferred_element_type=jnp.float32,
    )
    return jnp.sum(w, axis=1, keepdims=True), out


def begin_kernel(owners, per_device, heads, limit_ref, *refs):
    q_refs, key_refs = refs[:per_device], refs[per_device : per_device + owners]
    q_out, top_ref, total_ref, out_ref = refs[per_device + owners :]
    seq_index = lax.axis_index("seq")
    chip, core = seq_index // COPIES, seq_index % COPIES
    slots = key_refs[0].shape[1]
    width = LATENT + ROPE
    q = jnp.concatenate([ref[:, :width] for ref in q_refs], axis=0)

    fresh = q_refs[0][:, width:].astype(jnp.float32)
    fresh = jnp.concatenate(
        [fresh[n * SPEC : (n + 1) * SPEC] for n in range(width // ROPE)], axis=1
    )
    fresh = jnp.concatenate([fresh, jnp.zeros((16 - SPEC, width), jnp.float32)], axis=0)
    fresh = fresh.astype(jnp.bfloat16)
    f = lax.dot_general(
        q, fresh, (((1,), (1,)), ((), ())), preferred_element_type=jnp.float32
    )
    row = lax.broadcasted_iota(jnp.int32, f.shape, 0) % (SPEC * heads)
    key = lax.broadcasted_iota(jnp.int32, f.shape, 1)
    f = jnp.where(key <= row // heads, f * SCORE_SCALE, masked_value)

    starts = [((chip ^ partner(k, core)) * COPIES + core) * slots for k in range(owners)]
    s = block_scores(q, key_refs, starts, limit_ref)
    top = jnp.maximum(jnp.max(s, axis=1, keepdims=True), jnp.max(f, axis=1, keepdims=True))
    total, out = weigh(s, key_refs, top)
    w = jnp.exp(f - top)
    total += jnp.sum(w, axis=1, keepdims=True)
    out += jnp.dot(
        w.astype(jnp.bfloat16), fresh[:, :LATENT], preferred_element_type=jnp.float32
    )
    q_out[...] = q
    top_ref[...] = jnp.broadcast_to(top, top_ref.shape)
    total_ref[...] = jnp.broadcast_to(total, total_ref.shape)
    out_ref[...] = out


def finish_kernel(
    owners, per_device, limit_ref, q_ref, top_ref, total_ref, part_ref, pair_ref, *refs
):
    key_refs = [pair_ref.at[0], pair_ref.at[1], *refs[: owners - 2]]
    outs = refs[owners - 2 :]
    seq_index = lax.axis_index("seq")
    chip, core = seq_index // COPIES, seq_index % COPIES
    plane = lax.axis_index("head")
    slots = key_refs[0].shape[1]
    starts = [((chip ^ partner(k, 1 - core)) * COPIES + 1 - core) * slots for k in range(owners)]
    s = block_scores(q_ref[...], key_refs, starts, limit_ref)
    first = top_ref[:, :1]
    top = jnp.maximum(first, jnp.max(s, axis=1, keepdims=True))
    total, out = weigh(s, key_refs, top)
    scale = jnp.exp(first - top)
    total += total_ref[:, :1] * scale
    out += part_ref[...] * scale
    out = (out * (1.0 / total)).astype(jnp.bfloat16)
    piece = out.shape[0] // per_device
    sent_first = first_block(plane, chip, core)
    for k in range(per_device):
        for n in range(per_device):

            @pl.when(sent_first ^ k == n)
            def _():
                outs[k][...] = out[n * piece : (n + 1) * piece]


def project_kernel(per_device, w_ref, *refs):
    lat_refs, out_ref = refs[:-1], refs[-1]
    rows, heads, width = out_ref.shape
    first = first_back(lax.axis_index("seq") // COPIES, lax.axis_index("head"))
    parts = [jnp.where(first == a, lat_refs[1][...], lat_refs[0][...]) for a in range(per_device)]
    latent = jnp.concatenate(parts, axis=0)
    out = jnp.zeros((rows * heads, width), jnp.float32)
    own_head = lax.broadcasted_iota(jnp.int32, out.shape, 0) % heads
    step = 2 if heads % 2 == 0 else 1
    for h in range(0, heads, step):
        group = jnp.concatenate([w_ref[h + n] for n in range(step)], axis=1)
        product = jnp.dot(latent, group, preferred_element_type=jnp.float32)
        for n in range(step):
            out = jnp.where(own_head == h + n, product[:, n * width : (n + 1) * width], out)
    out_ref[...] = out.astype(out_ref.dtype).reshape(out_ref.shape)


def whole_sequences(seq_size, head_size, queries, new_latent, cache, lengths, w_uk, w_uv):
    rows, heads, q_width = queries.shape
    owners, slots, width = cache.shape
    per_device = rows // SPEC
    piece = SPEC * heads
    all_rows = per_device * piece
    params = pltpu.CompilerParams(vmem_limit_bytes=VMEM_LIMIT)
    vmem = pl.BlockSpec(memory_space=pltpu.VMEM)
    anywhere = pl.BlockSpec(memory_space=pl.ANY)
    both = ("seq", "head")
    devices = [(i, j) for i in range(seq_size) for j in range(head_size)]

    def flat(seq_index, head_index):
        return seq_index * head_size + head_index

    def in_hbm(x):
        return pltpu.with_memory_space_constraint(x, pltpu.HBM)

    def host(i, j):
        other = (i // COPIES) ^ (2 - ((j ^ (j >> 1)) & 1))
        return flat(((i % COPIES) * 2 + other // 2) * COPIES + other % 2, j)

    def owner(i, j, a):
        plane, chip = i // COPIES, i % COPIES * per_device + a
        return flat(chip * COPIES + 1 - j // 2, plane)

    def in_plane(move):
        return [(g * COPIES + t, move(g, t)) for g in range(owners) for t in range(COPIES)]

    *picked, packed, limit = pl.pallas_call(
        functools.partial(pick_kernel, per_device),
        out_shape=[jax.ShapeDtypeStruct((width, slots), cache.dtype)] * owners
        + [
            jax.ShapeDtypeStruct((all_rows, q_width + ROPE), queries.dtype),
            jax.ShapeDtypeStruct((8, slots), jnp.int32),
        ],
        in_specs=[anywhere] * 4,
        out_specs=[vmem] * (owners + 2),
        scratch_shapes=[
            pltpu.VMEM(queries.shape, queries.dtype),
            pltpu.VMEM(new_latent.shape, new_latent.dtype),
            pltpu.SMEM(lengths.shape, lengths.dtype),
            pltpu.SemaphoreType.DMA((3 + owners * COPY_PARTS,)),
        ],
        compiler_params=params,
        cost_estimate=LONG,
    )(*[in_hbm(x) for x in (jnp.swapaxes(cache, 1, 2), queries, new_latent, lengths)])
    moved = lax.ppermute(packed, both, [(flat(i, j), host(i, j)) for i, j in devices])
    *pieces, picked[-1] = pl.pallas_call(
        functools.partial(absorb_kernel, per_device),
        out_shape=[jax.ShapeDtypeStruct((piece, width + ROPE), cache.dtype)] * per_device
        + [jax.ShapeDtypeStruct((width, slots), cache.dtype)],
        in_specs=[vmem] * 2 + [anywhere],
        out_specs=[vmem] * per_device + [anywhere],
        input_output_aliases={2: per_device},
        compiler_params=params,
        cost_estimate=LONG,
    )(w_uk, moved, picked[-1])
    own_keys = [picked[0]] + [
        lax.ppermute(picked[k], "seq", in_plane(lambda g, t: (g ^ partner(k, t)) * COPIES + t))
        for k in range(1, owners)
    ]
    pair = pl.pallas_call(
        pair_kernel,
        out_shape=jax.ShapeDtypeStruct((2, *picked[0].shape), cache.dtype),
        in_specs=[vmem] * 2,
        out_specs=vmem,
        scratch_shapes=[pltpu.SemaphoreType.DMA((2,))],
        compiler_params=params,
    )(*own_keys[:2])
    other_core = in_plane(lambda g, t: g * COPIES + 1 - t)
    far_keys = [lax.ppermute(keys, "seq", other_core) for keys in [pair] + own_keys[2:]]

    arrived = [
        lax.ppermute(
            pieces[k],
            both,
            [(host(i, j), owner(i, j, leaves_as(k, j))) for i, j in devices],
        )
        for k in range(per_device)
    ]

    state = pl.pallas_call(
        functools.partial(begin_kernel, owners, per_device, heads),
        out_shape=[
            jax.ShapeDtypeStruct((all_rows, width), jnp.bfloat16),
            jax.ShapeDtypeStruct((all_rows, 128), jnp.float32),
            jax.ShapeDtypeStruct((all_rows, 128), jnp.float32),
            jax.ShapeDtypeStruct((all_rows, LATENT), jnp.float32),
        ],
        in_specs=[vmem] * (1 + per_device + owners),
        out_specs=[vmem] * 4,
        compiler_params=params,
        cost_estimate=LONG,
    )(limit, *arrived, *own_keys)
    latent = pl.pallas_call(
        functools.partial(finish_kernel, owners, per_device),
        out_shape=[jax.ShapeDtypeStruct((piece, LATENT), jnp.bfloat16)] * per_device,
        in_specs=[vmem] * (1 + len(state) + len(far_keys)),
        out_specs=[vmem] * per_device,
        compiler_params=params,
    )(limit, *state, *far_keys)

    back = [
        lax.ppermute(
            latent[k],
            both,
            [(owner(i, j, first_back(i // COPIES, j) ^ k), flat(i, j)) for i, j in devices],
        )
        for k in range(per_device)
    ]
    return pl.pallas_call(
        functools.partial(project_kernel, per_device),
        out_shape=jax.ShapeDtypeStruct((rows, heads, w_uv.shape[2]), jnp.bfloat16),
        in_specs=[vmem] * (1 + per_device),
        out_specs=vmem,
        compiler_params=params,
    )(w_uv, *back[::-1])


def local_partial(
    query_tile_block,
    key_tile_block,
    incoming_keys,
    len_block,
    offset,
    own_first,
    score_scale,
    head_count,
):
    scores = (
        jnp.einsum(
            "vfa,vja->vfj", query_tile_block, key_tile_block, preferred_element_type=jnp.float32
        )
        * score_scale
    )
    positions = offset + lax.broadcasted_iota(jnp.int32, (1, 1, key_tile_block.shape[1]), 2)
    visible = positions < len_block[:, None, None]
    fresh_scores = (
        jnp.einsum(
            "vfa,vja->vfj", query_tile_block, incoming_keys, preferred_element_type=jnp.float32
        )
        * score_scale
    )
    spec_count = incoming_keys.shape[1]
    row_spec = (
        lax.broadcasted_iota(jnp.int32, (1, query_tile_block.shape[1], spec_count), 1) // head_count
    )
    key_spec = lax.broadcasted_iota(jnp.int32, (1, query_tile_block.shape[1], spec_count), 2)
    causal = (key_spec <= row_spec) & own_first
    row_top = jnp.maximum(
        jnp.max(jnp.where(visible, scores, masked_value), axis=2),
        jnp.max(jnp.where(causal, fresh_scores, masked_value), axis=2),
    )
    weights = jnp.where(visible, jnp.exp(scores - row_top[..., None]), 0.0)
    fresh_weights = jnp.where(causal, jnp.exp(fresh_scores - row_top[..., None]), 0.0)
    running_totals = jnp.sum(weights, axis=2) + jnp.sum(fresh_weights, axis=2)
    weighted = jnp.einsum(
        "mpu,mui->mpi",
        weights.astype(jnp.bfloat16),
        key_tile_block[:, :, :LATENT],
        preferred_element_type=jnp.float32,
    )
    weighted = weighted + jnp.einsum(
        "mpu,mui->mpi",
        fresh_weights.astype(jnp.bfloat16),
        incoming_keys[:, :, :LATENT],
        preferred_element_type=jnp.float32,
    )
    return (row_top, running_totals, weighted)


def project_values(latent_rows, value_weight):
    return jnp.einsum("rhc,hcv->rhv", latent_rows, value_weight, precision=lax.Precision.HIGHEST)


def split_positions(queries, new_latent, cache, lengths, w_uk, w_uv):
    own_rows, head_count, _ = queries.shape
    score_scale = (NOPE + ROPE) ** (-0.5)
    gathered, new_all = (
        lax.all_gather(queries, "seq", axis=0, tiled=True),
        lax.all_gather(new_latent, "seq", axis=0, tiled=True),
    )
    absorbed = jnp.einsum(
        "rhn,hnc->rhc", gathered[:, :, :NOPE], w_uk, preferred_element_type=jnp.float32
    ).astype(jnp.bfloat16)
    q_all = jnp.concatenate([absorbed, gathered[:, :, NOPE:]], axis=2)
    total_rows = q_all.shape[0]
    seq_count = total_rows // SPEC
    query_slots = SPEC * head_count
    q_seq = q_all.reshape(seq_count, query_slots, q_all.shape[2])
    new_seq = new_all.reshape(seq_count, SPEC, new_all.shape[1])
    seq_index = lax.axis_index("seq")
    offset = seq_index * cache.shape[1]
    own_first = seq_index == 0
    row_top, running_totals, weighted = local_partial(
        q_seq,
        lax.all_gather(cache, "head", axis=0, tiled=True),
        new_seq,
        lengths,
        offset,
        own_first,
        score_scale,
        head_count,
    )
    value_weight = w_uv.astype(jnp.float32)
    global_top = lax.pmax(row_top, "seq")
    factor = jnp.exp(row_top - global_top)
    scaled_totals = (running_totals * factor).reshape(total_rows, head_count)
    scaled_weighted = (weighted * factor[..., None]).reshape(total_rows, head_count, LATENT)
    row_totals, row_weighted = (
        lax.psum_scatter(scaled_totals, "seq", scatter_dimension=0, tiled=True),
        lax.psum_scatter(scaled_weighted, "seq", scatter_dimension=0, tiled=True),
    )
    latent_output = row_weighted / row_totals[..., None]
    result = project_values(latent_output, value_weight)
    return result.astype(jnp.bfloat16)


def shards(seq_size, head_size, queries, new_latent, cache, lengths, w_uk, w_uv):
    rows, owners = queries.shape[0], cache.shape[0]
    per_device = rows // SPEC
    if (
        per_device == 2
        and rows % SPEC == 0
        and seq_size == COPIES * owners
        and head_size == owners == 4
        and cache.shape[2] % (16 * COPY_PARTS) == 0
    ):
        return whole_sequences(
            seq_size, head_size, queries, new_latent, cache, lengths, w_uk, w_uv
        )
    return split_positions(queries, new_latent, cache, lengths, w_uk, w_uv)


def solution(mesh):
    return jax.shard_map(
        functools.partial(shards, mesh.shape["seq"], mesh.shape["head"]),
        mesh=mesh,
        in_specs=(
            P("seq", "head", None),
            P("seq", None),
            P("head", "seq", None),
            P(),
            P("head", None, None),
            P("head", None, None),
        ),
        out_specs=P("seq", "head", None),
        check_vma=False,
    )
```

```python
import functools

import jax
import jax.numpy as jnp
from jax import lax
from jax.experimental import pallas as pl
from jax.experimental.pallas import tpu as pltpu
from jax.sharding import PartitionSpec as P

NOPE = 128
ROPE = 64
LATENT = 512
SPEC = 4
SCORE_SCALE = (NOPE + ROPE) ** (-0.5)
COPIES = 2
COPY_PARTS = 3
VMEM_LIMIT = 16 * 1024 * 1024
LONG = pl.CostEstimate(flops=2 * 10**10, bytes_accessed=0, transcendentals=0)

masked_value = -1e30


def leaves_as(k, head_shard):
    return (k + head_shard) % 2


def far_half(plane, pair):
    return 1 * (plane <= 2 * pair)


def first_back(home_chip, head_shard):
    far = 1 * (far_half(home_chip, head_shard // 2) == head_shard % 2)
    return home_chip % 2 ^ far


def first_block(plane, chip, core):
    near = 1 * (chip % 2 == plane % 2)
    return far_half(plane, 1 - core) ^ near ^ chip % 2


def partner(k, core):
    return (0, 3, 1 ^ 3 * core, 2 ^ 3 * core)[k]


def pick_kernel(per_device, cache_hbm, q_hbm, new_hbm, len_hbm, *refs):
    owners = cache_hbm.shape[0]
    blocks, (out_ref, limit_ref, q_ref, new_ref, len_ref, sem) = refs[:owners], refs[owners:]
    chip, core = lax.axis_index("seq") // COPIES, lax.axis_index("seq") % COPIES
    moves = [
        pltpu.make_async_copy(q_hbm, q_ref, sem.at[0]),
        pltpu.make_async_copy(new_hbm, new_ref, sem.at[1]),
        pltpu.make_async_copy(len_hbm, len_ref, sem.at[2]),
    ]
    part = cache_hbm.shape[1] // COPY_PARTS
    for k in range(owners):
        for n in range(COPY_PARTS):
            rows = pl.ds(n * part, part)
            moves.append(
                pltpu.make_async_copy(
                    cache_hbm.at[chip ^ partner(k, core), rows],
                    blocks[k].at[rows],
                    sem.at[3 + k * COPY_PARTS + n],
                )
            )
    for move in moves:
        move.start()
    moves[0].wait()
    moves[1].wait()
    heads, width = q_ref.shape[1:]
    fresh = new_ref[...].astype(jnp.float32)
    piece = SPEC * heads
    for a in range(per_device):
        rows = q_ref[a * SPEC : (a + 1) * SPEC].reshape(piece, width)
        own = fresh[a * SPEC : (a + 1) * SPEC]
        parts = [own[:, n : n + ROPE] for n in range(0, own.shape[1], ROPE)]
        spare = piece - SPEC * len(parts)
        if spare:
            parts.append(jnp.zeros((spare, ROPE), jnp.float32))
        own = jnp.concatenate(parts, axis=0).astype(rows.dtype)
        out_ref[a * piece : (a + 1) * piece] = jnp.concatenate([rows, own], axis=1)
    moves[2].wait()
    length = len_ref[lax.axis_index("head") * owners + chip]
    limit_ref[...] = jnp.full(limit_ref.shape, length, limit_ref.dtype)
    for move in moves[3:]:
        move.wait()


def pair_kernel(first_ref, second_ref, out_ref, sem):
    moves = [
        pltpu.make_async_copy(ref, out_ref.at[n], sem.at[n])
        for n, ref in enumerate((first_ref, second_ref))
    ]
    for move in moves:
        move.start()
    for move in moves:
        move.wait()


def absorb_kernel(per_device, w_ref, packed_ref, *outs):
    heads = w_ref.shape[0]
    piece = SPEC * heads
    nope = packed_ref[:, :NOPE]
    own_head = lax.broadcasted_iota(jnp.int32, nope.shape, 0) % heads
    spread = jnp.concatenate(
        [jnp.where(own_head == h, nope, jnp.zeros_like(nope)) for h in range(heads)], axis=1
    )
    absorbed = jnp.dot(
        spread, w_ref[...].reshape(heads * NOPE, LATENT), preferred_element_type=jnp.float32
    ).astype(jnp.bfloat16)
    for k in range(per_device):
        which = leaves_as(k, lax.axis_index("head"))
        for a in range(per_device):

            @pl.when(which == a)
            def _():
                rows = slice(a * piece, (a + 1) * piece)
                outs[k][:, :LATENT] = absorbed[rows]
                outs[k][:, LATENT:] = packed_ref[rows, NOPE:]


def block_scores(q, refs, starts, limit_ref):
    width = q.shape[1]
    keys = jnp.concatenate([ref[:width, :] for ref in refs], axis=1)
    limit = limit_ref[:1, :]
    lane = lax.broadcasted_iota(jnp.int32, limit.shape, 1)
    visible = jnp.concatenate([lane + start < limit for start in starts], axis=1)
    s = jnp.dot(q, keys, preferred_element_type=jnp.float32) * SCORE_SCALE
    return jnp.where(visible, s, masked_value)


def weigh(s, refs, top):
    w = jnp.exp(s - top)
    values = jnp.concatenate([ref[:LATENT, :] for ref in refs], axis=1)
    out = lax.dot_general(
        w.astype(jnp.bfloat16),
        values,
        (((1,), (1,)), ((), ())),
        preferred_element_type=jnp.float32,
    )
    return jnp.sum(w, axis=1, keepdims=True), out


def begin_kernel(owners, per_device, heads, limit_ref, *refs):
    q_refs, key_refs = refs[:per_device], refs[per_device : per_device + owners]
    q_out, top_ref, total_ref, out_ref = refs[per_device + owners :]
    seq_index = lax.axis_index("seq")
    chip, core = seq_index // COPIES, seq_index % COPIES
    slots = key_refs[0].shape[1]
    width = LATENT + ROPE
    q = jnp.concatenate([ref[:, :width] for ref in q_refs], axis=0)

    fresh = q_refs[0][:, width:].astype(jnp.float32)
    fresh = jnp.concatenate(
        [fresh[n * SPEC : (n + 1) * SPEC] for n in range(width // ROPE)], axis=1
    )
    fresh = jnp.concatenate([fresh, jnp.zeros((16 - SPEC, width), jnp.float32)], axis=0)
    fresh = fresh.astype(jnp.bfloat16)
    f = lax.dot_general(
        q, fresh, (((1,), (1,)), ((), ())), preferred_element_type=jnp.float32
    )
    row = lax.broadcasted_iota(jnp.int32, f.shape, 0) % (SPEC * heads)
    key = lax.broadcasted_iota(jnp.int32, f.shape, 1)
    f = jnp.where(key <= row // heads, f * SCORE_SCALE, masked_value)

    starts = [((chip ^ partner(k, core)) * COPIES + core) * slots for k in range(owners)]
    s = block_scores(q, key_refs, starts, limit_ref)
    top = jnp.maximum(jnp.max(s, axis=1, keepdims=True), jnp.max(f, axis=1, keepdims=True))
    total, out = weigh(s, key_refs, top)
    w = jnp.exp(f - top)
    total += jnp.sum(w, axis=1, keepdims=True)
    out += jnp.dot(
        w.astype(jnp.bfloat16), fresh[:, :LATENT], preferred_element_type=jnp.float32
    )
    q_out[...] = q
    top_ref[...] = jnp.broadcast_to(top, top_ref.shape)
    total_ref[...] = jnp.broadcast_to(total, total_ref.shape)
    out_ref[...] = out


def finish_kernel(
    owners, place, limit_ref, q_ref, top_ref, total_ref, part_ref, pair_ref, *refs
):
    key_refs = [pair_ref.at[0], pair_ref.at[1], *refs[: owners - 2]]
    out_ref = refs[owners - 2]
    seq_index = lax.axis_index("seq")
    chip, core = seq_index // COPIES, seq_index % COPIES
    plane = lax.axis_index("head")
    slots = key_refs[0].shape[1]
    piece = out_ref.shape[0]
    rows = pl.ds(pl.multiple_of((first_block(plane, chip, core) ^ place) * piece, piece), piece)
    starts = [((chip ^ partner(k, 1 - core)) * COPIES + 1 - core) * slots for k in range(owners)]
    s = block_scores(q_ref[rows, :], key_refs, starts, limit_ref)
    first = top_ref[rows, :][:, :1]
    top = jnp.maximum(first, jnp.max(s, axis=1, keepdims=True))
    total, out = weigh(s, key_refs, top)
    scale = jnp.exp(first - top)
    total += total_ref[rows, :][:, :1] * scale
    out += part_ref[rows, :] * scale
    out_ref[...] = (out * (1.0 / total)).astype(out_ref.dtype)


def project_kernel(per_device, w_ref, *refs):
    lat_refs, out_ref = refs[:-1], refs[-1]
    rows, heads, width = out_ref.shape
    first = first_back(lax.axis_index("seq") // COPIES, lax.axis_index("head"))
    parts = [jnp.where(first == a, lat_refs[1][...], lat_refs[0][...]) for a in range(per_device)]
    latent = jnp.concatenate(parts, axis=0)
    out = jnp.zeros((rows * heads, width), jnp.float32)
    own_head = lax.broadcasted_iota(jnp.int32, out.shape, 0) % heads
    step = 2 if heads % 2 == 0 else 1
    for h in range(0, heads, step):
        group = jnp.concatenate([w_ref[h + n] for n in range(step)], axis=1)
        product = jnp.dot(latent, group, preferred_element_type=jnp.float32)
        for n in range(step):
            out = jnp.where(own_head == h + n, product[:, n * width : (n + 1) * width], out)
    out_ref[...] = out.astype(out_ref.dtype).reshape(out_ref.shape)


def whole_sequences(seq_size, head_size, queries, new_latent, cache, lengths, w_uk, w_uv):
    rows, heads, q_width = queries.shape
    owners, slots, width = cache.shape
    per_device = rows // SPEC
    piece = SPEC * heads
    all_rows = per_device * piece
    params = pltpu.CompilerParams(vmem_limit_bytes=VMEM_LIMIT)
    vmem = pl.BlockSpec(memory_space=pltpu.VMEM)
    anywhere = pl.BlockSpec(memory_space=pl.ANY)
    both = ("seq", "head")
    devices = [(i, j) for i in range(seq_size) for j in range(head_size)]

    def flat(seq_index, head_index):
        return seq_index * head_size + head_index

    def in_hbm(x):
        return pltpu.with_memory_space_constraint(x, pltpu.HBM)

    def host(i, j):
        other = (i // COPIES) ^ (2 - ((j ^ (j >> 1)) & 1))
        return flat(((i % COPIES) * 2 + other // 2) * COPIES + other % 2, j)

    def owner(i, j, a):
        plane, chip = i // COPIES, i % COPIES * per_device + a
        return flat(chip * COPIES + 1 - j // 2, plane)

    def in_plane(move):
        return [(g * COPIES + t, move(g, t)) for g in range(owners) for t in range(COPIES)]

    *picked, packed, limit = pl.pallas_call(
        functools.partial(pick_kernel, per_device),
        out_shape=[jax.ShapeDtypeStruct((width, slots), cache.dtype)] * owners
        + [
            jax.ShapeDtypeStruct((all_rows, q_width + ROPE), queries.dtype),
            jax.ShapeDtypeStruct((8, slots), jnp.int32),
        ],
        in_specs=[anywhere] * 4,
        out_specs=[vmem] * (owners + 2),
        scratch_shapes=[
            pltpu.VMEM(queries.shape, queries.dtype),
            pltpu.VMEM(new_latent.shape, new_latent.dtype),
            pltpu.SMEM(lengths.shape, lengths.dtype),
            pltpu.SemaphoreType.DMA((3 + owners * COPY_PARTS,)),
        ],
        compiler_params=params,
        cost_estimate=LONG,
    )(*[in_hbm(x) for x in (jnp.swapaxes(cache, 1, 2), queries, new_latent, lengths)])
    moved = lax.ppermute(packed, both, [(flat(i, j), host(i, j)) for i, j in devices])
    own_keys = [picked[0]] + [
        lax.ppermute(picked[k], "seq", in_plane(lambda g, t: (g ^ partner(k, t)) * COPIES + t))
        for k in range(1, owners)
    ]
    pair = pl.pallas_call(
        pair_kernel,
        out_shape=jax.ShapeDtypeStruct((2, *picked[0].shape), cache.dtype),
        in_specs=[vmem] * 2,
        out_specs=vmem,
        scratch_shapes=[pltpu.SemaphoreType.DMA((2,))],
        compiler_params=params,
    )(*own_keys[:2])
    other_core = in_plane(lambda g, t: g * COPIES + 1 - t)
    far_keys = [lax.ppermute(keys, "seq", other_core) for keys in [pair] + own_keys[2:]]

    pieces = pl.pallas_call(
        functools.partial(absorb_kernel, per_device),
        out_shape=[jax.ShapeDtypeStruct((piece, width + ROPE), cache.dtype)] * per_device,
        in_specs=[vmem] * 2,
        out_specs=[vmem] * per_device,
        compiler_params=params,
        cost_estimate=LONG,
    )(w_uk, moved)
    arrived = [
        lax.ppermute(
            pieces[k],
            both,
            [(host(i, j), owner(i, j, leaves_as(k, j))) for i, j in devices],
        )
        for k in range(per_device)
    ]

    state = pl.pallas_call(
        functools.partial(begin_kernel, owners, per_device, heads),
        out_shape=[
            jax.ShapeDtypeStruct((all_rows, width), jnp.bfloat16),
            jax.ShapeDtypeStruct((all_rows, 128), jnp.float32),
            jax.ShapeDtypeStruct((all_rows, 128), jnp.float32),
            jax.ShapeDtypeStruct((all_rows, LATENT), jnp.float32),
        ],
        in_specs=[vmem] * (1 + per_device + owners),
        out_specs=[vmem] * 4,
        compiler_params=params,
        cost_estimate=LONG,
    )(limit, *arrived, *own_keys)
    latent = [
        pl.pallas_call(
            functools.partial(finish_kernel, owners, k),
            out_shape=jax.ShapeDtypeStruct((piece, LATENT), jnp.bfloat16),
            in_specs=[vmem] * (1 + len(state) + len(far_keys)),
            out_specs=vmem,
            compiler_params=params,
            cost_estimate=LONG if k else None,
        )(limit, *state, *far_keys)
        for k in range(per_device)
    ]

    back = [
        lax.ppermute(
            latent[k],
            both,
            [(owner(i, j, first_back(i // COPIES, j) ^ k), flat(i, j)) for i, j in devices],
        )
        for k in range(per_device)
    ]
    return pl.pallas_call(
        functools.partial(project_kernel, per_device),
        out_shape=jax.ShapeDtypeStruct((rows, heads, w_uv.shape[2]), jnp.bfloat16),
        in_specs=[vmem] * (1 + per_device),
        out_specs=vmem,
        compiler_params=params,
    )(w_uv, *back[::-1])


def local_partial(
    query_tile_block,
    key_tile_block,
    incoming_keys,
    len_block,
    offset,
    own_first,
    score_scale,
    head_count,
):
    scores = (
        jnp.einsum(
            "vfa,vja->vfj", query_tile_block, key_tile_block, preferred_element_type=jnp.float32
        )
        * score_scale
    )
    positions = offset + lax.broadcasted_iota(jnp.int32, (1, 1, key_tile_block.shape[1]), 2)
    visible = positions < len_block[:, None, None]
    fresh_scores = (
        jnp.einsum(
            "vfa,vja->vfj", query_tile_block, incoming_keys, preferred_element_type=jnp.float32
        )
        * score_scale
    )
    spec_count = incoming_keys.shape[1]
    row_spec = (
        lax.broadcasted_iota(jnp.int32, (1, query_tile_block.shape[1], spec_count), 1) // head_count
    )
    key_spec = lax.broadcasted_iota(jnp.int32, (1, query_tile_block.shape[1], spec_count), 2)
    causal = (key_spec <= row_spec) & own_first
    row_top = jnp.maximum(
        jnp.max(jnp.where(visible, scores, masked_value), axis=2),
        jnp.max(jnp.where(causal, fresh_scores, masked_value), axis=2),
    )
    weights = jnp.where(visible, jnp.exp(scores - row_top[..., None]), 0.0)
    fresh_weights = jnp.where(causal, jnp.exp(fresh_scores - row_top[..., None]), 0.0)
    running_totals = jnp.sum(weights, axis=2) + jnp.sum(fresh_weights, axis=2)
    weighted = jnp.einsum(
        "mpu,mui->mpi",
        weights.astype(jnp.bfloat16),
        key_tile_block[:, :, :LATENT],
        preferred_element_type=jnp.float32,
    )
    weighted = weighted + jnp.einsum(
        "mpu,mui->mpi",
        fresh_weights.astype(jnp.bfloat16),
        incoming_keys[:, :, :LATENT],
        preferred_element_type=jnp.float32,
    )
    return (row_top, running_totals, weighted)


def project_values(latent_rows, value_weight):
    return jnp.einsum("rhc,hcv->rhv", latent_rows, value_weight, precision=lax.Precision.HIGHEST)


def split_positions(queries, new_latent, cache, lengths, w_uk, w_uv):
    own_rows, head_count, _ = queries.shape
    score_scale = (NOPE + ROPE) ** (-0.5)
    gathered, new_all = (
        lax.all_gather(queries, "seq", axis=0, tiled=True),
        lax.all_gather(new_latent, "seq", axis=0, tiled=True),
    )
    absorbed = jnp.einsum(
        "rhn,hnc->rhc", gathered[:, :, :NOPE], w_uk, preferred_element_type=jnp.float32
    ).astype(jnp.bfloat16)
    q_all = jnp.concatenate([absorbed, gathered[:, :, NOPE:]], axis=2)
    total_rows = q_all.shape[0]
    seq_count = total_rows // SPEC
    query_slots = SPEC * head_count
    q_seq = q_all.reshape(seq_count, query_slots, q_all.shape[2])
    new_seq = new_all.reshape(seq_count, SPEC, new_all.shape[1])
    seq_index = lax.axis_index("seq")
    offset = seq_index * cache.shape[1]
    own_first = seq_index == 0
    row_top, running_totals, weighted = local_partial(
        q_seq,
        lax.all_gather(cache, "head", axis=0, tiled=True),
        new_seq,
        lengths,
        offset,
        own_first,
        score_scale,
        head_count,
    )
    value_weight = w_uv.astype(jnp.float32)
    global_top = lax.pmax(row_top, "seq")
    factor = jnp.exp(row_top - global_top)
    scaled_totals = (running_totals * factor).reshape(total_rows, head_count)
    scaled_weighted = (weighted * factor[..., None]).reshape(total_rows, head_count, LATENT)
    row_totals, row_weighted = (
        lax.psum_scatter(scaled_totals, "seq", scatter_dimension=0, tiled=True),
        lax.psum_scatter(scaled_weighted, "seq", scatter_dimension=0, tiled=True),
    )
    latent_output = row_weighted / row_totals[..., None]
    result = project_values(latent_output, value_weight)
    return result.astype(jnp.bfloat16)


def shards(seq_size, head_size, queries, new_latent, cache, lengths, w_uk, w_uv):
    rows, owners = queries.shape[0], cache.shape[0]
    per_device = rows // SPEC
    if (
        per_device == 2
        and rows % SPEC == 0
        and seq_size == COPIES * owners
        and head_size == owners == 4
        and cache.shape[2] % (16 * COPY_PARTS) == 0
    ):
        return whole_sequences(
            seq_size, head_size, queries, new_latent, cache, lengths, w_uk, w_uv
        )
    return split_positions(queries, new_latent, cache, lengths, w_uk, w_uv)


def solution(mesh):
    return jax.shard_map(
        functools.partial(shards, mesh.shape["seq"], mesh.shape["head"]),
        mesh=mesh,
        in_specs=(
            P("seq", "head", None),
            P("seq", None),
            P("head", "seq", None),
            P(),
            P("head", None, None),
            P("head", None, None),
        ),
        out_specs=P("seq", "head", None),
        check_vma=False,
    )
```

```python
import functools

import jax
import jax.numpy as jnp
from jax import lax
from jax.experimental import pallas as pl
from jax.experimental.pallas import tpu as pltpu
from jax.sharding import PartitionSpec as P

NOPE = 128
ROPE = 64
LATENT = 512
SPEC = 4
SCORE_SCALE = (NOPE + ROPE) ** (-0.5)
COPIES = 2
COPY_PARTS = 3
VMEM_LIMIT = 16 * 1024 * 1024
LONG = pl.CostEstimate(flops=2 * 10**10, bytes_accessed=0, transcendentals=0)

masked_value = -1e30


def leaves_as(k, head_shard):
    return (k + head_shard + 1) % 2


def far_half(plane, pair):
    return 1 * (plane <= 2 * pair)


def first_back(home_chip, head_shard):
    far = 1 * (far_half(home_chip, head_shard // 2) == head_shard % 2)
    return home_chip % 2 ^ far


def first_block(plane, chip, core):
    near = 1 * (chip % 2 == plane % 2)
    return far_half(plane, 1 - core) ^ near ^ 1 - chip % 2


def partner(k, core):
    return (0, 3, 2 ^ 3 * core, 1 ^ 3 * core)[k]


def pick_kernel(per_device, cache_hbm, q_hbm, new_hbm, len_hbm, *refs):
    owners = cache_hbm.shape[0]
    blocks, (out_ref, limit_ref, q_ref, new_ref, len_ref, sem) = refs[:owners], refs[owners:]
    chip, core = lax.axis_index("seq") // COPIES, lax.axis_index("seq") % COPIES
    moves = [
        pltpu.make_async_copy(q_hbm, q_ref, sem.at[0]),
        pltpu.make_async_copy(new_hbm, new_ref, sem.at[1]),
        pltpu.make_async_copy(len_hbm, len_ref, sem.at[2]),
    ]
    part = cache_hbm.shape[1] // COPY_PARTS
    for k in range(owners):
        for n in range(COPY_PARTS):
            rows = pl.ds(n * part, part)
            moves.append(
                pltpu.make_async_copy(
                    cache_hbm.at[chip ^ partner(k, core), rows],
                    blocks[k].at[rows],
                    sem.at[3 + k * COPY_PARTS + n],
                )
            )
    for move in moves:
        move.start()
    moves[0].wait()
    moves[1].wait()
    heads, width = q_ref.shape[1:]
    fresh = new_ref[...].astype(jnp.float32)
    piece = SPEC * heads
    for a in range(per_device):
        rows = q_ref[a * SPEC : (a + 1) * SPEC].reshape(piece, width)
        own = fresh[a * SPEC : (a + 1) * SPEC]
        parts = [own[:, n : n + ROPE] for n in range(0, own.shape[1], ROPE)]
        spare = piece - SPEC * len(parts)
        if spare:
            parts.append(jnp.zeros((spare, ROPE), jnp.float32))
        own = jnp.concatenate(parts, axis=0).astype(rows.dtype)
        out_ref[a * piece : (a + 1) * piece] = jnp.concatenate([rows, own], axis=1)
    moves[2].wait()
    length = len_ref[lax.axis_index("head") * owners + chip]
    limit_ref[...] = jnp.full(limit_ref.shape, length, limit_ref.dtype)
    for move in moves[3:]:
        move.wait()


def pair_kernel(first_ref, second_ref, out_ref, sem):
    moves = [
        pltpu.make_async_copy(ref, out_ref.at[n], sem.at[n])
        for n, ref in enumerate((first_ref, second_ref))
    ]
    for move in moves:
        move.start()
    for move in moves:
        move.wait()


def absorb_kernel(per_device, w_ref, packed_ref, *outs):
    heads = w_ref.shape[0]
    piece = SPEC * heads
    nope = packed_ref[:, :NOPE]
    own_head = lax.broadcasted_iota(jnp.int32, nope.shape, 0) % heads
    spread = jnp.concatenate(
        [jnp.where(own_head == h, nope, jnp.zeros_like(nope)) for h in range(heads)], axis=1
    )
    absorbed = jnp.dot(
        spread, w_ref[...].reshape(heads * NOPE, LATENT), preferred_element_type=jnp.float32
    ).astype(jnp.bfloat16)
    for k in range(per_device):
        which = leaves_as(k, lax.axis_index("head"))
        for a in range(per_device):

            @pl.when(which == a)
            def _():
                rows = slice(a * piece, (a + 1) * piece)
                outs[k][:, :LATENT] = absorbed[rows]
                outs[k][:, LATENT:] = packed_ref[rows, NOPE:]


def block_scores(q, refs, starts, limit_ref):
    width = q.shape[1]
    keys = jnp.concatenate([ref[:width, :] for ref in refs], axis=1)
    limit = limit_ref[:1, :]
    lane = lax.broadcasted_iota(jnp.int32, limit.shape, 1)
    visible = jnp.concatenate([lane + start < limit for start in starts], axis=1)
    s = jnp.dot(q, keys, preferred_element_type=jnp.float32) * SCORE_SCALE
    return jnp.where(visible, s, masked_value)


def weigh(s, refs, top):
    w = jnp.exp(s - top)
    values = jnp.concatenate([ref[:LATENT, :] for ref in refs], axis=1)
    out = lax.dot_general(
        w.astype(jnp.bfloat16),
        values,
        (((1,), (1,)), ((), ())),
        preferred_element_type=jnp.float32,
    )
    return jnp.sum(w, axis=1, keepdims=True), out


def begin_kernel(owners, per_device, heads, limit_ref, *refs):
    q_refs, key_refs = refs[:per_device], refs[per_device : per_device + owners]
    q_out, top_ref, total_ref, out_ref = refs[per_device + owners :]
    seq_index = lax.axis_index("seq")
    chip, core = seq_index // COPIES, seq_index % COPIES
    slots = key_refs[0].shape[1]
    width = LATENT + ROPE
    q = jnp.concatenate([ref[:, :width] for ref in q_refs], axis=0)

    fresh = q_refs[0][:, width:].astype(jnp.float32)
    fresh = jnp.concatenate(
        [fresh[n * SPEC : (n + 1) * SPEC] for n in range(width // ROPE)], axis=1
    )
    fresh = jnp.concatenate([fresh, jnp.zeros((16 - SPEC, width), jnp.float32)], axis=0)
    fresh = fresh.astype(jnp.bfloat16)
    f = lax.dot_general(
        q, fresh, (((1,), (1,)), ((), ())), preferred_element_type=jnp.float32
    )
    row = lax.broadcasted_iota(jnp.int32, f.shape, 0) % (SPEC * heads)
    key = lax.broadcasted_iota(jnp.int32, f.shape, 1)
    f = jnp.where(key <= row // heads, f * SCORE_SCALE, masked_value)

    starts = [((chip ^ partner(k, core)) * COPIES + core) * slots for k in range(owners)]
    s = block_scores(q, key_refs, starts, limit_ref)
    top = jnp.maximum(jnp.max(s, axis=1, keepdims=True), jnp.max(f, axis=1, keepdims=True))
    total, out = weigh(s, key_refs, top)
    w = jnp.exp(f - top)
    total += jnp.sum(w, axis=1, keepdims=True)
    out += jnp.dot(
        w.astype(jnp.bfloat16), fresh[:, :LATENT], preferred_element_type=jnp.float32
    )
    q_out[...] = q
    top_ref[...] = jnp.broadcast_to(top, top_ref.shape)
    total_ref[...] = jnp.broadcast_to(total, total_ref.shape)
    out_ref[...] = out


def finish_kernel(
    owners, per_device, limit_ref, q_ref, top_ref, total_ref, part_ref, pair_ref, *refs
):
    key_refs = [pair_ref.at[0], pair_ref.at[1], *refs[: owners - 2]]
    outs = refs[owners - 2 :]
    seq_index = lax.axis_index("seq")
    chip, core = seq_index // COPIES, seq_index % COPIES
    plane = lax.axis_index("head")
    slots = key_refs[0].shape[1]
    starts = [((chip ^ partner(k, 1 - core)) * COPIES + 1 - core) * slots for k in range(owners)]
    s = block_scores(q_ref[...], key_refs, starts, limit_ref)
    first = top_ref[:, :1]
    top = jnp.maximum(first, jnp.max(s, axis=1, keepdims=True))
    total, out = weigh(s, key_refs, top)
    scale = jnp.exp(first - top)
    total += total_ref[:, :1] * scale
    out += part_ref[...] * scale
    out = (out * (1.0 / total)).astype(jnp.bfloat16)
    piece = out.shape[0] // per_device
    sent_first = first_block(plane, chip, core)
    for k in range(per_device):
        for n in range(per_device):

            @pl.when(sent_first ^ k == n)
            def _():
                outs[k][...] = out[n * piece : (n + 1) * piece]


def project_kernel(per_device, w_ref, *refs):
    lat_refs, out_ref = refs[:-1], refs[-1]
    rows, heads, width = out_ref.shape
    first = first_back(lax.axis_index("seq") // COPIES, lax.axis_index("head"))
    parts = [jnp.where(first == a, lat_refs[1][...], lat_refs[0][...]) for a in range(per_device)]
    latent = jnp.concatenate(parts, axis=0)
    out = jnp.zeros((rows * heads, width), jnp.float32)
    own_head = lax.broadcasted_iota(jnp.int32, out.shape, 0) % heads
    step = 2 if heads % 2 == 0 else 1
    for h in range(0, heads, step):
        group = jnp.concatenate([w_ref[h + n] for n in range(step)], axis=1)
        product = jnp.dot(latent, group, preferred_element_type=jnp.float32)
        for n in range(step):
            out = jnp.where(own_head == h + n, product[:, n * width : (n + 1) * width], out)
    out_ref[...] = out.astype(out_ref.dtype).reshape(out_ref.shape)


def whole_sequences(seq_size, head_size, queries, new_latent, cache, lengths, w_uk, w_uv):
    rows, heads, q_width = queries.shape
    owners, slots, width = cache.shape
    per_device = rows // SPEC
    piece = SPEC * heads
    all_rows = per_device * piece
    params = pltpu.CompilerParams(vmem_limit_bytes=VMEM_LIMIT)
    vmem = pl.BlockSpec(memory_space=pltpu.VMEM)
    anywhere = pl.BlockSpec(memory_space=pl.ANY)
    both = ("seq", "head")
    devices = [(i, j) for i in range(seq_size) for j in range(head_size)]

    def flat(seq_index, head_index):
        return seq_index * head_size + head_index

    def in_hbm(x):
        return pltpu.with_memory_space_constraint(x, pltpu.HBM)

    def host(i, j):
        other = (i // COPIES) ^ (2 - ((j ^ (j >> 1)) & 1))
        return flat(((i % COPIES) * 2 + other // 2) * COPIES + other % 2, j)

    def owner(i, j, a):
        plane, chip = i // COPIES, i % COPIES * per_device + a
        return flat(chip * COPIES + 1 - j // 2, plane)

    def in_plane(move):
        return [(g * COPIES + t, move(g, t)) for g in range(owners) for t in range(COPIES)]

    *picked, packed, limit = pl.pallas_call(
        functools.partial(pick_kernel, per_device),
        out_shape=[jax.ShapeDtypeStruct((width, slots), cache.dtype)] * owners
        + [
            jax.ShapeDtypeStruct((all_rows, q_width + ROPE), queries.dtype),
            jax.ShapeDtypeStruct((8, slots), jnp.int32),
        ],
        in_specs=[anywhere] * 4,
        out_specs=[vmem] * (owners + 2),
        scratch_shapes=[
            pltpu.VMEM(queries.shape, queries.dtype),
            pltpu.VMEM(new_latent.shape, new_latent.dtype),
            pltpu.SMEM(lengths.shape, lengths.dtype),
            pltpu.SemaphoreType.DMA((3 + owners * COPY_PARTS,)),
        ],
        compiler_params=params,
        cost_estimate=LONG,
    )(*[in_hbm(x) for x in (jnp.swapaxes(cache, 1, 2), queries, new_latent, lengths)])
    moved = lax.ppermute(packed, both, [(flat(i, j), host(i, j)) for i, j in devices])
    own_keys = [picked[0]] + [
        lax.ppermute(picked[k], "seq", in_plane(lambda g, t: (g ^ partner(k, t)) * COPIES + t))
        for k in range(1, owners)
    ]
    pair = pl.pallas_call(
        pair_kernel,
        out_shape=jax.ShapeDtypeStruct((2, *picked[0].shape), cache.dtype),
        in_specs=[vmem] * 2,
        out_specs=vmem,
        scratch_shapes=[pltpu.SemaphoreType.DMA((2,))],
        compiler_params=params,
    )(*own_keys[:2])
    other_core = in_plane(lambda g, t: g * COPIES + 1 - t)
    far_keys = [lax.ppermute(keys, "seq", other_core) for keys in [pair] + own_keys[2:]]

    pieces = pl.pallas_call(
        functools.partial(absorb_kernel, per_device),
        out_shape=[jax.ShapeDtypeStruct((piece, width + ROPE), cache.dtype)] * per_device,
        in_specs=[vmem] * 2,
        out_specs=[vmem] * per_device,
        compiler_params=params,
        cost_estimate=LONG,
    )(w_uk, moved)
    arrived = [
        lax.ppermute(
            pieces[k],
            both,
            [(host(i, j), owner(i, j, leaves_as(k, j))) for i, j in devices],
        )
        for k in range(per_device)
    ]

    state = pl.pallas_call(
        functools.partial(begin_kernel, owners, per_device, heads),
        out_shape=[
            jax.ShapeDtypeStruct((all_rows, width), jnp.bfloat16),
            jax.ShapeDtypeStruct((all_rows, 128), jnp.float32),
            jax.ShapeDtypeStruct((all_rows, 128), jnp.float32),
            jax.ShapeDtypeStruct((all_rows, LATENT), jnp.float32),
        ],
        in_specs=[vmem] * (1 + per_device + owners),
        out_specs=[vmem] * 4,
        compiler_params=params,
        cost_estimate=LONG,
    )(limit, *arrived, *own_keys)
    latent = pl.pallas_call(
        functools.partial(finish_kernel, owners, per_device),
        out_shape=[jax.ShapeDtypeStruct((piece, LATENT), jnp.bfloat16)] * per_device,
        in_specs=[vmem] * (1 + len(state) + len(far_keys)),
        out_specs=[vmem] * per_device,
        compiler_params=params,
    )(limit, *state, *far_keys)

    back = [
        lax.ppermute(
            latent[k],
            both,
            [(owner(i, j, first_back(i // COPIES, j) ^ k), flat(i, j)) for i, j in devices],
        )
        for k in range(per_device)
    ]
    return pl.pallas_call(
        functools.partial(project_kernel, per_device),
        out_shape=jax.ShapeDtypeStruct((rows, heads, w_uv.shape[2]), jnp.bfloat16),
        in_specs=[vmem] * (1 + per_device),
        out_specs=vmem,
        compiler_params=params,
    )(w_uv, *back[::-1])


def local_partial(
    query_tile_block,
    key_tile_block,
    incoming_keys,
    len_block,
    offset,
    own_first,
    score_scale,
    head_count,
):
    scores = (
        jnp.einsum(
            "vfa,vja->vfj", query_tile_block, key_tile_block, preferred_element_type=jnp.float32
        )
        * score_scale
    )
    positions = offset + lax.broadcasted_iota(jnp.int32, (1, 1, key_tile_block.shape[1]), 2)
    visible = positions < len_block[:, None, None]
    fresh_scores = (
        jnp.einsum(
            "vfa,vja->vfj", query_tile_block, incoming_keys, preferred_element_type=jnp.float32
        )
        * score_scale
    )
    spec_count = incoming_keys.shape[1]
    row_spec = (
        lax.broadcasted_iota(jnp.int32, (1, query_tile_block.shape[1], spec_count), 1) // head_count
    )
    key_spec = lax.broadcasted_iota(jnp.int32, (1, query_tile_block.shape[1], spec_count), 2)
    causal = (key_spec <= row_spec) & own_first
    row_top = jnp.maximum(
        jnp.max(jnp.where(visible, scores, masked_value), axis=2),
        jnp.max(jnp.where(causal, fresh_scores, masked_value), axis=2),
    )
    weights = jnp.where(visible, jnp.exp(scores - row_top[..., None]), 0.0)
    fresh_weights = jnp.where(causal, jnp.exp(fresh_scores - row_top[..., None]), 0.0)
    running_totals = jnp.sum(weights, axis=2) + jnp.sum(fresh_weights, axis=2)
    weighted = jnp.einsum(
        "mpu,mui->mpi",
        weights.astype(jnp.bfloat16),
        key_tile_block[:, :, :LATENT],
        preferred_element_type=jnp.float32,
    )
    weighted = weighted + jnp.einsum(
        "mpu,mui->mpi",
        fresh_weights.astype(jnp.bfloat16),
        incoming_keys[:, :, :LATENT],
        preferred_element_type=jnp.float32,
    )
    return (row_top, running_totals, weighted)


def project_values(latent_rows, value_weight):
    return jnp.einsum("rhc,hcv->rhv", latent_rows, value_weight, precision=lax.Precision.HIGHEST)


def split_positions(queries, new_latent, cache, lengths, w_uk, w_uv):
    own_rows, head_count, _ = queries.shape
    score_scale = (NOPE + ROPE) ** (-0.5)
    gathered, new_all = (
        lax.all_gather(queries, "seq", axis=0, tiled=True),
        lax.all_gather(new_latent, "seq", axis=0, tiled=True),
    )
    absorbed = jnp.einsum(
        "rhn,hnc->rhc", gathered[:, :, :NOPE], w_uk, preferred_element_type=jnp.float32
    ).astype(jnp.bfloat16)
    q_all = jnp.concatenate([absorbed, gathered[:, :, NOPE:]], axis=2)
    total_rows = q_all.shape[0]
    seq_count = total_rows // SPEC
    query_slots = SPEC * head_count
    q_seq = q_all.reshape(seq_count, query_slots, q_all.shape[2])
    new_seq = new_all.reshape(seq_count, SPEC, new_all.shape[1])
    seq_index = lax.axis_index("seq")
    offset = seq_index * cache.shape[1]
    own_first = seq_index == 0
    row_top, running_totals, weighted = local_partial(
        q_seq,
        lax.all_gather(cache, "head", axis=0, tiled=True),
        new_seq,
        lengths,
        offset,
        own_first,
        score_scale,
        head_count,
    )
    value_weight = w_uv.astype(jnp.float32)
    global_top = lax.pmax(row_top, "seq")
    factor = jnp.exp(row_top - global_top)
    scaled_totals = (running_totals * factor).reshape(total_rows, head_count)
    scaled_weighted = (weighted * factor[..., None]).reshape(total_rows, head_count, LATENT)
    row_totals, row_weighted = (
        lax.psum_scatter(scaled_totals, "seq", scatter_dimension=0, tiled=True),
        lax.psum_scatter(scaled_weighted, "seq", scatter_dimension=0, tiled=True),
    )
    latent_output = row_weighted / row_totals[..., None]
    result = project_values(latent_output, value_weight)
    return result.astype(jnp.bfloat16)


def shards(seq_size, head_size, queries, new_latent, cache, lengths, w_uk, w_uv):
    rows, owners = queries.shape[0], cache.shape[0]
    per_device = rows // SPEC
    if (
        per_device == 2
        and rows % SPEC == 0
        and seq_size == COPIES * owners
        and head_size == owners == 4
        and cache.shape[2] % (16 * COPY_PARTS) == 0
    ):
        return whole_sequences(
            seq_size, head_size, queries, new_latent, cache, lengths, w_uk, w_uv
        )
    return split_positions(queries, new_latent, cache, lengths, w_uk, w_uv)


def solution(mesh):
    return jax.shard_map(
        functools.partial(shards, mesh.shape["seq"], mesh.shape["head"]),
        mesh=mesh,
        in_specs=(
            P("seq", "head", None),
            P("seq", None),
            P("head", "seq", None),
            P(),
            P("head", None, None),
            P("head", None, None),
        ),
        out_specs=P("seq", "head", None),
        check_vma=False,
    )
```

```python
import functools

import jax
import jax.numpy as jnp
from jax import lax
from jax.experimental import pallas as pl
from jax.experimental.pallas import tpu as pltpu
from jax.sharding import PartitionSpec as P

NOPE = 128
ROPE = 64
LATENT = 512
SPEC = 4
SCORE_SCALE = (NOPE + ROPE) ** (-0.5)
COPIES = 2
COPY_PARTS = 3
VMEM_LIMIT = 16 * 1024 * 1024
LONG = pl.CostEstimate(flops=2 * 10**10, bytes_accessed=0, transcendentals=0)

masked_value = -1e30


def leaves_as(k, head_shard):
    return (k + head_shard + 1) % 2


def far_half(plane, pair):
    return 1 * (plane <= 2 * pair)


def first_back(home_chip, head_shard):
    far = 1 * (far_half(home_chip, head_shard // 2) == head_shard % 2)
    return home_chip % 2 ^ far


def first_block(plane, chip, core):
    near = 1 * (chip % 2 == plane % 2)
    return far_half(plane, 1 - core) ^ near ^ 1 - chip % 2


def partner(k, core):
    return (0, 1 ^ 3 * core, 3, 2 ^ 3 * core)[k]


def pick_kernel(per_device, cache_hbm, q_hbm, new_hbm, len_hbm, *refs):
    owners = cache_hbm.shape[0]
    blocks, (out_ref, limit_ref, q_ref, new_ref, len_ref, sem) = refs[:owners], refs[owners:]
    chip, core = lax.axis_index("seq") // COPIES, lax.axis_index("seq") % COPIES
    moves = [
        pltpu.make_async_copy(q_hbm, q_ref, sem.at[0]),
        pltpu.make_async_copy(new_hbm, new_ref, sem.at[1]),
        pltpu.make_async_copy(len_hbm, len_ref, sem.at[2]),
    ]
    part = cache_hbm.shape[1] // COPY_PARTS
    for k in range(owners):
        for n in range(COPY_PARTS):
            rows = pl.ds(n * part, part)
            moves.append(
                pltpu.make_async_copy(
                    cache_hbm.at[chip ^ partner(k, core), rows],
                    blocks[k].at[rows],
                    sem.at[3 + k * COPY_PARTS + n],
                )
            )
    for move in moves:
        move.start()
    moves[0].wait()
    moves[1].wait()
    heads, width = q_ref.shape[1:]
    fresh = new_ref[...].astype(jnp.float32)
    piece = SPEC * heads
    for a in range(per_device):
        rows = q_ref[a * SPEC : (a + 1) * SPEC].reshape(piece, width)
        own = fresh[a * SPEC : (a + 1) * SPEC]
        parts = [own[:, n : n + ROPE] for n in range(0, own.shape[1], ROPE)]
        spare = piece - SPEC * len(parts)
        if spare:
            parts.append(jnp.zeros((spare, ROPE), jnp.float32))
        own = jnp.concatenate(parts, axis=0).astype(rows.dtype)
        out_ref[a * piece : (a + 1) * piece] = jnp.concatenate([rows, own], axis=1)
    moves[2].wait()
    length = len_ref[lax.axis_index("head") * owners + chip]
    limit_ref[...] = jnp.full(limit_ref.shape, length, limit_ref.dtype)
    for move in moves[3:]:
        move.wait()


def pair_kernel(first_ref, second_ref, out_ref, sem):
    moves = [
        pltpu.make_async_copy(ref, out_ref.at[n], sem.at[n])
        for n, ref in enumerate((first_ref, second_ref))
    ]
    for move in moves:
        move.start()
    for move in moves:
        move.wait()


def absorb_kernel(per_device, w_ref, packed_ref, *outs):
    heads = w_ref.shape[0]
    piece = SPEC * heads
    nope = packed_ref[:, :NOPE]
    own_head = lax.broadcasted_iota(jnp.int32, nope.shape, 0) % heads
    spread = jnp.concatenate(
        [jnp.where(own_head == h, nope, jnp.zeros_like(nope)) for h in range(heads)], axis=1
    )
    absorbed = jnp.dot(
        spread, w_ref[...].reshape(heads * NOPE, LATENT), preferred_element_type=jnp.float32
    ).astype(jnp.bfloat16)
    for k in range(per_device):
        which = leaves_as(k, lax.axis_index("head"))
        for a in range(per_device):

            @pl.when(which == a)
            def _():
                rows = slice(a * piece, (a + 1) * piece)
                outs[k][:, :LATENT] = absorbed[rows]
                outs[k][:, LATENT:] = packed_ref[rows, NOPE:]


def block_scores(q, refs, starts, limit_ref):
    width = q.shape[1]
    keys = jnp.concatenate([ref[:width, :] for ref in refs], axis=1)
    limit = limit_ref[:1, :]
    lane = lax.broadcasted_iota(jnp.int32, limit.shape, 1)
    visible = jnp.concatenate([lane + start < limit for start in starts], axis=1)
    s = jnp.dot(q, keys, preferred_element_type=jnp.float32) * SCORE_SCALE
    return jnp.where(visible, s, masked_value)


def weigh(s, refs, top):
    w = jnp.exp(s - top)
    values = jnp.concatenate([ref[:LATENT, :] for ref in refs], axis=1)
    out = lax.dot_general(
        w.astype(jnp.bfloat16),
        values,
        (((1,), (1,)), ((), ())),
        preferred_element_type=jnp.float32,
    )
    return jnp.sum(w, axis=1, keepdims=True), out


def begin_kernel(owners, per_device, heads, limit_ref, *refs):
    q_refs, key_refs = refs[:per_device], refs[per_device : per_device + owners]
    q_out, top_ref, total_ref, out_ref = refs[per_device + owners :]
    seq_index = lax.axis_index("seq")
    chip, core = seq_index // COPIES, seq_index % COPIES
    slots = key_refs[0].shape[1]
    width = LATENT + ROPE
    q = jnp.concatenate([ref[:, :width] for ref in q_refs], axis=0)

    fresh = q_refs[0][:, width:].astype(jnp.float32)
    fresh = jnp.concatenate(
        [fresh[n * SPEC : (n + 1) * SPEC] for n in range(width // ROPE)], axis=1
    )
    fresh = jnp.concatenate([fresh, jnp.zeros((16 - SPEC, width), jnp.float32)], axis=0)
    fresh = fresh.astype(jnp.bfloat16)
    f = lax.dot_general(
        q, fresh, (((1,), (1,)), ((), ())), preferred_element_type=jnp.float32
    )
    row = lax.broadcasted_iota(jnp.int32, f.shape, 0) % (SPEC * heads)
    key = lax.broadcasted_iota(jnp.int32, f.shape, 1)
    f = jnp.where(key <= row // heads, f * SCORE_SCALE, masked_value)

    starts = [((chip ^ partner(k, core)) * COPIES + core) * slots for k in range(owners)]
    s = block_scores(q, key_refs, starts, limit_ref)
    top = jnp.maximum(jnp.max(s, axis=1, keepdims=True), jnp.max(f, axis=1, keepdims=True))
    total, out = weigh(s, key_refs, top)
    w = jnp.exp(f - top)
    total += jnp.sum(w, axis=1, keepdims=True)
    out += jnp.dot(
        w.astype(jnp.bfloat16), fresh[:, :LATENT], preferred_element_type=jnp.float32
    )
    q_out[...] = q
    top_ref[...] = jnp.broadcast_to(top, top_ref.shape)
    total_ref[...] = jnp.broadcast_to(total, total_ref.shape)
    out_ref[...] = out


def finish_kernel(
    owners, per_device, limit_ref, q_ref, top_ref, total_ref, part_ref, pair_ref, *refs
):
    key_refs = [pair_ref.at[0], pair_ref.at[1], *refs[: owners - 2]]
    outs = refs[owners - 2 :]
    seq_index = lax.axis_index("seq")
    chip, core = seq_index // COPIES, seq_index % COPIES
    plane = lax.axis_index("head")
    slots = key_refs[0].shape[1]
    starts = [((chip ^ partner(k, 1 - core)) * COPIES + 1 - core) * slots for k in range(owners)]
    s = block_scores(q_ref[...], key_refs, starts, limit_ref)
    first = top_ref[:, :1]
    top = jnp.maximum(first, jnp.max(s, axis=1, keepdims=True))
    total, out = weigh(s, key_refs, top)
    scale = jnp.exp(first - top)
    total += total_ref[:, :1] * scale
    out += part_ref[...] * scale
    out = (out * (1.0 / total)).astype(jnp.bfloat16)
    piece = out.shape[0] // per_device
    sent_first = first_block(plane, chip, core)
    for k in range(per_device):
        for n in range(per_device):

            @pl.when(sent_first ^ k == n)
            def _():
                outs[k][...] = out[n * piece : (n + 1) * piece]


def project_kernel(per_device, w_ref, *refs):
    lat_refs, out_ref = refs[:-1], refs[-1]
    rows, heads, width = out_ref.shape
    first = first_back(lax.axis_index("seq") // COPIES, lax.axis_index("head"))
    parts = [jnp.where(first == a, lat_refs[1][...], lat_refs[0][...]) for a in range(per_device)]
    latent = jnp.concatenate(parts, axis=0)
    out = jnp.zeros((rows * heads, width), jnp.float32)
    own_head = lax.broadcasted_iota(jnp.int32, out.shape, 0) % heads
    step = 2 if heads % 2 == 0 else 1
    for h in range(0, heads, step):
        group = jnp.concatenate([w_ref[h + n] for n in range(step)], axis=1)
        product = jnp.dot(latent, group, preferred_element_type=jnp.float32)
        for n in range(step):
            out = jnp.where(own_head == h + n, product[:, n * width : (n + 1) * width], out)
    out_ref[...] = out.astype(out_ref.dtype).reshape(out_ref.shape)


def whole_sequences(seq_size, head_size, queries, new_latent, cache, lengths, w_uk, w_uv):
    rows, heads, q_width = queries.shape
    owners, slots, width = cache.shape
    per_device = rows // SPEC
    piece = SPEC * heads
    all_rows = per_device * piece
    params = pltpu.CompilerParams(vmem_limit_bytes=VMEM_LIMIT)
    vmem = pl.BlockSpec(memory_space=pltpu.VMEM)
    anywhere = pl.BlockSpec(memory_space=pl.ANY)
    both = ("seq", "head")
    devices = [(i, j) for i in range(seq_size) for j in range(head_size)]

    def flat(seq_index, head_index):
        return seq_index * head_size + head_index

    def in_hbm(x):
        return pltpu.with_memory_space_constraint(x, pltpu.HBM)

    def host(i, j):
        other = (i // COPIES) ^ (2 - ((j ^ (j >> 1)) & 1))
        return flat(((i % COPIES) * 2 + other // 2) * COPIES + other % 2, j)

    def owner(i, j, a):
        plane, chip = i // COPIES, i % COPIES * per_device + a
        return flat(chip * COPIES + 1 - j // 2, plane)

    def in_plane(move):
        return [(g * COPIES + t, move(g, t)) for g in range(owners) for t in range(COPIES)]

    *picked, packed, limit = pl.pallas_call(
        functools.partial(pick_kernel, per_device),
        out_shape=[jax.ShapeDtypeStruct((width, slots), cache.dtype)] * owners
        + [
            jax.ShapeDtypeStruct((all_rows, q_width + ROPE), queries.dtype),
            jax.ShapeDtypeStruct((8, slots), jnp.int32),
        ],
        in_specs=[anywhere] * 4,
        out_specs=[vmem] * (owners + 2),
        scratch_shapes=[
            pltpu.VMEM(queries.shape, queries.dtype),
            pltpu.VMEM(new_latent.shape, new_latent.dtype),
            pltpu.SMEM(lengths.shape, lengths.dtype),
            pltpu.SemaphoreType.DMA((3 + owners * COPY_PARTS,)),
        ],
        compiler_params=params,
        cost_estimate=LONG,
    )(*[in_hbm(x) for x in (jnp.swapaxes(cache, 1, 2), queries, new_latent, lengths)])
    moved = lax.ppermute(packed, both, [(flat(i, j), host(i, j)) for i, j in devices])
    own_keys = [picked[0]] + [
        lax.ppermute(picked[k], "seq", in_plane(lambda g, t: (g ^ partner(k, t)) * COPIES + t))
        for k in range(1, owners)
    ]
    pair = pl.pallas_call(
        pair_kernel,
        out_shape=jax.ShapeDtypeStruct((2, *picked[0].shape), cache.dtype),
        in_specs=[vmem] * 2,
        out_specs=vmem,
        scratch_shapes=[pltpu.SemaphoreType.DMA((2,))],
        compiler_params=params,
    )(*own_keys[:2])
    other_core = in_plane(lambda g, t: g * COPIES + 1 - t)
    far_keys = [lax.ppermute(keys, "seq", other_core) for keys in [pair] + own_keys[2:]]

    pieces = pl.pallas_call(
        functools.partial(absorb_kernel, per_device),
        out_shape=[jax.ShapeDtypeStruct((piece, width + ROPE), cache.dtype)] * per_device,
        in_specs=[vmem] * 2,
        out_specs=[vmem] * per_device,
        compiler_params=params,
        cost_estimate=LONG,
    )(w_uk, moved)
    arrived = [
        lax.ppermute(
            pieces[k],
            both,
            [(host(i, j), owner(i, j, leaves_as(k, j))) for i, j in devices],
        )
        for k in range(per_device)
    ]

    state = pl.pallas_call(
        functools.partial(begin_kernel, owners, per_device, heads),
        out_shape=[
            jax.ShapeDtypeStruct((all_rows, width), jnp.bfloat16),
            jax.ShapeDtypeStruct((all_rows, 128), jnp.float32),
            jax.ShapeDtypeStruct((all_rows, 128), jnp.float32),
            jax.ShapeDtypeStruct((all_rows, LATENT), jnp.float32),
        ],
        in_specs=[vmem] * (1 + per_device + owners),
        out_specs=[vmem] * 4,
        compiler_params=params,
        cost_estimate=LONG,
    )(limit, *arrived, *own_keys)
    latent = pl.pallas_call(
        functools.partial(finish_kernel, owners, per_device),
        out_shape=[jax.ShapeDtypeStruct((piece, LATENT), jnp.bfloat16)] * per_device,
        in_specs=[vmem] * (1 + len(state) + len(far_keys)),
        out_specs=[vmem] * per_device,
        compiler_params=params,
    )(limit, *state, *far_keys)

    back = [
        lax.ppermute(
            latent[k],
            both,
            [(owner(i, j, first_back(i // COPIES, j) ^ k), flat(i, j)) for i, j in devices],
        )
        for k in range(per_device)
    ]
    return pl.pallas_call(
        functools.partial(project_kernel, per_device),
        out_shape=jax.ShapeDtypeStruct((rows, heads, w_uv.shape[2]), jnp.bfloat16),
        in_specs=[vmem] * (1 + per_device),
        out_specs=vmem,
        compiler_params=params,
    )(w_uv, *back[::-1])


def local_partial(
    query_tile_block,
    key_tile_block,
    incoming_keys,
    len_block,
    offset,
    own_first,
    score_scale,
    head_count,
):
    scores = (
        jnp.einsum(
            "vfa,vja->vfj", query_tile_block, key_tile_block, preferred_element_type=jnp.float32
        )
        * score_scale
    )
    positions = offset + lax.broadcasted_iota(jnp.int32, (1, 1, key_tile_block.shape[1]), 2)
    visible = positions < len_block[:, None, None]
    fresh_scores = (
        jnp.einsum(
            "vfa,vja->vfj", query_tile_block, incoming_keys, preferred_element_type=jnp.float32
        )
        * score_scale
    )
    spec_count = incoming_keys.shape[1]
    row_spec = (
        lax.broadcasted_iota(jnp.int32, (1, query_tile_block.shape[1], spec_count), 1) // head_count
    )
    key_spec = lax.broadcasted_iota(jnp.int32, (1, query_tile_block.shape[1], spec_count), 2)
    causal = (key_spec <= row_spec) & own_first
    row_top = jnp.maximum(
        jnp.max(jnp.where(visible, scores, masked_value), axis=2),
        jnp.max(jnp.where(causal, fresh_scores, masked_value), axis=2),
    )
    weights = jnp.where(visible, jnp.exp(scores - row_top[..., None]), 0.0)
    fresh_weights = jnp.where(causal, jnp.exp(fresh_scores - row_top[..., None]), 0.0)
    running_totals = jnp.sum(weights, axis=2) + jnp.sum(fresh_weights, axis=2)
    weighted = jnp.einsum(
        "mpu,mui->mpi",
        weights.astype(jnp.bfloat16),
        key_tile_block[:, :, :LATENT],
        preferred_element_type=jnp.float32,
    )
    weighted = weighted + jnp.einsum(
        "mpu,mui->mpi",
        fresh_weights.astype(jnp.bfloat16),
        incoming_keys[:, :, :LATENT],
        preferred_element_type=jnp.float32,
    )
    return (row_top, running_totals, weighted)


def project_values(latent_rows, value_weight):
    return jnp.einsum("rhc,hcv->rhv", latent_rows, value_weight, precision=lax.Precision.HIGHEST)


def split_positions(queries, new_latent, cache, lengths, w_uk, w_uv):
    own_rows, head_count, _ = queries.shape
    score_scale = (NOPE + ROPE) ** (-0.5)
    gathered, new_all = (
        lax.all_gather(queries, "seq", axis=0, tiled=True),
        lax.all_gather(new_latent, "seq", axis=0, tiled=True),
    )
    absorbed = jnp.einsum(
        "rhn,hnc->rhc", gathered[:, :, :NOPE], w_uk, preferred_element_type=jnp.float32
    ).astype(jnp.bfloat16)
    q_all = jnp.concatenate([absorbed, gathered[:, :, NOPE:]], axis=2)
    total_rows = q_all.shape[0]
    seq_count = total_rows // SPEC
    query_slots = SPEC * head_count
    q_seq = q_all.reshape(seq_count, query_slots, q_all.shape[2])
    new_seq = new_all.reshape(seq_count, SPEC, new_all.shape[1])
    seq_index = lax.axis_index("seq")
    offset = seq_index * cache.shape[1]
    own_first = seq_index == 0
    row_top, running_totals, weighted = local_partial(
        q_seq,
        lax.all_gather(cache, "head", axis=0, tiled=True),
        new_seq,
        lengths,
        offset,
        own_first,
        score_scale,
        head_count,
    )
    value_weight = w_uv.astype(jnp.float32)
    global_top = lax.pmax(row_top, "seq")
    factor = jnp.exp(row_top - global_top)
    scaled_totals = (running_totals * factor).reshape(total_rows, head_count)
    scaled_weighted = (weighted * factor[..., None]).reshape(total_rows, head_count, LATENT)
    row_totals, row_weighted = (
        lax.psum_scatter(scaled_totals, "seq", scatter_dimension=0, tiled=True),
        lax.psum_scatter(scaled_weighted, "seq", scatter_dimension=0, tiled=True),
    )
    latent_output = row_weighted / row_totals[..., None]
    result = project_values(latent_output, value_weight)
    return result.astype(jnp.bfloat16)


def shards(seq_size, head_size, queries, new_latent, cache, lengths, w_uk, w_uv):
    rows, owners = queries.shape[0], cache.shape[0]
    per_device = rows // SPEC
    if (
        per_device == 2
        and rows % SPEC == 0
        and seq_size == COPIES * owners
        and head_size == owners == 4
        and cache.shape[2] % (16 * COPY_PARTS) == 0
    ):
        return whole_sequences(
            seq_size, head_size, queries, new_latent, cache, lengths, w_uk, w_uv
        )
    return split_positions(queries, new_latent, cache, lengths, w_uk, w_uv)


def solution(mesh):
    return jax.shard_map(
        functools.partial(shards, mesh.shape["seq"], mesh.shape["head"]),
        mesh=mesh,
        in_specs=(
            P("seq", "head", None),
            P("seq", None),
            P("head", "seq", None),
            P(),
            P("head", None, None),
            P("head", None, None),
        ),
        out_specs=P("seq", "head", None),
        check_vma=False,
    )
```

```python
import functools

import jax
import jax.numpy as jnp
from jax import lax
from jax.experimental import pallas as pl
from jax.experimental.pallas import tpu as pltpu
from jax.sharding import PartitionSpec as P

NOPE = 128
ROPE = 64
LATENT = 512
SPEC = 4
SCORE_SCALE = (NOPE + ROPE) ** (-0.5)
COPIES = 2
COPY_PARTS = 3
VMEM_LIMIT = 16 * 1024 * 1024
LONG = pl.CostEstimate(flops=2 * 10**10, bytes_accessed=0, transcendentals=0)

masked_value = -1e30


def leaves_as(k, head_shard):
    return (k + head_shard) % 2


def far_half(plane, pair):
    return 1 * (plane <= 2 * pair)


def first_back(home_chip, head_shard):
    far = 1 * (far_half(home_chip, head_shard // 2) == head_shard % 2)
    return home_chip % 2 ^ far


def first_block(plane, chip, core):
    near = 1 * (chip % 2 == plane % 2)
    return far_half(plane, 1 - core) ^ near ^ chip % 2


def partner(k, core):
    return (0, 3, 1 ^ 3 * core, 2 ^ 3 * core)[k]


def pick_kernel(per_device, cache_hbm, q_hbm, new_hbm, len_hbm, *refs):
    owners = cache_hbm.shape[0]
    blocks, (out_ref, limit_ref, q_ref, new_ref, len_ref, sem) = refs[:owners], refs[owners:]
    chip, core = lax.axis_index("seq") // COPIES, lax.axis_index("seq") % COPIES
    moves = [
        pltpu.make_async_copy(q_hbm, q_ref, sem.at[0]),
        pltpu.make_async_copy(new_hbm, new_ref, sem.at[1]),
        pltpu.make_async_copy(len_hbm, len_ref, sem.at[2]),
    ]
    part = cache_hbm.shape[1] // COPY_PARTS
    for k in range(owners):
        for n in range(COPY_PARTS):
            rows = pl.ds(n * part, part)
            moves.append(
                pltpu.make_async_copy(
                    cache_hbm.at[chip ^ partner(k, core), rows],
                    blocks[k].at[rows],
                    sem.at[3 + k * COPY_PARTS + n],
                )
            )
    for move in moves[:2] + moves[3:] + moves[2:3]:
        move.start()
    moves[0].wait()
    moves[1].wait()
    heads, width = q_ref.shape[1:]
    fresh = new_ref[...].astype(jnp.float32)
    piece = SPEC * heads
    for a in range(per_device):
        rows = q_ref[a * SPEC : (a + 1) * SPEC].reshape(piece, width)
        own = fresh[a * SPEC : (a + 1) * SPEC]
        parts = [own[:, n : n + ROPE] for n in range(0, own.shape[1], ROPE)]
        spare = piece - SPEC * len(parts)
        if spare:
            parts.append(jnp.zeros((spare, ROPE), jnp.float32))
        own = jnp.concatenate(parts, axis=0).astype(rows.dtype)
        out_ref[a * piece : (a + 1) * piece] = jnp.concatenate([rows, own], axis=1)
    moves[2].wait()
    length = len_ref[lax.axis_index("head") * owners + chip]
    limit_ref[...] = jnp.full(limit_ref.shape, length, limit_ref.dtype)
    for move in moves[3:]:
        move.wait()


def pair_kernel(first_ref, second_ref, out_ref, sem):
    moves = [
        pltpu.make_async_copy(ref, out_ref.at[n], sem.at[n])
        for n, ref in enumerate((first_ref, second_ref))
    ]
    for move in moves:
        move.start()
    for move in moves:
        move.wait()


def absorb_kernel(per_device, w_ref, packed_ref, *outs):
    heads = w_ref.shape[0]
    piece = SPEC * heads
    nope = packed_ref[:, :NOPE]
    own_head = lax.broadcasted_iota(jnp.int32, nope.shape, 0) % heads
    spread = jnp.concatenate(
        [jnp.where(own_head == h, nope, jnp.zeros_like(nope)) for h in range(heads)], axis=1
    )
    absorbed = jnp.dot(
        spread, w_ref[...].reshape(heads * NOPE, LATENT), preferred_element_type=jnp.float32
    ).astype(jnp.bfloat16)
    for k in range(per_device):
        which = leaves_as(k, lax.axis_index("head"))
        for a in range(per_device):

            @pl.when(which == a)
            def _():
                rows = slice(a * piece, (a + 1) * piece)
                outs[k][:, :LATENT] = absorbed[rows]
                outs[k][:, LATENT:] = packed_ref[rows, NOPE:]


def block_scores(q, refs, starts, limit_ref):
    width = q.shape[1]
    keys = jnp.concatenate([ref[:width, :] for ref in refs], axis=1)
    limit = limit_ref[:1, :]
    lane = lax.broadcasted_iota(jnp.int32, limit.shape, 1)
    visible = jnp.concatenate([lane + start < limit for start in starts], axis=1)
    s = jnp.dot(q, keys, preferred_element_type=jnp.float32) * SCORE_SCALE
    return jnp.where(visible, s, masked_value)


def weigh(s, refs, top):
    w = jnp.exp(s - top)
    values = jnp.concatenate([ref[:LATENT, :] for ref in refs], axis=1)
    out = lax.dot_general(
        w.astype(jnp.bfloat16),
        values,
        (((1,), (1,)), ((), ())),
        preferred_element_type=jnp.float32,
    )
    return jnp.sum(w, axis=1, keepdims=True), out


def begin_kernel(owners, per_device, heads, limit_ref, *refs):
    q_refs, key_refs = refs[:per_device], refs[per_device : per_device + owners]
    q_out, top_ref, total_ref, out_ref = refs[per_device + owners :]
    seq_index = lax.axis_index("seq")
    chip, core = seq_index // COPIES, seq_index % COPIES
    slots = key_refs[0].shape[1]
    width = LATENT + ROPE
    q = jnp.concatenate([ref[:, :width] for ref in q_refs], axis=0)

    fresh = q_refs[0][:, width:].astype(jnp.float32)
    fresh = jnp.concatenate(
        [fresh[n * SPEC : (n + 1) * SPEC] for n in range(width // ROPE)], axis=1
    )
    fresh = jnp.concatenate([fresh, jnp.zeros((16 - SPEC, width), jnp.float32)], axis=0)
    fresh = fresh.astype(jnp.bfloat16)
    f = lax.dot_general(
        q, fresh, (((1,), (1,)), ((), ())), preferred_element_type=jnp.float32
    )
    row = lax.broadcasted_iota(jnp.int32, f.shape, 0) % (SPEC * heads)
    key = lax.broadcasted_iota(jnp.int32, f.shape, 1)
    f = jnp.where(key <= row // heads, f * SCORE_SCALE, masked_value)

    starts = [((chip ^ partner(k, core)) * COPIES + core) * slots for k in range(owners)]
    s = block_scores(q, key_refs, starts, limit_ref)
    top = jnp.maximum(jnp.max(s, axis=1, keepdims=True), jnp.max(f, axis=1, keepdims=True))
    total, out = weigh(s, key_refs, top)
    w = jnp.exp(f - top)
    total += jnp.sum(w, axis=1, keepdims=True)
    out += jnp.dot(
        w.astype(jnp.bfloat16), fresh[:, :LATENT], preferred_element_type=jnp.float32
    )
    q_out[...] = q
    top_ref[...] = jnp.broadcast_to(top, top_ref.shape)
    total_ref[...] = jnp.broadcast_to(total, total_ref.shape)
    out_ref[...] = out


def finish_kernel(
    owners, per_device, limit_ref, q_ref, top_ref, total_ref, part_ref, pair_ref, *refs
):
    key_refs = [pair_ref.at[0], pair_ref.at[1], *refs[: owners - 2]]
    outs = refs[owners - 2 :]
    seq_index = lax.axis_index("seq")
    chip, core = seq_index // COPIES, seq_index % COPIES
    plane = lax.axis_index("head")
    slots = key_refs[0].shape[1]
    starts = [((chip ^ partner(k, 1 - core)) * COPIES + 1 - core) * slots for k in range(owners)]
    s = block_scores(q_ref[...], key_refs, starts, limit_ref)
    first = top_ref[:, :1]
    top = jnp.maximum(first, jnp.max(s, axis=1, keepdims=True))
    total, out = weigh(s, key_refs, top)
    scale = jnp.exp(first - top)
    total += total_ref[:, :1] * scale
    out += part_ref[...] * scale
    out = (out * (1.0 / total)).astype(jnp.bfloat16)
    piece = out.shape[0] // per_device
    sent_first = first_block(plane, chip, core)
    for k in range(per_device):
        for n in range(per_device):

            @pl.when(sent_first ^ k == n)
            def _():
                outs[k][...] = out[n * piece : (n + 1) * piece]


def project_kernel(per_device, w_ref, *refs):
    lat_refs, out_ref = refs[:-1], refs[-1]
    rows, heads, width = out_ref.shape
    first = first_back(lax.axis_index("seq") // COPIES, lax.axis_index("head"))
    parts = [jnp.where(first == a, lat_refs[1][...], lat_refs[0][...]) for a in range(per_device)]
    latent = jnp.concatenate(parts, axis=0)
    out = jnp.zeros((rows * heads, width), jnp.float32)
    own_head = lax.broadcasted_iota(jnp.int32, out.shape, 0) % heads
    step = 2 if heads % 2 == 0 else 1
    for h in range(0, heads, step):
        group = jnp.concatenate([w_ref[h + n] for n in range(step)], axis=1)
        product = jnp.dot(latent, group, preferred_element_type=jnp.float32)
        for n in range(step):
            out = jnp.where(own_head == h + n, product[:, n * width : (n + 1) * width], out)
    out_ref[...] = out.astype(out_ref.dtype).reshape(out_ref.shape)


def whole_sequences(seq_size, head_size, queries, new_latent, cache, lengths, w_uk, w_uv):
    rows, heads, q_width = queries.shape
    owners, slots, width = cache.shape
    per_device = rows // SPEC
    piece = SPEC * heads
    all_rows = per_device * piece
    params = pltpu.CompilerParams(vmem_limit_bytes=VMEM_LIMIT)
    vmem = pl.BlockSpec(memory_space=pltpu.VMEM)
    anywhere = pl.BlockSpec(memory_space=pl.ANY)
    both = ("seq", "head")
    devices = [(i, j) for i in range(seq_size) for j in range(head_size)]

    def flat(seq_index, head_index):
        return seq_index * head_size + head_index

    def in_hbm(x):
        return pltpu.with_memory_space_constraint(x, pltpu.HBM)

    def host(i, j):
        other = (i // COPIES) ^ (2 - ((j ^ (j >> 1)) & 1))
        return flat(((i % COPIES) * 2 + other // 2) * COPIES + other % 2, j)

    def owner(i, j, a):
        plane, chip = i // COPIES, i % COPIES * per_device + a
        return flat(chip * COPIES + 1 - j // 2, plane)

    def in_plane(move):
        return [(g * COPIES + t, move(g, t)) for g in range(owners) for t in range(COPIES)]

    *picked, packed, limit = pl.pallas_call(
        functools.partial(pick_kernel, per_device),
        out_shape=[jax.ShapeDtypeStruct((width, slots), cache.dtype)] * owners
        + [
            jax.ShapeDtypeStruct((all_rows, q_width + ROPE), queries.dtype),
            jax.ShapeDtypeStruct((8, slots), jnp.int32),
        ],
        in_specs=[anywhere] * 4,
        out_specs=[vmem] * (owners + 2),
        scratch_shapes=[
            pltpu.VMEM(queries.shape, queries.dtype),
            pltpu.VMEM(new_latent.shape, new_latent.dtype),
            pltpu.SMEM(lengths.shape, lengths.dtype),
            pltpu.SemaphoreType.DMA((3 + owners * COPY_PARTS,)),
        ],
        compiler_params=params,
        cost_estimate=LONG,
    )(*[in_hbm(x) for x in (jnp.swapaxes(cache, 1, 2), queries, new_latent, lengths)])
    moved = lax.ppermute(packed, both, [(flat(i, j), host(i, j)) for i, j in devices])
    own_keys = [picked[0]] + [
        lax.ppermute(picked[k], "seq", in_plane(lambda g, t: (g ^ partner(k, t)) * COPIES + t))
        for k in range(1, owners)
    ]
    pair = pl.pallas_call(
        pair_kernel,
        out_shape=jax.ShapeDtypeStruct((2, *picked[0].shape), cache.dtype),
        in_specs=[vmem] * 2,
        out_specs=vmem,
        scratch_shapes=[pltpu.SemaphoreType.DMA((2,))],
        compiler_params=params,
    )(*own_keys[:2])
    other_core = in_plane(lambda g, t: g * COPIES + 1 - t)
    far_keys = [lax.ppermute(keys, "seq", other_core) for keys in [pair] + own_keys[2:]]

    pieces = pl.pallas_call(
        functools.partial(absorb_kernel, per_device),
        out_shape=[jax.ShapeDtypeStruct((piece, width + ROPE), cache.dtype)] * per_device,
        in_specs=[vmem] * 2,
        out_specs=[vmem] * per_device,
        compiler_params=params,
        cost_estimate=LONG,
    )(w_uk, moved)
    arrived = [
        lax.ppermute(
            pieces[k],
            both,
            [(host(i, j), owner(i, j, leaves_as(k, j))) for i, j in devices],
        )
        for k in range(per_device)
    ]

    state = pl.pallas_call(
        functools.partial(begin_kernel, owners, per_device, heads),
        out_shape=[
            jax.ShapeDtypeStruct((all_rows, width), jnp.bfloat16),
            jax.ShapeDtypeStruct((all_rows, 128), jnp.float32),
            jax.ShapeDtypeStruct((all_rows, 128), jnp.float32),
            jax.ShapeDtypeStruct((all_rows, LATENT), jnp.float32),
        ],
        in_specs=[vmem] * (1 + per_device + owners),
        out_specs=[vmem] * 4,
        compiler_params=params,
        cost_estimate=LONG,
    )(limit, *arrived, *own_keys)
    latent = pl.pallas_call(
        functools.partial(finish_kernel, owners, per_device),
        out_shape=[jax.ShapeDtypeStruct((piece, LATENT), jnp.bfloat16)] * per_device,
        in_specs=[vmem] * (1 + len(state) + len(far_keys)),
        out_specs=[vmem] * per_device,
        compiler_params=params,
    )(limit, *state, *far_keys)

    back = [
        lax.ppermute(
            latent[k],
            both,
            [(owner(i, j, first_back(i // COPIES, j) ^ k), flat(i, j)) for i, j in devices],
        )
        for k in range(per_device)
    ]
    return pl.pallas_call(
        functools.partial(project_kernel, per_device),
        out_shape=jax.ShapeDtypeStruct((rows, heads, w_uv.shape[2]), jnp.bfloat16),
        in_specs=[vmem] * (1 + per_device),
        out_specs=vmem,
        compiler_params=params,
    )(w_uv, *back[::-1])


def local_partial(
    query_tile_block,
    key_tile_block,
    incoming_keys,
    len_block,
    offset,
    own_first,
    score_scale,
    head_count,
):
    scores = (
        jnp.einsum(
            "vfa,vja->vfj", query_tile_block, key_tile_block, preferred_element_type=jnp.float32
        )
        * score_scale
    )
    positions = offset + lax.broadcasted_iota(jnp.int32, (1, 1, key_tile_block.shape[1]), 2)
    visible = positions < len_block[:, None, None]
    fresh_scores = (
        jnp.einsum(
            "vfa,vja->vfj", query_tile_block, incoming_keys, preferred_element_type=jnp.float32
        )
        * score_scale
    )
    spec_count = incoming_keys.shape[1]
    row_spec = (
        lax.broadcasted_iota(jnp.int32, (1, query_tile_block.shape[1], spec_count), 1) // head_count
    )
    key_spec = lax.broadcasted_iota(jnp.int32, (1, query_tile_block.shape[1], spec_count), 2)
    causal = (key_spec <= row_spec) & own_first
    row_top = jnp.maximum(
        jnp.max(jnp.where(visible, scores, masked_value), axis=2),
        jnp.max(jnp.where(causal, fresh_scores, masked_value), axis=2),
    )
    weights = jnp.where(visible, jnp.exp(scores - row_top[..., None]), 0.0)
    fresh_weights = jnp.where(causal, jnp.exp(fresh_scores - row_top[..., None]), 0.0)
    running_totals = jnp.sum(weights, axis=2) + jnp.sum(fresh_weights, axis=2)
    weighted = jnp.einsum(
        "mpu,mui->mpi",
        weights.astype(jnp.bfloat16),
        key_tile_block[:, :, :LATENT],
        preferred_element_type=jnp.float32,
    )
    weighted = weighted + jnp.einsum(
        "mpu,mui->mpi",
        fresh_weights.astype(jnp.bfloat16),
        incoming_keys[:, :, :LATENT],
        preferred_element_type=jnp.float32,
    )
    return (row_top, running_totals, weighted)


def project_values(latent_rows, value_weight):
    return jnp.einsum("rhc,hcv->rhv", latent_rows, value_weight, precision=lax.Precision.HIGHEST)


def split_positions(queries, new_latent, cache, lengths, w_uk, w_uv):
    own_rows, head_count, _ = queries.shape
    score_scale = (NOPE + ROPE) ** (-0.5)
    gathered, new_all = (
        lax.all_gather(queries, "seq", axis=0, tiled=True),
        lax.all_gather(new_latent, "seq", axis=0, tiled=True),
    )
    absorbed = jnp.einsum(
        "rhn,hnc->rhc", gathered[:, :, :NOPE], w_uk, preferred_element_type=jnp.float32
    ).astype(jnp.bfloat16)
    q_all = jnp.concatenate([absorbed, gathered[:, :, NOPE:]], axis=2)
    total_rows = q_all.shape[0]
    seq_count = total_rows // SPEC
    query_slots = SPEC * head_count
    q_seq = q_all.reshape(seq_count, query_slots, q_all.shape[2])
    new_seq = new_all.reshape(seq_count, SPEC, new_all.shape[1])
    seq_index = lax.axis_index("seq")
    offset = seq_index * cache.shape[1]
    own_first = seq_index == 0
    row_top, running_totals, weighted = local_partial(
        q_seq,
        lax.all_gather(cache, "head", axis=0, tiled=True),
        new_seq,
        lengths,
        offset,
        own_first,
        score_scale,
        head_count,
    )
    value_weight = w_uv.astype(jnp.float32)
    global_top = lax.pmax(row_top, "seq")
    factor = jnp.exp(row_top - global_top)
    scaled_totals = (running_totals * factor).reshape(total_rows, head_count)
    scaled_weighted = (weighted * factor[..., None]).reshape(total_rows, head_count, LATENT)
    row_totals, row_weighted = (
        lax.psum_scatter(scaled_totals, "seq", scatter_dimension=0, tiled=True),
        lax.psum_scatter(scaled_weighted, "seq", scatter_dimension=0, tiled=True),
    )
    latent_output = row_weighted / row_totals[..., None]
    result = project_values(latent_output, value_weight)
    return result.astype(jnp.bfloat16)


def shards(seq_size, head_size, queries, new_latent, cache, lengths, w_uk, w_uv):
    rows, owners = queries.shape[0], cache.shape[0]
    per_device = rows // SPEC
    if (
        per_device == 2
        and rows % SPEC == 0
        and seq_size == COPIES * owners
        and head_size == owners == 4
        and cache.shape[2] % (16 * COPY_PARTS) == 0
    ):
        return whole_sequences(
            seq_size, head_size, queries, new_latent, cache, lengths, w_uk, w_uv
        )
    return split_positions(queries, new_latent, cache, lengths, w_uk, w_uv)


def solution(mesh):
    return jax.shard_map(
        functools.partial(shards, mesh.shape["seq"], mesh.shape["head"]),
        mesh=mesh,
        in_specs=(
            P("seq", "head", None),
            P("seq", None),
            P("head", "seq", None),
            P(),
            P("head", None, None),
            P("head", None, None),
        ),
        out_specs=P("seq", "head", None),
        check_vma=False,
    )
```
